128 devices in a mesh: ctx: 64 (over x, z_hi, y, core), fsdp: 2 (over z_lo).
Axes of the slice: x: 4, y: 4, z: 4 (z_hi: 2, z_lo: 2; z = z_hi * 2 + z_lo), core: 2. Of those that a mesh axis runs over, the one named last changes fastest.
Arguments:
- hidden: bfloat16 [16384, 960], P(('fsdp', 'ctx')), parts along dimension 0, may hold values from -16 to 16
- attn_gain: bfloat16 [1920], P(('fsdp', 'ctx')), parts along dimension 0, may hold values from 0.5 to 1.5
- w_q: bfloat16 [1920, 960], P(('fsdp', 'ctx')), parts along dimension 0, may hold values from -0.1875 to 0.1875
- w_k: bfloat16 [1920, 320], P(('fsdp', 'ctx')), parts along dimension 0, may hold values from -0.1875 to 0.1875
- w_v: bfloat16 [1920, 320], P(('fsdp', 'ctx')), parts along dimension 0, may hold values from -0.1875 to 0.1875
- w_o: bfloat16 [1920, 960], P(('fsdp', 'ctx')), parts along dimension 0, may hold values from -1.5 to 1.5
- mlp_gain: bfloat16 [1920], P(('fsdp', 'ctx')), parts along dimension 0, may hold values from 0.5 to 1.5
- w_gate: bfloat16 [1920, 2560], P(('fsdp', 'ctx')), parts along dimension 0, may hold values from -0.1875 to 0.1875
- w_up: bfloat16 [1920, 2560], P(('fsdp', 'ctx')), parts along dimension 0, may hold values from -0.1875 to 0.1875
- w_down: bfloat16 [5120, 960], P(('fsdp', 'ctx')), parts along dimension 0, may hold values from -0.125 to 0.125
- cotangent: bfloat16 [16384, 960], P(('fsdp', 'ctx')), parts along dimension 0, may hold values from -6 to 6
- doc_lengths: int32 [6], P('fsdp'), parts along dimension 0, may hold values from 1024 to 4096, as said below
- span_order: int32 [128], P('fsdp'), parts along dimension 0, may hold values from 0 to 63, as said below
Outputs:
- output: bfloat16 [16384, 960], P(('fsdp', 'ctx')), parts along dimension 0
- grad_hidden: bfloat16 [16384, 960], P(('fsdp', 'ctx')), parts along dimension 0
- grad_attn_gain: float32 [1920], P(('fsdp', 'ctx')), parts along dimension 0
- grad_w_q: float32 [1920, 960], P(('fsdp', 'ctx')), parts along dimension 0
- grad_w_k: float32 [1920, 320], P(('fsdp', 'ctx')), parts along dimension 0
- grad_w_v: float32 [1920, 320], P(('fsdp', 'ctx')), parts along dimension 0
- grad_w_o: float32 [1920, 960], P(('fsdp', 'ctx')), parts along dimension 0
- grad_mlp_gain: float32 [1920], P(('fsdp', 'ctx')), parts along dimension 0
- grad_w_gate: float32 [1920, 2560], P(('fsdp', 'ctx')), parts along dimension 0
- grad_w_up: float32 [1920, 2560], P(('fsdp', 'ctx')), parts along dimension 0
- grad_w_down: float32 [5120, 960], P(('fsdp', 'ctx')), parts along dimension 0
The draws below stay inside these ranges and needn't reach their ends.
There are 2 independent parts, one for each index of `fsdp`. The reference program is written for one: setup_inputs(seed, part) draws one part's arguments, and reference() takes and returns one part's arrays. A program takes and returns all parts, laid end to end along the dimension named above; each array names one. Nothing has to cross between parts.
Inputs may be any that keep to these rules, and one draw needn't show every extreme that they name: `doc_lengths`: the lengths of the 3 documents in stream order; they sum to 8192 and one of them has 4096 tokens. A permutation of the blocks: rows i * 128 to i * 128 + 127 of every token array are stream positions span_order[i] * 128 onward.
All inputs are finite; a program needn't handle non-finite values.
Results may differ from the reference program's by a relative error of at most 0.033.
Values may be sent and summed in bfloat16 or wider, within the bound.
A program may use at most 256 MiB of HBM per device.

```python
import jax
import jax.numpy as jnp
from jax import lax

D = 960
HEADS = 15
KV_HEADS = 5
HEAD = 64
FF = 2560
TOK_DEV = 128
DOCS = 3
GROUP = 3
SPANS = 64
TOKENS = 8192


def shared_layout(key):
    key_second, key_place, key_score, key_shuffle = jax.random.split(key, 4)
    half_len = TOKENS // 2
    second_len = jax.random.randint(key_second, (), TOKENS // 8, 3 * TOKENS // 8 + 1)
    third_len = half_len - second_len
    long_slot = jax.random.randint(key_place, (), 0, 3)
    doc_slots = jnp.arange(DOCS)
    lengths = jnp.where(doc_slots == long_slot, half_len, jnp.where(doc_slots == (long_slot + 1) % 3, second_len, third_len)).astype(jnp.int32)
    long_start = jnp.sum(jnp.where(doc_slots < long_slot, lengths, 0))
    span_ids = jnp.arange(SPANS)
    inside = (span_ids * TOK_DEV > long_start) & ((span_ids + 1) * TOK_DEV <= long_start + half_len)
    scores = jax.random.randint(key_score, (SPANS,), 0, 1 << 20) * SPANS + span_ids
    scores = jnp.where(inside, scores, scores + (1 << 28))
    ranking = jnp.argsort(scores)
    remaining = ranking[3:][jax.random.permutation(key_shuffle, SPANS - 3)]
    middle = SPANS // 2
    placed = jnp.concatenate([ranking[0:1], remaining[:middle - 1], ranking[1:2], remaining[middle - 1:], ranking[2:3]])
    return (lengths, placed.astype(jnp.int32))


def draw_doc_lengths(key, part):
    layout = shared_layout(key)
    return layout[0]


def draw_span_order(key, part):
    layout = shared_layout(key)
    return layout[1]


def strengthened(values, rng, source, target, blocks, factor):
    def block_of(position):
        return (jnp.arange(values.shape[position]) // (values.shape[position] // blocks)).reshape((-1,) + (1,) * (values.ndim - 1 - position))

    first = jax.random.permutation(rng, blocks)[block_of(target)]
    other_side = (block_of(target) + blocks // 2) % blocks
    return jnp.where((block_of(source) == first) | (block_of(source) == other_side), factor * values, values)


def block_levels(stream_key, extent, pieces, least, top_value):
    loudness = 1.0
    for axis_at, blocks in pieces:
        draws = jax.random.uniform(jax.random.fold_in(jax.random.fold_in(stream_key, 6), axis_at), (blocks,), jnp.float32, least / len(pieces), top_value / len(pieces))
        loudness = loudness * jnp.repeat(jnp.exp(draws), extent[axis_at] // blocks).reshape((-1,) + (1,) * (len(extent) - 1 - axis_at))
    return loudness


def noise(stream_key, extent, width, reach, shards=(), kind=jnp.bfloat16):
    entries = jax.random.normal(stream_key, extent, jnp.float32) * width
    if len(shards) > 0:
        entries = block_levels(stream_key, extent, shards, -0.22, 0.18) * entries
    return jnp.clip(entries, min=-reach, max=reach).astype(kind)


def bell_draw_with(own_key, dims, width, most, cuts, heavy, kind=jnp.bfloat16):
    values = width * jax.random.normal(own_key, dims, jnp.float32)
    if cuts:
        values = values * block_levels(own_key, dims, cuts, -0.22, 0.18)
    return jnp.clip(strengthened(values, jax.random.fold_in(own_key, 3), *heavy), -most, most).astype(kind)


def setup_inputs(seed: int = 0, part: int = 0) -> dict:
    seeds = jax.random.split(jax.random.key(seed), 14)
    part_keys = jax.random.split(jax.random.fold_in(seeds[13], part), 14)
    return {
        "hidden": bell_draw_with(part_keys[0], (TOKENS, D), 1.0, 16.0, ((0, 64),), (0, 1, 64, 4.0)),
        "attn_gain": jnp.clip(1.0 + 0.1 * jax.random.normal(part_keys[1], (D,), jnp.float32), 0.5, 1.5).astype(jnp.bfloat16),
        "w_q": noise(part_keys[2], (D, HEADS * HEAD), D ** -0.5, 0.1875, ((0, 64),)),
        "w_k": noise(part_keys[3], (D, KV_HEADS * HEAD), D ** -0.5, 0.1875, ((0, 64),)),
        "w_v": noise(part_keys[4], (D, KV_HEADS * HEAD), D ** -0.5, 0.1875, ((0, 64),)),
        "w_o": noise(part_keys[5], (HEADS * HEAD, D), (max(HEADS * HEAD // 64, 1)) ** -0.5, 1.5, ((0, 64),)),
        "mlp_gain": jnp.clip(1.0 + 0.1 * jax.random.normal(part_keys[6], (D,), jnp.float32), 0.5, 1.5).astype(jnp.bfloat16),
        "w_gate": noise(part_keys[7], (D, FF), D ** -0.5, 0.1875, ((0, 64),)),
        "w_up": noise(part_keys[8], (D, FF), D ** -0.5, 0.1875, ((0, 64),)),
        "w_down": noise(part_keys[9], (FF, D), FF ** -0.5, 0.125, ((0, 64),)),
        "cotangent": noise(part_keys[10], (TOKENS, D), 1.0, 6.0, ((0, 64),)),
        "doc_lengths": draw_doc_lengths(jax.random.fold_in(jax.random.fold_in(seeds[13], part), 71), part),
        "span_order": draw_span_order(jax.random.fold_in(jax.random.fold_in(seeds[13], part), 71), part),
    }


EPSILON = 1e-05
ROPE_BASE = 100000.0
MASKED_SCORE = -1e+30

@jax.custom_vjp
def low(v):
    return lax.optimization_barrier(v.astype(jnp.bfloat16)).astype(jnp.float32)

@jax.custom_vjp
def low_back(v):
    return v

def low_keep(v):
    return (low(v), None)

def low_pass(kept, grad):
    return (grad,)

def back_keep(v):
    return (v, None)

def back_low(kept, grad):
    return (low(grad),)
low.defvjp(low_keep, low_pass)
low_back.defvjp(back_keep, back_low)

def matmul_high(left, right):
    return jnp.dot(left, right, precision=lax.Precision.HIGHEST, preferred_element_type=jnp.float32)

def locate_rows(doc_lengths, span_order):
    row_ids = jnp.arange(TOKENS, dtype=jnp.int32)
    stream = span_order[row_ids // TOK_DEV] * TOK_DEV + row_ids % TOK_DEV
    first_end = doc_lengths[0]
    second_end = doc_lengths[0] + doc_lengths[1]
    document = (stream >= first_end).astype(jnp.int32) + (stream >= second_end).astype(jnp.int32)
    doc_start = jnp.where(document == 0, 0, jnp.where(document == 1, first_end, second_end)).astype(jnp.int32)
    return (stream, document, stream - doc_start)

def rope_tables(place):
    halves = jnp.arange(HEAD // 2, dtype=jnp.float32)
    frequency = ROPE_BASE ** (-2.0 * halves / HEAD)
    angles = place.astype(jnp.float32)[:, None] * frequency[None, :]
    return (jnp.cos(angles)[:, None, :], jnp.sin(angles)[:, None, :])

def rotate(head_rows, cos_table, sin_table):
    half_size = head_rows.shape[-1] // 2
    first_half = head_rows[..., :half_size]
    second_half = head_rows[..., half_size:]
    return jnp.concatenate([first_half * cos_table - second_half * sin_table, second_half * cos_table + first_half * sin_table], axis=-1)

def attend(q_rot, k_rot, value_rows, stream, document):
    block_len = min(256, TOKENS)
    blocks = TOKENS // block_len
    scale = HEAD ** (-0.5)
    query_blocks = q_rot.reshape(blocks, block_len, KV_HEADS, GROUP, HEAD)

    def query_block(packed):
        block_query, block_stream, block_doc = packed
        raw_scores = jnp.einsum('tkgd,skd->tkgs', block_query, k_rot, precision=lax.Precision.HIGHEST)
        scores = low_back(raw_scores) * scale
        allowed = (document[None, :] == block_doc[:, None]) & (stream[None, :] <= block_stream[:, None])
        scores = jnp.where(allowed[:, None, None, :], scores, MASKED_SCORE)
        highest = lax.optimization_barrier(jnp.max(scores, axis=3, keepdims=True))
        weights = jnp.exp(scores - highest)
        weights = weights / lax.optimization_barrier(jnp.sum(weights, axis=3, keepdims=True))
        return jnp.einsum('tkgs,skd->tkgd', low(weights), value_rows, precision=lax.Precision.HIGHEST)
    attended = lax.map(jax.checkpoint(query_block), (query_blocks, stream.reshape(blocks, block_len), document.reshape(blocks, block_len)))
    return attended.reshape(TOKENS, HEADS * HEAD)

def reference(hidden, attn_gain, w_q, w_k, w_v, w_o, mlp_gain, w_gate, w_up, w_down, cotangent, doc_lengths, span_order):
    stream, document, place = locate_rows(doc_lengths, span_order)
    cos_table, sin_table = rope_tables(place)

    def layer(inputs, gain_attn, query_weight, key_weight, value_weight, out_weight, gain_mlp, gate_weight, up_weight, down_weight):
        inv_one = lax.rsqrt(lax.optimization_barrier(jnp.mean(inputs * inputs, axis=1, keepdims=True)) + EPSILON)
        normed = low(inputs * inv_one * gain_attn)
        query = low_back(matmul_high(normed, query_weight)).reshape(TOKENS, HEADS, HEAD)
        key_rows = low_back(matmul_high(normed, key_weight)).reshape(TOKENS, KV_HEADS, HEAD)
        value_rows = low(low_back(matmul_high(normed, value_weight))).reshape(TOKENS, KV_HEADS, HEAD)
        q_rot = low(rotate(query, cos_table, sin_table))
        k_rot = low(rotate(key_rows, cos_table, sin_table))
        attended = attend(q_rot, k_rot, value_rows, stream, document)
        attn_in = low(low_back(attended))
        resid = inputs + low_back(matmul_high(attn_in, out_weight))
        inv_two = lax.rsqrt(lax.optimization_barrier(jnp.mean(resid * resid, axis=1, keepdims=True)) + EPSILON)
        mnormed = low(resid * inv_two * gain_mlp)
        gate = low_back(matmul_high(mnormed, gate_weight))
        up_rows = low_back(matmul_high(mnormed, up_weight))
        act = low(jax.nn.silu(gate) * up_rows)
        return resid + matmul_high(act, down_weight)
    floats = (hidden.astype(jnp.float32), attn_gain.astype(jnp.float32), w_q.astype(jnp.float32), w_k.astype(jnp.float32), w_v.astype(jnp.float32), w_o.astype(jnp.float32), mlp_gain.astype(jnp.float32), w_gate.astype(jnp.float32), w_up.astype(jnp.float32), w_down.astype(jnp.float32))
    result, pullback = jax.vjp(layer, *floats)
    grads = pullback(cotangent.astype(jnp.float32))
    return (result.astype(jnp.bfloat16), grads[0].astype(jnp.bfloat16), grads[1], grads[2], grads[3], grads[4], grads[5], grads[6], grads[7], grads[8], grads[9])
```

```python
import jax
import jax.numpy as jnp
from jax import lax
from jax.experimental import pallas as pl
from jax.experimental.pallas import tpu as pltpu
from jax.sharding import PartitionSpec as P

HEAD = 64
EPSILON = 1e-05
ROPE_BASE = 100000.0
MASKED = -1e30
WIDE = 1024
WIDTH = 960
BF = jnp.bfloat16
F32 = jnp.float32
MESH = pl.DeviceIdType.MESH
DMA = pltpu.SemaphoreType.DMA
ANY = pl.BlockSpec(memory_space=pl.ANY)
VMEM = pl.BlockSpec(memory_space=pltpu.VMEM)
SMEM = pl.BlockSpec(memory_space=pltpu.SMEM)
LIMIT = 56 * 2**20
TILE = 4
OWNED_KV = (0, 1, 1, 2, 2, 3, 4, 4)
SELECT = ((0, 0), (0, 1), (0, 0), (1, 1), (0, 1), (1, 1), (0, 0), (0, 0))


def dot(a, b):
    return lax.dot_general(a, b, (((1,), (0,)), ((), ())), preferred_element_type=F32)


def dot_nt(a, b):
    return lax.dot_general(a, b, (((1,), (1,)), ((), ())), preferred_element_type=F32)


def dot_tn(a, b):
    return lax.dot_general(a, b, (((0,), (0,)), ((), ())), preferred_element_type=F32)


def shaped(shape, dtype):
    return jax.ShapeDtypeStruct(shape, dtype)


def place():
    i = lax.axis_index("ctx")
    return i // 16, (i // 8) % 2, (i // 2) % 4, i % 2


def at(x, z, y, c):
    return {"ctx": (((x + 4) % 4) * 2 + z) * 8 + ((y + 4) % 4) * 2 + c}


def send(src, dst, ssem, rsem, device):
    copy = pltpu.make_async_remote_copy(
        src, dst, ssem, rsem, device_id=device, device_id_type=MESH
    )
    copy.start()
    return copy


def greet(kinds):
    x, z, y, c = place()
    who = []
    if "x" in kinds:
        who += [at(x + 1, z, y, c), at(x - 1, z, y, c), at(x, 1 - z, y, c)]
    if "f" in kinds:
        who += [at(x, z, y + d, (c + e) % 2) for d in range(4) for e in range(2) if d + e]
    elif "y" in kinds:
        who += [at(x, z, y + d, c) for d in (1, 2, 3)] + [at(x, z, y, 1 - c)]
    elif "s" in kinds:
        who += [at(x, z, y, 1 - c)]
    barrier = pltpu.get_barrier_semaphore()
    for device in who:
        pl.semaphore_signal(barrier, inc=1, device_id=device, device_id_type=MESH)
    pl.semaphore_wait(barrier, len(who))


def half_lead(ref, k):
    n = ref.shape[0] // 2
    return ref.at[pl.ds(k * n, n)]


def half_lanes(ref, k):
    n = ref.shape[-1] // 2
    return ref.at[:, pl.ds(k * n, n)]


class RingGather:
    sems = [DMA((9,)), DMA((9,)), DMA(())]

    def __init__(self, src, dst, half, ssem, rsem, lsem, arrived=None):
        self.src, self.dst, self.half = src, dst, half
        self.ssem, self.rsem, self.lsem = ssem, rsem, lsem
        self.arrived = arrived or (lambda block: None)
        self.copies = {}

    def push(self, n, src, dst, device):
        self.copies[n] = send(src, dst, self.ssem.at[n], self.rsem.at[n], device)

    def start(self):
        x, z, y, c = place()
        me = self.dst.at[x * 2 + z]
        self.push(0, self.src, me, at(x, 1 - z, y, c))
        self.push(1, self.src, me, at(x + 1, z, y, c))
        self.push(2, self.src, me, at(x - 1, z, y, c))
        self.local = pltpu.make_async_copy(self.src, me, self.lsem)
        self.local.start()

    def relay_z(self):
        x, z, y, c = place()
        block = self.dst.at[x * 2 + 1 - z]
        self.copies[0].wait_recv()
        self.push(3, block, block, at(x + 1, z, y, c))
        self.push(4, block, block, at(x - 1, z, y, c))
        self.arrived(x * 2 + 1 - z)

    def relay_x(self, k):
        x, z, y, c = place()
        zz = z if k == 0 else 1 - z
        left, right = ((x + 3) % 4) * 2 + zz, ((x + 1) % 4) * 2 + zz
        self.copies[1 + 2 * k].wait_recv()
        part = self.half(self.dst.at[left], 0)
        self.push(5 + 2 * k, part, part, at(x + 1, z, y, c))
        self.arrived(left)
        self.copies[2 + 2 * k].wait_recv()
        part = self.half(self.dst.at[right], 1)
        self.push(6 + 2 * k, part, part, at(x - 1, z, y, c))
        self.arrived(right)

    def land(self, k):
        x, z, y, c = place()
        zz = z if k == 0 else 1 - z
        self.copies[5 + 2 * k].wait_recv()
        self.copies[6 + 2 * k].wait_recv()
        self.arrived(((x + 2) % 4) * 2 + zz)

    def finish(self):
        self.local.wait()
        for n in range(9):
            self.copies[n].wait_send()


def run_ring_gathers(rings):
    for ring in rings:
        ring.relay_z()
    for k in (0, 1):
        for ring in rings:
            ring.relay_x(k)
    for k in (0, 1):
        for ring in rings:
            ring.land(k)


class RowGather:
    sems = [DMA((8,)), DMA((8,)), DMA(())]

    def __init__(self, src, dst, ssem, rsem, lsem):
        self.src, self.dst = src, dst
        self.ssem, self.rsem, self.lsem = ssem, rsem, lsem
        self.copies = {}

    def push(self, n, src, dst, device):
        self.copies[n] = send(src, dst, self.ssem.at[n], self.rsem.at[n], device)

    def start(self):
        x, z, y, c = place()
        me = self.dst.at[y * 2 + c]
        for d in (1, 3, 2):
            self.push(d, self.src, me, at(x, z, y + d, c))
        self.push(0, self.src, me, at(x, z, y, 1 - c))
        self.local = pltpu.make_async_copy(self.src, me, self.lsem)
        self.local.start()

    def relay(self):
        x, z, y, c = place()
        for d in (1, 3, 2):
            self.copies[d].wait_recv()
            block = self.dst.at[((y - d + 4) % 4) * 2 + c]
            self.push(4 + d, block, block, at(x, z, y, 1 - c))

    def finish(self):
        self.local.wait()
        for n in (0, 5, 7, 6):
            self.copies[n].wait_recv()
        for n in (0, 1, 2, 3, 5, 6, 7):
            self.copies[n].wait_send()


class Swap:
    sems = [DMA((8,)), DMA((8,)), DMA(())]

    def __init__(self, src, dst, ssem, rsem, lsem):
        self.src, self.dst = src, dst
        self.ssem, self.rsem, self.lsem = ssem, rsem, lsem

    def start(self):
        x, z, y, c = place()
        me = y * 2 + c
        self.copies = []
        for d in (2, 1, 3, 0):
            for e in (0, 1):
                if d + e:
                    n = d * 2 + e
                    to = ((y + d) % 4) * 2 + (c + e) % 2
                    self.copies.append(
                        send(
                            self.src.at[to],
                            self.dst.at[me],
                            self.ssem.at[n],
                            self.rsem.at[n],
                            at(x, z, y + d, (c + e) % 2),
                        )
                    )
        self.local = pltpu.make_async_copy(self.src.at[me], self.dst.at[me], self.lsem)
        self.local.start()

    def finish(self):
        self.local.wait()
        for copy in self.copies:
            copy.wait()


class RowSum:
    @staticmethod
    def scratch(shape):
        return [
            pltpu.VMEM((4,) + shape, BF),
            pltpu.VMEM((4,) + shape, BF),
            pltpu.VMEM((4,) + shape, BF),
            DMA((8,)),
            DMA((8,)),
        ]

    def __init__(self, blk, first, mixed, second, ssem, rsem):
        self.blk, self.first, self.mixed, self.second = blk, first, mixed, second
        self.ssem, self.rsem = ssem, rsem
        self.copies = {}

    def push(self, n, src, dst, device):
        self.copies[n] = send(src, dst, self.ssem.at[n], self.rsem.at[n], device)

    def start(self):
        x, z, y, c = place()
        for d in (2, 1, 3, 0):
            to = ((y + d) % 4) * 2 + 1 - c
            self.push(d, self.blk.at[to], self.first.at[d], at(x, z, y, 1 - c))

    def relay(self):
        x, z, y, c = place()
        for d in (2, 1, 3):
            self.copies[d].wait_recv()
            own = self.blk[((y + d) % 4) * 2 + c].astype(F32)
            self.mixed[d] = (own + self.first[d].astype(F32)).astype(BF)
            self.push(4 + d, self.mixed.at[d], self.second.at[d], at(x, z, y + d, c))

    def total(self):
        x, z, y, c = place()
        self.copies[0].wait_recv()
        total = self.blk[y * 2 + c].astype(F32) + self.first[0].astype(F32)
        for d in (1, 3, 2):
            self.copies[4 + d].wait_recv()
            total = total + self.second[d].astype(F32)
        return total

    def finish(self):
        for n in (0, 1, 2, 3, 5, 6, 7):
            self.copies[n].wait_send()


class RingSum:
    @staticmethod
    def scratch(shape, lanes):
        if lanes:
            part = shape[:-1] + (shape[-1] // 2,)
        else:
            part = (shape[0] // 2,) + shape[1:]
        return [
            pltpu.VMEM((4,) + part, BF),
            pltpu.VMEM((4,) + shape, BF),
            pltpu.VMEM((4,) + shape, BF),
            pltpu.VMEM((2,) + shape, BF),
            DMA((9,)),
            DMA((9,)),
        ]

    def __init__(self, blk, lanes, parts, mixed, heard, across, ssem, rsem):
        self.blk, self.half = blk, half_lanes if lanes else half_lead
        self.parts, self.mixed, self.heard, self.across = parts, mixed, heard, across
        self.ssem, self.rsem = ssem, rsem
        self.copies = {}

    def push(self, n, src, dst, device):
        self.copies[n] = send(src, dst, self.ssem.at[n], self.rsem.at[n], device)

    def start(self, k):
        x, z, y, c = place()
        zz = 1 - z if k == 0 else z
        far = self.blk.at[((x + 2) % 4) * 2 + zz]
        self.push(4 * k, self.half(far, 0), self.parts.at[2 * k], at(x + 1, z, y, c))
        self.push(4 * k + 1, self.half(far, 1), self.parts.at[2 * k + 1], at(x - 1, z, y, c))

    def relay(self, k):
        x, z, y, c = place()
        zz = 1 - z if k == 0 else z
        for side, step in ((0, 1), (1, 3)):
            n = 2 * k + side
            mixed = self.mixed.at[n]
            source = self.blk.at[((x + step) % 4) * 2 + zz]
            mine, other = self.half(source, side), self.half(source, 1 - side)
            self.half(mixed, 1 - side)[...] = other[...]
            self.copies[4 * k + side].wait_recv()
            self.half(mixed, side)[...] = (
                mine[...].astype(F32) + self.parts[n].astype(F32)
            ).astype(BF)
            self.push(4 * k + 2 + side, mixed, self.heard.at[n], at(x + step, z, y, c))

    def total(self, k):
        x, z, y, c = place()
        zz = 1 - z if k == 0 else z
        total = self.blk[x * 2 + zz].astype(F32)
        for side in (0, 1):
            self.copies[4 * k + 2 + side].wait_recv()
            total = total + self.heard[2 * k + side].astype(F32)
        if k == 0:
            self.across[0] = total.astype(BF)
            self.push(8, self.across.at[0], self.across.at[1], at(x, 1 - z, y, c))
            return None
        self.copies[8].wait_recv()
        return total + self.across[1].astype(F32)

    def finish(self):
        for n in range(9):
            self.copies[n].wait_send()


def comm_call(name, number, kernel, out_shape, in_specs, out_specs, scratch, args):
    return pl.pallas_call(
        kernel,
        out_shape=out_shape,
        in_specs=in_specs,
        out_specs=out_specs,
        scratch_shapes=scratch,
        compiler_params=pltpu.CompilerParams(
            collective_id=number, has_side_effects=True, vmem_limit_bytes=LIMIT
        ),
        name=name,
    )(*args)


def split(refs, counts):
    parts, begin = [], 0
    for n in counts:
        parts.append(refs[begin : begin + n])
        begin += n
    return parts


def gather_first(xp, wp1, wp2, wo):
    def kernel(xp, wp1, wp2, wo, rows, w1, w2own, wos, w1own, *sems):
        a, b, b2, d, e = split(sems, (3, 3, 3, 3, 3))
        greet("xf")
        swap = Swap(wp1, w1own, *b)
        swap2 = Swap(wp2, w2own, *b2)
        gather = RowGather(xp, rows, *a)
        ring_o = RingGather(wo, wos, half_lanes, *e)
        swap.start()
        gather.start()
        ring_o.start()
        swap2.start()
        swap.finish()
        ring_1 = RingGather(w1own, w1, half_lead, *d)
        ring_1.start()
        gather.relay()
        run_ring_gathers([ring_1, ring_o])
        swap2.finish()
        gather.finish()
        ring_1.finish()
        ring_o.finish()

    return comm_call(
        "gather_first",
        1,
        kernel,
        (
            shaped((8, 128, WIDE), BF),
            shaped((8, 8, 16, 384), BF),
            shaped((8, 16, 768), BF),
            shaped((8, 16, WIDE), BF),
        ),
        [ANY] * 4,
        (ANY,) * 4,
        [pltpu.VMEM((8, 16, 384), BF)]
        + RowGather.sems
        + Swap.sems
        + Swap.sems
        + RingGather.sems
        + RingGather.sems,
        (xp, wp1, wp2, wo),
    )


def gather_keys(kv, wos, cp):
    def kernel(kv, wos, cp, kv2, wo, cot, *sems):
        a, b, d, (hs, hr) = split(sems, (3, 3, 3, 2))
        x, z, y, c = place()
        greet("xy")
        hand = []

        def arrived(block):
            n = len(hand)
            piece = kv2.at[c, block]
            hand.append(send(piece, piece, hs.at[n], hr.at[n], at(x, z, y, 1 - c)))

        ring = RingGather(kv, kv2.at[c], half_lead, *a, arrived=arrived)
        gather_o = RowGather(wos, wo, *b)
        gather_c = RowGather(cp, cot, *d)
        ring.start()
        gather_o.start()
        gather_c.start()
        me = kv2.at[c, x * 2 + z]
        hand.append(send(kv, me, hs.at[0], hr.at[0], at(x, z, y, 1 - c)))
        ring.relay_z()
        ring.relay_x(0)
        gather_o.relay()
        ring.relay_x(1)
        gather_c.relay()
        ring.land(0)
        ring.land(1)
        for copy in hand:
            copy.wait()
        gather_o.finish()
        gather_c.finish()
        ring.finish()

    return comm_call(
        "gather_keys",
        2,
        kernel,
        (
            shaped((2, 8, 1024, 128), BF),
            shaped((8, 8, 16, WIDE), BF),
            shaped((8, 128, WIDE), BF),
        ),
        [ANY] * 3,
        (ANY,) * 3,
        RingGather.sems + RowGather.sems + RowGather.sems + [DMA((8,)), DMA((8,))],
        (kv, wos, cp),
    )


def gather_heads(att, w2own, wd):
    def kernel(att, w2own, wd, atts, w2, wds, *sems):
        a, b, d = split(sems, (3, 3, 3))
        greet("xy")
        gather = RowGather(att, atts, *a)
        ring_2 = RingGather(w2own, w2, half_lead, *b)
        ring_d = RingGather(wd, wds, half_lanes, *d)
        gather.start()
        ring_2.start()
        ring_d.start()
        gather.relay()
        run_ring_gathers([ring_2, ring_d])
        gather.finish()
        ring_2.finish()
        ring_d.finish()

    return comm_call(
        "gather_heads",
        3,
        kernel,
        (
            shaped((8, 1024, 128), BF),
            shaped((8, 8, 16, 768), BF),
            shaped((8, 48, WIDE), BF),
        ),
        [ANY] * 3,
        (ANY,) * 3,
        RowGather.sems + RingGather.sems + RingGather.sems,
        (att, w2own, wd),
    )


def sum_feed(dmn, gw2, gwd):
    def kernel(dmn, gw2, gwd, dmn_sum, gw2_sum, gwd_sum, *refs):
        a, b, d = split(refs, (5, 6, 6))
        greet("xy")
        rows = RowSum(dmn, *a)
        ring_2 = RingSum(gw2, False, *b)
        ring_d = RingSum(gwd, True, *d)
        rows.start()
        for k in (0, 1):
            ring_2.start(k)
            ring_d.start(k)
        rows.relay()
        for k in (0, 1):
            ring_2.relay(k)
            ring_d.relay(k)
        dmn_sum[...] = rows.total()
        ring_2.total(0)
        ring_d.total(0)
        gw2_sum[...] = ring_2.total(1).astype(BF)
        gwd_sum[...] = ring_d.total(1)
        rows.finish()
        ring_2.finish()
        ring_d.finish()

    return comm_call(
        "sum_feed",
        4,
        kernel,
        (shaped((128, WIDE), F32), shaped((8, 16, 896), BF), shaped((48, WIDE), F32)),
        [VMEM] * 3,
        (VMEM,) * 3,
        RowSum.scratch((128, WIDE))
        + RingSum.scratch((8, 16, 896), False)
        + RingSum.scratch((48, WIDE), True),
        (dmn, gw2, gwd),
    )


def swap_heads(d_att):
    def kernel(d_att, out, *sems):
        greet("f")
        swap = Swap(d_att, out, *sems)
        swap.start()
        swap.finish()

    return comm_call(
        "swap_heads", 5, kernel, shaped((8, 128, 128), BF), [ANY], ANY, Swap.sems, (d_att,)
    )


def sum_keys(dkv, outp, gwo):
    def kernel(dkv, outp, gwo, dkv_sum, out_sum, gwo_sum, blk, from_core, hs, hr, *refs):
        a, b, d = split(refs, (6, 5, 5))
        x, z, y, c = place()
        greet("xy")
        order = [(2, 1), (2, 0), (1, 1), (3, 1), (1, 0), (3, 0), (0, 1), (0, 0)]
        where = [((x + p) % 4) * 2 + (1 - z if q else z) for p, q in order]
        hand = [
            send(dkv.at[1 - c, g], from_core.at[n], hs.at[n], hr.at[n], at(x, z, y, 1 - c))
            for n, g in enumerate(where)
        ]
        rows_o = RowSum(outp, *b)
        rows_w = RowSum(gwo, *d)
        rows_o.start()
        rows_w.start()
        ring = RingSum(blk, False, *a)

        def fold(n):
            g = where[n]
            hand[n].wait_recv()
            blk[g] = (dkv[c, g].astype(F32) + from_core[n].astype(F32)).astype(BF)

        fold(0)
        ring.start(0)
        fold(1)
        ring.start(1)
        rows_o.relay()
        for n in range(2, 8):
            fold(n)
        ring.relay(0)
        ring.relay(1)
        rows_w.relay()
        ring.total(0)
        dkv_sum[...] = ring.total(1)
        out_sum[...] = rows_o.total()
        gwo_sum[...] = rows_w.total().astype(BF)
        for copy in hand:
            copy.wait_send()
        ring.finish()
        rows_o.finish()
        rows_w.finish()

    return comm_call(
        "sum_keys",
        6,
        kernel,
        (shaped((1024, 128), F32), shaped((128, WIDE), F32), shaped((128, WIDE), BF)),
        [VMEM] * 3,
        (VMEM,) * 3,
        [pltpu.VMEM((8, 1024, 128), BF), pltpu.VMEM((8, 1024, 128), BF), DMA((8,)), DMA((8,))]
        + RingSum.scratch((1024, 128), False)
        + RowSum.scratch((128, WIDE))
        + RowSum.scratch((128, WIDE)),
        (dkv, outp, gwo),
    )


def sum_normed(dn, gw1, gwo):
    def kernel(dn, gw1, gwo, dn_sum, gw1_sum, gwo_sum, *refs):
        a, b, d = split(refs, (5, 6, 6))
        greet("xy")
        rows = RowSum(dn, *a)
        ring_1 = RingSum(gw1, False, *b)
        ring_o = RingSum(gwo, True, *d)
        rows.start()
        for k in (0, 1):
            ring_1.start(k)
            ring_o.start(k)
        rows.relay()
        for k in (0, 1):
            ring_1.relay(k)
            ring_o.relay(k)
        ring_1.total(0)
        ring_o.total(0)
        gw1_sum[...] = ring_1.total(1).astype(BF)
        gwo_sum[...] = ring_o.total(1)
        dn_sum[...] = rows.total()
        rows.finish()
        ring_1.finish()
        ring_o.finish()

    return comm_call(
        "sum_normed",
        7,
        kernel,
        (shaped((128, WIDE), F32), shaped((8, 16, 384), BF), shaped((16, WIDE), F32)),
        [VMEM] * 3,
        (VMEM,) * 3,
        RowSum.scratch((128, WIDE))
        + RingSum.scratch((8, 16, 384), False)
        + RingSum.scratch((16, WIDE), True),
        (dn, gw1, gwo),
    )


def swap_grads(gw1, gw2):
    def kernel(gw1, gw2, out1, out2, *sems):
        a, b = split(sems, (3, 3))
        greet("f")
        one, two = Swap(gw1, out1, *a), Swap(gw2, out2, *b)
        one.start()
        two.start()
        one.finish()
        two.finish()

    return comm_call(
        "swap_grads",
        8,
        kernel,
        (shaped((8, 16, 384), BF), shaped((8, 16, 896), BF)),
        [ANY] * 2,
        (ANY,) * 2,
        Swap.sems + Swap.sems,
        (gw1, gw2),
    )


def lanes_of(shape):
    return lax.broadcasted_iota(jnp.int32, shape, len(shape) - 1)


def partner(v):
    lane = lanes_of(v.shape)
    return jnp.where(lane % 64 < 32, pltpu.roll(v, 96, 1), pltpu.roll(v, 32, 1))


def project(rows, w1, cos_t, sin_t):
    def kernel(x_ref, w_ref, cos_ref, sin_ref, n_ref, q_ref, kv_ref, g_ref):
        @pl.when(pl.program_id(0) == 0)
        def _():
            eye = (
                lax.broadcasted_iota(jnp.int32, (8, 128), 0) == lanes_of((8, 128))
            ).astype(BF)
            g_ref[...] = dot_nt(eye, w_ref[:, 256:384])

        x = x_ref[...].astype(F32)
        inv = lax.rsqrt(jnp.sum(x * x, axis=1, keepdims=True) * (1.0 / WIDTH) + EPSILON)
        normed = (x * inv * g_ref[0:1, :]).astype(BF)
        n_ref[...] = normed
        out = dot(normed, w_ref[:, 0:256])
        cos_v, sin_v = cos_ref[...], sin_ref[...]
        lane = lanes_of((128, 128))
        q, kv = out[:, 0:128], out[:, 128:256]
        q = (q * cos_v + partner(q) * sin_v).astype(BF).astype(F32) * 0.125
        k = kv * cos_v + partner(kv) * sin_v
        kv_ref[...] = jnp.where(lane < 64, k, kv).astype(BF)
        q_ref[0] = jnp.where(lane < 64, q, 0.0).astype(BF)
        q_ref[1] = jnp.where(lane < 64, pltpu.roll(q, 64, 1), 0.0).astype(BF)

    block = lambda w: pl.BlockSpec((128, w), lambda i: (i, 0))
    return pl.pallas_call(
        kernel,
        grid=(8,),
        out_shape=(
            shaped((1024, WIDE), BF),
            shaped((2, 1024, 128), BF),
            shaped((1024, 128), BF),
            shaped((8, WIDE), F32),
        ),
        in_specs=[block(WIDE), pl.BlockSpec((WIDE, 384), lambda i: (0, 0)), block(128), block(128)],
        out_specs=(
            block(WIDE),
            pl.BlockSpec((2, 128, 128), lambda i: (0, i, 0)),
            block(128),
            pl.BlockSpec((8, WIDE), lambda i: (0, 0)),
        ),
        compiler_params=pltpu.CompilerParams(vmem_limit_bytes=LIMIT),
        name="project",
    )(rows, w1, cos_t, sin_t)


def doc_start(pos, ends):
    return jnp.where(pos < ends[0], 0, jnp.where(pos < ends[1], ends[0], ends[1]))


def span_range(span, ends):
    begin = doc_start(span * 128, ends) // 128
    return begin, (span - begin + TILE) // TILE


def attend(inverse, spans, select, ends, q, kv):
    keys = TILE * 128

    def kernel(inverse, spans, select, ends, q_ref, kv_ref, o_ref, lse_ref, s_ref):
        span = spans[pl.program_id(0)]
        begin, count = span_range(span, ends)
        pos = span * 128 + lax.broadcasted_iota(jnp.int32, (128, 1), 0)
        low = doc_start(pos, ends)
        lane = lanes_of((128, 128))
        sel = (select[0], select[1])
        qs = (q_ref[0], q_ref[1])

        def load(h, j):
            t = begin + j * TILE
            return jnp.concatenate(
                [
                    kv_ref[sel[h], pl.ds(inverse[jnp.minimum(t + i, 63)] * 128, 128), :]
                    for i in range(TILE)
                ],
                axis=0,
            )

        def cols(j):
            return pl.ds(pl.multiple_of(j * keys, keys), keys)

        def fold(op, v):
            out = v[:, 0:128]
            for i in range(1, TILE):
                out = op(out, v[:, i * 128 : (i + 1) * 128])
            return out

        def scores(j, high):
            kpos = (begin + j * TILE) * 128 + lanes_of((1, keys))
            allowed = (kpos >= low) & (kpos <= pos)
            out = []
            for h in (0, 1):
                s = jnp.where(allowed, dot_nt(qs[h], load(h, j)), MASKED)
                s_ref[h, :, cols(j)] = s
                out.append(jnp.maximum(high[h], fold(jnp.maximum, s)))
            return tuple(out)

        start = jnp.full((128, 128), MASKED, F32)
        high = lax.fori_loop(0, count, scores, (start, start))
        high = [jnp.max(v, axis=1, keepdims=True) for v in high]

        def weigh(j, state):
            out = []
            for h in (0, 1):
                total, acc = state[h]
                p = jnp.exp(s_ref[h, :, cols(j)] - high[h])
                out.append((total + fold(jnp.add, p), acc + dot(p.astype(BF), load(h, j))))
            return tuple(out)

        zero = jnp.zeros((128, 128), F32)
        state = lax.fori_loop(0, count, weigh, ((zero, zero), (zero, zero)))
        outs = []
        for h in (0, 1):
            total = jnp.sum(state[h][0], axis=1, keepdims=True)
            outs.append(state[h][1] / total)
            lse = jnp.broadcast_to(high[h] + jnp.log(total), (128, 128))
            lse_ref[0, h : h + 1, :] = lse.T[0:1, :]
        o_ref[...] = jnp.where(lane < 64, pltpu.roll(outs[0], 64, 1), outs[1]).astype(BF)

    return pl.pallas_call(
        kernel,
        grid_spec=pltpu.PrefetchScalarGridSpec(
            num_scalar_prefetch=4,
            grid=(8,),
            in_specs=[
                pl.BlockSpec((2, 128, 128), lambda i, *_: (0, i, 0)),
                pl.BlockSpec((2, 8192, 128), lambda i, *_: (0, 0, 0)),
            ],
            out_specs=(
                pl.BlockSpec((128, 128), lambda i, *_: (i, 0)),
                pl.BlockSpec((1, 8, 128), lambda i, *_: (i, 0, 0)),
            ),
            scratch_shapes=[pltpu.VMEM((2, 128, 9 * keys), F32)],
        ),
        out_shape=(shaped((1024, 128), BF), shaped((8, 8, 128), F32)),
        compiler_params=pltpu.CompilerParams(vmem_limit_bytes=LIMIT),
        name="attend",
    )(inverse, spans, select, ends, q, kv)


def attend_back(inverse, spans, select, ends, q, kv, d_att, att, lse):
    keys = TILE * 128

    def kernel(
        inverse, spans, select, ends, q_ref, kv_ref, d_ref, o_ref, lse_ref, dq_ref, dkv_ref,
        acc_ref, kt_ref,
    ):
        step = pl.program_id(0)

        @pl.when(step == 0)
        def _():
            eye = (
                lax.broadcasted_iota(jnp.int32, (64, 128), 0) == lanes_of((64, 128))
            ).astype(BF)

            @pl.loop(0, 16)
            def _(n):
                for s in (0, 1):
                    part = pl.ds(pl.multiple_of(n * 512, 512), 512)
                    kt_ref[s, :, part] = dot_nt(eye, kv_ref[s, part, :]).astype(BF)
                    acc_ref[s, part, :] = jnp.zeros((512, 128), F32)

        span = spans[step]
        begin, count = span_range(span, ends)
        pos = span * 128 + lanes_of((1, 128))
        low = doc_start(pos, ends)
        lane = lanes_of((128, 128))
        sel = (select[0], select[1])
        d_both = d_ref[...].astype(F32)
        d_pad = (
            jnp.where(lane >= 64, pltpu.roll(d_both, 64, 1), 0.0).astype(BF),
            jnp.where(lane >= 64, d_both, 0.0).astype(BF),
        )
        pair = [jnp.concatenate([q_ref[h], d_pad[h]], axis=0) for h in (0, 1)]
        mixed = (d_both * o_ref[...].astype(F32)).T
        delta = [jnp.sum(mixed[64 * h : 64 * h + 64], axis=0, keepdims=True) for h in (0, 1)]
        lses = [lse_ref[0, h : h + 1, :] for h in (0, 1)]

        def body(j, state):
            t = begin + j * TILE
            where = [inverse[jnp.minimum(t + i, 63)] * 128 for i in range(TILE)]
            where = [pl.ds(pl.multiple_of(v, 128), 128) for v in where]
            kpos = t * 128 + lax.broadcasted_iota(jnp.int32, (keys, 1), 0)
            allowed = (kpos >= low) & (kpos <= pos)
            out = []
            for h in (0, 1):
                kv_t = jnp.concatenate([kv_ref[sel[h], w, :] for w in where], axis=0)
                k_t = jnp.concatenate([kt_ref[sel[h], :, w] for w in where], axis=1)
                both = dot_nt(kv_t, pair[h])
                p = jnp.where(allowed, jnp.exp(both[:, 0:128] - lses[h]), 0.0)
                d_s = (p * (both[:, 128:256] - delta[h])).astype(BF)
                d_kv = dot(jnp.concatenate([d_s, p.astype(BF)], axis=1), pair[h])
                for i, w in enumerate(where):
                    acc_ref[sel[h], w, :] += d_kv[i * 128 : (i + 1) * 128]
                out.append(state[h] + dot(k_t, d_s))
            return tuple(out)

        zero = jnp.zeros((64, 128), F32)
        state = lax.fori_loop(0, count, body, (zero, zero))
        dq_ref[...] = jnp.concatenate(state, axis=0).T * 0.125

        @pl.when(step == 7)
        def _():
            @pl.loop(0, 16)
            def _(n):
                for s in (0, 1):
                    part = pl.ds(pl.multiple_of(n * 512, 512), 512)
                    dkv_ref[s, part, :] = acc_ref[s, part, :].astype(BF)

    return pl.pallas_call(
        kernel,
        grid_spec=pltpu.PrefetchScalarGridSpec(
            num_scalar_prefetch=4,
            grid=(8,),
            in_specs=[
                pl.BlockSpec((2, 128, 128), lambda i, *_: (0, i, 0)),
                pl.BlockSpec((2, 8192, 128), lambda i, *_: (0, 0, 0)),
                pl.BlockSpec((128, 128), lambda i, *_: (i, 0)),
                pl.BlockSpec((128, 128), lambda i, *_: (i, 0)),
                pl.BlockSpec((1, 8, 128), lambda i, *_: (i, 0, 0)),
            ],
            out_specs=(
                pl.BlockSpec((128, 128), lambda i, *_: (i, 0)),
                pl.BlockSpec((2, 8192, 128), lambda i, *_: (0, 0, 0)),
            ),
            scratch_shapes=[pltpu.VMEM((2, 8192, 128), F32), pltpu.VMEM((2, 64, 8192), BF)],
        ),
        out_shape=(shaped((1024, 128), F32), shaped((2, 8192, 128), BF)),
        compiler_params=pltpu.CompilerParams(vmem_limit_bytes=LIMIT),
        name="attend_back",
    )(inverse, spans, select, ends, q, kv, d_att, att, lse)


def column_of(row):
    return jnp.concatenate(
        [jnp.broadcast_to(row[:, i * 128 : (i + 1) * 128], (128, 128)).T for i in range(8)], axis=0
    )


def feed(rows, atts, wo, w2, wd, cot, gains):
    def kernel(
        x_ref, a_ref, wo_ref, w2_ref, wd_ref, c_ref, g_ref,
        r_ref, out_ref, dmn_ref, gw2_ref, gwd_ref, acc2, accd, accg,
    ):
        step = pl.program_id(0)

        @pl.when(step == 0)
        def _():
            acc2[...] = jnp.zeros_like(acc2)
            accd[...] = jnp.zeros_like(accd)
            accg[...] = jnp.zeros_like(accg)

        att = jnp.concatenate([a_ref[f] for f in range(8)], axis=1)
        resid = x_ref[...].astype(F32) + dot(att, wo_ref[...])
        r_ref[...] = resid
        inv = lax.rsqrt(jnp.sum(resid * resid, axis=1, keepdims=True) * (1.0 / WIDTH) + EPSILON)
        scaled = resid * inv
        mnormed = (scaled * g_ref[1:2, :]).astype(BF)
        both = dot(mnormed, w2_ref[...])
        gate, up = both[:, 0:384], both[:, 384:768]
        sigma = 1.0 / (1.0 + jnp.exp(-gate))
        silu = gate * sigma
        act = (silu * up).astype(BF)
        out_ref[...] = dot(act, wd_ref[...]).astype(BF)
        cot = c_ref[...]
        d_act = dot_nt(cot, wd_ref[...])
        d_gate = (d_act * up * sigma * (1.0 + gate * (1.0 - sigma))).astype(BF)
        d_up = (d_act * silu).astype(BF)
        d_both = jnp.concatenate([d_gate, d_up], axis=1)
        acc2[...] += dot_tn(mnormed, d_both)
        accd[...] += dot_tn(act, cot)
        d_mn = dot_nt(d_both, w2_ref[...])
        dmn_ref[...] = d_mn.astype(BF)
        accg[0:1, :] += jnp.sum(d_mn * scaled, axis=0, keepdims=True)

        @pl.when(step == 3)
        def _():
            gw2_ref[:, 0:768] = acc2[...].astype(BF)
            gw2_ref[:, 768:896] = column_of(accg[0:1, :]).astype(BF)
            gwd_ref[...] = accd[...].astype(BF)

    block = pl.BlockSpec((256, WIDE), lambda i: (i, 0))
    whole = lambda *s: pl.BlockSpec(s, lambda i: (0,) * len(s))
    return pl.pallas_call(
        kernel,
        grid=(4,),
        out_shape=(
            shaped((1024, WIDE), F32),
            shaped((1024, WIDE), BF),
            shaped((1024, WIDE), BF),
            shaped((1024, 896), BF),
            shaped((384, WIDE), BF),
        ),
        in_specs=[
            block,
            pl.BlockSpec((8, 256, 128), lambda i: (0, i, 0)),
            whole(1024, WIDE),
            whole(1024, 768),
            whole(384, WIDE),
            block,
            whole(8, WIDE),
        ],
        out_specs=(block, block, block, whole(1024, 896), whole(384, WIDE)),
        scratch_shapes=[
            pltpu.VMEM((1024, 768), F32),
            pltpu.VMEM((384, WIDE), F32),
            pltpu.VMEM((8, WIDE), F32),
        ],
        compiler_params=pltpu.CompilerParams(vmem_limit_bytes=LIMIT),
        name="feed",
    )(rows, atts, wo, w2, wd, cot, gains)


def turn(me, dmn, cp, resid, gains, atts, wo, spread):
    def kernel(me_ref, dmn_ref, c_ref, r_ref, g_ref, a_ref, wo_ref, e_ref, dr_ref, da_ref, gw_ref):
        resid = r_ref[...]
        inv = lax.rsqrt(jnp.sum(resid * resid, axis=1, keepdims=True) * (1.0 / WIDTH) + EPSILON)
        e = dmn_ref[...] * g_ref[1:2, :]
        mean = jnp.sum(e * resid, axis=1, keepdims=True) * (1.0 / WIDTH)
        d_resid = c_ref[...].astype(F32) + inv * e - resid * (inv * inv * inv * mean)
        dr_ref[...] = d_resid
        mixed = d_resid.astype(BF)
        d_att = dot_nt(mixed, wo_ref[...]).astype(BF)
        for f in range(8):
            da_ref[f] = d_att[:, f * 128 : (f + 1) * 128]
        att = jnp.concatenate([a_ref[f] for f in range(8)], axis=1)
        att = dot(att, e_ref[...]).astype(BF)
        gw = dot_tn(att, mixed).astype(BF)
        for g in range(8):
            for f in range(8):
                n = (8 * g + f) * 16
                gw_ref[f, g * 16 : (g + 1) * 16, :] = gw[n : n + 16]

    whole = lambda *s: pl.BlockSpec(s, lambda i, me: (0,) * len(s))
    return pl.pallas_call(
        kernel,
        grid_spec=pltpu.PrefetchScalarGridSpec(
            num_scalar_prefetch=1,
            grid=(1,),
            in_specs=[
                whole(128, WIDE),
                whole(128, WIDE),
                pl.BlockSpec((128, WIDE), lambda i, me: (me[0], 0)),
                whole(8, WIDE),
                pl.BlockSpec((8, 128, 128), lambda i, me: (0, me[0], 0)),
                whole(1024, WIDE),
                whole(1024, WIDE),
            ],
            out_specs=(whole(128, WIDE), whole(8, 128, 128), whole(8, 128, WIDE)),
        ),
        out_shape=(
            shaped((128, WIDE), F32),
            shaped((8, 128, 128), BF),
            shaped((8, 128, WIDE), BF),
        ),
        compiler_params=pltpu.CompilerParams(vmem_limit_bytes=LIMIT),
        name="turn",
    )(me, dmn, cp, resid, gains, atts, wo, spread)


def project_back(dq, dkv, cos_t, sin_t, w1, normed, rows):
    def kernel(dq_ref, dkv_ref, cos_ref, sin_ref, w_ref, n_ref, x_ref, dn_ref, gw_ref, acc, accg):
        step = pl.program_id(0)

        @pl.when(step == 0)
        def _():
            acc[...] = jnp.zeros_like(acc)
            accg[...] = jnp.zeros_like(accg)

        cos_v, sin_v = cos_ref[...], sin_ref[...]
        dq, dkv = dq_ref[...], dkv_ref[...]
        dq = dq * cos_v - partner(dq) * sin_v
        dk = dkv * cos_v - partner(dkv) * sin_v
        dkv = jnp.where(lanes_of((128, 128)) < 64, dk, dkv)
        d_all = jnp.concatenate([dq, dkv], axis=1).astype(BF)
        acc[...] += dot_tn(n_ref[...], d_all)
        dn = dot_nt(d_all, w_ref[:, 0:256])
        dn_ref[...] = dn.astype(BF)
        x = x_ref[...].astype(F32)
        inv = lax.rsqrt(jnp.sum(x * x, axis=1, keepdims=True) * (1.0 / WIDTH) + EPSILON)
        accg[0:1, :] += jnp.sum(dn * (x * inv), axis=0, keepdims=True)

        @pl.when(step == 7)
        def _():
            gw_ref[:, 0:256] = acc[...].astype(BF)
            gw_ref[:, 256:384] = column_of(accg[0:1, :]).astype(BF)

    block = lambda w: pl.BlockSpec((128, w), lambda i: (i, 0))
    whole = lambda *s: pl.BlockSpec(s, lambda i: (0,) * len(s))
    return pl.pallas_call(
        kernel,
        grid=(8,),
        out_shape=(shaped((1024, WIDE), BF), shaped((1024, 384), BF)),
        in_specs=[
            block(128), block(128), block(128), block(128), whole(WIDE, 384), block(WIDE), block(WIDE)
        ],
        out_specs=(block(WIDE), whole(1024, 384)),
        scratch_shapes=[pltpu.VMEM((1024, 256), F32), pltpu.VMEM((8, WIDE), F32)],
        compiler_params=pltpu.CompilerParams(vmem_limit_bytes=LIMIT),
        name="project_back",
    )(dq, dkv, cos_t, sin_t, w1, normed, rows)


def spread_matrix(rows, used):
    j = lax.broadcasted_iota(jnp.int32, (rows, WIDE), 0)
    k = lax.broadcasted_iota(jnp.int32, (rows, WIDE), 1)
    hit = ((k // 16) * 15 + k % 16 == j) & (k % 16 < 15) & (j < used)
    return hit.astype(BF)


def pad_rows(v, n):
    return jnp.pad(v, ((0, n - v.shape[0]), (0, 0)))


def local(
    hidden, attn_gain, w_q, w_k, w_v, w_o, mlp_gain, w_gate, w_up, w_down, cotangent,
    doc_lengths, span_order,
):
    i = lax.axis_index("ctx")
    group, me = i // 8, i % 8
    first_end = doc_lengths[0]
    second_end = doc_lengths[0] + doc_lengths[1]
    ends = jnp.stack([first_end, second_end])
    spans = lax.dynamic_slice(span_order, (group * 8,), (8,))
    ids = jnp.arange(64, dtype=jnp.int32)
    inverse = jnp.sum(jnp.where(span_order[None, :] == ids[:, None], ids[None, :], 0), axis=1)
    select = jnp.asarray(SELECT, jnp.int32)[me]

    stream = (spans[:, None] * 128 + jnp.arange(128, dtype=jnp.int32)[None, :]).reshape(1024, 1)
    spot = (stream - doc_start(stream, ends)).astype(F32)
    lane = jnp.arange(128, dtype=jnp.int32)
    frequency = ROPE_BASE ** (-2.0 * (lane % 32).astype(F32) / HEAD)
    angle = spot * frequency[None, :]
    cos_t = jnp.cos(angle)
    sin_t = jnp.where(lane % 64 < 32, -1.0, 1.0)[None, :] * jnp.sin(angle)

    spread = spread_matrix(1024, WIDTH)
    widen = lambda v: dot(v, spread[:WIDTH]).astype(BF)
    xp, cp = widen(hidden), widen(cotangent)
    wq = jnp.pad(w_q, ((0, 1), (0, 64))).reshape(16, 8, 128)
    wk = pad_rows(w_k, 16).reshape(16, 5, 64)
    wv = pad_rows(w_v, 16).reshape(16, 5, 64)
    owned = lambda w: jnp.stack([w[:, h] for h in OWNED_KV], axis=1)
    gain = jnp.pad(jnp.stack([attn_gain, mlp_gain], axis=1), ((0, 1), (0, 126)))
    gain = jnp.broadcast_to(gain[:, None, :], (16, 8, 128))
    wp1 = jnp.concatenate([wq, owned(wk), owned(wv), gain], axis=2).transpose(1, 0, 2)

    def columns(w):
        w = pad_rows(w, 16).reshape(16, 8, 8, 40)
        w = jnp.pad(w, ((0, 0), (0, 0), (0, 0), (0, 8)))
        return w.transpose(2, 0, 1, 3).reshape(8, 16, 384)

    wp2 = jnp.concatenate([columns(w_gate), columns(w_up)], axis=2)
    wop = widen(pad_rows(w_o, 16))
    wdp = widen(pad_rows(w_down, 48))

    rows, w1, w2own, wos = gather_first(xp, wp1, wp2, wop)
    rows = rows.reshape(1024, WIDE)
    w1 = w1.reshape(1024, 384)
    normed, q, kv_own, gains = project(rows, w1, cos_t, sin_t)
    kv, wo, cot = gather_keys(kv_own, wos, cp)
    kv = kv.reshape(2, 8192, 128)
    cot = cot.reshape(1024, WIDE)
    wo = wo.transpose(1, 0, 2, 3)[:, :, :15].reshape(WIDTH, WIDE)
    wo = pad_rows(wo, 1024)
    att, lse = attend(inverse, spans, select, ends, q, kv)
    atts, w2, wd = gather_heads(att, w2own, wdp)
    w2 = w2.reshape(1024, 768)
    wd = wd.reshape(384, WIDE)
    resid, outp, dmn, gw2, gwd = feed(rows, atts, wo, w2, wd, cot, gains)
    dmn_sum, gw2s, gwds = sum_feed(
        dmn.reshape(8, 128, WIDE), gw2.reshape(8, 8, 16, 896), gwd.reshape(8, 48, WIDE)
    )
    me_row = me.reshape(1)
    d_resid, d_att, gwo = turn(me_row, dmn_sum, cp, resid, gains, atts, wo, spread)
    d_att = swap_heads(d_att).reshape(1024, 128)
    dq, dkv = attend_back(inverse, spans, select, ends, q, kv, d_att, att, lse)
    dkv_sum, out_sum, gwo = sum_keys(
        dkv.reshape(2, 8, 1024, 128), outp.reshape(8, 128, WIDE), gwo
    )
    dn, gw1 = project_back(dq, dkv_sum, cos_t, sin_t, w1, normed, rows)
    dn_sum, gw1s, gwo = sum_normed(
        dn.reshape(8, 128, WIDE), gw1.reshape(8, 8, 16, 384), gwo.reshape(8, 16, WIDE)
    )
    gw1s, gw2s = swap_grads(gw1s, gw2s)

    narrow = lambda v: dot_nt(v, spread[:WIDTH])
    x = xp.astype(F32)
    inv = lax.rsqrt(jnp.sum(x * x, axis=1, keepdims=True) * (1.0 / WIDTH) + EPSILON)
    c = dn_sum * gains[0:1]
    mean = jnp.sum(c * x, axis=1, keepdims=True) * (1.0 / WIDTH)
    d_x = d_resid + inv * c - x * (inv * inv * inv * mean)
    grad_hidden = narrow(d_x.astype(BF)).astype(BF)
    own = lax.dynamic_slice(resid, (me * 128, 0), (128, WIDE))
    output = narrow((own + out_sum).astype(BF)).astype(BF)

    gw1s = gw1s[:, :15].astype(F32)
    gw2s = gw2s[:, :15].astype(F32)
    g_q = gw1s[:, :, 0:128].transpose(1, 0, 2).reshape(15, 1024)[:, :WIDTH]

    def heads(part):
        return jnp.concatenate(
            [sum(part[f] for f in range(8) if OWNED_KV[f] == h) for h in range(5)], axis=1
        )

    g_k = heads(gw1s[:, :, 128:192])
    g_v = heads(gw1s[:, :, 192:256])
    g_attn = jnp.sum(gw1s[:, :, 256], axis=0)
    g_mlp = jnp.sum(gw2s[:, :, 768], axis=0)

    def columns_back(part):
        part = part.reshape(8, 15, 8, 48)[..., :40]
        return part.transpose(1, 2, 0, 3).reshape(15, 2560)

    g_gate = columns_back(gw2s[:, :, 0:384])
    g_up = columns_back(gw2s[:, :, 384:768])
    squeeze = lambda v: v.reshape(-1, 64, 16)[:, :, :15].reshape(-1, WIDTH)
    return (
        output,
        grad_hidden,
        g_attn,
        g_q,
        g_k,
        g_v,
        squeeze(gwo[:15]),
        g_mlp,
        g_gate,
        g_up,
        squeeze(gwds[:40]),
    )


def solution(mesh):
    both = ("fsdp", "ctx")
    wide, thin, part = P(both, None), P(both), P("fsdp")
    return jax.shard_map(
        local,
        mesh=mesh,
        in_specs=(wide, thin, wide, wide, wide, wide, thin, wide, wide, wide, wide, part, part),
        out_specs=(wide, wide, thin, wide, wide, wide, wide, thin, wide, wide, wide),
        check_vma=False,
    )
```

```python
import jax
import jax.numpy as jnp
import numpy as np
from jax import lax
from jax.experimental import pallas as pl
from jax.experimental.pallas import tpu as pltpu
from jax.sharding import PartitionSpec as P

HEAD = 64
EPSILON = 1e-05
ROPE_BASE = 100000.0
MASKED = -1e30
WIDE = 1024
WIDTH = 960
BF = jnp.bfloat16
F32 = jnp.float32
MESH = pl.DeviceIdType.MESH
DMA = pltpu.SemaphoreType.DMA
ANY = pl.BlockSpec(memory_space=pl.ANY)
VMEM = pl.BlockSpec(memory_space=pltpu.VMEM)
SMEM = pl.BlockSpec(memory_space=pltpu.SMEM)
LIMIT = 56 * 2**20
TILE = 4
OWNED_KV = (0, 1, 1, 2, 2, 3, 4, 4)
SELECT = ((0, 0), (0, 1), (0, 0), (1, 1), (0, 1), (1, 1), (0, 0), (0, 0))


def dot(a, b):
    return lax.dot_general(a, b, (((1,), (0,)), ((), ())), preferred_element_type=F32)


def dot_nt(a, b):
    return lax.dot_general(a, b, (((1,), (1,)), ((), ())), preferred_element_type=F32)


def dot_tn(a, b):
    return lax.dot_general(a, b, (((0,), (0,)), ((), ())), preferred_element_type=F32)


def shaped(shape, dtype):
    return jax.ShapeDtypeStruct(shape, dtype)


def place():
    i = lax.axis_index("ctx")
    return i // 16, (i // 8) % 2, (i // 2) % 4, i % 2


def at(x, z, y, c):
    return {"ctx": (((x + 4) % 4) * 2 + z) * 8 + ((y + 4) % 4) * 2 + c}


def send(src, dst, ssem, rsem, device):
    copy = pltpu.make_async_remote_copy(
        src, dst, ssem, rsem, device_id=device, device_id_type=MESH
    )
    copy.start()
    return copy


def hail(kinds):
    x, z, y, c = place()
    who = []
    if "x" in kinds:
        who += [at(x + 1, z, y, c), at(x - 1, z, y, c), at(x, 1 - z, y, c)]
    if "f" in kinds:
        who += [at(x, z, y + d, (c + e) % 2) for d in range(4) for e in range(2) if d + e]
    elif "y" in kinds:
        who += [at(x, z, y + d, c) for d in (1, 2, 3)] + [at(x, z, y, 1 - c)]
    barrier = pltpu.get_barrier_semaphore()
    for device in who:
        pl.semaphore_signal(barrier, inc=1, device_id=device, device_id_type=MESH)
    return len(who)


def greet(kinds):
    pl.semaphore_wait(pltpu.get_barrier_semaphore(), hail(kinds))


def half_lead(ref, k):
    n = ref.shape[0] // 2
    return ref.at[pl.ds(k * n, n)]


def half_lanes(ref, k):
    n = ref.shape[-1] // 2
    return ref.at[:, pl.ds(k * n, n)]


class RingGather:
    sems = [DMA((9,)), DMA((9,)), DMA(())]

    def __init__(self, src, dst, half, ssem, rsem, lsem, arrived=None):
        self.src, self.dst, self.half = src, dst, half
        self.ssem, self.rsem, self.lsem = ssem, rsem, lsem
        self.arrived = arrived or (lambda block: None)
        self.copies = {}

    def push(self, n, src, dst, device):
        self.copies[n] = send(src, dst, self.ssem.at[n], self.rsem.at[n], device)

    def start(self):
        x, z, y, c = place()
        me = self.dst.at[x * 2 + z]
        self.push(0, self.src, me, at(x, 1 - z, y, c))
        self.push(1, self.src, me, at(x + 1, z, y, c))
        self.push(2, self.src, me, at(x - 1, z, y, c))
        self.local = pltpu.make_async_copy(self.src, me, self.lsem)
        self.local.start()

    def relay_z(self):
        x, z, y, c = place()
        block = self.dst.at[x * 2 + 1 - z]
        self.copies[0].wait_recv()
        self.push(3, block, block, at(x + 1, z, y, c))
        self.push(4, block, block, at(x - 1, z, y, c))
        self.arrived(x * 2 + 1 - z)

    def relay_x(self, k):
        x, z, y, c = place()
        zz = z if k == 0 else 1 - z
        left, right = ((x + 3) % 4) * 2 + zz, ((x + 1) % 4) * 2 + zz
        self.copies[1 + 2 * k].wait_recv()
        part = self.half(self.dst.at[left], 0)
        self.push(5 + 2 * k, part, part, at(x + 1, z, y, c))
        self.arrived(left)
        self.copies[2 + 2 * k].wait_recv()
        part = self.half(self.dst.at[right], 1)
        self.push(6 + 2 * k, part, part, at(x - 1, z, y, c))
        self.arrived(right)

    def land(self, k):
        x, z, y, c = place()
        zz = z if k == 0 else 1 - z
        self.copies[5 + 2 * k].wait_recv()
        self.copies[6 + 2 * k].wait_recv()
        self.arrived(((x + 2) % 4) * 2 + zz)

    def finish(self):
        self.local.wait()
        for n in range(9):
            self.copies[n].wait_send()


def run_ring_gathers(rings):
    for ring in rings:
        ring.relay_z()
    for k in (0, 1):
        for ring in rings:
            ring.relay_x(k)
    for k in (0, 1):
        for ring in rings:
            ring.land(k)


class RowGather:
    sems = [DMA((8,)), DMA((8,)), DMA(())]

    def __init__(self, src, dst, ssem, rsem, lsem):
        self.src, self.dst = src, dst
        self.ssem, self.rsem, self.lsem = ssem, rsem, lsem
        self.copies = {}

    def push(self, n, src, dst, device):
        self.copies[n] = send(src, dst, self.ssem.at[n], self.rsem.at[n], device)

    def start(self):
        x, z, y, c = place()
        me = self.dst.at[y * 2 + c]
        self.push(1, self.src, me, at(x, z, y + 1, c))
        self.push(2, self.src, me, at(x, z, y - 1, c))
        self.push(0, self.src, me, at(x, z, y, 1 - c))
        self.local = pltpu.make_async_copy(self.src, me, self.lsem)
        self.local.start()

    def relay(self):
        x, z, y, c = place()
        for n, step, side in ((1, 3, 0), (2, 1, 1)):
            self.copies[n].wait_recv()
            block = self.dst.at[((y + step) % 4) * 2 + c]
            part = half_lead(block, side)
            self.push(2 + n, part, part, at(x, z, y + 4 - step, c))
            self.push(4 + n, block, block, at(x, z, y, 1 - c))

    def land(self):
        x, z, y, c = place()
        self.copies[3].wait_recv()
        self.copies[4].wait_recv()
        block = self.dst.at[((y + 2) % 4) * 2 + c]
        self.push(7, block, block, at(x, z, y, 1 - c))

    def finish(self):
        self.local.wait()
        for n in (0, 5, 6, 7):
            self.copies[n].wait_recv()
        for n in range(8):
            self.copies[n].wait_send()


class Swap:
    sems = [DMA((8,)), DMA((8,)), DMA(())]

    def __init__(self, src, dst, ssem, rsem, lsem):
        self.src, self.dst = src, dst
        self.ssem, self.rsem, self.lsem = ssem, rsem, lsem

    def start(self):
        x, z, y, c = place()
        me = y * 2 + c
        self.copies = []
        for d in (2, 1, 3, 0):
            for e in (0, 1):
                if d + e:
                    n = d * 2 + e
                    to = ((y + d) % 4) * 2 + (c + e) % 2
                    self.copies.append(
                        send(
                            self.src.at[to],
                            self.dst.at[me],
                            self.ssem.at[n],
                            self.rsem.at[n],
                            at(x, z, y + d, (c + e) % 2),
                        )
                    )
        self.local = pltpu.make_async_copy(self.src.at[me], self.dst.at[me], self.lsem)
        self.local.start()

    def finish(self):
        self.local.wait()
        for copy in self.copies:
            copy.wait()


class RowSum:
    @staticmethod
    def scratch(shape):
        return [
            pltpu.VMEM((4,) + shape, BF),
            pltpu.VMEM((4,) + shape, BF),
            pltpu.VMEM((4,) + shape, BF),
            DMA((8,)),
            DMA((8,)),
        ]

    def __init__(self, blk, first, mixed, second, ssem, rsem):
        self.blk, self.first, self.mixed, self.second = blk, first, mixed, second
        self.ssem, self.rsem = ssem, rsem
        self.copies = {}

    def push(self, n, src, dst, device):
        self.copies[n] = send(src, dst, self.ssem.at[n], self.rsem.at[n], device)

    def start(self):
        x, z, y, c = place()
        for d in (2, 1, 3, 0):
            to = ((y + d) % 4) * 2 + 1 - c
            self.push(d, self.blk.at[to], self.first.at[d], at(x, z, y, 1 - c))

    def relay(self):
        x, z, y, c = place()
        for d in (2, 1, 3):
            self.copies[d].wait_recv()
            own = self.blk[((y + d) % 4) * 2 + c].astype(F32)
            self.mixed[d] = (own + self.first[d].astype(F32)).astype(BF)
            self.push(4 + d, self.mixed.at[d], self.second.at[d], at(x, z, y + d, c))

    def total(self):
        x, z, y, c = place()
        self.copies[0].wait_recv()
        total = self.blk[y * 2 + c].astype(F32) + self.first[0].astype(F32)
        for d in (1, 3, 2):
            self.copies[4 + d].wait_recv()
            total = total + self.second[d].astype(F32)
        return total

    def finish(self):
        for n in (0, 1, 2, 3, 5, 6, 7):
            self.copies[n].wait_send()


class RingSum:
    @staticmethod
    def scratch(shape, lanes):
        if lanes:
            part = shape[:-1] + (shape[-1] // 2,)
        else:
            part = (shape[0] // 2,) + shape[1:]
        return [
            pltpu.VMEM((4,) + part, BF),
            pltpu.VMEM((4,) + shape, BF),
            pltpu.VMEM((4,) + shape, BF),
            pltpu.VMEM((2,) + shape, BF),
            DMA((9,)),
            DMA((9,)),
        ]

    def __init__(self, blk, lanes, parts, mixed, heard, across, ssem, rsem):
        self.blk, self.half = blk, half_lanes if lanes else half_lead
        self.parts, self.mixed, self.heard, self.across = parts, mixed, heard, across
        self.ssem, self.rsem = ssem, rsem
        self.copies = {}

    def push(self, n, src, dst, device):
        self.copies[n] = send(src, dst, self.ssem.at[n], self.rsem.at[n], device)

    def start(self, k):
        x, z, y, c = place()
        zz = 1 - z if k == 0 else z
        far = self.blk.at[((x + 2) % 4) * 2 + zz]
        self.push(4 * k, self.half(far, 0), self.parts.at[2 * k], at(x + 1, z, y, c))
        self.push(4 * k + 1, self.half(far, 1), self.parts.at[2 * k + 1], at(x - 1, z, y, c))

    def relay(self, k):
        x, z, y, c = place()
        zz = 1 - z if k == 0 else z
        for side, step in ((0, 1), (1, 3)):
            n = 2 * k + side
            mixed = self.mixed.at[n]
            source = self.blk.at[((x + step) % 4) * 2 + zz]
            mine, other = self.half(source, side), self.half(source, 1 - side)
            self.half(mixed, 1 - side)[...] = other[...]
            self.copies[4 * k + side].wait_recv()
            self.half(mixed, side)[...] = (
                mine[...].astype(F32) + self.parts[n].astype(F32)
            ).astype(BF)
            self.push(4 * k + 2 + side, mixed, self.heard.at[n], at(x + step, z, y, c))

    def total(self, k):
        x, z, y, c = place()
        zz = 1 - z if k == 0 else z
        total = self.blk[x * 2 + zz].astype(F32)
        for side in (0, 1):
            self.copies[4 * k + 2 + side].wait_recv()
            total = total + self.heard[2 * k + side].astype(F32)
        if k == 0:
            self.across[0] = total.astype(BF)
            self.push(8, self.across.at[0], self.across.at[1], at(x, 1 - z, y, c))
            return None
        self.copies[8].wait_recv()
        return total + self.across[1].astype(F32)

    def finish(self):
        for n in range(9):
            self.copies[n].wait_send()


def comm_call(name, number, kernel, out_shape, in_specs, out_specs, scratch, args):
    return pl.pallas_call(
        kernel,
        out_shape=out_shape,
        in_specs=in_specs,
        out_specs=out_specs,
        scratch_shapes=scratch,
        compiler_params=pltpu.CompilerParams(
            collective_id=number, has_side_effects=True, vmem_limit_bytes=LIMIT
        ),
        name=name,
    )(*args)


def split(refs, counts):
    parts, begin = [], 0
    for n in counts:
        parts.append(refs[begin : begin + n])
        begin += n
    return parts


def spread_value(rows):
    j = lax.broadcasted_iota(jnp.int32, (rows, WIDE), 0)
    k = lax.broadcasted_iota(jnp.int32, (rows, WIDE), 1)
    hit = ((k // 16) * 15 + k % 16 == j) & (k % 16 < 15)
    return jnp.where(hit, 1.0, 0.0).astype(BF)


def gather_first(
    hidden, cot, w_q, w_k, w_v, w_o, w_gate, w_up, w_down, gain1, gain2, ends, span_order, frequency
):
    def kernel(
        hidden, cot, w_q, w_k, w_v, w_o, w_gate, w_up, w_down, gain1, gain2, ends, order, freq,
        rows, w1, wos, wds, xp, cp, wp2, cos_t, sin_t, wp1, wop, wdp, w1own, *sems,
    ):
        a, b, d, e, e2 = split(sems, (3, 3, 3, 3, 3))
        x, z, y, c = place()
        partners = hail("xf")

        q = jnp.concatenate([w_q[...].astype(F32), jnp.zeros((15, 64), F32)], axis=1)
        k, v = w_k[...].astype(F32), w_v[...].astype(F32)
        gains = jnp.concatenate(
            [gain1[...].astype(F32), gain2[...].astype(F32), jnp.zeros((15, 126), F32)], axis=1
        )
        wp1[...] = jnp.zeros(wp1.shape, BF)
        for f in range(8):
            n = OWNED_KV[f] * 64
            wp1[f, 0:15, 0:128] = q[:, 128 * f : 128 * f + 128].astype(BF)
            wp1[f, 0:15, 128:256] = jnp.concatenate(
                [k[:, n : n + 64], v[:, n : n + 64]], axis=1
            ).astype(BF)
            wp1[f, 0:15, 256:384] = gains.astype(BF)

        pl.semaphore_wait(pltpu.get_barrier_semaphore(), partners)
        swap = Swap(wp1, w1own, *b)
        swap.start()
        spread = spread_value(WIDTH)
        xp[...] = dot(hidden[...], spread).astype(BF)
        gather = RowGather(xp, rows, *a)
        gather.start()
        wop[...] = jnp.zeros(wop.shape, BF)
        wop[0:15, :] = dot(w_o[...], spread).astype(BF)
        wdp[...] = jnp.zeros(wdp.shape, BF)
        wdp[0:40, :] = dot(w_down[...], spread).astype(BF)
        ring_o = RingGather(wop, wos, half_lanes, *e)
        ring_d = RingGather(wdp, wds, half_lanes, *e2)
        ring_o.start()
        ring_d.start()
        swap.finish()
        ring_1 = RingGather(w1own, w1, half_lead, *d)
        ring_1.start()
        cp[...] = dot(cot[...], spread).astype(BF)
        gather.relay()
        rings = [ring_1, ring_o, ring_d]
        for ring in rings:
            ring.relay_z()

        wp2[...] = jnp.zeros(wp2.shape, BF)
        gap = jnp.zeros((15, 8), F32)
        for m, ref in ((0, w_gate), (384, w_up)):
            w = ref[...].astype(F32)
            for f in range(8):
                parts = []
                for g in range(8):
                    n = (8 * g + f) * 40
                    parts += [w[:, n : n + 40], gap]
                wp2[f, 0:15, m : m + 384] = jnp.concatenate(parts, axis=1).astype(BF)

        for k in (0, 1):
            for ring in rings:
                ring.relay_x(k)

        lane = lanes_of((1, 128))
        sign = jnp.where(lane % 64 < 32, -1.0, 1.0)

        @pl.loop(0, 8)
        def _(n):
            pos = order[(x * 2 + z) * 8 + n] * 128
            pos = pos + lax.broadcasted_iota(jnp.int32, (128, 1), 0)
            angle = (pos - doc_start(pos, ends)).astype(F32) * freq[...]
            part = pl.ds(pl.multiple_of(n * 128, 128), 128)
            cos_t[part, :] = jnp.cos(angle)
            sin_t[part, :] = sign * jnp.sin(angle)

        gather.land()
        for k in (0, 1):
            for ring in rings:
                ring.land(k)
        gather.finish()
        for ring in rings:
            ring.finish()

    return comm_call(
        "gather_first",
        1,
        kernel,
        (
            shaped((8, 128, WIDE), BF),
            shaped((8, 8, 16, 384), BF),
            shaped((8, 16, WIDE), BF),
            shaped((8, 48, WIDE), BF),
            shaped((128, WIDE), BF),
            shaped((128, WIDE), BF),
            shaped((8, 16, 768), BF),
            shaped((1024, 128), F32),
            shaped((1024, 128), F32),
        ),
        [VMEM] * 11 + [SMEM, SMEM, VMEM],
        (ANY,) * 4 + (VMEM,) * 5,
        [
            pltpu.VMEM((8, 16, 384), BF),
            pltpu.VMEM((16, WIDE), BF),
            pltpu.VMEM((48, WIDE), BF),
            pltpu.VMEM((8, 16, 384), BF),
        ]
        + RowGather.sems
        + Swap.sems
        + RingGather.sems * 3,
        (
            hidden, cot, w_q, w_k, w_v, w_o, w_gate, w_up, w_down, gain1, gain2, ends, span_order,
            frequency,
        ),
    )


def gather_keys(kv, wos, cp, wp2):
    def kernel(kv, wos, cp, wp2, kv2, wo, cot, w2own, *sems):
        a, b, d, e, (hs, hr) = split(sems, (3, 3, 3, 3, 2))
        x, z, y, c = place()
        greet("xf")
        hand = []

        def arrived(block):
            n = len(hand)
            piece = kv2.at[c, block]
            hand.append(send(piece, piece, hs.at[n], hr.at[n], at(x, z, y, 1 - c)))

        ring = RingGather(kv, kv2.at[c], half_lead, *a, arrived=arrived)
        gather_o = RowGather(wos, wo, *b)
        gather_c = RowGather(cp, cot, *d)
        swap = Swap(wp2, w2own, *e)
        ring.start()
        gather_o.start()
        gather_c.start()
        swap.start()
        me = kv2.at[c, x * 2 + z]
        hand.append(send(kv, me, hs.at[0], hr.at[0], at(x, z, y, 1 - c)))
        ring.relay_z()
        gather_o.relay()
        ring.relay_x(0)
        gather_c.relay()
        ring.relay_x(1)
        gather_o.land()
        gather_c.land()
        ring.land(0)
        ring.land(1)
        for copy in hand:
            copy.wait()
        swap.finish()
        gather_o.finish()
        gather_c.finish()
        ring.finish()

    return comm_call(
        "gather_keys",
        2,
        kernel,
        (
            shaped((2, 8, 1024, 128), BF),
            shaped((8, 8, 16, WIDE), BF),
            shaped((8, 128, WIDE), BF),
            shaped((8, 16, 768), BF),
        ),
        [ANY] * 4,
        (ANY,) * 4,
        RingGather.sems + RowGather.sems * 2 + Swap.sems + [DMA((8,)), DMA((8,))],
        (kv, wos, cp, wp2),
    )


def gather_heads(att, w2own, wo):
    def kernel(att, w2own, wo, atts, w2, packed, *sems):
        a, b = split(sems, (3, 3))
        greet("xy")
        gather = RowGather(att, atts, *a)
        ring = RingGather(w2own, w2, half_lead, *b)
        gather.start()
        ring.start()
        whole = jnp.concatenate([wo[f, g] for g in range(8) for f in range(8)], axis=0)

        def pack(n):
            j = lax.broadcasted_iota(jnp.int32, (256, WIDE), 0) + n * 256
            k = lax.broadcasted_iota(jnp.int32, (256, WIDE), 1)
            hit = ((k // 16) * 15 + k % 16 == j) & (k % 16 < 15)
            packed[pl.ds(n * 256, 256), :] = dot(
                jnp.where(hit, 1.0, 0.0).astype(BF), whole
            ).astype(BF)

        pack(0)
        ring.relay_z()
        gather.relay()
        pack(1)
        ring.relay_x(0)
        pack(2)
        ring.relay_x(1)
        gather.land()
        pack(3)
        ring.land(0)
        ring.land(1)
        gather.finish()
        ring.finish()

    return comm_call(
        "gather_heads",
        3,
        kernel,
        (shaped((8, 1024, 128), BF), shaped((8, 8, 16, 768), BF), shaped((WIDE, WIDE), BF)),
        [ANY, ANY, VMEM],
        (ANY, ANY, VMEM),
        RowGather.sems + RingGather.sems,
        (att, w2own, wo),
    )


def sum_feed(dmn, outp, gw2, gwd):
    def kernel(dmn, outp, gw2, gwd, dmn_sum, out_sum, gw2_sum, gwd_sum, *refs):
        a, a2, b, d = split(refs, (5, 5, 6, 6))
        greet("xy")
        rows, rows_o = RowSum(dmn, *a), RowSum(outp, *a2)
        ring_2, ring_d = RingSum(gw2, False, *b), RingSum(gwd, True, *d)
        rows.start()
        for k in (0, 1):
            ring_2.start(k)
            ring_d.start(k)
        rows_o.start()
        rows.relay()
        rows_o.relay()
        for k in (0, 1):
            ring_2.relay(k)
            ring_d.relay(k)
        dmn_sum[...] = rows.total()
        ring_2.total(0)
        ring_d.total(0)
        out_sum[...] = rows_o.total()
        gw2_sum[...] = ring_2.total(1).astype(BF)
        gwd_sum[...] = ring_d.total(1)
        rows.finish()
        rows_o.finish()
        ring_2.finish()
        ring_d.finish()

    return comm_call(
        "sum_feed",
        4,
        kernel,
        (
            shaped((128, WIDE), F32),
            shaped((128, WIDE), F32),
            shaped((8, 16, 896), BF),
            shaped((48, WIDE), F32),
        ),
        [VMEM] * 4,
        (VMEM,) * 4,
        RowSum.scratch((128, WIDE)) * 2
        + RingSum.scratch((8, 16, 896), False)
        + RingSum.scratch((48, WIDE), True),
        (dmn, outp, gw2, gwd),
    )


def swap_heads(d_att):
    def kernel(d_att, out, *sems):
        greet("f")
        swap = Swap(d_att, out, *sems)
        swap.start()
        swap.finish()

    return comm_call(
        "swap_heads", 5, kernel, shaped((8, 128, 128), BF), [ANY], ANY, Swap.sems, (d_att,)
    )


def sum_keys(dkv, gwo):
    def kernel(dkv, gwo, dkv_sum, gwo_sum, blk, from_core, hs, hr, *refs):
        a, d = split(refs, (6, 5))
        x, z, y, c = place()
        greet("xy")
        order = [(2, 1), (2, 0), (1, 1), (3, 1), (1, 0), (3, 0), (0, 1), (0, 0)]
        where = [((x + p) % 4) * 2 + (1 - z if q else z) for p, q in order]
        hand = [
            send(dkv.at[1 - c, g], from_core.at[n], hs.at[n], hr.at[n], at(x, z, y, 1 - c))
            for n, g in enumerate(where)
        ]
        rows_w = RowSum(gwo, *d)
        rows_w.start()
        ring = RingSum(blk, False, *a)

        def fold(n):
            g = where[n]
            hand[n].wait_recv()
            blk[g] = (dkv[c, g].astype(F32) + from_core[n].astype(F32)).astype(BF)

        fold(0)
        ring.start(0)
        fold(1)
        ring.start(1)
        for n in range(2, 6):
            fold(n)
        rows_w.relay()
        ring.relay(0)
        ring.relay(1)
        fold(6)
        fold(7)
        ring.total(0)
        gwo_sum[...] = rows_w.total().astype(BF)
        dkv_sum[...] = ring.total(1)
        for copy in hand:
            copy.wait_send()
        ring.finish()
        rows_w.finish()

    return comm_call(
        "sum_keys",
        6,
        kernel,
        (shaped((1024, 128), F32), shaped((128, WIDE), BF)),
        [VMEM] * 2,
        (VMEM,) * 2,
        [pltpu.VMEM((8, 1024, 128), BF), pltpu.VMEM((8, 1024, 128), BF), DMA((8,)), DMA((8,))]
        + RingSum.scratch((1024, 128), False)
        + RowSum.scratch((128, WIDE)),
        (dkv, gwo),
    )


def sum_normed(dn, gw1, gwo):
    def kernel(dn, gw1, gwo, dn_sum, gw1_sum, gwo_sum, *refs):
        a, b, d = split(refs, (5, 6, 6))
        greet("xy")
        rows = RowSum(dn, *a)
        ring_1 = RingSum(gw1, False, *b)
        ring_o = RingSum(gwo, True, *d)
        rows.start()
        for k in (0, 1):
            ring_1.start(k)
            ring_o.start(k)
        rows.relay()
        for k in (0, 1):
            ring_1.relay(k)
            ring_o.relay(k)
        ring_1.total(0)
        ring_o.total(0)
        gw1_sum[...] = ring_1.total(1).astype(BF)
        gwo_sum[...] = ring_o.total(1)
        dn_sum[...] = rows.total()
        rows.finish()
        ring_1.finish()
        ring_o.finish()

    return comm_call(
        "sum_normed",
        7,
        kernel,
        (shaped((128, WIDE), F32), shaped((8, 16, 384), BF), shaped((16, WIDE), F32)),
        [VMEM] * 3,
        (VMEM,) * 3,
        RowSum.scratch((128, WIDE))
        + RingSum.scratch((8, 16, 384), False)
        + RingSum.scratch((16, WIDE), True),
        (dn, gw1, gwo),
    )


def swap_grads(gw1, gw2):
    def kernel(gw1, gw2, out1, out2, *sems):
        a, b = split(sems, (3, 3))
        greet("f")
        one, two = Swap(gw1, out1, *a), Swap(gw2, out2, *b)
        one.start()
        two.start()
        one.finish()
        two.finish()

    return comm_call(
        "swap_grads",
        8,
        kernel,
        (shaped((8, 16, 384), BF), shaped((8, 16, 896), BF)),
        [ANY] * 2,
        (ANY,) * 2,
        Swap.sems + Swap.sems,
        (gw1, gw2),
    )


def lanes_of(shape):
    return lax.broadcasted_iota(jnp.int32, shape, len(shape) - 1)


def partner(v):
    lane = lanes_of(v.shape)
    return jnp.where(lane % 64 < 32, pltpu.roll(v, 96, 1), pltpu.roll(v, 32, 1))


def project(rows, w1, cos_t, sin_t):
    def kernel(x_ref, w_ref, cos_ref, sin_ref, n_ref, q_ref, kv_ref, g_ref):
        @pl.when(pl.program_id(0) == 0)
        def _():
            eye = (
                lax.broadcasted_iota(jnp.int32, (8, 128), 0) == lanes_of((8, 128))
            ).astype(BF)
            g_ref[...] = dot_nt(eye, w_ref[:, 256:384])

        x = x_ref[...].astype(F32)
        inv = lax.rsqrt(jnp.sum(x * x, axis=1, keepdims=True) * (1.0 / WIDTH) + EPSILON)
        normed = (x * inv * g_ref[0:1, :]).astype(BF)
        n_ref[...] = normed
        out = dot(normed, w_ref[:, 0:256])
        cos_v, sin_v = cos_ref[...], sin_ref[...]
        lane = lanes_of((256, 128))
        q, kv = out[:, 0:128], out[:, 128:256]
        q = (q * cos_v + partner(q) * sin_v).astype(BF).astype(F32) * 0.125
        k = kv * cos_v + partner(kv) * sin_v
        kv_ref[...] = jnp.where(lane < 64, k, kv).astype(BF)
        q_ref[0] = jnp.where(lane < 64, q, 0.0).astype(BF)
        q_ref[1] = jnp.where(lane < 64, pltpu.roll(q, 64, 1), 0.0).astype(BF)

    block = lambda w: pl.BlockSpec((256, w), lambda i: (i, 0))
    return pl.pallas_call(
        kernel,
        grid=(4,),
        out_shape=(
            shaped((1024, WIDE), BF),
            shaped((2, 1024, 128), BF),
            shaped((1024, 128), BF),
            shaped((8, WIDE), F32),
        ),
        in_specs=[block(WIDE), pl.BlockSpec((WIDE, 384), lambda i: (0, 0)), block(128), block(128)],
        out_specs=(
            block(WIDE),
            pl.BlockSpec((2, 256, 128), lambda i: (0, i, 0)),
            block(128),
            pl.BlockSpec((8, WIDE), lambda i: (0, 0)),
        ),
        compiler_params=pltpu.CompilerParams(vmem_limit_bytes=LIMIT),
        name="project",
    )(rows, w1, cos_t, sin_t)


def doc_start(pos, ends):
    return jnp.where(pos < ends[0], 0, jnp.where(pos < ends[1], ends[0], ends[1]))

def key_range(span, ends):
    begin = doc_start(span * 128, ends) // 128
    count = span - begin + 1
    runs = (count + 3) // 8
    return begin, runs, jnp.where(count > runs * 8, 1, 0)


def attend(inverse, spans, select, ends, q, kv):
    def kernel(inverse, spans, select, ends, q_ref, kv_ref, o_ref, lse_ref, s_ref):
        lane = lanes_of((128, 128))
        sel = (select[0], select[1])

        @pl.loop(0, 8)
        def _(b):
            span = spans[b]
            begin, runs, rest = key_range(span, ends)
            pos = span * 128 + lanes_of((1, 256)) % 128
            low = doc_start(pos, ends)
            rows = pl.ds(pl.multiple_of(b * 128, 128), 128)
            none = jnp.zeros((128, 128), BF)
            pair = jnp.concatenate(
                [
                    jnp.concatenate([q_ref[0, rows, :], none], axis=1),
                    jnp.concatenate([none, q_ref[1, rows, :]], axis=1),
                ],
                axis=0,
            )

            def load(h, t, n):
                return jnp.concatenate(
                    [
                        kv_ref[sel[h], pl.ds(inverse[jnp.minimum(t + i, 63)] * 128, 128), :]
                        for i in range(n)
                    ],
                    axis=0,
                )

            def held(t, n):
                return pl.ds(pl.multiple_of((t - begin) * 128, 512), n * 128)

            def scores(n, t, high):
                kpos = t * 128 + lax.broadcasted_iota(jnp.int32, (n * 128, 1), 0)
                allowed = (kpos >= low) & (kpos <= pos)
                keys = jnp.concatenate([load(0, t, n), load(1, t, n)], axis=1)
                s = jnp.where(allowed, dot_nt(keys, pair), MASKED)
                s_ref[held(t, n), :] = s
                return jnp.maximum(high, jnp.max(s.reshape(n * 16, 8, 256), axis=0))

            def over(step, state):
                state = lax.fori_loop(0, runs, lambda j, v: step(8, begin + j * 8, v), state)
                return lax.fori_loop(0, rest, lambda j, v: step(4, begin + runs * 8, v), state)

            high = over(scores, jnp.full((8, 256), MASKED, F32))
            high = jnp.max(high, axis=0, keepdims=True)

            def weigh(n, t, state):
                total, acc = state
                p = jnp.exp(s_ref[held(t, n), :] - high)
                total = total + jnp.sum(p.reshape(n * 16, 8, 256), axis=0)
                values = jnp.where(lanes_of((n * 128, 128)) < 64, pltpu.roll(load(0, t, n), 64, 1), load(1, t, n))
                return total, acc + dot_tn(values, p.astype(BF))

            total, acc = over(weigh, (jnp.zeros((8, 256), F32), jnp.zeros((128, 256), F32)))
            total = jnp.sum(total, axis=0, keepdims=True)
            lse = high + jnp.log(total)
            lse_ref[b, 0:1, :] = lse[:, 0:128]
            lse_ref[b, 1:2, :] = lse[:, 128:256]
            acc = acc / total
            acc = jnp.concatenate([acc[0:64, 0:128], acc[64:128, 128:256]], axis=0)
            o_ref[rows, :] = acc.T.astype(BF)

    return pl.pallas_call(
        kernel,
        in_specs=[SMEM, SMEM, SMEM, SMEM, VMEM, VMEM],
        out_specs=(VMEM, VMEM),
        scratch_shapes=[pltpu.VMEM((40 * 128, 256), F32)],
        out_shape=(shaped((1024, 128), BF), shaped((8, 8, 128), F32)),
        compiler_params=pltpu.CompilerParams(vmem_limit_bytes=LIMIT),
        name="attend",
    )(inverse, spans, select, ends, q, kv)


def attend_back(inverse, spans, select, ends, q, kv, d_att, att, lse):
    def kernel(
        inverse, spans, select, ends, q_ref, kv_ref, d_ref, o_ref, lse_ref, dq_ref, dkv_ref,
        acc_ref,
    ):
        lane = lanes_of((128, 128))
        sel = (select[0], select[1])

        @pl.loop(0, 16)
        def _(n):
            for s in (0, 1):
                part = pl.ds(pl.multiple_of(n * 512, 512), 512)
                acc_ref[s, part, :] = jnp.zeros((512, 128), F32)

        @pl.loop(0, 8)
        def _(b):
            span = spans[b]
            begin, runs, rest = key_range(span, ends)
            pos = span * 128 + lanes_of((1, 128))
            low = doc_start(pos, ends)
            rows = pl.ds(pl.multiple_of(b * 128, 128), 128)
            d_both = d_ref[rows, :].astype(F32)
            d_pad = (
                jnp.where(lane >= 64, pltpu.roll(d_both, 64, 1), 0.0).astype(BF),
                jnp.where(lane >= 64, d_both, 0.0).astype(BF),
            )
            pair = [jnp.concatenate([q_ref[h, rows, :], d_pad[h]], axis=0) for h in (0, 1)]
            mixed = (d_both * o_ref[rows, :].astype(F32)).T
            delta = [jnp.sum(mixed[64 * h : 64 * h + 64], axis=0, keepdims=True) for h in (0, 1)]
            lses = [lse_ref[b, h : h + 1, :] for h in (0, 1)]

            def step(n, t, state):
                where = [inverse[jnp.minimum(t + i, 63)] * 128 for i in range(n)]
                where = [pl.ds(pl.multiple_of(v, 128), 128) for v in where]
                kpos = t * 128 + lax.broadcasted_iota(jnp.int32, (n * 128, 1), 0)
                allowed = (kpos >= low) & (kpos <= pos)
                d_ss, kvs = [], []
                for h in (0, 1):
                    kv_t = jnp.concatenate([kv_ref[sel[h], w, :] for w in where], axis=0)
                    kvs.append(kv_t)
                    both = dot_nt(kv_t, pair[h])
                    p = jnp.where(allowed, jnp.exp(both[:, 0:128] - lses[h]), 0.0)
                    d_s = (p * (both[:, 128:256] - delta[h])).astype(BF)
                    d_ss.append(d_s)
                    d_kv = dot(jnp.concatenate([d_s, p.astype(BF)], axis=1), pair[h])
                    for i, w in enumerate(where):
                        acc_ref[sel[h], w, :] += d_kv[i * 128 : (i + 1) * 128]
                lanes = lanes_of((n * 128, 128))
                keys = jnp.where(lanes < 64, kvs[0], pltpu.roll(kvs[1], 64, 1))
                return state + dot_tn(keys, jnp.concatenate(d_ss, axis=1))

            state = jnp.zeros((128, 256), F32)
            state = lax.fori_loop(0, runs, lambda j, v: step(8, begin + j * 8, v), state)
            state = lax.fori_loop(0, rest, lambda j, v: step(4, begin + runs * 8, v), state)
            state = jnp.concatenate([state[0:64, 0:128], state[64:128, 128:256]], axis=0)
            dq_ref[rows, :] = state.T * 0.125

        @pl.loop(0, 16)
        def _(n):
            for s in (0, 1):
                part = pl.ds(pl.multiple_of(n * 512, 512), 512)
                dkv_ref[s, part, :] = acc_ref[s, part, :].astype(BF)

    return pl.pallas_call(
        kernel,
        in_specs=[SMEM, SMEM, SMEM, SMEM] + [VMEM] * 5,
        out_specs=(VMEM, VMEM),
        scratch_shapes=[pltpu.VMEM((2, 8192, 128), F32)],
        out_shape=(shaped((1024, 128), F32), shaped((2, 8192, 128), BF)),
        compiler_params=pltpu.CompilerParams(vmem_limit_bytes=LIMIT),
        name="attend_back",
    )(inverse, spans, select, ends, q, kv, d_att, att, lse)


def column_of(row):
    return jnp.concatenate(
        [jnp.broadcast_to(row[:, i * 128 : (i + 1) * 128], (128, 128)).T for i in range(8)], axis=0
    )


def feed(rows, atts, wo, w2, wd, cot, gains):
    def kernel(
        x_ref, a_ref, wo_ref, w2_ref, wd_ref, c_ref, g_ref,
        r_ref, out_ref, dmn_ref, gw2_ref, gwd_ref, acc2, accd, accg,
    ):
        step = pl.program_id(0)

        @pl.when(step == 0)
        def _():
            acc2[...] = jnp.zeros_like(acc2)
            accd[...] = jnp.zeros_like(accd)
            accg[...] = jnp.zeros_like(accg)

        att = jnp.concatenate([a_ref[f] for f in range(8)], axis=1)
        resid = x_ref[...].astype(F32) + dot(att, wo_ref[...])
        r_ref[...] = resid
        inv = lax.rsqrt(jnp.sum(resid * resid, axis=1, keepdims=True) * (1.0 / WIDTH) + EPSILON)
        scaled = resid * inv
        mnormed = (scaled * g_ref[1:2, :]).astype(BF)
        both = dot(mnormed, w2_ref[...])
        gate, up = both[:, 0:384], both[:, 384:768]
        sigma = 1.0 / (1.0 + jnp.exp(-gate))
        silu = gate * sigma
        act = (silu * up).astype(BF)
        out_ref[...] = dot(act, wd_ref[...]).astype(BF)
        cot = c_ref[...]
        d_act = dot_nt(cot, wd_ref[...])
        d_gate = (d_act * up * sigma * (1.0 + gate * (1.0 - sigma))).astype(BF)
        d_up = (d_act * silu).astype(BF)
        d_both = jnp.concatenate([d_gate, d_up], axis=1)
        acc2[...] += dot_tn(mnormed, d_both)
        accd[...] += dot_tn(act, cot)
        d_mn = dot_nt(d_both, w2_ref[...])
        dmn_ref[...] = d_mn.astype(BF)
        accg[0:1, :] += jnp.sum(d_mn * scaled, axis=0, keepdims=True)

        @pl.when(step == 3)
        def _():
            gw2_ref[:, 0:768] = acc2[...].astype(BF)
            gw2_ref[:, 768:896] = column_of(accg[0:1, :]).astype(BF)
            gwd_ref[...] = accd[...].astype(BF)

    block = pl.BlockSpec((256, WIDE), lambda i: (i, 0))
    whole = lambda *s: pl.BlockSpec(s, lambda i: (0,) * len(s))
    return pl.pallas_call(
        kernel,
        grid=(4,),
        out_shape=(
            shaped((1024, WIDE), F32),
            shaped((1024, WIDE), BF),
            shaped((1024, WIDE), BF),
            shaped((1024, 896), BF),
            shaped((384, WIDE), BF),
        ),
        in_specs=[
            block,
            pl.BlockSpec((8, 256, 128), lambda i: (0, i, 0)),
            whole(1024, WIDE),
            whole(1024, 768),
            whole(384, WIDE),
            block,
            whole(8, WIDE),
        ],
        out_specs=(block, block, block, whole(1024, 896), whole(384, WIDE)),
        scratch_shapes=[
            pltpu.VMEM((1024, 768), F32),
            pltpu.VMEM((384, WIDE), F32),
            pltpu.VMEM((8, WIDE), F32),
        ],
        compiler_params=pltpu.CompilerParams(vmem_limit_bytes=LIMIT),
        name="feed",
    )(rows, atts, wo, w2, wd, cot, gains)


def turn(me, dmn, out_sum, cp, resid, gains, atts, wo):
    def kernel(
        me_ref, dmn_ref, s_ref, c_ref, r_ref, g_ref, a_ref, wo_ref, out_ref, dr_ref, da_ref, gw_ref
    ):
        spread = spread_value(WIDE)
        resid = r_ref[...]
        out_ref[...] = dot_nt((resid + s_ref[...]).astype(BF), spread[0:WIDTH]).astype(BF)
        inv = lax.rsqrt(jnp.sum(resid * resid, axis=1, keepdims=True) * (1.0 / WIDTH) + EPSILON)
        e = dmn_ref[...] * g_ref[1:2, :]
        mean = jnp.sum(e * resid, axis=1, keepdims=True) * (1.0 / WIDTH)
        d_resid = c_ref[...].astype(F32) + inv * e - resid * (inv * inv * inv * mean)
        dr_ref[...] = d_resid
        mixed = d_resid.astype(BF)
        d_att = dot_nt(mixed, wo_ref[...]).astype(BF)
        for f in range(8):
            da_ref[f] = d_att[:, f * 128 : (f + 1) * 128]
        att = jnp.concatenate([a_ref[f] for f in range(8)], axis=1)
        att = dot(att, spread).astype(BF)
        gw = dot_tn(att, mixed).astype(BF)
        for g in range(8):
            for f in range(8):
                n = (8 * g + f) * 16
                gw_ref[f, g * 16 : (g + 1) * 16, :] = gw[n : n + 16]

    whole = lambda *s: pl.BlockSpec(s, lambda i, me: (0,) * len(s))
    return pl.pallas_call(
        kernel,
        grid_spec=pltpu.PrefetchScalarGridSpec(
            num_scalar_prefetch=1,
            grid=(1,),
            in_specs=[
                whole(128, WIDE),
                whole(128, WIDE),
                whole(128, WIDE),
                pl.BlockSpec((128, WIDE), lambda i, me: (me[0], 0)),
                whole(8, WIDE),
                pl.BlockSpec((8, 128, 128), lambda i, me: (0, me[0], 0)),
                whole(1024, WIDE),
            ],
            out_specs=(whole(128, WIDTH), whole(128, WIDE), whole(8, 128, 128), whole(8, 128, WIDE)),
        ),
        out_shape=(
            shaped((128, WIDTH), BF),
            shaped((128, WIDE), F32),
            shaped((8, 128, 128), BF),
            shaped((8, 128, WIDE), BF),
        ),
        compiler_params=pltpu.CompilerParams(vmem_limit_bytes=LIMIT),
        name="turn",
    )(me, dmn, out_sum, cp, resid, gains, atts, wo)


def project_back(dq, dkv, cos_t, sin_t, w1, normed, rows):
    def kernel(dq_ref, dkv_ref, cos_ref, sin_ref, w_ref, n_ref, x_ref, dn_ref, gw_ref, acc, accg):
        step = pl.program_id(0)

        @pl.when(step == 0)
        def _():
            acc[...] = jnp.zeros_like(acc)
            accg[...] = jnp.zeros_like(accg)

        cos_v, sin_v = cos_ref[...], sin_ref[...]
        dq, dkv = dq_ref[...], dkv_ref[...]
        dq = dq * cos_v - partner(dq) * sin_v
        dk = dkv * cos_v - partner(dkv) * sin_v
        dkv = jnp.where(lanes_of((256, 128)) < 64, dk, dkv)
        d_all = jnp.concatenate([dq, dkv], axis=1).astype(BF)
        acc[...] += dot_tn(n_ref[...], d_all)
        dn = dot_nt(d_all, w_ref[:, 0:256])
        dn_ref[...] = dn.astype(BF)
        x = x_ref[...].astype(F32)
        inv = lax.rsqrt(jnp.sum(x * x, axis=1, keepdims=True) * (1.0 / WIDTH) + EPSILON)
        accg[0:1, :] += jnp.sum(dn * (x * inv), axis=0, keepdims=True)

        @pl.when(step == 3)
        def _():
            gw_ref[:, 0:256] = acc[...].astype(BF)
            gw_ref[:, 256:384] = column_of(accg[0:1, :]).astype(BF)

    block = lambda w: pl.BlockSpec((256, w), lambda i: (i, 0))
    whole = lambda *s: pl.BlockSpec(s, lambda i: (0,) * len(s))
    return pl.pallas_call(
        kernel,
        grid=(4,),
        out_shape=(shaped((1024, WIDE), BF), shaped((1024, 384), BF)),
        in_specs=[
            block(128), block(128), block(128), block(128), whole(WIDE, 384), block(WIDE), block(WIDE)
        ],
        out_specs=(block(WIDE), whole(1024, 384)),
        scratch_shapes=[pltpu.VMEM((1024, 256), F32), pltpu.VMEM((8, WIDE), F32)],
        compiler_params=pltpu.CompilerParams(vmem_limit_bytes=LIMIT),
        name="project_back",
    )(dq, dkv, cos_t, sin_t, w1, normed, rows)


def finish(dn, d_resid, xp, gains, gw1, gw2, gwo, gwd):
    def kernel(
        dn, dr, x, g, w1, w2, wo, wd, gh, g_attn, g_mlp, g_q, g_k, g_v, g_o, g_gate, g_up, g_down
    ):
        spread = spread_value(WIDTH)
        x = x[...].astype(F32)
        inv = lax.rsqrt(jnp.sum(x * x, axis=1, keepdims=True) * (1.0 / WIDTH) + EPSILON)
        c = dn[...] * g[0:1, :]
        mean = jnp.sum(c * x, axis=1, keepdims=True) * (1.0 / WIDTH)
        d_x = dr[...] + inv * c - x * (inv * inv * inv * mean)
        gh[...] = dot_nt(d_x.astype(BF), spread).astype(BF)

        def squeeze(v):
            top = v.astype(BF)
            low = (v - top.astype(F32)).astype(BF)
            return dot_nt(top, spread) + dot_nt(low, spread)

        g_o[...] = squeeze(wo[...])[0:15]
        g_down[...] = squeeze(wd[...])[0:40]
        one = [w1[f].astype(F32)[0:15] for f in range(8)]
        g_q[...] = jnp.concatenate([v[:, 0:128] for v in one], axis=1)[:, 0:WIDTH]

        def heads(n):
            return jnp.concatenate(
                [
                    sum(one[f][:, n : n + 64] for f in range(8) if OWNED_KV[f] == h)
                    for h in range(5)
                ],
                axis=1,
            )

        g_k[...] = heads(128)
        g_v[...] = heads(192)
        g_attn[...] = sum(v[:, 256:384] for v in one)
        two = [w2[f].astype(F32)[0:15] for f in range(8)]
        g_mlp[...] = sum(v[:, 768:896] for v in two)
        for m, ref in ((0, g_gate), (384, g_up)):
            for n in range(0, 8, 2):
                ref[:, n * 320 : n * 320 + 640] = jnp.concatenate(
                    [
                        two[f][:, m + 48 * k : m + 48 * k + 40]
                        for k in (n, n + 1)
                        for f in range(8)
                    ],
                    axis=1,
                )

    return pl.pallas_call(
        kernel,
        out_shape=(
            shaped((128, WIDTH), BF),
            shaped((15, 128), F32),
            shaped((15, 128), F32),
            shaped((15, WIDTH), F32),
            shaped((15, 320), F32),
            shaped((15, 320), F32),
            shaped((15, WIDTH), F32),
            shaped((15, 2560), F32),
            shaped((15, 2560), F32),
            shaped((40, WIDTH), F32),
        ),
        in_specs=[VMEM] * 8,
        out_specs=(VMEM,) * 10,
        compiler_params=pltpu.CompilerParams(vmem_limit_bytes=LIMIT),
        name="finish",
    )(dn, d_resid, xp, gains, gw1, gw2, gwo, gwd)


def local(
    hidden, attn_gain, w_q, w_k, w_v, w_o, mlp_gain, w_gate, w_up, w_down, cotangent,
    doc_lengths, span_order,
):
    i = lax.axis_index("ctx")
    group, me = i // 8, i % 8
    ends = jnp.stack([doc_lengths[0], doc_lengths[0] + doc_lengths[1]])
    spans = lax.dynamic_slice(span_order, (group * 8,), (8,))
    ids = jnp.arange(64, dtype=jnp.int32)
    inverse = jnp.sum(jnp.where(span_order[None, :] == ids[:, None], ids[None, :], 0), axis=1)
    select = jnp.asarray(SELECT, jnp.int32)[me]
    frequency = ROPE_BASE ** (-2.0 * (np.arange(128) % 32) / HEAD)
    frequency = jnp.asarray(frequency, F32).reshape(1, 128)

    rows, w1, wos, wds, xp, cp, wp2, cos_t, sin_t = gather_first(
        hidden, cotangent, w_q, w_k, w_v, w_o, w_gate, w_up, w_down, attn_gain.reshape(15, 1),
        mlp_gain.reshape(15, 1), ends, span_order, frequency,
    )
    rows = rows.reshape(1024, WIDE)
    w1 = w1.reshape(1024, 384)
    normed, q, kv_own, gains = project(rows, w1, cos_t, sin_t)
    kv, wo, cot, w2own = gather_keys(kv_own, wos, cp, wp2)
    kv = kv.reshape(2, 8192, 128)
    att, lse = attend(inverse, spans, select, ends, q, kv)
    atts, w2, wo = gather_heads(att, w2own, wo)
    resid, outp, dmn, gw2, gwd = feed(
        rows, atts, wo, w2.reshape(1024, 768), wds.reshape(384, WIDE), cot.reshape(1024, WIDE), gains
    )
    dmn_sum, out_sum, gw2s, gwds = sum_feed(
        dmn.reshape(8, 128, WIDE),
        outp.reshape(8, 128, WIDE),
        gw2.reshape(8, 8, 16, 896),
        gwd.reshape(8, 48, WIDE),
    )
    output, d_resid, d_att, gwo = turn(
        me.reshape(1), dmn_sum, out_sum, cp, resid, gains, atts, wo
    )
    d_att = swap_heads(d_att).reshape(1024, 128)
    dq, dkv = attend_back(inverse, spans, select, ends, q, kv, d_att, att, lse)
    dkv_sum, gwo = sum_keys(dkv.reshape(2, 8, 1024, 128), gwo)
    dn, gw1 = project_back(dq, dkv_sum, cos_t, sin_t, w1, normed, rows)
    dn_sum, gw1s, gwos = sum_normed(
        dn.reshape(8, 128, WIDE), gw1.reshape(8, 8, 16, 384), gwo.reshape(8, 16, WIDE)
    )
    gw1s, gw2s = swap_grads(gw1s, gw2s)
    grad_hidden, g_attn, g_mlp, g_q, g_k, g_v, g_o, g_gate, g_up, g_down = finish(
        dn_sum, d_resid, xp, gains, gw1s, gw2s, gwos, gwds
    )
    return (
        output, grad_hidden, g_attn[:, 0], g_q, g_k, g_v, g_o, g_mlp[:, 1], g_gate, g_up, g_down
    )


def solution(mesh):
    both = ("fsdp", "ctx")
    wide, thin, part = P(both, None), P(both), P("fsdp")
    return jax.shard_map(
        local,
        mesh=mesh,
        in_specs=(wide, thin, wide, wide, wide, wide, thin, wide, wide, wide, wide, part, part),
        out_specs=(wide, wide, thin, wide, wide, wide, wide, thin, wide, wide, wide),
        check_vma=False,
    )
```

```python
import jax
import jax.numpy as jnp
import numpy as np
from jax import lax
from jax.experimental import pallas as pl
from jax.experimental.pallas import tpu as pltpu
from jax.sharding import PartitionSpec as P

HEAD = 64
EPSILON = 1e-05
ROPE_BASE = 100000.0
MASKED = -1e30
WIDE = 1024
WIDTH = 960
BF = jnp.bfloat16
F32 = jnp.float32
MESH = pl.DeviceIdType.MESH
DMA = pltpu.SemaphoreType.DMA
ANY = pl.BlockSpec(memory_space=pl.ANY)
VMEM = pl.BlockSpec(memory_space=pltpu.VMEM)
SMEM = pl.BlockSpec(memory_space=pltpu.SMEM)
LIMIT = 56 * 2**20
TILE = 4
OWNED_KV = (0, 1, 1, 2, 2, 3, 4, 4)
SELECT = ((0, 0), (0, 1), (0, 0), (1, 1), (0, 1), (1, 1), (0, 0), (0, 0))


def dot(a, b):
    return lax.dot_general(a, b, (((1,), (0,)), ((), ())), preferred_element_type=F32)


def dot_nt(a, b):
    return lax.dot_general(a, b, (((1,), (1,)), ((), ())), preferred_element_type=F32)


def dot_tn(a, b):
    return lax.dot_general(a, b, (((0,), (0,)), ((), ())), preferred_element_type=F32)


def shaped(shape, dtype):
    return jax.ShapeDtypeStruct(shape, dtype)


def place():
    i = lax.axis_index("ctx")
    return i // 16, (i // 8) % 2, (i // 2) % 4, i % 2


def at(x, z, y, c):
    return {"ctx": (((x + 4) % 4) * 2 + z) * 8 + ((y + 4) % 4) * 2 + c}


def send(src, dst, ssem, rsem, device):
    copy = pltpu.make_async_remote_copy(
        src, dst, ssem, rsem, device_id=device, device_id_type=MESH
    )
    copy.start()
    return copy


def hail(kinds):
    x, z, y, c = place()
    who = []
    if "x" in kinds:
        who += [at(x + 1, z, y, c), at(x - 1, z, y, c), at(x, 1 - z, y, c)]
    if "f" in kinds:
        who += [at(x, z, y + d, (c + e) % 2) for d in range(4) for e in range(2) if d + e]
    elif "y" in kinds:
        who += [at(x, z, y + d, c) for d in (1, 2, 3)] + [at(x, z, y, 1 - c)]
    barrier = pltpu.get_barrier_semaphore()
    for device in who:
        pl.semaphore_signal(barrier, inc=1, device_id=device, device_id_type=MESH)
    return len(who)


def greet(kinds):
    pl.semaphore_wait(pltpu.get_barrier_semaphore(), hail(kinds))


def half_lead(ref, k):
    n = ref.shape[0] // 2
    return ref.at[pl.ds(k * n, n)]


def half_lanes(ref, k):
    n = ref.shape[-1] // 2
    return ref.at[:, pl.ds(k * n, n)]


class RingGather:
    sems = [DMA((9,)), DMA((9,)), DMA(())]

    def __init__(self, src, dst, half, ssem, rsem, lsem, arrived=None):
        self.src, self.dst, self.half = src, dst, half
        self.ssem, self.rsem, self.lsem = ssem, rsem, lsem
        self.arrived = arrived or (lambda block: None)
        self.copies = {}

    def push(self, n, src, dst, device):
        self.copies[n] = send(src, dst, self.ssem.at[n], self.rsem.at[n], device)

    def start(self):
        x, z, y, c = place()
        me = self.dst.at[x * 2 + z]
        self.push(0, self.src, me, at(x, 1 - z, y, c))
        self.push(1, self.src, me, at(x + 1, z, y, c))
        self.push(2, self.src, me, at(x - 1, z, y, c))
        self.local = pltpu.make_async_copy(self.src, me, self.lsem)
        self.local.start()

    def relay_z(self):
        x, z, y, c = place()
        block = self.dst.at[x * 2 + 1 - z]
        self.copies[0].wait_recv()
        self.push(3, block, block, at(x + 1, z, y, c))
        self.push(4, block, block, at(x - 1, z, y, c))
        self.arrived(x * 2 + 1 - z)

    def relay_x(self, k):
        x, z, y, c = place()
        zz = z if k == 0 else 1 - z
        left, right = ((x + 3) % 4) * 2 + zz, ((x + 1) % 4) * 2 + zz
        self.copies[1 + 2 * k].wait_recv()
        part = self.half(self.dst.at[left], 0)
        self.push(5 + 2 * k, part, part, at(x + 1, z, y, c))
        self.arrived(left)
        self.copies[2 + 2 * k].wait_recv()
        part = self.half(self.dst.at[right], 1)
        self.push(6 + 2 * k, part, part, at(x - 1, z, y, c))
        self.arrived(right)

    def land(self, k):
        x, z, y, c = place()
        zz = z if k == 0 else 1 - z
        self.copies[5 + 2 * k].wait_recv()
        self.copies[6 + 2 * k].wait_recv()
        self.arrived(((x + 2) % 4) * 2 + zz)

    def finish(self):
        self.local.wait()
        for n in range(9):
            self.copies[n].wait_send()


def run_ring_gathers(rings):
    for ring in rings:
        ring.relay_z()
    for k in (0, 1):
        for ring in rings:
            ring.relay_x(k)
    for k in (0, 1):
        for ring in rings:
            ring.land(k)


class RowGather:
    sems = [DMA((8,)), DMA((8,)), DMA(())]

    def __init__(self, src, dst, ssem, rsem, lsem):
        self.src, self.dst = src, dst
        self.ssem, self.rsem, self.lsem = ssem, rsem, lsem
        self.copies = {}

    def push(self, n, src, dst, device):
        self.copies[n] = send(src, dst, self.ssem.at[n], self.rsem.at[n], device)

    def start(self):
        x, z, y, c = place()
        me = self.dst.at[y * 2 + c]
        self.push(1, self.src, me, at(x, z, y + 1, c))
        self.push(2, self.src, me, at(x, z, y - 1, c))
        self.push(0, self.src, me, at(x, z, y, 1 - c))
        self.local = pltpu.make_async_copy(self.src, me, self.lsem)
        self.local.start()

    def relay(self):
        x, z, y, c = place()
        for n, step, side in ((1, 3, 0), (2, 1, 1)):
            self.copies[n].wait_recv()
            block = self.dst.at[((y + step) % 4) * 2 + c]
            part = half_lead(block, side)
            self.push(2 + n, part, part, at(x, z, y + 4 - step, c))
            self.push(4 + n, block, block, at(x, z, y, 1 - c))

    def land(self):
        x, z, y, c = place()
        self.copies[3].wait_recv()
        self.copies[4].wait_recv()
        block = self.dst.at[((y + 2) % 4) * 2 + c]
        self.push(7, block, block, at(x, z, y, 1 - c))

    def finish(self):
        self.local.wait()
        for n in (0, 5, 6, 7):
            self.copies[n].wait_recv()
        for n in range(8):
            self.copies[n].wait_send()


class Swap:
    sems = [DMA((8,)), DMA((8,)), DMA(())]

    def __init__(self, src, dst, ssem, rsem, lsem):
        self.src, self.dst = src, dst
        self.ssem, self.rsem, self.lsem = ssem, rsem, lsem

    def start(self):
        x, z, y, c = place()
        me = y * 2 + c
        self.copies = []
        for d in (2, 1, 3, 0):
            for e in (0, 1):
                if d + e:
                    n = d * 2 + e
                    to = ((y + d) % 4) * 2 + (c + e) % 2
                    self.copies.append(
                        send(
                            self.src.at[to],
                            self.dst.at[me],
                            self.ssem.at[n],
                            self.rsem.at[n],
                            at(x, z, y + d, (c + e) % 2),
                        )
                    )
        self.local = pltpu.make_async_copy(self.src.at[me], self.dst.at[me], self.lsem)
        self.local.start()

    def finish(self):
        self.local.wait()
        for copy in self.copies:
            copy.wait()


class RowSum:
    @staticmethod
    def scratch(shape):
        return [
            pltpu.VMEM((4,) + shape, BF),
            pltpu.VMEM((4,) + shape, BF),
            pltpu.VMEM((4,) + shape, BF),
            DMA((8,)),
            DMA((8,)),
        ]

    def __init__(self, blk, first, mixed, second, ssem, rsem):
        self.blk, self.first, self.mixed, self.second = blk, first, mixed, second
        self.ssem, self.rsem = ssem, rsem
        self.copies = {}

    def push(self, n, src, dst, device):
        self.copies[n] = send(src, dst, self.ssem.at[n], self.rsem.at[n], device)

    def hand(self, d):
        x, z, y, c = place()
        to = ((y + d) % 4) * 2 + 1 - c
        self.push(d, self.blk.at[to], self.first.at[d], at(x, z, y, 1 - c))

    def start(self):
        for d in (2, 1, 3, 0):
            self.hand(d)

    def relay(self):
        x, z, y, c = place()
        for d in (2, 1, 3):
            self.copies[d].wait_recv()
            own = self.blk[((y + d) % 4) * 2 + c].astype(F32)
            self.mixed[d] = (own + self.first[d].astype(F32)).astype(BF)
            self.push(4 + d, self.mixed.at[d], self.second.at[d], at(x, z, y + d, c))

    def total(self):
        x, z, y, c = place()
        self.copies[0].wait_recv()
        total = self.blk[y * 2 + c].astype(F32) + self.first[0].astype(F32)
        for d in (1, 3, 2):
            self.copies[4 + d].wait_recv()
            total = total + self.second[d].astype(F32)
        return total

    def finish(self):
        for n in (0, 1, 2, 3, 5, 6, 7):
            self.copies[n].wait_send()


class RingSum:
    @staticmethod
    def scratch(shape, lanes):
        if lanes:
            part = shape[:-1] + (shape[-1] // 2,)
        else:
            part = (shape[0] // 2,) + shape[1:]
        return [
            pltpu.VMEM((4,) + part, BF),
            pltpu.VMEM((4,) + shape, BF),
            pltpu.VMEM((4,) + shape, BF),
            pltpu.VMEM((2,) + shape, BF),
            DMA((9,)),
            DMA((9,)),
        ]

    def __init__(self, blk, lanes, parts, mixed, heard, across, ssem, rsem):
        self.blk, self.half = blk, half_lanes if lanes else half_lead
        self.parts, self.mixed, self.heard, self.across = parts, mixed, heard, across
        self.ssem, self.rsem = ssem, rsem
        self.copies = {}

    def push(self, n, src, dst, device):
        self.copies[n] = send(src, dst, self.ssem.at[n], self.rsem.at[n], device)

    def start(self, k):
        x, z, y, c = place()
        zz = 1 - z if k == 0 else z
        far = self.blk.at[((x + 2) % 4) * 2 + zz]
        self.push(4 * k, self.half(far, 0), self.parts.at[2 * k], at(x + 1, z, y, c))
        self.push(4 * k + 1, self.half(far, 1), self.parts.at[2 * k + 1], at(x - 1, z, y, c))

    def relay(self, k):
        x, z, y, c = place()
        zz = 1 - z if k == 0 else z
        for side, step in ((0, 1), (1, 3)):
            n = 2 * k + side
            mixed = self.mixed.at[n]
            source = self.blk.at[((x + step) % 4) * 2 + zz]
            mine, other = self.half(source, side), self.half(source, 1 - side)
            self.half(mixed, 1 - side)[...] = other[...]
            self.copies[4 * k + side].wait_recv()
            self.half(mixed, side)[...] = (
                mine[...].astype(F32) + self.parts[n].astype(F32)
            ).astype(BF)
            self.push(4 * k + 2 + side, mixed, self.heard.at[n], at(x + step, z, y, c))

    def total(self, k):
        x, z, y, c = place()
        zz = 1 - z if k == 0 else z
        total = self.blk[x * 2 + zz].astype(F32)
        for side in (0, 1):
            self.copies[4 * k + 2 + side].wait_recv()
            total = total + self.heard[2 * k + side].astype(F32)
        if k == 0:
            self.across[0] = total.astype(BF)
            self.push(8, self.across.at[0], self.across.at[1], at(x, 1 - z, y, c))
            return None
        self.copies[8].wait_recv()
        return total + self.across[1].astype(F32)

    def finish(self):
        for n in range(9):
            self.copies[n].wait_send()


def comm_call(name, number, kernel, out_shape, in_specs, out_specs, scratch, args):
    return pl.pallas_call(
        kernel,
        out_shape=out_shape,
        in_specs=in_specs,
        out_specs=out_specs,
        scratch_shapes=scratch,
        compiler_params=pltpu.CompilerParams(
            collective_id=number, has_side_effects=True, vmem_limit_bytes=LIMIT
        ),
        name=name,
    )(*args)


def split(refs, counts):
    parts, begin = [], 0
    for n in counts:
        parts.append(refs[begin : begin + n])
        begin += n
    return parts


def spread_value(rows):
    j = lax.broadcasted_iota(jnp.int32, (rows, WIDE), 0)
    k = lax.broadcasted_iota(jnp.int32, (rows, WIDE), 1)
    hit = ((k // 16) * 15 + k % 16 == j) & (k % 16 < 15)
    return jnp.where(hit, 1.0, 0.0).astype(BF)


def gather_first(
    hidden, cot, w_q, w_k, w_v, w_o, w_gate, w_up, w_down, gain1, gain2, ends, span_order, frequency
):
    def kernel(
        hidden, cot, w_q, w_k, w_v, w_o, w_gate, w_up, w_down, gain1, gain2, ends, order, freq,
        rows, w1, wos, wds, xp, cp, wp2, cos_t, sin_t, wp1, wop, wdp, w1own, *sems,
    ):
        a, b, d, e, e2 = split(sems, (3, 3, 3, 3, 3))
        x, z, y, c = place()
        partners = hail("xf")

        q = jnp.concatenate([w_q[...].astype(F32), jnp.zeros((15, 64), F32)], axis=1)
        k, v = w_k[...].astype(F32), w_v[...].astype(F32)
        gains = jnp.concatenate(
            [gain1[...].astype(F32), gain2[...].astype(F32), jnp.zeros((15, 126), F32)], axis=1
        )
        wp1[...] = jnp.zeros(wp1.shape, BF)
        for f in range(8):
            n = OWNED_KV[f] * 64
            wp1[f, 0:15, 0:128] = q[:, 128 * f : 128 * f + 128].astype(BF)
            wp1[f, 0:15, 128:256] = jnp.concatenate(
                [k[:, n : n + 64], v[:, n : n + 64]], axis=1
            ).astype(BF)
            wp1[f, 0:15, 256:384] = gains.astype(BF)

        pl.semaphore_wait(pltpu.get_barrier_semaphore(), partners)
        swap = Swap(wp1, w1own, *b)
        swap.start()
        spread = spread_value(WIDTH)
        xp[...] = dot(hidden[...], spread).astype(BF)
        gather = RowGather(xp, rows, *a)
        gather.start()
        wop[...] = jnp.zeros(wop.shape, BF)
        wop[0:15, :] = dot(w_o[...], spread).astype(BF)
        wdp[...] = jnp.zeros(wdp.shape, BF)
        wdp[0:40, :] = dot(w_down[...], spread).astype(BF)
        ring_o = RingGather(wop, wos, half_lanes, *e)
        ring_d = RingGather(wdp, wds, half_lanes, *e2)
        ring_o.start()
        ring_d.start()
        swap.finish()
        ring_1 = RingGather(w1own, w1, half_lead, *d)
        ring_1.start()
        cp[...] = dot(cot[...], spread).astype(BF)
        gather.relay()
        rings = [ring_1, ring_o, ring_d]
        for ring in rings:
            ring.relay_z()

        wp2[...] = jnp.zeros(wp2.shape, BF)
        gap = jnp.zeros((15, 8), F32)
        for m, ref in ((0, w_gate), (384, w_up)):
            w = ref[...].astype(F32)
            for f in range(8):
                parts = []
                for g in range(8):
                    n = (8 * g + f) * 40
                    parts += [w[:, n : n + 40], gap]
                wp2[f, 0:15, m : m + 384] = jnp.concatenate(parts, axis=1).astype(BF)

        for k in (0, 1):
            for ring in rings:
                ring.relay_x(k)

        lane = lanes_of((1, 128))
        sign = jnp.where(lane % 64 < 32, -1.0, 1.0)

        @pl.loop(0, 8)
        def _(n):
            pos = order[(x * 2 + z) * 8 + n] * 128
            pos = pos + lax.broadcasted_iota(jnp.int32, (128, 1), 0)
            angle = (pos - doc_start(pos, ends)).astype(F32) * freq[...]
            part = pl.ds(pl.multiple_of(n * 128, 128), 128)
            cos_t[part, :] = jnp.cos(angle)
            sin_t[part, :] = sign * jnp.sin(angle)

        gather.land()
        for k in (0, 1):
            for ring in rings:
                ring.land(k)
        gather.finish()
        for ring in rings:
            ring.finish()

    return comm_call(
        "gather_first",
        1,
        kernel,
        (
            shaped((8, 128, WIDE), BF),
            shaped((8, 8, 16, 384), BF),
            shaped((8, 16, WIDE), BF),
            shaped((8, 48, WIDE), BF),
            shaped((128, WIDE), BF),
            shaped((128, WIDE), BF),
            shaped((8, 16, 768), BF),
            shaped((1024, 128), F32),
            shaped((1024, 128), F32),
        ),
        [VMEM] * 11 + [SMEM, SMEM, VMEM],
        (ANY,) * 4 + (VMEM,) * 5,
        [
            pltpu.VMEM((8, 16, 384), BF),
            pltpu.VMEM((16, WIDE), BF),
            pltpu.VMEM((48, WIDE), BF),
            pltpu.VMEM((8, 16, 384), BF),
        ]
        + RowGather.sems
        + Swap.sems
        + RingGather.sems * 3,
        (
            hidden, cot, w_q, w_k, w_v, w_o, w_gate, w_up, w_down, gain1, gain2, ends, span_order,
            frequency,
        ),
    )


def gather_keys(kv, wos, cp, wp2):
    def kernel(kv, wos, cp, wp2, kv2, wo, cot, w2own, *sems):
        a, b, d, e, (hs, hr) = split(sems, (3, 3, 3, 3, 2))
        x, z, y, c = place()
        greet("xf")
        hand = []

        def arrived(block):
            n = len(hand)
            piece = kv2.at[c, block]
            hand.append(send(piece, piece, hs.at[n], hr.at[n], at(x, z, y, 1 - c)))

        ring = RingGather(kv, kv2.at[c], half_lead, *a, arrived=arrived)
        gather_o = RowGather(wos, wo, *b)
        gather_c = RowGather(cp, cot, *d)
        swap = Swap(wp2, w2own, *e)
        ring.start()
        gather_o.start()
        gather_c.start()
        swap.start()
        me = kv2.at[c, x * 2 + z]
        hand.append(send(kv, me, hs.at[0], hr.at[0], at(x, z, y, 1 - c)))
        ring.relay_z()
        gather_o.relay()
        ring.relay_x(0)
        gather_c.relay()
        ring.relay_x(1)
        gather_o.land()
        gather_c.land()
        ring.land(0)
        ring.land(1)
        for copy in hand:
            copy.wait()
        swap.finish()
        gather_o.finish()
        gather_c.finish()
        ring.finish()

    return comm_call(
        "gather_keys",
        2,
        kernel,
        (
            shaped((2, 8, 1024, 128), BF),
            shaped((8, 8, 16, WIDE), BF),
            shaped((8, 128, WIDE), BF),
            shaped((8, 16, 768), BF),
        ),
        [ANY] * 4,
        (ANY,) * 4,
        RingGather.sems + RowGather.sems * 2 + Swap.sems + [DMA((8,)), DMA((8,))],
        (kv, wos, cp, wp2),
    )


def inverse_rms(v):
    return lax.rsqrt(jnp.sum(v * v, axis=1, keepdims=True) * (1.0 / WIDTH) + EPSILON)


def feed(att, w2own, wo, rows, wd, cot, gains):
    def kernel(
        att, w2own, wo, x_ref, wd, cot, gains,
        output, d_resid, d_heads, gwo, gw2_sum, gwd_sum,
        atts, w2, packed, d_act, resid, normed, act, d_both, dmn, outp, gw2, gwd, accg, da,
        *refs,
    ):
        a, b, s, r1, r2, t1, t2 = split(refs, (3, 3, 3, 5, 5, 6, 6))
        x, z, y, c = place()
        me = y * 2 + c
        greet("xf")
        gather = RowGather(att, atts, *a)
        ring = RingGather(w2own, w2, half_lead, *b)
        gather.start()
        ring.start()

        def place_rows(n, size):
            return pl.ds(pl.multiple_of(n * size, size), size)

        whole = jnp.concatenate([wo[f, g] for g in range(8) for f in range(8)], axis=0)

        def pack(n):
            j = lax.broadcasted_iota(jnp.int32, (256, WIDE), 0) + n * 256
            k = lax.broadcasted_iota(jnp.int32, (256, WIDE), 1)
            hit = ((k // 16) * 15 + k % 16 == j) & (k % 16 < 15)
            packed[pl.ds(n * 256, 256), :] = dot(
                jnp.where(hit, 1.0, 0.0).astype(BF), whole
            ).astype(BF)

        pack(0)
        pack(1)
        ring.relay_z()
        gather.relay()
        pack(2)
        pack(3)
        ring.relay_x(0)

        @pl.loop(0, 4)
        def _(n):
            part = place_rows(n, 256)
            d_act[part, :] = dot_nt(cot[part, :], wd[...])

        ring.relay_x(1)
        gather.land()
        gather.finish()

        @pl.loop(0, 4)
        def _(n):
            part = place_rows(n, 256)
            heads = jnp.concatenate([atts[f, part, :] for f in range(8)], axis=1)
            v = x_ref[part, :].astype(F32) + dot(heads, packed[...])
            resid[part, :] = v
            normed[part, :] = (v * inverse_rms(v) * gains[1:2, :]).astype(BF)

        ring.land(0)
        ring.land(1)
        ring.finish()
        w2_all = w2.reshape(WIDE, 768)

        @pl.loop(0, 4)
        def _(n):
            part = place_rows(n, 256)
            both = dot(normed[part, :], w2_all[...])
            gate, up = both[:, 0:384], both[:, 384:768]
            sigma = 1.0 / (1.0 + jnp.exp(-gate))
            silu = gate * sigma
            act[part, :] = (silu * up).astype(BF)
            d = d_act[part, :]
            d_both[part, 0:384] = (d * up * sigma * (1.0 + gate * (1.0 - sigma))).astype(BF)
            d_both[part, 384:768] = (d * silu).astype(BF)

        sum_n, sum_o = RowSum(dmn, *r1), RowSum(outp, *r2)
        ring_2, ring_d = RingSum(gw2, False, *t1), RingSum(gwd, True, *t2)
        accg[...] = jnp.zeros(accg.shape, F32)

        def back(to):
            part = place_rows(to, 128)
            d = dot_nt(d_both[part, :], w2_all[...])
            v = resid[part, :]
            accg[0:1, :] += jnp.sum(d * (v * inverse_rms(v)), axis=0, keepdims=True)
            dmn[to] = d.astype(BF)

        for d in (2, 1, 3, 0):
            back(((y + d) % 4) * 2 + 1 - c)
            sum_n.hand(d)
        for d in (2, 1, 3, 0):
            back(((y + d) % 4) * 2 + c)
        sum_n.relay()

        def weights(g):
            part = place_rows(g, 128)
            gw2[g, :, :, 0:768] = (
                dot_tn(normed[:, part], d_both[...]).astype(BF).reshape(8, 16, 768)
            )
            column = jnp.broadcast_to(accg[0:1, part], (128, 128)).T
            gw2[g, :, :, 768:896] = column.astype(BF).reshape(8, 16, 128)

        order = [(2, 1), (2, 0), (1, 1), (3, 1), (1, 0), (3, 0), (0, 1), (0, 0)]
        where = [((x + p) % 4) * 2 + (1 - z if q else z) for p, q in order]
        weights(where[0])
        ring_2.start(0)
        weights(where[1])
        ring_2.start(1)
        gwd[...] = dot_tn(act[...], cot[...]).astype(BF).reshape(8, 48, WIDE)
        ring_d.start(0)
        ring_d.start(1)
        for n in range(2, 8):
            weights(where[n])

        @pl.loop(0, 8)
        def _(n):
            outp[n] = dot(act[place_rows(n, 128), :], wd[...]).astype(BF)

        sum_o.start()
        for k in (0, 1):
            ring_2.relay(k)
            ring_d.relay(k)
        sum_o.relay()

        mine = place_rows(me, 128)
        d_normed = sum_n.total()
        v = resid[mine, :]
        inv = inverse_rms(v)
        e = d_normed * gains[1:2, :]
        mean = jnp.sum(e * v, axis=1, keepdims=True) * (1.0 / WIDTH)
        d_v = cot[mine, :].astype(F32) + inv * e - v * (inv * inv * inv * mean)
        d_resid[...] = d_v
        mixed = d_v.astype(BF)
        d_att = dot_nt(mixed, packed[...]).astype(BF)
        for f in range(8):
            da[f] = d_att[:, f * 128 : (f + 1) * 128]
        swap = Swap(da, d_heads, *s)
        swap.start()
        spread = spread_value(WIDE)
        heads = jnp.concatenate([atts[f, mine, :] for f in range(8)], axis=1)
        gw = dot_tn(dot(heads, spread).astype(BF), mixed).astype(BF)
        for g in range(8):
            for f in range(8):
                n = (8 * g + f) * 16
                gwo[f, g * 16 : (g + 1) * 16, :] = gw[n : n + 16]
        ring_2.total(0)
        ring_d.total(0)
        output[...] = dot_nt((v + sum_o.total()).astype(BF), spread[0:WIDTH]).astype(BF)
        gw2_sum[...] = ring_2.total(1).astype(BF)
        gwd_sum[...] = ring_d.total(1)
        swap.finish()
        sum_n.finish()
        sum_o.finish()
        ring_2.finish()
        ring_d.finish()

    return comm_call(
        "feed",
        3,
        kernel,
        (
            shaped((128, WIDTH), BF),
            shaped((128, WIDE), F32),
            shaped((8, 128, 128), BF),
            shaped((8, 128, WIDE), BF),
            shaped((8, 16, 896), BF),
            shaped((48, WIDE), F32),
        ),
        [ANY, ANY] + [VMEM] * 5,
        (VMEM, VMEM, ANY, VMEM, VMEM, VMEM),
        [
            pltpu.VMEM((8, 1024, 128), BF),
            pltpu.VMEM((8, 8, 16, 768), BF),
            pltpu.VMEM((WIDE, WIDE), BF),
            pltpu.VMEM((1024, 384), F32),
            pltpu.VMEM((1024, WIDE), F32),
            pltpu.VMEM((1024, WIDE), BF),
            pltpu.VMEM((1024, 384), BF),
            pltpu.VMEM((1024, 768), BF),
            pltpu.VMEM((8, 128, WIDE), BF),
            pltpu.VMEM((8, 128, WIDE), BF),
            pltpu.VMEM((8, 8, 16, 896), BF),
            pltpu.VMEM((8, 48, WIDE), BF),
            pltpu.VMEM((8, WIDE), F32),
            pltpu.VMEM((8, 128, 128), BF),
        ]
        + RowGather.sems
        + RingGather.sems
        + Swap.sems
        + RowSum.scratch((128, WIDE)) * 2
        + RingSum.scratch((8, 16, 896), False)
        + RingSum.scratch((48, WIDE), True),
        (att, w2own, wo, rows, wd, cot, gains),
    )


def sum_keys(dkv, gwo):
    def kernel(dkv, gwo, dkv_sum, gwo_sum, blk, from_core, hs, hr, *refs):
        a, d = split(refs, (6, 5))
        x, z, y, c = place()
        greet("xy")
        order = [(2, 1), (2, 0), (1, 1), (3, 1), (1, 0), (3, 0), (0, 1), (0, 0)]
        where = [((x + p) % 4) * 2 + (1 - z if q else z) for p, q in order]
        hand = [
            send(dkv.at[1 - c, g], from_core.at[n], hs.at[n], hr.at[n], at(x, z, y, 1 - c))
            for n, g in enumerate(where)
        ]
        rows_w = RowSum(gwo, *d)
        rows_w.start()
        ring = RingSum(blk, False, *a)

        def fold(n):
            g = where[n]
            hand[n].wait_recv()
            blk[g] = (dkv[c, g].astype(F32) + from_core[n].astype(F32)).astype(BF)

        fold(0)
        ring.start(0)
        fold(1)
        ring.start(1)
        for n in range(2, 6):
            fold(n)
        rows_w.relay()
        ring.relay(0)
        ring.relay(1)
        fold(6)
        fold(7)
        ring.total(0)
        gwo_sum[...] = rows_w.total().astype(BF)
        dkv_sum[...] = ring.total(1)
        for copy in hand:
            copy.wait_send()
        ring.finish()
        rows_w.finish()

    return comm_call(
        "sum_keys",
        6,
        kernel,
        (shaped((1024, 128), F32), shaped((128, WIDE), BF)),
        [VMEM] * 2,
        (VMEM,) * 2,
        [pltpu.VMEM((8, 1024, 128), BF), pltpu.VMEM((8, 1024, 128), BF), DMA((8,)), DMA((8,))]
        + RingSum.scratch((1024, 128), False)
        + RowSum.scratch((128, WIDE)),
        (dkv, gwo),
    )


def sum_normed(dn, gw1, gwo):
    def kernel(dn, gw1, gwo, dn_sum, gw1_sum, gwo_sum, *refs):
        a, b, d = split(refs, (5, 6, 6))
        greet("xy")
        rows = RowSum(dn, *a)
        ring_1 = RingSum(gw1, False, *b)
        ring_o = RingSum(gwo, True, *d)
        rows.start()
        for k in (0, 1):
            ring_1.start(k)
            ring_o.start(k)
        rows.relay()
        for k in (0, 1):
            ring_1.relay(k)
            ring_o.relay(k)
        ring_1.total(0)
        ring_o.total(0)
        gw1_sum[...] = ring_1.total(1).astype(BF)
        gwo_sum[...] = ring_o.total(1)
        dn_sum[...] = rows.total()
        rows.finish()
        ring_1.finish()
        ring_o.finish()

    return comm_call(
        "sum_normed",
        7,
        kernel,
        (shaped((128, WIDE), F32), shaped((8, 16, 384), BF), shaped((16, WIDE), F32)),
        [VMEM] * 3,
        (VMEM,) * 3,
        RowSum.scratch((128, WIDE))
        + RingSum.scratch((8, 16, 384), False)
        + RingSum.scratch((16, WIDE), True),
        (dn, gw1, gwo),
    )


def swap_grads(gw1, gw2):
    def kernel(gw1, gw2, out1, out2, *sems):
        a, b = split(sems, (3, 3))
        greet("f")
        one, two = Swap(gw1, out1, *a), Swap(gw2, out2, *b)
        one.start()
        two.start()
        one.finish()
        two.finish()

    return comm_call(
        "swap_grads",
        8,
        kernel,
        (shaped((8, 16, 384), BF), shaped((8, 16, 896), BF)),
        [ANY] * 2,
        (ANY,) * 2,
        Swap.sems + Swap.sems,
        (gw1, gw2),
    )


def lanes_of(shape):
    return lax.broadcasted_iota(jnp.int32, shape, len(shape) - 1)


def partner(v):
    lane = lanes_of(v.shape)
    return jnp.where(lane % 64 < 32, pltpu.roll(v, 96, 1), pltpu.roll(v, 32, 1))


def project(rows, w1, cos_t, sin_t):
    def kernel(x_ref, w_ref, cos_ref, sin_ref, n_ref, q_ref, kv_ref, g_ref):
        @pl.when(pl.program_id(0) == 0)
        def _():
            eye = (
                lax.broadcasted_iota(jnp.int32, (8, 128), 0) == lanes_of((8, 128))
            ).astype(BF)
            g_ref[...] = dot_nt(eye, w_ref[:, 256:384])

        x = x_ref[...].astype(F32)
        inv = lax.rsqrt(jnp.sum(x * x, axis=1, keepdims=True) * (1.0 / WIDTH) + EPSILON)
        normed = (x * inv * g_ref[0:1, :]).astype(BF)
        n_ref[...] = normed
        out = dot(normed, w_ref[:, 0:256])
        cos_v, sin_v = cos_ref[...], sin_ref[...]
        lane = lanes_of((256, 128))
        q, kv = out[:, 0:128], out[:, 128:256]
        q = (q * cos_v + partner(q) * sin_v).astype(BF).astype(F32) * 0.125
        k = kv * cos_v + partner(kv) * sin_v
        kv_ref[...] = jnp.where(lane < 64, k, kv).astype(BF)
        q_ref[0] = jnp.where(lane < 64, q, 0.0).astype(BF)
        q_ref[1] = jnp.where(lane < 64, pltpu.roll(q, 64, 1), 0.0).astype(BF)

    block = lambda w: pl.BlockSpec((256, w), lambda i: (i, 0))
    return pl.pallas_call(
        kernel,
        grid=(4,),
        out_shape=(
            shaped((1024, WIDE), BF),
            shaped((2, 1024, 128), BF),
            shaped((1024, 128), BF),
            shaped((8, WIDE), F32),
        ),
        in_specs=[block(WIDE), pl.BlockSpec((WIDE, 384), lambda i: (0, 0)), block(128), block(128)],
        out_specs=(
            block(WIDE),
            pl.BlockSpec((2, 256, 128), lambda i: (0, i, 0)),
            block(128),
            pl.BlockSpec((8, WIDE), lambda i: (0, 0)),
        ),
        compiler_params=pltpu.CompilerParams(vmem_limit_bytes=LIMIT),
        name="project",
    )(rows, w1, cos_t, sin_t)


def doc_start(pos, ends):
    return jnp.where(pos < ends[0], 0, jnp.where(pos < ends[1], ends[0], ends[1]))

def key_range(span, ends):
    begin = doc_start(span * 128, ends) // 128
    count = span - begin + 1
    runs = (count + 3) // 8
    return begin, runs, jnp.where(count > runs * 8, 1, 0)


def attend(inverse, spans, select, ends, q, kv):
    def kernel(inverse, spans, select, ends, q_ref, kv_ref, o_ref, lse_ref, s_ref):
        lane = lanes_of((128, 128))
        sel = (select[0], select[1])

        @pl.loop(0, 8)
        def _(b):
            span = spans[b]
            begin, runs, rest = key_range(span, ends)
            pos = span * 128 + lanes_of((1, 256)) % 128
            low = doc_start(pos, ends)
            rows = pl.ds(pl.multiple_of(b * 128, 128), 128)
            none = jnp.zeros((128, 128), BF)
            pair = jnp.concatenate(
                [
                    jnp.concatenate([q_ref[0, rows, :], none], axis=1),
                    jnp.concatenate([none, q_ref[1, rows, :]], axis=1),
                ],
                axis=0,
            )

            def load(h, t, n):
                return jnp.concatenate(
                    [
                        kv_ref[sel[h], pl.ds(inverse[jnp.minimum(t + i, 63)] * 128, 128), :]
                        for i in range(n)
                    ],
                    axis=0,
                )

            def held(t, n):
                return pl.ds(pl.multiple_of((t - begin) * 128, 512), n * 128)

            def scores(n, t, high):
                kpos = t * 128 + lax.broadcasted_iota(jnp.int32, (n * 128, 1), 0)
                allowed = (kpos >= low) & (kpos <= pos)
                keys = jnp.concatenate([load(0, t, n), load(1, t, n)], axis=1)
                s = jnp.where(allowed, dot_nt(keys, pair), MASKED)
                s_ref[held(t, n), :] = s
                return jnp.maximum(high, jnp.max(s.reshape(n * 16, 8, 256), axis=0))

            def over(step, state):
                state = lax.fori_loop(0, runs, lambda j, v: step(8, begin + j * 8, v), state)
                return lax.fori_loop(0, rest, lambda j, v: step(4, begin + runs * 8, v), state)

            high = over(scores, jnp.full((8, 256), MASKED, F32))
            high = jnp.max(high, axis=0, keepdims=True)

            def weigh(n, t, state):
                total, acc = state
                p = jnp.exp(s_ref[held(t, n), :] - high)
                total = total + jnp.sum(p.reshape(n * 16, 8, 256), axis=0)
                values = jnp.where(lanes_of((n * 128, 128)) < 64, pltpu.roll(load(0, t, n), 64, 1), load(1, t, n))
                return total, acc + dot_tn(values, p.astype(BF))

            total, acc = over(weigh, (jnp.zeros((8, 256), F32), jnp.zeros((128, 256), F32)))
            total = jnp.sum(total, axis=0, keepdims=True)
            lse = high + jnp.log(total)
            lse_ref[b, 0:1, :] = lse[:, 0:128]
            lse_ref[b, 1:2, :] = lse[:, 128:256]
            acc = acc / total
            acc = jnp.concatenate([acc[0:64, 0:128], acc[64:128, 128:256]], axis=0)
            o_ref[rows, :] = acc.T.astype(BF)

    return pl.pallas_call(
        kernel,
        in_specs=[SMEM, SMEM, SMEM, SMEM, VMEM, VMEM],
        out_specs=(VMEM, VMEM),
        scratch_shapes=[pltpu.VMEM((40 * 128, 256), F32)],
        out_shape=(shaped((1024, 128), BF), shaped((8, 8, 128), F32)),
        compiler_params=pltpu.CompilerParams(vmem_limit_bytes=LIMIT),
        name="attend",
    )(inverse, spans, select, ends, q, kv)


def attend_back(inverse, spans, select, ends, q, kv, d_att, att, lse):
    def kernel(
        inverse, spans, select, ends, q_ref, kv_ref, d_ref, o_ref, lse_ref, dq_ref, dkv_ref,
        acc_ref,
    ):
        lane = lanes_of((128, 128))
        sel = (select[0], select[1])

        @pl.loop(0, 16)
        def _(n):
            for s in (0, 1):
                part = pl.ds(pl.multiple_of(n * 512, 512), 512)
                acc_ref[s, part, :] = jnp.zeros((512, 128), F32)

        @pl.loop(0, 8)
        def _(b):
            span = spans[b]
            begin, runs, rest = key_range(span, ends)
            pos = span * 128 + lanes_of((1, 128))
            low = doc_start(pos, ends)
            rows = pl.ds(pl.multiple_of(b * 128, 128), 128)
            d_both = d_ref[rows, :].astype(F32)
            d_pad = (
                jnp.where(lane >= 64, pltpu.roll(d_both, 64, 1), 0.0).astype(BF),
                jnp.where(lane >= 64, d_both, 0.0).astype(BF),
            )
            pair = [jnp.concatenate([q_ref[h, rows, :], d_pad[h]], axis=0) for h in (0, 1)]
            mixed = (d_both * o_ref[rows, :].astype(F32)).T
            delta = [jnp.sum(mixed[64 * h : 64 * h + 64], axis=0, keepdims=True) for h in (0, 1)]
            lses = [lse_ref[b, h : h + 1, :] for h in (0, 1)]

            def step(n, t, state):
                where = [inverse[jnp.minimum(t + i, 63)] * 128 for i in range(n)]
                where = [pl.ds(pl.multiple_of(v, 128), 128) for v in where]
                kpos = t * 128 + lax.broadcasted_iota(jnp.int32, (n * 128, 1), 0)
                allowed = (kpos >= low) & (kpos <= pos)
                d_ss, kvs = [], []
                for h in (0, 1):
                    kv_t = jnp.concatenate([kv_ref[sel[h], w, :] for w in where], axis=0)
                    kvs.append(kv_t)
                    both = dot_nt(kv_t, pair[h])
                    p = jnp.where(allowed, jnp.exp(both[:, 0:128] - lses[h]), 0.0)
                    d_s = (p * (both[:, 128:256] - delta[h])).astype(BF)
                    d_ss.append(d_s)
                    d_kv = dot(jnp.concatenate([d_s, p.astype(BF)], axis=1), pair[h])
                    for i, w in enumerate(where):
                        acc_ref[sel[h], w, :] += d_kv[i * 128 : (i + 1) * 128]
                lanes = lanes_of((n * 128, 128))
                keys = jnp.where(lanes < 64, kvs[0], pltpu.roll(kvs[1], 64, 1))
                return state + dot_tn(keys, jnp.concatenate(d_ss, axis=1))

            state = jnp.zeros((128, 256), F32)
            state = lax.fori_loop(0, runs, lambda j, v: step(8, begin + j * 8, v), state)
            state = lax.fori_loop(0, rest, lambda j, v: step(4, begin + runs * 8, v), state)
            state = jnp.concatenate([state[0:64, 0:128], state[64:128, 128:256]], axis=0)
            dq_ref[rows, :] = state.T * 0.125

        @pl.loop(0, 16)
        def _(n):
            for s in (0, 1):
                part = pl.ds(pl.multiple_of(n * 512, 512), 512)
                dkv_ref[s, part, :] = acc_ref[s, part, :].astype(BF)

    return pl.pallas_call(
        kernel,
        in_specs=[SMEM, SMEM, SMEM, SMEM] + [VMEM] * 5,
        out_specs=(VMEM, VMEM),
        scratch_shapes=[pltpu.VMEM((2, 8192, 128), F32)],
        out_shape=(shaped((1024, 128), F32), shaped((2, 8192, 128), BF)),
        compiler_params=pltpu.CompilerParams(vmem_limit_bytes=LIMIT),
        name="attend_back",
    )(inverse, spans, select, ends, q, kv, d_att, att, lse)


def column_of(row):
    return jnp.concatenate(
        [jnp.broadcast_to(row[:, i * 128 : (i + 1) * 128], (128, 128)).T for i in range(8)], axis=0
    )


def project_back(dq, dkv, cos_t, sin_t, w1, normed, rows):
    def kernel(dq_ref, dkv_ref, cos_ref, sin_ref, w_ref, n_ref, x_ref, dn_ref, gw_ref, acc, accg):
        step = pl.program_id(0)

        @pl.when(step == 0)
        def _():
            acc[...] = jnp.zeros_like(acc)
            accg[...] = jnp.zeros_like(accg)

        cos_v, sin_v = cos_ref[...], sin_ref[...]
        dq, dkv = dq_ref[...], dkv_ref[...]
        dq = dq * cos_v - partner(dq) * sin_v
        dk = dkv * cos_v - partner(dkv) * sin_v
        dkv = jnp.where(lanes_of((256, 128)) < 64, dk, dkv)
        d_all = jnp.concatenate([dq, dkv], axis=1).astype(BF)
        acc[...] += dot_tn(n_ref[...], d_all)
        dn = dot_nt(d_all, w_ref[:, 0:256])
        dn_ref[...] = dn.astype(BF)
        x = x_ref[...].astype(F32)
        inv = lax.rsqrt(jnp.sum(x * x, axis=1, keepdims=True) * (1.0 / WIDTH) + EPSILON)
        accg[0:1, :] += jnp.sum(dn * (x * inv), axis=0, keepdims=True)

        @pl.when(step == 3)
        def _():
            gw_ref[:, 0:256] = acc[...].astype(BF)
            gw_ref[:, 256:384] = column_of(accg[0:1, :]).astype(BF)

    block = lambda w: pl.BlockSpec((256, w), lambda i: (i, 0))
    whole = lambda *s: pl.BlockSpec(s, lambda i: (0,) * len(s))
    return pl.pallas_call(
        kernel,
        grid=(4,),
        out_shape=(shaped((1024, WIDE), BF), shaped((1024, 384), BF)),
        in_specs=[
            block(128), block(128), block(128), block(128), whole(WIDE, 384), block(WIDE), block(WIDE)
        ],
        out_specs=(block(WIDE), whole(1024, 384)),
        scratch_shapes=[pltpu.VMEM((1024, 256), F32), pltpu.VMEM((8, WIDE), F32)],
        compiler_params=pltpu.CompilerParams(vmem_limit_bytes=LIMIT),
        name="project_back",
    )(dq, dkv, cos_t, sin_t, w1, normed, rows)


def finish(dn, d_resid, xp, gains, gw1, gw2, gwo, gwd):
    def kernel(
        dn, dr, x, g, w1, w2, wo, wd, gh, g_attn, g_mlp, g_q, g_k, g_v, g_o, g_gate, g_up, g_down
    ):
        spread = spread_value(WIDTH)
        x = x[...].astype(F32)
        inv = lax.rsqrt(jnp.sum(x * x, axis=1, keepdims=True) * (1.0 / WIDTH) + EPSILON)
        c = dn[...] * g[0:1, :]
        mean = jnp.sum(c * x, axis=1, keepdims=True) * (1.0 / WIDTH)
        d_x = dr[...] + inv * c - x * (inv * inv * inv * mean)
        gh[...] = dot_nt(d_x.astype(BF), spread).astype(BF)

        def squeeze(v):
            top = v.astype(BF)
            low = (v - top.astype(F32)).astype(BF)
            return dot_nt(top, spread) + dot_nt(low, spread)

        g_o[...] = squeeze(wo[...])[0:15]
        g_down[...] = squeeze(wd[...])[0:40]
        one = [w1[f].astype(F32)[0:15] for f in range(8)]
        g_q[...] = jnp.concatenate([v[:, 0:128] for v in one], axis=1)[:, 0:WIDTH]

        def heads(n):
            return jnp.concatenate(
                [
                    sum(one[f][:, n : n + 64] for f in range(8) if OWNED_KV[f] == h)
                    for h in range(5)
                ],
                axis=1,
            )

        g_k[...] = heads(128)
        g_v[...] = heads(192)
        g_attn[...] = sum(v[:, 256:384] for v in one)
        two = [w2[f].astype(F32)[0:15] for f in range(8)]
        g_mlp[...] = sum(v[:, 768:896] for v in two)
        for m, ref in ((0, g_gate), (384, g_up)):
            for n in range(0, 8, 2):
                ref[:, n * 320 : n * 320 + 640] = jnp.concatenate(
                    [
                        two[f][:, m + 48 * k : m + 48 * k + 40]
                        for k in (n, n + 1)
                        for f in range(8)
                    ],
                    axis=1,
                )

    return pl.pallas_call(
        kernel,
        out_shape=(
            shaped((128, WIDTH), BF),
            shaped((15, 128), F32),
            shaped((15, 128), F32),
            shaped((15, WIDTH), F32),
            shaped((15, 320), F32),
            shaped((15, 320), F32),
            shaped((15, WIDTH), F32),
            shaped((15, 2560), F32),
            shaped((15, 2560), F32),
            shaped((40, WIDTH), F32),
        ),
        in_specs=[VMEM] * 8,
        out_specs=(VMEM,) * 10,
        compiler_params=pltpu.CompilerParams(vmem_limit_bytes=LIMIT),
        name="finish",
    )(dn, d_resid, xp, gains, gw1, gw2, gwo, gwd)


def local(
    hidden, attn_gain, w_q, w_k, w_v, w_o, mlp_gain, w_gate, w_up, w_down, cotangent,
    doc_lengths, span_order,
):
    i = lax.axis_index("ctx")
    group, me = i // 8, i % 8
    ends = jnp.stack([doc_lengths[0], doc_lengths[0] + doc_lengths[1]])
    spans = lax.dynamic_slice(span_order, (group * 8,), (8,))
    ids = jnp.arange(64, dtype=jnp.int32)
    inverse = jnp.sum(jnp.where(span_order[None, :] == ids[:, None], ids[None, :], 0), axis=1)
    select = jnp.asarray(SELECT, jnp.int32)[me]
    frequency = ROPE_BASE ** (-2.0 * (np.arange(128) % 32) / HEAD)
    frequency = jnp.asarray(frequency, F32).reshape(1, 128)

    rows, w1, wos, wds, xp, cp, wp2, cos_t, sin_t = gather_first(
        hidden, cotangent, w_q, w_k, w_v, w_o, w_gate, w_up, w_down, attn_gain.reshape(15, 1),
        mlp_gain.reshape(15, 1), ends, span_order, frequency,
    )
    rows = rows.reshape(1024, WIDE)
    w1 = w1.reshape(1024, 384)
    normed, q, kv_own, gains = project(rows, w1, cos_t, sin_t)
    kv, wo, cot, w2own = gather_keys(kv_own, wos, cp, wp2)
    kv = kv.reshape(2, 8192, 128)
    att, lse = attend(inverse, spans, select, ends, q, kv)
    output, d_resid, d_heads, gwo, gw2s, gwds = feed(
        att, w2own, wo, rows, wds.reshape(384, WIDE), cot.reshape(1024, WIDE), gains
    )
    d_att = d_heads.reshape(1024, 128)
    dq, dkv = attend_back(inverse, spans, select, ends, q, kv, d_att, att, lse)
    dkv_sum, gwo = sum_keys(dkv.reshape(2, 8, 1024, 128), gwo)
    dn, gw1 = project_back(dq, dkv_sum, cos_t, sin_t, w1, normed, rows)
    dn_sum, gw1s, gwos = sum_normed(
        dn.reshape(8, 128, WIDE), gw1.reshape(8, 8, 16, 384), gwo.reshape(8, 16, WIDE)
    )
    gw1s, gw2s = swap_grads(gw1s, gw2s)
    grad_hidden, g_attn, g_mlp, g_q, g_k, g_v, g_o, g_gate, g_up, g_down = finish(
        dn_sum, d_resid, xp, gains, gw1s, gw2s, gwos, gwds
    )
    return (
        output, grad_hidden, g_attn[:, 0], g_q, g_k, g_v, g_o, g_mlp[:, 1], g_gate, g_up, g_down
    )


def solution(mesh):
    both = ("fsdp", "ctx")
    wide, thin, part = P(both, None), P(both), P("fsdp")
    return jax.shard_map(
        local,
        mesh=mesh,
        in_specs=(wide, thin, wide, wide, wide, wide, thin, wide, wide, wide, wide, part, part),
        out_specs=(wide, wide, thin, wide, wide, wide, wide, thin, wide, wide, wide),
        check_vma=False,
    )
```

```python
import jax
import jax.numpy as jnp
import numpy as np
from jax import lax
from jax.experimental import pallas as pl
from jax.experimental.pallas import tpu as pltpu
from jax.sharding import PartitionSpec as P

HEAD = 64
EPSILON = 1e-05
ROPE_BASE = 100000.0
MASKED = -1e30
WIDE = 1024
WIDTH = 960
BF = jnp.bfloat16
F32 = jnp.float32
MESH = pl.DeviceIdType.MESH
DMA = pltpu.SemaphoreType.DMA
ANY = pl.BlockSpec(memory_space=pl.ANY)
VMEM = pl.BlockSpec(memory_space=pltpu.VMEM)
SMEM = pl.BlockSpec(memory_space=pltpu.SMEM)
LIMIT = 56 * 2**20
OWNED_KV = (0, 1, 1, 2, 2, 3, 4, 4)


def dot(a, b):
    return lax.dot_general(a, b, (((1,), (0,)), ((), ())), preferred_element_type=F32)


def dot_nt(a, b):
    return lax.dot_general(a, b, (((1,), (1,)), ((), ())), preferred_element_type=F32)


def dot_tn(a, b):
    return lax.dot_general(a, b, (((0,), (0,)), ((), ())), preferred_element_type=F32)


def shaped(shape, dtype):
    return jax.ShapeDtypeStruct(shape, dtype)


def place():
    i = lax.axis_index("ctx")
    return i // 16, (i // 8) % 2, (i // 2) % 4, i % 2


def at(x, z, y, c):
    return {"ctx": (((x + 4) % 4) * 2 + z) * 8 + ((y + 4) % 4) * 2 + c}


def send(src, dst, ssem, rsem, device):
    copy = pltpu.make_async_remote_copy(
        src, dst, ssem, rsem, device_id=device, device_id_type=MESH
    )
    copy.start()
    return copy


def hail(kinds):
    x, z, y, c = place()
    who = []
    if "x" in kinds:
        who += [at(x + 1, z, y, c), at(x - 1, z, y, c), at(x, 1 - z, y, c)]
    if "f" in kinds:
        who += [at(x, z, y + d, (c + e) % 2) for d in range(4) for e in range(2) if d + e]
    elif "y" in kinds:
        who += [at(x, z, y + d, c) for d in (1, 2, 3)] + [at(x, z, y, 1 - c)]
    barrier = pltpu.get_barrier_semaphore()
    for device in who:
        pl.semaphore_signal(barrier, inc=1, device_id=device, device_id_type=MESH)
    return len(who)


def greet(kinds):
    pl.semaphore_wait(pltpu.get_barrier_semaphore(), hail(kinds))


def half_lead(ref, k):
    n = ref.shape[0] // 2
    return ref.at[pl.ds(k * n, n)]


def half_lanes(ref, k):
    n = ref.shape[-1] // 2
    return ref.at[:, pl.ds(k * n, n)]


class RingGather:
    sems = [DMA((9,)), DMA((9,)), DMA(())]

    def __init__(self, src, dst, half, ssem, rsem, lsem, arrived=None):
        self.src, self.dst, self.half = src, dst, half
        self.ssem, self.rsem, self.lsem = ssem, rsem, lsem
        self.arrived = arrived or (lambda block: None)
        self.copies = {}

    def push(self, n, src, dst, device):
        self.copies[n] = send(src, dst, self.ssem.at[n], self.rsem.at[n], device)

    def start(self):
        x, z, y, c = place()
        me = self.dst.at[x * 2 + z]
        self.push(0, self.src, me, at(x, 1 - z, y, c))
        self.push(1, self.src, me, at(x + 1, z, y, c))
        self.push(2, self.src, me, at(x - 1, z, y, c))
        self.local = pltpu.make_async_copy(self.src, me, self.lsem)
        self.local.start()

    def relay_z(self):
        x, z, y, c = place()
        block = self.dst.at[x * 2 + 1 - z]
        self.copies[0].wait_recv()
        self.push(3, block, block, at(x + 1, z, y, c))
        self.push(4, block, block, at(x - 1, z, y, c))
        self.arrived(x * 2 + 1 - z)

    def relay_x(self, k):
        x, z, y, c = place()
        zz = z if k == 0 else 1 - z
        left, right = ((x + 3) % 4) * 2 + zz, ((x + 1) % 4) * 2 + zz
        self.copies[1 + 2 * k].wait_recv()
        part = self.half(self.dst.at[left], 0)
        self.push(5 + 2 * k, part, part, at(x + 1, z, y, c))
        self.arrived(left)
        self.copies[2 + 2 * k].wait_recv()
        part = self.half(self.dst.at[right], 1)
        self.push(6 + 2 * k, part, part, at(x - 1, z, y, c))
        self.arrived(right)

    def land(self, k):
        x, z, y, c = place()
        zz = z if k == 0 else 1 - z
        self.copies[5 + 2 * k].wait_recv()
        self.copies[6 + 2 * k].wait_recv()
        self.arrived(((x + 2) % 4) * 2 + zz)

    def sent(self):
        for n in range(9):
            self.copies[n].wait_send()

    def finish(self):
        self.local.wait()
        self.sent()


def run_ring_gathers(rings):
    for ring in rings:
        ring.relay_z()
    for k in (0, 1):
        for ring in rings:
            ring.relay_x(k)
    for k in (0, 1):
        for ring in rings:
            ring.land(k)


class RowGather:
    sems = [DMA((8,)), DMA((8,)), DMA(())]

    def __init__(self, src, dst, ssem, rsem, lsem):
        self.src, self.dst = src, dst
        self.ssem, self.rsem, self.lsem = ssem, rsem, lsem
        self.copies = {}

    def push(self, n, src, dst, device):
        self.copies[n] = send(src, dst, self.ssem.at[n], self.rsem.at[n], device)

    def start(self):
        x, z, y, c = place()
        me = self.dst.at[y * 2 + c]
        self.push(1, self.src, me, at(x, z, y + 1, c))
        self.push(2, self.src, me, at(x, z, y - 1, c))
        self.push(0, self.src, me, at(x, z, y, 1 - c))
        self.local = pltpu.make_async_copy(self.src, me, self.lsem)
        self.local.start()

    def relay(self):
        x, z, y, c = place()
        for n, step, side in ((1, 3, 0), (2, 1, 1)):
            self.copies[n].wait_recv()
            block = self.dst.at[((y + step) % 4) * 2 + c]
            part = half_lead(block, side)
            self.push(2 + n, part, part, at(x, z, y + 4 - step, c))
            self.push(4 + n, block, block, at(x, z, y, 1 - c))

    def land(self):
        x, z, y, c = place()
        self.copies[3].wait_recv()
        self.copies[4].wait_recv()
        block = self.dst.at[((y + 2) % 4) * 2 + c]
        self.push(7, block, block, at(x, z, y, 1 - c))

    def finish(self):
        self.local.wait()
        for n in (0, 5, 6, 7):
            self.copies[n].wait_recv()
        for n in range(8):
            self.copies[n].wait_send()


class Swap:
    sems = [DMA((8,)), DMA((8,)), DMA(())]

    def __init__(self, src, dst, ssem, rsem, lsem):
        self.src, self.dst = src, dst
        self.ssem, self.rsem, self.lsem = ssem, rsem, lsem

    def start(self):
        x, z, y, c = place()
        me = y * 2 + c
        self.copies = []
        for d in (2, 1, 3, 0):
            for e in (0, 1):
                if d + e:
                    n = d * 2 + e
                    to = ((y + d) % 4) * 2 + (c + e) % 2
                    self.copies.append(
                        send(
                            self.src.at[to],
                            self.dst.at[me],
                            self.ssem.at[n],
                            self.rsem.at[n],
                            at(x, z, y + d, (c + e) % 2),
                        )
                    )
        self.local = pltpu.make_async_copy(self.src.at[me], self.dst.at[me], self.lsem)
        self.local.start()

    def finish(self):
        self.local.wait()
        for copy in self.copies:
            copy.wait()


class RowSum:
    @staticmethod
    def scratch(shape):
        return [
            pltpu.VMEM((4,) + shape, BF),
            pltpu.VMEM((4,) + shape, BF),
            pltpu.VMEM((4,) + shape, BF),
            DMA((8,)),
            DMA((8,)),
        ]

    def __init__(self, blk, first, mixed, second, ssem, rsem):
        self.blk, self.first, self.mixed, self.second = blk, first, mixed, second
        self.ssem, self.rsem = ssem, rsem
        self.copies = {}

    def push(self, n, src, dst, device):
        self.copies[n] = send(src, dst, self.ssem.at[n], self.rsem.at[n], device)

    def hand(self, d):
        x, z, y, c = place()
        to = ((y + d) % 4) * 2 + 1 - c
        self.push(d, self.blk.at[to], self.first.at[d], at(x, z, y, 1 - c))

    def start(self):
        for d in (2, 1, 3, 0):
            self.hand(d)

    def relay(self):
        x, z, y, c = place()
        for d in (2, 1, 3):
            self.copies[d].wait_recv()
            own = self.blk[((y + d) % 4) * 2 + c].astype(F32)
            self.mixed[d] = (own + self.first[d].astype(F32)).astype(BF)
            self.push(4 + d, self.mixed.at[d], self.second.at[d], at(x, z, y + d, c))

    def total(self):
        x, z, y, c = place()
        self.copies[0].wait_recv()
        total = self.blk[y * 2 + c].astype(F32) + self.first[0].astype(F32)
        for d in (1, 3, 2):
            self.copies[4 + d].wait_recv()
            total = total + self.second[d].astype(F32)
        return total

    def finish(self):
        for n in (0, 1, 2, 3, 5, 6, 7):
            self.copies[n].wait_send()


class RingSum:
    @staticmethod
    def scratch(shape, lanes):
        if lanes:
            part = shape[:-1] + (shape[-1] // 2,)
        else:
            part = (shape[0] // 2,) + shape[1:]
        return [
            pltpu.VMEM((4,) + part, BF),
            pltpu.VMEM((4,) + shape, BF),
            pltpu.VMEM((4,) + shape, BF),
            pltpu.VMEM((2,) + shape, BF),
            DMA((9,)),
            DMA((9,)),
        ]

    def __init__(self, blk, lanes, parts, mixed, heard, across, ssem, rsem):
        self.blk, self.half = blk, half_lanes if lanes else half_lead
        self.parts, self.mixed, self.heard, self.across = parts, mixed, heard, across
        self.ssem, self.rsem = ssem, rsem
        self.copies = {}

    def push(self, n, src, dst, device):
        self.copies[n] = send(src, dst, self.ssem.at[n], self.rsem.at[n], device)

    def start(self, k):
        x, z, y, c = place()
        zz = 1 - z if k == 0 else z
        far = self.blk.at[((x + 2) % 4) * 2 + zz]
        self.push(4 * k, self.half(far, 0), self.parts.at[2 * k], at(x + 1, z, y, c))
        self.push(4 * k + 1, self.half(far, 1), self.parts.at[2 * k + 1], at(x - 1, z, y, c))

    def relay(self, k):
        x, z, y, c = place()
        zz = 1 - z if k == 0 else z
        for side, step in ((0, 1), (1, 3)):
            n = 2 * k + side
            mixed = self.mixed.at[n]
            source = self.blk.at[((x + step) % 4) * 2 + zz]
            mine, other = self.half(source, side), self.half(source, 1 - side)
            self.half(mixed, 1 - side)[...] = other[...]
            self.copies[4 * k + side].wait_recv()
            self.half(mixed, side)[...] = (
                mine[...].astype(F32) + self.parts[n].astype(F32)
            ).astype(BF)
            self.push(4 * k + 2 + side, mixed, self.heard.at[n], at(x + step, z, y, c))

    def total(self, k):
        x, z, y, c = place()
        zz = 1 - z if k == 0 else z
        total = self.blk[x * 2 + zz].astype(F32)
        for side in (0, 1):
            self.copies[4 * k + 2 + side].wait_recv()
            total = total + self.heard[2 * k + side].astype(F32)
        if k == 0:
            self.across[0] = total.astype(BF)
            self.push(8, self.across.at[0], self.across.at[1], at(x, 1 - z, y, c))
            return None
        self.copies[8].wait_recv()
        return total + self.across[1].astype(F32)

    def finish(self):
        for n in range(9):
            self.copies[n].wait_send()


def comm_call(name, number, kernel, out_shape, in_specs, out_specs, scratch, args):
    return pl.pallas_call(
        kernel,
        out_shape=out_shape,
        in_specs=in_specs,
        out_specs=out_specs,
        scratch_shapes=scratch,
        compiler_params=pltpu.CompilerParams(
            collective_id=number, has_side_effects=True, vmem_limit_bytes=LIMIT
        ),
        name=name,
    )(*args)


def split(refs, counts):
    parts, begin = [], 0
    for n in counts:
        parts.append(refs[begin : begin + n])
        begin += n
    return parts


def spread_value(rows):
    j = lax.broadcasted_iota(jnp.int32, (rows, WIDE), 0)
    k = lax.broadcasted_iota(jnp.int32, (rows, WIDE), 1)
    hit = ((k // 16) * 15 + k % 16 == j) & (k % 16 < 15)
    return jnp.where(hit, 1.0, 0.0).astype(BF)


def first(
    hidden_t, cot_t, w_q, w_k, w_v, w_o, w_gate, w_up, w_down, gain1, gain2, lengths, span_order, freq
):
    def kernel(
        hidden_t, cot_t, w_q, w_k, w_v, w_o, w_gate, w_up, w_down, gain1, gain2, lengths, order, freq,
        rows, w1, wds, wo, cot, w2own, normed, q_rot, kv2, gains, cos_t, sin_t,
        xp, cp, wp1, wp2, wop, wdp, wos, w1own, kv, *sems,
    ):
        a, b, d, e, e2, ac, ao, b2, k0, k1, (hs, hr) = split(sems, (3,) * 10 + (2,))
        x, z, y, c = place()
        partners = hail("xf")

        q = jnp.concatenate([w_q[...].astype(F32), jnp.zeros((15, 64), F32)], axis=1)
        k, v = w_k[...].astype(F32), w_v[...].astype(F32)
        gap = jnp.zeros((1, 113), F32)
        both = jnp.concatenate(
            [
                jnp.concatenate([ref[...].astype(F32).reshape(1, 15), gap], axis=1)
                for ref in (gain1, gain2)
            ]
            + [jnp.zeros((126, 128), F32)],
            axis=0,
        ).T[0:15]
        wp1[...] = jnp.zeros(wp1.shape, BF)
        for f in range(8):
            n = OWNED_KV[f] * 64
            wp1[f, 0:15, 0:128] = q[:, 128 * f : 128 * f + 128].astype(BF)
            wp1[f, 0:15, 128:256] = jnp.concatenate(
                [k[:, n : n + 64], v[:, n : n + 64]], axis=1
            ).astype(BF)
            wp1[f, 0:15, 256:384] = both.astype(BF)

        pl.semaphore_wait(pltpu.get_barrier_semaphore(), partners)
        swap = Swap(wp1, w1own, *b)
        swap.start()
        spread = spread_value(WIDTH)
        xp[...] = dot_tn(hidden_t[...], spread).astype(BF)
        gather = RowGather(xp, rows, *a)
        gather.start()
        wop[...] = jnp.zeros(wop.shape, BF)
        wop[0:15, :] = dot(w_o[...], spread).astype(BF)
        wdp[...] = jnp.zeros(wdp.shape, BF)
        wdp[0:40, :] = dot(w_down[...], spread).astype(BF)
        ring_o = RingGather(wop, wos, half_lanes, *e)
        ring_d = RingGather(wdp, wds, half_lanes, *e2)
        swap.finish()
        ring_1 = RingGather(w1own, w1, half_lead, *d)
        ring_1.start()
        ring_o.start()
        ring_d.start()
        cp[...] = dot_tn(cot_t[...], spread).astype(BF)
        gather.relay()
        gather_c = RowGather(cp, cot, *ac)
        gather_c.start()
        rings = [ring_1, ring_o, ring_d]
        for ring in rings:
            ring.relay_z()

        wp2[...] = jnp.zeros(wp2.shape, BF)
        gap = jnp.zeros((15, 8), F32)
        for m, ref in ((0, w_gate), (384, w_up)):
            w = ref[...].astype(F32)
            for f in range(8):
                parts = []
                for g in range(8):
                    n = (8 * g + f) * 40
                    parts += [w[:, n : n + 40], gap]
                wp2[f, 0:15, m : m + 384] = jnp.concatenate(parts, axis=1).astype(BF)
        swap2 = Swap(wp2, w2own, *b2)
        swap2.start()

        for k in (0, 1):
            for ring in rings:
                ring.relay_x(k)

        lane = lanes_of((1, 128))
        sign = jnp.where(lane % 64 < 32, -1.0, 1.0)

        ends = doc_ends(lengths)

        @pl.loop(0, 8)
        def _(n):
            pos = order[(x * 2 + z) * 8 + n] * 128
            pos = pos + lax.broadcasted_iota(jnp.int32, (128, 1), 0)
            angle = (pos - doc_start(pos, ends)).astype(F32) * freq[...]
            part = pl.ds(pl.multiple_of(n * 128, 128), 128)
            cos_t[part, :] = jnp.cos(angle)
            sin_t[part, :] = sign * jnp.sin(angle)

        gather.land()
        for k in (0, 1):
            for ring in rings:
                ring.land(k)
        ring_o.local.wait()
        gather_o = RowGather(wos, wo, *ao)
        gather_o.start()
        gather.finish()
        ring_1.local.wait()

        w = w1.reshape(WIDE, 384)
        eye = (lax.broadcasted_iota(jnp.int32, (8, 128), 0) == lanes_of((8, 128))).astype(BF)
        gains[...] = dot_nt(eye, w[:, 256:384])
        lane = lanes_of((256, 128))

        def project(n):
            part = pl.ds(n * 256, 256)
            xs = jnp.concatenate([rows[2 * n], rows[2 * n + 1]], axis=0).astype(F32)
            v = (xs * inverse_rms(xs) * gains[0:1, :]).astype(BF)
            normed[part, :] = v
            out = dot(v, w[:, 0:256])
            cos_v, sin_v = cos_t[part, :], sin_t[part, :]
            qs, ks = out[:, 0:128], out[:, 128:256]
            qs = (qs * cos_v + partner(qs) * sin_v).astype(BF).astype(F32) * 0.125
            kv[part, :] = jnp.where(lane < 64, ks * cos_v + partner(ks) * sin_v, ks).astype(BF)
            q_rot[0, part, :] = jnp.where(lane < 64, qs, 0.0).astype(BF)
            q_rot[1, part, :] = jnp.where(lane < 64, pltpu.roll(qs, 64, 1), 0.0).astype(BF)

        hand = []

        def pass_on(piece):
            n = len(hand)
            hand.append(send(piece, piece, hs.at[n], hr.at[n], at(x, z, y, 1 - c)))

        key_rings = []
        for h, own in ((0, k0), (1, k1)):
            mine = kv.at[pl.ds(512 * h, 512)]
            spot = pl.ds(512 * h, 512)
            ring = RingGather(
                mine,
                kv2.at[c, :, spot],
                half_lead,
                *own,
                arrived=lambda block, spot=spot: pass_on(kv2.at[c, block, spot]),
            )
            project(2 * h)
            project(2 * h + 1)
            ring.start()
            n = len(hand)
            hand.append(
                send(
                    mine, kv2.at[c, x * 2 + z, spot], hs.at[n], hr.at[n], at(x, z, y, 1 - c)
                )
            )
            key_rings.append(ring)
            if h == 0:
                gather_c.relay()

        for ring in key_rings:
            ring.relay_z()
        gather_o.relay()
        for ring in key_rings:
            ring.relay_x(0)
        gather_c.land()
        for ring in key_rings:
            ring.relay_x(1)
        gather_o.land()
        for k in (0, 1):
            for ring in key_rings:
                ring.land(k)
        for copy in hand:
            copy.wait()
        swap2.finish()
        gather_o.finish()
        gather_c.finish()
        for ring in [ring_d] + key_rings:
            ring.finish()
        for ring in (ring_1, ring_o):
            ring.sent()

    return comm_call(
        "first",
        1,
        kernel,
        (
            shaped((8, 128, WIDE), BF),
            shaped((8, 8, 16, 384), BF),
            shaped((8, 48, WIDE), BF),
            shaped((8, 8, 16, WIDE), BF),
            shaped((8, 128, WIDE), BF),
            shaped((8, 16, 768), BF),
            shaped((1024, WIDE), BF),
            shaped((2, 1024, 128), BF),
            shaped((2, 8, 1024, 128), BF),
            shaped((8, WIDE), F32),
            shaped((1024, 128), F32),
            shaped((1024, 128), F32),
        ),
        [VMEM] * 11 + [SMEM, SMEM, VMEM],
        (VMEM, VMEM, ANY, ANY, ANY, ANY, VMEM, VMEM, ANY, VMEM, VMEM, VMEM),
        [
            pltpu.VMEM((128, WIDE), BF),
            pltpu.VMEM((128, WIDE), BF),
            pltpu.VMEM((8, 16, 384), BF),
            pltpu.VMEM((8, 16, 768), BF),
            pltpu.VMEM((16, WIDE), BF),
            pltpu.VMEM((48, WIDE), BF),
            pltpu.VMEM((8, 16, WIDE), BF),
            pltpu.VMEM((8, 16, 384), BF),
            pltpu.VMEM((1024, 128), BF),
        ]
        + RowGather.sems
        + Swap.sems
        + RingGather.sems * 3
        + RowGather.sems * 2
        + Swap.sems
        + RingGather.sems * 2
        + [DMA((16,)), DMA((16,))],
        (
            hidden_t, cot_t, w_q, w_k, w_v, w_o, w_gate, w_up, w_down, gain1, gain2, lengths,
            span_order, freq,
        ),
    )


def inverse_rms(v):
    return lax.rsqrt(jnp.sum(v * v, axis=1, keepdims=True) * (1.0 / WIDTH) + EPSILON)


def feed(att, w2own, wo, rows, wd, cot, gains):
    def kernel(
        att, w2own, wo, x_ref, wd, cot, gains,
        output, d_resid, d_heads, gwo, gw2_sum, gwd_sum,
        atts, w2, packed, d_act, resid, normed, act, d_both, dmn, outp, gw2, gwd, accg, da,
        *refs,
    ):
        a, b, s, r1, r2, t1, t2 = split(refs, (3, 3, 3, 5, 5, 6, 6))
        x, z, y, c = place()
        me = y * 2 + c
        greet("xf")
        gather = RowGather(att, atts, *a)
        ring = RingGather(w2own, w2, half_lead, *b)
        gather.start()
        ring.start()

        def place_rows(n, size):
            return pl.ds(pl.multiple_of(n * size, size), size)

        whole = jnp.concatenate([wo[f, g] for g in range(8) for f in range(8)], axis=0)

        def pack(n):
            j = lax.broadcasted_iota(jnp.int32, (256, WIDE), 0) + n * 256
            k = lax.broadcasted_iota(jnp.int32, (256, WIDE), 1)
            hit = ((k // 16) * 15 + k % 16 == j) & (k % 16 < 15)
            packed[pl.ds(n * 256, 256), :] = dot(
                jnp.where(hit, 1.0, 0.0).astype(BF), whole
            ).astype(BF)

        pack(0)
        pack(1)
        ring.relay_z()
        gather.relay()
        pack(2)
        pack(3)
        ring.relay_x(0)

        @pl.loop(0, 4)
        def _(n):
            part = place_rows(n, 256)
            d_act[part, :] = dot_nt(cot[part, :], wd[...])

        ring.relay_x(1)
        gather.land()
        gather.finish()

        @pl.loop(0, 4)
        def _(n):
            part = place_rows(n, 256)
            heads = jnp.concatenate([atts[f, part, :] for f in range(8)], axis=1)
            v = x_ref[part, :].astype(F32) + dot(heads, packed[...])
            resid[part, :] = v
            normed[part, :] = (v * inverse_rms(v) * gains[1:2, :]).astype(BF)

        ring.land(0)
        ring.land(1)
        ring.finish()
        w2_all = w2.reshape(WIDE, 768)

        @pl.loop(0, 4)
        def _(n):
            part = place_rows(n, 256)
            both = dot(normed[part, :], w2_all[...])
            gate, up = both[:, 0:384], both[:, 384:768]
            sigma = 1.0 / (1.0 + jnp.exp(-gate))
            silu = gate * sigma
            act[part, :] = (silu * up).astype(BF)
            d = d_act[part, :]
            d_both[part, 0:384] = (d * up * sigma * (1.0 + gate * (1.0 - sigma))).astype(BF)
            d_both[part, 384:768] = (d * silu).astype(BF)

        sum_n, sum_o = RowSum(dmn, *r1), RowSum(outp, *r2)
        ring_2, ring_d = RingSum(gw2, False, *t1), RingSum(gwd, True, *t2)
        accg[...] = jnp.zeros(accg.shape, F32)

        def back(to):
            part = place_rows(to, 128)
            d = dot_nt(d_both[part, :], w2_all[...])
            v = resid[part, :]
            accg[0:1, :] += jnp.sum(d * (v * inverse_rms(v)), axis=0, keepdims=True)
            dmn[to] = d.astype(BF)

        for d in (2, 1, 3, 0):
            back(((y + d) % 4) * 2 + 1 - c)
            sum_n.hand(d)
        for d in (2, 1, 3, 0):
            back(((y + d) % 4) * 2 + c)
        sum_n.relay()

        def weights(g):
            part = place_rows(g, 128)
            gw2[g, :, :, 0:768] = (
                dot_tn(normed[:, part], d_both[...]).astype(BF).reshape(8, 16, 768)
            )
            column = jnp.broadcast_to(accg[0:1, part], (128, 128)).T
            gw2[g, :, :, 768:896] = column.astype(BF).reshape(8, 16, 128)

        order = [(2, 1), (2, 0), (1, 1), (3, 1), (1, 0), (3, 0), (0, 1), (0, 0)]
        where = [((x + p) % 4) * 2 + (1 - z if q else z) for p, q in order]
        weights(where[0])
        ring_2.start(0)
        weights(where[1])
        ring_2.start(1)
        gwd[...] = dot_tn(act[...], cot[...]).astype(BF).reshape(8, 48, WIDE)
        ring_d.start(0)
        ring_d.start(1)
        for n in range(2, 8):
            weights(where[n])

        @pl.loop(0, 8)
        def _(n):
            outp[n] = dot(act[place_rows(n, 128), :], wd[...]).astype(BF)

        sum_o.start()
        for k in (0, 1):
            ring_2.relay(k)
            ring_d.relay(k)
        sum_o.relay()

        mine = place_rows(me, 128)
        d_normed = sum_n.total()
        v = resid[mine, :]
        inv = inverse_rms(v)
        e = d_normed * gains[1:2, :]
        mean = jnp.sum(e * v, axis=1, keepdims=True) * (1.0 / WIDTH)
        d_v = cot[mine, :].astype(F32) + inv * e - v * (inv * inv * inv * mean)
        d_resid[...] = d_v
        mixed = d_v.astype(BF)
        d_att = dot_nt(mixed, packed[...]).astype(BF)
        for f in range(8):
            da[f] = d_att[:, f * 128 : (f + 1) * 128]
        swap = Swap(da, d_heads, *s)
        swap.start()
        spread = spread_value(WIDE)
        heads = jnp.concatenate([atts[f, mine, :] for f in range(8)], axis=1)
        gw = dot_tn(dot(heads, spread).astype(BF), mixed).astype(BF)
        for g in range(8):
            for f in range(8):
                n = (8 * g + f) * 16
                gwo[f, g * 16 : (g + 1) * 16, :] = gw[n : n + 16]
        ring_2.total(0)
        ring_d.total(0)
        output[...] = dot_nt(spread[0:WIDTH], (v + sum_o.total()).astype(BF)).astype(BF)
        gw2_sum[...] = ring_2.total(1).astype(BF)
        gwd_sum[...] = ring_d.total(1)
        swap.finish()
        sum_n.finish()
        sum_o.finish()
        ring_2.finish()
        ring_d.finish()

    return comm_call(
        "feed",
        3,
        kernel,
        (
            shaped((WIDTH, 128), BF),
            shaped((128, WIDE), F32),
            shaped((8, 128, 128), BF),
            shaped((8, 128, WIDE), BF),
            shaped((8, 16, 896), BF),
            shaped((48, WIDE), F32),
        ),
        [ANY, ANY] + [VMEM] * 5,
        (VMEM, VMEM, ANY, VMEM, VMEM, VMEM),
        [
            pltpu.VMEM((8, 1024, 128), BF),
            pltpu.VMEM((8, 8, 16, 768), BF),
            pltpu.VMEM((WIDE, WIDE), BF),
            pltpu.VMEM((1024, 384), F32),
            pltpu.VMEM((1024, WIDE), F32),
            pltpu.VMEM((1024, WIDE), BF),
            pltpu.VMEM((1024, 384), BF),
            pltpu.VMEM((1024, 768), BF),
            pltpu.VMEM((8, 128, WIDE), BF),
            pltpu.VMEM((8, 128, WIDE), BF),
            pltpu.VMEM((8, 8, 16, 896), BF),
            pltpu.VMEM((8, 48, WIDE), BF),
            pltpu.VMEM((8, WIDE), F32),
            pltpu.VMEM((8, 128, 128), BF),
        ]
        + RowGather.sems
        + RingGather.sems
        + Swap.sems
        + RowSum.scratch((128, WIDE)) * 2
        + RingSum.scratch((8, 16, 896), False)
        + RingSum.scratch((48, WIDE), True),
        (att, w2own, wo, rows, wd, cot, gains),
    )


def last(dkv, gwo, dq, cos_t, sin_t, w1, normed, rows, d_resid, gains, gw2s, gwd):
    def kernel(
        dkv, gwo, dq, cos_t, sin_t, w1, normed, rows, dr, gains, gw2s, wd,
        gh, g_attn, g_mlp, g_q, g_k, g_v, g_o, g_gate, g_up, g_down,
        blk, from_core, gwos, gw1, dnq, d_kv, dn, accg, one, two, gw1s, hs, hr, *refs,
    ):
        a, b, d, e, e2, s1, s2 = split(refs, (6, 5, 5, 6, 6, 3, 3))
        x, z, y, c = place()
        me = y * 2 + c
        greet("xf")
        order = [(2, 1), (2, 0), (1, 1), (3, 1), (1, 0), (3, 0), (0, 1), (0, 0)]
        where = [((x + p) % 4) * 2 + (1 - z if q else z) for p, q in order]
        hand = [
            send(dkv.at[1 - c, g], from_core.at[n], hs.at[n], hr.at[n], at(x, z, y, 1 - c))
            for n, g in enumerate(where)
        ]
        sum_w = RowSum(gwo, *b)
        sum_w.start()
        swap2 = Swap(gw2s, two, *s2)
        swap2.start()
        ring = RingSum(blk, False, *a)

        def fold(n):
            g = where[n]
            hand[n].wait_recv()
            blk[g] = (dkv[c, g].astype(F32) + from_core[n].astype(F32)).astype(BF)

        fold(0)
        ring.start(0)
        fold(1)
        ring.start(1)
        for n in range(2, 6):
            fold(n)
        sum_w.relay()
        spread = spread_value(WIDTH)
        accg[...] = jnp.zeros(accg.shape, F32)

        def place_rows(n, size):
            return pl.ds(pl.multiple_of(n * size, size), size)

        def queries(n):
            part = place_rows(n, 256)
            v = dq[part, :]
            v = (v * cos_t[part, :] - partner(v) * sin_t[part, :]).astype(BF)
            d_kv[part, 0:128] = v
            dnq[part, :] = dot_nt(v, w1[:, 0:128])

        queries(0)
        queries(1)
        ring.relay(0)
        queries(2)
        queries(3)
        ring.relay(1)
        fold(6)
        fold(7)

        def weights_q(n):
            part = place_rows(n, 128)
            gw1[n, :, :, 0:128] = (
                dot_tn(normed[:, part], d_kv[:, 0:128]).astype(BF).reshape(8, 16, 128)
            )

        for n in range(4):
            weights_q(n)
        gwos[...] = sum_w.total().astype(BF).reshape(8, 16, WIDE)
        ring_o = RingSum(gwos, True, *e2)
        ring_o.start(0)
        ring_o.start(1)
        ring.total(0)
        for n in range(4, 8):
            weights_q(n)
        swap2.finish()
        for m, ref in ((0, g_gate), (384, g_up)):
            for n in range(0, 8, 2):
                ref[:, n * 320 : n * 320 + 640] = jnp.concatenate(
                    [
                        two[f, :, m + 48 * k : m + 48 * k + 40].astype(F32)[0:15]
                        for k in (n, n + 1)
                        for f in range(8)
                    ],
                    axis=1,
                )
        g_mlp[...] = sum(two[f, :, 768:896].astype(F32) for f in range(8))[0:15]

        def squeeze(v):
            top = v.astype(BF)
            low = (v - top.astype(F32)).astype(BF)
            return dot_nt(top, spread) + dot_nt(low, spread)

        g_down[...] = squeeze(wd[...])[0:40]
        ring_o.relay(0)
        ring_o.relay(1)

        v = ring.total(1)
        turned = v * cos_t[...] - partner(v) * sin_t[...]
        d_kv[:, 128:256] = jnp.where(lanes_of((1024, 128)) < 64, turned, v).astype(BF)
        sum_n = RowSum(dn, *d)

        def back(to):
            part = place_rows(to, 128)
            v = dnq[part, :] + dot_nt(d_kv[part, 128:256], w1[:, 128:256])
            dn[to] = v.astype(BF)
            xs = rows[to].astype(F32)
            accg[0:1, :] += jnp.sum(v * (xs * inverse_rms(xs)), axis=0, keepdims=True)

        for n in (2, 1, 3, 0):
            back(((y + n) % 4) * 2 + 1 - c)
            sum_n.hand(n)
        for n in (2, 1, 3, 0):
            back(((y + n) % 4) * 2 + c)

        def weights_k(g):
            part = place_rows(g, 128)
            gw1[g, :, :, 128:256] = (
                dot_tn(normed[:, part], d_kv[:, 128:256]).astype(BF).reshape(8, 16, 128)
            )
            column = jnp.broadcast_to(accg[0:1, part], (128, 128)).T
            gw1[g, :, :, 256:384] = column.astype(BF).reshape(8, 16, 128)

        ring_1 = RingSum(gw1, False, *e)
        weights_k(where[0])
        ring_1.start(0)
        weights_k(where[1])
        ring_1.start(1)
        sum_n.relay()
        for n in range(2, 8):
            weights_k(where[n])
        ring_1.relay(0)
        ring_1.relay(1)
        ring_o.total(0)
        ring_1.total(0)
        g_o[...] = squeeze(ring_o.total(1))[0:15]
        gw1s[...] = ring_1.total(1).astype(BF)
        swap1 = Swap(gw1s, one, *s1)
        swap1.start()

        xs = rows[me].astype(F32)
        inv = inverse_rms(xs)
        t = sum_n.total() * gains[0:1, :]
        mean = jnp.sum(t * xs, axis=1, keepdims=True) * (1.0 / WIDTH)
        d_x = dr[...] + inv * t - xs * (inv * inv * inv * mean)
        gh[...] = dot_nt(spread, d_x.astype(BF)).astype(BF)
        swap1.finish()
        ones = [one[f].astype(F32)[0:15] for f in range(8)]
        g_q[...] = jnp.concatenate([v[:, 0:128] for v in ones], axis=1)[:, 0:WIDTH]

        def heads(n):
            return jnp.concatenate(
                [
                    sum(ones[f][:, n : n + 64] for f in range(8) if OWNED_KV[f] == h)
                    for h in range(5)
                ],
                axis=1,
            )

        g_k[...] = heads(128)
        g_v[...] = heads(192)
        g_attn[...] = sum(v[:, 256:384] for v in ones)
        for copy in hand:
            copy.wait_send()
        ring.finish()
        ring_1.finish()
        ring_o.finish()
        sum_w.finish()
        sum_n.finish()

    return comm_call(
        "last",
        6,
        kernel,
        (
            shaped((WIDTH, 128), BF),
            shaped((15, 128), F32),
            shaped((15, 128), F32),
            shaped((15, WIDTH), F32),
            shaped((15, 320), F32),
            shaped((15, 320), F32),
            shaped((15, WIDTH), F32),
            shaped((15, 2560), F32),
            shaped((15, 2560), F32),
            shaped((40, WIDTH), F32),
        ),
        [VMEM] * 12,
        (VMEM,) * 10,
        [
            pltpu.VMEM((8, 1024, 128), BF),
            pltpu.VMEM((8, 1024, 128), BF),
            pltpu.VMEM((8, 16, WIDE), BF),
            pltpu.VMEM((8, 8, 16, 384), BF),
            pltpu.VMEM((1024, WIDE), F32),
            pltpu.VMEM((1024, 256), BF),
            pltpu.VMEM((8, 128, WIDE), BF),
            pltpu.VMEM((8, WIDE), F32),
            pltpu.VMEM((8, 16, 384), BF),
            pltpu.VMEM((8, 16, 896), BF),
            pltpu.VMEM((8, 16, 384), BF),
            DMA((8,)),
            DMA((8,)),
        ]
        + RingSum.scratch((1024, 128), False)
        + RowSum.scratch((128, WIDE)) * 2
        + RingSum.scratch((8, 16, 384), False)
        + RingSum.scratch((16, WIDE), True)
        + Swap.sems * 2,
        (dkv, gwo, dq, cos_t, sin_t, w1, normed, rows, d_resid, gains, gw2s, gwd),
    )


def lanes_of(shape):
    return lax.broadcasted_iota(jnp.int32, shape, len(shape) - 1)


def partner(v):
    lane = lanes_of(v.shape)
    return jnp.where(lane % 64 < 32, pltpu.roll(v, 96, 1), pltpu.roll(v, 32, 1))


def doc_ends(lengths):
    return lengths[0], lengths[0] + lengths[1]


def doc_start(pos, ends):
    return jnp.where(pos < ends[0], 0, jnp.where(pos < ends[1], ends[0], ends[1]))

def layout(order, inverse):
    @pl.loop(0, 64)
    def _(n):
        inverse[order[n]] = n

    i = lax.axis_index("ctx")
    f = i % 8
    upper = (f == 3) | (f == 5)
    return i // 8, (
        jnp.where(upper, 1, 0),
        jnp.where(upper | (f == 1) | (f == 4), 1, 0),
    )


def key_range(span, ends):
    begin = doc_start(span * 128, ends) // 128
    count = span - begin + 1
    runs = (count + 3) // 8
    return begin, runs, jnp.where(count > runs * 8, 1, 0)


def attend(lengths, order, q, kv):
    def kernel(lengths, order, q_ref, kv_ref, o_ref, lse_ref, s_ref, inverse):
        group, sel = layout(order, inverse)
        ends = doc_ends(lengths)

        @pl.loop(0, 8)
        def _(b):
            span = order[group * 8 + b]
            begin, runs, rest = key_range(span, ends)
            pos = span * 128 + lanes_of((1, 256)) % 128
            low = doc_start(pos, ends)
            rows = pl.ds(pl.multiple_of(b * 128, 128), 128)
            none = jnp.zeros((128, 128), BF)
            pair = jnp.concatenate(
                [
                    jnp.concatenate([q_ref[0, rows, :], none], axis=1),
                    jnp.concatenate([none, q_ref[1, rows, :]], axis=1),
                ],
                axis=0,
            )

            def load(h, t, n):
                return jnp.concatenate(
                    [
                        kv_ref[sel[h], pl.ds(inverse[jnp.minimum(t + i, 63)] * 128, 128), :]
                        for i in range(n)
                    ],
                    axis=0,
                )

            def held(t, n):
                return pl.ds(pl.multiple_of((t - begin) * 128, 512), n * 128)

            def scores(n, t, high):
                kpos = t * 128 + lax.broadcasted_iota(jnp.int32, (n * 128, 1), 0)
                allowed = (kpos >= low) & (kpos <= pos)
                keys = jnp.concatenate([load(0, t, n), load(1, t, n)], axis=1)
                s = jnp.where(allowed, dot_nt(keys, pair), MASKED)
                s_ref[held(t, n), :] = s
                return jnp.maximum(high, jnp.max(s.reshape(n * 16, 8, 256), axis=0))

            def over(step, state):
                state = lax.fori_loop(0, runs, lambda j, v: step(8, begin + j * 8, v), state)
                return lax.fori_loop(0, rest, lambda j, v: step(4, begin + runs * 8, v), state)

            high = over(scores, jnp.full((8, 256), MASKED, F32))
            high = jnp.max(high, axis=0, keepdims=True)

            def weigh(n, t, state):
                total, acc = state
                p = jnp.exp(s_ref[held(t, n), :] - high)
                total = total + jnp.sum(p.reshape(n * 16, 8, 256), axis=0)
                values = jnp.where(lanes_of((n * 128, 128)) < 64, pltpu.roll(load(0, t, n), 64, 1), load(1, t, n))
                return total, acc + dot_tn(values, p.astype(BF))

            total, acc = over(weigh, (jnp.zeros((8, 256), F32), jnp.zeros((128, 256), F32)))
            total = jnp.sum(total, axis=0, keepdims=True)
            lse = high + jnp.log(total)
            lse_ref[b, 0:1, :] = lse[:, 0:128]
            lse_ref[b, 1:2, :] = lse[:, 128:256]
            acc = acc / total
            acc = jnp.concatenate([acc[0:64, 0:128], acc[64:128, 128:256]], axis=0)
            o_ref[rows, :] = acc.T.astype(BF)

    return pl.pallas_call(
        kernel,
        in_specs=[SMEM, SMEM, VMEM, VMEM],
        out_specs=(VMEM, VMEM),
        scratch_shapes=[pltpu.VMEM((40 * 128, 256), F32), pltpu.SMEM((64,), jnp.int32)],
        out_shape=(shaped((1024, 128), BF), shaped((8, 8, 128), F32)),
        compiler_params=pltpu.CompilerParams(vmem_limit_bytes=LIMIT),
        name="attend",
    )(lengths, order, q, kv)


def attend_back(lengths, order, q, kv, d_att, att, lse):
    def kernel(
        lengths, order, q_ref, kv_ref, d_ref, o_ref, lse_ref, dq_ref, dkv_ref, acc_ref, inverse
    ):
        lane = lanes_of((128, 128))
        group, sel = layout(order, inverse)
        ends = doc_ends(lengths)

        @pl.loop(0, 16)
        def _(n):
            for s in (0, 1):
                part = pl.ds(pl.multiple_of(n * 512, 512), 512)
                acc_ref[s, part, :] = jnp.zeros((512, 128), F32)

        @pl.loop(0, 8)
        def _(b):
            span = order[group * 8 + b]
            begin, runs, rest = key_range(span, ends)
            pos = span * 128 + lanes_of((1, 128))
            low = doc_start(pos, ends)
            rows = pl.ds(pl.multiple_of(b * 128, 128), 128)
            d_both = d_ref[rows, :].astype(F32)
            d_pad = (
                jnp.where(lane >= 64, pltpu.roll(d_both, 64, 1), 0.0).astype(BF),
                jnp.where(lane >= 64, d_both, 0.0).astype(BF),
            )
            pair = [jnp.concatenate([q_ref[h, rows, :], d_pad[h]], axis=0) for h in (0, 1)]
            mixed = (d_both * o_ref[rows, :].astype(F32)).T
            delta = [jnp.sum(mixed[64 * h : 64 * h + 64], axis=0, keepdims=True) for h in (0, 1)]
            lses = [lse_ref[b, h : h + 1, :] for h in (0, 1)]

            def step(n, t, state):
                where = [inverse[jnp.minimum(t + i, 63)] * 128 for i in range(n)]
                where = [pl.ds(pl.multiple_of(v, 128), 128) for v in where]
                kpos = t * 128 + lax.broadcasted_iota(jnp.int32, (n * 128, 1), 0)
                allowed = (kpos >= low) & (kpos <= pos)
                d_ss, kvs = [], []
                for h in (0, 1):
                    kv_t = jnp.concatenate([kv_ref[sel[h], w, :] for w in where], axis=0)
                    kvs.append(kv_t)
                    both = dot_nt(kv_t, pair[h])
                    p = jnp.where(allowed, jnp.exp(both[:, 0:128] - lses[h]), 0.0)
                    d_s = (p * (both[:, 128:256] - delta[h])).astype(BF)
                    d_ss.append(d_s)
                    d_kv = dot(jnp.concatenate([d_s, p.astype(BF)], axis=1), pair[h])
                    for i, w in enumerate(where):
                        acc_ref[sel[h], w, :] += d_kv[i * 128 : (i + 1) * 128]
                lanes = lanes_of((n * 128, 128))
                keys = jnp.where(lanes < 64, kvs[0], pltpu.roll(kvs[1], 64, 1))
                return state + dot_tn(keys, jnp.concatenate(d_ss, axis=1))

            state = jnp.zeros((128, 256), F32)
            state = lax.fori_loop(0, runs, lambda j, v: step(8, begin + j * 8, v), state)
            state = lax.fori_loop(0, rest, lambda j, v: step(4, begin + runs * 8, v), state)
            state = jnp.concatenate([state[0:64, 0:128], state[64:128, 128:256]], axis=0)
            dq_ref[rows, :] = state.T * 0.125

        @pl.loop(0, 16)
        def _(n):
            for s in (0, 1):
                part = pl.ds(pl.multiple_of(n * 512, 512), 512)
                dkv_ref[s, part, :] = acc_ref[s, part, :].astype(BF)

    return pl.pallas_call(
        kernel,
        in_specs=[SMEM, SMEM] + [VMEM] * 5,
        out_specs=(VMEM, VMEM),
        scratch_shapes=[pltpu.VMEM((2, 8192, 128), F32), pltpu.SMEM((64,), jnp.int32)],
        out_shape=(shaped((1024, 128), F32), shaped((2, 8192, 128), BF)),
        compiler_params=pltpu.CompilerParams(vmem_limit_bytes=LIMIT),
        name="attend_back",
    )(lengths, order, q, kv, d_att, att, lse)


def hand_out(parts):
    def kernel(*refs):
        n = len(refs) // 2
        for k, (src, dst) in enumerate(zip(refs[:n], refs[n:])):
            if dst.shape == (15,):
                wide = jnp.concatenate([src[...], jnp.zeros((113, 128), F32)], axis=0)
                dst[...] = wide.T[0:1, 0:15].reshape(15)
            else:
                dst[...] = src[...]

    shapes = [(15,) if v.shape == (15, 128) else v.shape for v in parts]
    return pl.pallas_call(
        kernel,
        out_shape=tuple(shaped(s, v.dtype) for s, v in zip(shapes, parts)),
        in_specs=[VMEM] * len(parts),
        out_specs=(VMEM,) * len(parts),
        compiler_params=pltpu.CompilerParams(vmem_limit_bytes=LIMIT),
        name="hand_out",
    )(*parts)


def local(
    hidden, attn_gain, w_q, w_k, w_v, w_o, mlp_gain, w_gate, w_up, w_down, cotangent,
    doc_lengths, span_order,
):
    frequency = ROPE_BASE ** (-2.0 * (np.arange(128) % 32) / HEAD)
    frequency = jnp.asarray(frequency, F32).reshape(1, 128)

    rows, w1, wds, wo, cot, w2own, normed, q, kv, gains, cos_t, sin_t = first(
        hidden.T, cotangent.T, w_q, w_k, w_v, w_o, w_gate, w_up, w_down, attn_gain, mlp_gain,
        doc_lengths, span_order, frequency,
    )
    kv = kv.reshape(2, 8192, 128)
    att, lse = attend(doc_lengths, span_order, q, kv)
    output, d_resid, d_heads, gwo, gw2s, gwds = feed(
        att, w2own, wo, rows.reshape(1024, WIDE), wds.reshape(384, WIDE),
        cot.reshape(1024, WIDE), gains,
    )
    d_att = d_heads.reshape(1024, 128)
    dq, dkv = attend_back(doc_lengths, span_order, q, kv, d_att, att, lse)
    grads = last(
        dkv.reshape(2, 8, 1024, 128), gwo, dq, cos_t, sin_t, w1.reshape(WIDE, 384), normed, rows,
        d_resid, gains, gw2s, gwds,
    )
    output, grad_hidden, g_attn, g_mlp, g_q, g_k, g_v, g_o, g_gate, g_up, g_down = hand_out(
        (output,) + tuple(grads)
    )
    return (
        output.T, grad_hidden.T, g_attn, g_q, g_k, g_v, g_o, g_mlp, g_gate, g_up, g_down
    )


def solution(mesh):
    both = ("fsdp", "ctx")
    wide, thin, part = P(both, None), P(both), P("fsdp")
    return jax.shard_map(
        local,
        mesh=mesh,
        in_specs=(wide, thin, wide, wide, wide, wide, thin, wide, wide, wide, wide, part, part),
        out_specs=(wide, wide, thin, wide, wide, wide, wide, thin, wide, wide, wide),
        check_vma=False,
    )
```

```python
import jax
import jax.numpy as jnp
import numpy as np
from jax import lax
from jax.experimental import pallas as pl
from jax.experimental.pallas import tpu as pltpu
from jax.sharding import PartitionSpec as P

HEAD = 64
EPSILON = 1e-05
ROPE_BASE = 100000.0
MASKED = -1e30
WIDE = 1024
WIDTH = 960
BF = jnp.bfloat16
F32 = jnp.float32
MESH = pl.DeviceIdType.MESH
DMA = pltpu.SemaphoreType.DMA
ANY = pl.BlockSpec(memory_space=pl.ANY)
VMEM = pl.BlockSpec(memory_space=pltpu.VMEM)
SMEM = pl.BlockSpec(memory_space=pltpu.SMEM)
LIMIT = 56 * 2**20
OWNED_KV = (0, 1, 1, 2, 2, 3, 4, 4)


def dot(a, b):
    return lax.dot_general(a, b, (((1,), (0,)), ((), ())), preferred_element_type=F32)


def dot_nt(a, b):
    return lax.dot_general(a, b, (((1,), (1,)), ((), ())), preferred_element_type=F32)


def dot_tn(a, b):
    return lax.dot_general(a, b, (((0,), (0,)), ((), ())), preferred_element_type=F32)


def shaped(shape, dtype):
    return jax.ShapeDtypeStruct(shape, dtype)


def place():
    i = lax.axis_index("ctx")
    return i // 16, (i // 8) % 2, (i // 2) % 4, i % 2


def at(x, z, y, c):
    return {"ctx": (((x + 4) % 4) * 2 + z) * 8 + ((y + 4) % 4) * 2 + c}


def send(src, dst, ssem, rsem, device):
    copy = pltpu.make_async_remote_copy(
        src, dst, ssem, rsem, device_id=device, device_id_type=MESH
    )
    copy.start()
    return copy


def hail(kinds):
    x, z, y, c = place()
    who = []
    if "x" in kinds:
        who += [at(x + 1, z, y, c), at(x - 1, z, y, c), at(x, 1 - z, y, c)]
    if "f" in kinds:
        who += [at(x, z, y + d, (c + e) % 2) for d in range(4) for e in range(2) if d + e]
    elif "y" in kinds:
        who += [at(x, z, y + d, c) for d in (1, 2, 3)] + [at(x, z, y, 1 - c)]
    barrier = pltpu.get_barrier_semaphore()
    for device in who:
        pl.semaphore_signal(barrier, inc=1, device_id=device, device_id_type=MESH)
    return len(who)


def greet(kinds):
    pl.semaphore_wait(pltpu.get_barrier_semaphore(), hail(kinds))


def half_lead(ref, k):
    n = ref.shape[0] // 2
    return ref.at[pl.ds(k * n, n)]


def half_lanes(ref, k):
    n = ref.shape[-1] // 2
    return ref.at[:, pl.ds(k * n, n)]


class RingGather:
    sems = [DMA((9,)), DMA((9,)), DMA(())]

    def __init__(self, src, dst, half, ssem, rsem, lsem, arrived=None):
        self.src, self.dst, self.half = src, dst, half
        self.ssem, self.rsem, self.lsem = ssem, rsem, lsem
        self.arrived = arrived or (lambda block: None)
        self.copies = {}

    def push(self, n, src, dst, device):
        self.copies[n] = send(src, dst, self.ssem.at[n], self.rsem.at[n], device)

    def start(self):
        x, z, y, c = place()
        me = self.dst.at[x * 2 + z]
        self.push(0, self.src, me, at(x, 1 - z, y, c))
        self.push(1, self.src, me, at(x + 1, z, y, c))
        self.push(2, self.src, me, at(x - 1, z, y, c))
        self.local = pltpu.make_async_copy(self.src, me, self.lsem)
        self.local.start()

    def relay_z(self):
        x, z, y, c = place()
        block = self.dst.at[x * 2 + 1 - z]
        self.copies[0].wait_recv()
        self.push(3, block, block, at(x + 1, z, y, c))
        self.push(4, block, block, at(x - 1, z, y, c))
        self.arrived(x * 2 + 1 - z)

    def relay_x(self, k):
        x, z, y, c = place()
        zz = z if k == 0 else 1 - z
        left, right = ((x + 3) % 4) * 2 + zz, ((x + 1) % 4) * 2 + zz
        self.copies[1 + 2 * k].wait_recv()
        part = self.half(self.dst.at[left], 0)
        self.push(5 + 2 * k, part, part, at(x + 1, z, y, c))
        self.arrived(left)
        self.copies[2 + 2 * k].wait_recv()
        part = self.half(self.dst.at[right], 1)
        self.push(6 + 2 * k, part, part, at(x - 1, z, y, c))
        self.arrived(right)

    def land(self, k):
        x, z, y, c = place()
        zz = z if k == 0 else 1 - z
        self.copies[5 + 2 * k].wait_recv()
        self.copies[6 + 2 * k].wait_recv()
        self.arrived(((x + 2) % 4) * 2 + zz)

    def sent(self):
        for n in range(9):
            self.copies[n].wait_send()

    def finish(self):
        self.local.wait()
        self.sent()


def run_ring_gathers(rings):
    for ring in rings:
        ring.relay_z()
    for k in (0, 1):
        for ring in rings:
            ring.relay_x(k)
    for k in (0, 1):
        for ring in rings:
            ring.land(k)


class RowGather:
    sems = [DMA((8,)), DMA((8,)), DMA(())]

    def __init__(self, src, dst, ssem, rsem, lsem):
        self.src, self.dst = src, dst
        self.ssem, self.rsem, self.lsem = ssem, rsem, lsem
        self.copies = {}

    def push(self, n, src, dst, device):
        self.copies[n] = send(src, dst, self.ssem.at[n], self.rsem.at[n], device)

    def start(self):
        x, z, y, c = place()
        me = self.dst.at[y * 2 + c]
        self.push(1, self.src, me, at(x, z, y + 1, c))
        self.push(2, self.src, me, at(x, z, y - 1, c))
        self.push(0, self.src, me, at(x, z, y, 1 - c))
        self.local = pltpu.make_async_copy(self.src, me, self.lsem)
        self.local.start()

    def relay(self):
        x, z, y, c = place()
        for n, step, side in ((1, 3, 0), (2, 1, 1)):
            self.copies[n].wait_recv()
            block = self.dst.at[((y + step) % 4) * 2 + c]
            part = half_lead(block, side)
            self.push(2 + n, part, part, at(x, z, y + 4 - step, c))
            self.push(4 + n, block, block, at(x, z, y, 1 - c))

    def land(self):
        x, z, y, c = place()
        self.copies[3].wait_recv()
        self.copies[4].wait_recv()
        block = self.dst.at[((y + 2) % 4) * 2 + c]
        self.push(7, block, block, at(x, z, y, 1 - c))

    def finish(self):
        self.local.wait()
        for n in (0, 5, 6, 7):
            self.copies[n].wait_recv()
        for n in range(8):
            self.copies[n].wait_send()


class Swap:
    sems = [DMA((8,)), DMA((8,)), DMA(())]

    def __init__(self, src, dst, ssem, rsem, lsem):
        self.src, self.dst = src, dst
        self.ssem, self.rsem, self.lsem = ssem, rsem, lsem

    def start(self):
        x, z, y, c = place()
        me = y * 2 + c
        self.copies = []
        for d in (2, 1, 3, 0):
            for e in (0, 1):
                if d + e:
                    n = d * 2 + e
                    to = ((y + d) % 4) * 2 + (c + e) % 2
                    self.copies.append(
                        send(
                            self.src.at[to],
                            self.dst.at[me],
                            self.ssem.at[n],
                            self.rsem.at[n],
                            at(x, z, y + d, (c + e) % 2),
                        )
                    )
        self.local = pltpu.make_async_copy(self.src.at[me], self.dst.at[me], self.lsem)
        self.local.start()

    def finish(self):
        self.local.wait()
        for copy in self.copies:
            copy.wait()


class RowSum:
    @staticmethod
    def scratch(shape):
        return [
            pltpu.VMEM((4,) + shape, BF),
            pltpu.VMEM((4,) + shape, BF),
            pltpu.VMEM((4,) + shape, BF),
            DMA((8,)),
            DMA((8,)),
        ]

    def __init__(self, blk, first, mixed, second, ssem, rsem):
        self.blk, self.first, self.mixed, self.second = blk, first, mixed, second
        self.ssem, self.rsem = ssem, rsem
        self.copies = {}

    def push(self, n, src, dst, device):
        self.copies[n] = send(src, dst, self.ssem.at[n], self.rsem.at[n], device)

    def hand(self, d):
        x, z, y, c = place()
        to = ((y + d) % 4) * 2 + 1 - c
        self.push(d, self.blk.at[to], self.first.at[d], at(x, z, y, 1 - c))

    def start(self):
        for d in (2, 1, 3, 0):
            self.hand(d)

    def relay(self):
        x, z, y, c = place()
        for d in (2, 1, 3):
            self.copies[d].wait_recv()
            own = self.blk[((y + d) % 4) * 2 + c].astype(F32)
            self.mixed[d] = (own + self.first[d].astype(F32)).astype(BF)
            self.push(4 + d, self.mixed.at[d], self.second.at[d], at(x, z, y + d, c))

    def total(self):
        x, z, y, c = place()
        self.copies[0].wait_recv()
        total = self.blk[y * 2 + c].astype(F32) + self.first[0].astype(F32)
        for d in (1, 3, 2):
            self.copies[4 + d].wait_recv()
            total = total + self.second[d].astype(F32)
        return total

    def finish(self):
        for n in (0, 1, 2, 3, 5, 6, 7):
            self.copies[n].wait_send()


class RingSum:
    @staticmethod
    def scratch(shape, lanes):
        if lanes:
            part = shape[:-1] + (shape[-1] // 2,)
        else:
            part = (shape[0] // 2,) + shape[1:]
        return [
            pltpu.VMEM((4,) + part, BF),
            pltpu.VMEM((4,) + shape, BF),
            pltpu.VMEM((4,) + shape, BF),
            pltpu.VMEM((2,) + shape, BF),
            DMA((9,)),
            DMA((9,)),
        ]

    def __init__(self, blk, lanes, parts, mixed, heard, across, ssem, rsem):
        self.blk, self.half = blk, half_lanes if lanes else half_lead
        self.parts, self.mixed, self.heard, self.across = parts, mixed, heard, across
        self.ssem, self.rsem = ssem, rsem
        self.copies = {}

    def push(self, n, src, dst, device):
        self.copies[n] = send(src, dst, self.ssem.at[n], self.rsem.at[n], device)

    def start(self, k):
        x, z, y, c = place()
        zz = 1 - z if k == 0 else z
        far = self.blk.at[((x + 2) % 4) * 2 + zz]
        self.push(4 * k, self.half(far, 0), self.parts.at[2 * k], at(x + 1, z, y, c))
        self.push(4 * k + 1, self.half(far, 1), self.parts.at[2 * k + 1], at(x - 1, z, y, c))

    def relay(self, k):
        x, z, y, c = place()
        zz = 1 - z if k == 0 else z
        for side, step in ((0, 1), (1, 3)):
            n = 2 * k + side
            mixed = self.mixed.at[n]
            source = self.blk.at[((x + step) % 4) * 2 + zz]
            mine, other = self.half(source, side), self.half(source, 1 - side)
            self.half(mixed, 1 - side)[...] = other[...]
            self.copies[4 * k + side].wait_recv()
            self.half(mixed, side)[...] = (
                mine[...].astype(F32) + self.parts[n].astype(F32)
            ).astype(BF)
            self.push(4 * k + 2 + side, mixed, self.heard.at[n], at(x + step, z, y, c))

    def total(self, k):
        x, z, y, c = place()
        zz = 1 - z if k == 0 else z
        total = self.blk[x * 2 + zz].astype(F32)
        for side in (0, 1):
            self.copies[4 * k + 2 + side].wait_recv()
            total = total + self.heard[2 * k + side].astype(F32)
        if k == 0:
            self.across[0] = total.astype(BF)
            self.push(8, self.across.at[0], self.across.at[1], at(x, 1 - z, y, c))
            return None
        self.copies[8].wait_recv()
        return total + self.across[1].astype(F32)

    def finish(self):
        for n in range(9):
            self.copies[n].wait_send()


def fetch(src, dst, sem):
    copy = pltpu.make_async_copy(src, dst, sem)
    copy.start()
    return copy


def columns_of_gains(gain1, gain2):
    gap = jnp.zeros((1, 113), F32)
    return jnp.concatenate(
        [
            jnp.concatenate([ref[...].astype(F32).reshape(1, 15), gap], axis=1)
            for ref in (gain1, gain2)
        ]
        + [jnp.zeros((126, 128), F32)],
        axis=0,
    ).T[0:15]


def comm_call(name, number, kernel, out_shape, in_specs, out_specs, scratch, args):
    return pl.pallas_call(
        kernel,
        out_shape=out_shape,
        in_specs=in_specs,
        out_specs=out_specs,
        scratch_shapes=scratch,
        compiler_params=pltpu.CompilerParams(
            collective_id=number, has_side_effects=True, vmem_limit_bytes=LIMIT
        ),
        name=name,
    )(*args)


def split(refs, counts):
    parts, begin = [], 0
    for n in counts:
        parts.append(refs[begin : begin + n])
        begin += n
    return parts


def spread_value(rows):
    j = lax.broadcasted_iota(jnp.int32, (rows, WIDE), 0)
    k = lax.broadcasted_iota(jnp.int32, (rows, WIDE), 1)
    hit = ((k // 16) * 15 + k % 16 == j) & (k % 16 < 15)
    return jnp.where(hit, 1.0, 0.0).astype(BF)


def first(
    hidden_t, cot_t, w_q, w_k, w_v, w_o, w_gate, w_up, w_down, gain1, gain2, lengths, span_order, freq
):
    def kernel(
        hidden_t, cot_t, w_q, w_k, w_v, w_o, w_gate, w_up, w_down, gain1, gain2, lengths, order, freq,
        rows_out, w1_out, wds, wo, cot, w2own, normed_out, q_out, kv2, cos_out, sin_out,
        rows, w1, normed, q_rot, cos_t, sin_t, xp, cp, wp1, wp2, wop, wdp, wos, w1own, kv, outs,
        *sems,
    ):
        a, b, d, e, e2, ac, ao, b2, k0, k1, (hs, hr) = split(sems, (3,) * 10 + (2,))
        x, z, y, c = place()
        partners = hail("xf")

        gains = columns_of_gains(gain1, gain2)
        q = jnp.concatenate([w_q[...].astype(F32), jnp.zeros((15, 64), F32)], axis=1)
        q, k, v = (w * gains[:, 0:1] for w in (q, w_k[...].astype(F32), w_v[...].astype(F32)))
        wp1[...] = jnp.zeros(wp1.shape, BF)
        for f in range(8):
            n = OWNED_KV[f] * 64
            wp1[f, 0:15, 0:128] = q[:, 128 * f : 128 * f + 128].astype(BF)
            wp1[f, 0:15, 128:256] = jnp.concatenate(
                [k[:, n : n + 64], v[:, n : n + 64]], axis=1
            ).astype(BF)
        spread = spread_value(WIDTH)
        xp[...] = dot_tn(hidden_t[...], spread).astype(BF)

        pl.semaphore_wait(pltpu.get_barrier_semaphore(), partners)
        swap = Swap(wp1, w1own, *b)
        swap.start()
        gather = RowGather(xp, rows, *a)
        gather.start()
        wop[...] = jnp.zeros(wop.shape, BF)
        wop[0:15, :] = dot(w_o[...], spread).astype(BF)
        wdp[...] = jnp.zeros(wdp.shape, BF)
        wdp[0:40, :] = dot(w_down[...], spread).astype(BF)
        ring_o = RingGather(wop, wos, half_lanes, *e)
        ring_d = RingGather(wdp, wds, half_lanes, *e2)
        swap.finish()
        ring_1 = RingGather(w1own, w1, half_lead, *d)
        ring_1.start()
        ring_o.start()
        ring_d.start()
        cp[...] = dot_tn(cot_t[...], spread).astype(BF)
        gather.relay()
        gather_c = RowGather(cp, cot, *ac)
        gather_c.start()
        rings = [ring_1, ring_o, ring_d]
        for ring in rings:
            ring.relay_z()

        wp2[...] = jnp.zeros(wp2.shape, BF)
        gap = jnp.zeros((15, 8), F32)
        for m, ref in ((0, w_gate), (384, w_up)):
            w = ref[...].astype(F32) * gains[:, 1:2]
            for f in range(8):
                parts = []
                for g in range(8):
                    n = (8 * g + f) * 40
                    parts += [w[:, n : n + 40], gap]
                wp2[f, 0:15, m : m + 384] = jnp.concatenate(parts, axis=1).astype(BF)
        swap2 = Swap(wp2, w2own, *b2)
        swap2.start()

        for k in (0, 1):
            for ring in rings:
                ring.relay_x(k)

        lane = lanes_of((1, 128))
        sign = jnp.where(lane % 64 < 32, -1.0, 1.0)
        ends = doc_ends(lengths)

        @pl.loop(0, 8)
        def _(n):
            pos = order[(x * 2 + z) * 8 + n] * 128
            pos = pos + lax.broadcasted_iota(jnp.int32, (128, 1), 0)
            angle = (pos - doc_start(pos, ends)).astype(F32) * freq[...]
            part = pl.ds(pl.multiple_of(n * 128, 128), 128)
            cos_t[part, :] = jnp.cos(angle)
            sin_t[part, :] = sign * jnp.sin(angle)

        written = [fetch(cos_t, cos_out, outs.at[0]), fetch(sin_t, sin_out, outs.at[1])]
        gather.land()
        for k in (0, 1):
            for ring in rings:
                ring.land(k)
        ring_o.local.wait()
        gather_o = RowGather(wos, wo, *ao)
        gather_o.start()
        gather.finish()
        ring_1.local.wait()
        written += [fetch(rows, rows_out, outs.at[2]), fetch(w1, w1_out, outs.at[3])]

        w = w1.reshape(WIDE, 256)
        lane = lanes_of((256, 128))

        def project(n):
            part = pl.ds(n * 256, 256)
            xs = jnp.concatenate([rows[2 * n], rows[2 * n + 1]], axis=0).astype(F32)
            v = (xs * inverse_rms(xs)).astype(BF)
            normed[part, :] = v
            out = dot(v, w[...])
            cos_v, sin_v = cos_t[part, :], sin_t[part, :]
            qs, ks = out[:, 0:128], out[:, 128:256]
            qs = (qs * cos_v + partner(qs) * sin_v).astype(BF).astype(F32) * 0.125
            kv[part, :] = jnp.where(lane < 64, ks * cos_v + partner(ks) * sin_v, ks).astype(BF)
            q_rot[0, part, :] = jnp.where(lane < 64, qs, 0.0).astype(BF)
            q_rot[1, part, :] = jnp.where(lane < 64, pltpu.roll(qs, 64, 1), 0.0).astype(BF)

        hand = []

        def pass_on(piece):
            n = len(hand)
            hand.append(send(piece, piece, hs.at[n], hr.at[n], at(x, z, y, 1 - c)))

        key_rings = []
        for h, own in ((0, k0), (1, k1)):
            mine = kv.at[pl.ds(512 * h, 512)]
            spot = pl.ds(512 * h, 512)
            ring = RingGather(
                mine,
                kv2.at[c, :, spot],
                half_lead,
                *own,
                arrived=lambda block, spot=spot: pass_on(kv2.at[c, block, spot]),
            )
            project(2 * h)
            project(2 * h + 1)
            ring.start()
            n = len(hand)
            hand.append(
                send(
                    mine, kv2.at[c, x * 2 + z, spot], hs.at[n], hr.at[n], at(x, z, y, 1 - c)
                )
            )
            key_rings.append(ring)
            if h == 0:
                gather_c.relay()

        written += [fetch(normed, normed_out, outs.at[4]), fetch(q_rot, q_out, outs.at[5])]
        for ring in key_rings:
            ring.relay_z()
        gather_o.relay()
        for ring in key_rings:
            ring.relay_x(0)
        gather_c.land()
        for ring in key_rings:
            ring.relay_x(1)
        gather_o.land()
        for k in (0, 1):
            for ring in key_rings:
                ring.land(k)
        for copy in hand:
            copy.wait()
        swap2.finish()
        gather_o.finish()
        gather_c.finish()
        for ring in [ring_d] + key_rings:
            ring.finish()
        for ring in (ring_1, ring_o):
            ring.sent()
        for copy in written:
            copy.wait()

    return comm_call(
        "first",
        1,
        kernel,
        (
            shaped((8, 128, WIDE), BF),
            shaped((8, 8, 16, 256), BF),
            shaped((8, 48, WIDE), BF),
            shaped((8, 8, 16, WIDE), BF),
            shaped((8, 128, WIDE), BF),
            shaped((8, 16, 768), BF),
            shaped((1024, WIDE), BF),
            shaped((2, 1024, 128), BF),
            shaped((2, 8, 1024, 128), BF),
            shaped((1024, 128), F32),
            shaped((1024, 128), F32),
        ),
        [VMEM] * 11 + [SMEM, SMEM, VMEM],
        (ANY,) * 11,
        [
            pltpu.VMEM((8, 128, WIDE), BF),
            pltpu.VMEM((8, 8, 16, 256), BF),
            pltpu.VMEM((1024, WIDE), BF),
            pltpu.VMEM((2, 1024, 128), BF),
            pltpu.VMEM((1024, 128), F32),
            pltpu.VMEM((1024, 128), F32),
            pltpu.VMEM((128, WIDE), BF),
            pltpu.VMEM((128, WIDE), BF),
            pltpu.VMEM((8, 16, 256), BF),
            pltpu.VMEM((8, 16, 768), BF),
            pltpu.VMEM((16, WIDE), BF),
            pltpu.VMEM((48, WIDE), BF),
            pltpu.VMEM((8, 16, WIDE), BF),
            pltpu.VMEM((8, 16, 256), BF),
            pltpu.VMEM((1024, 128), BF),
            DMA((6,)),
        ]
        + RowGather.sems
        + Swap.sems
        + RingGather.sems * 3
        + RowGather.sems * 2
        + Swap.sems
        + RingGather.sems * 2
        + [DMA((16,)), DMA((16,))],
        (
            hidden_t, cot_t, w_q, w_k, w_v, w_o, w_gate, w_up, w_down, gain1, gain2, lengths,
            span_order, freq,
        ),
    )


def inverse_rms(v):
    return lax.rsqrt(jnp.sum(v * v, axis=1, keepdims=True) * (1.0 / WIDTH) + EPSILON)


def feed(att, w2own, wo, rows, wd, cot):
    def kernel(
        att, w2own, wo_in, rows_in, wd_in, cot_in,
        output, d_resid, d_heads, gwo_out, gw2_sum, gwd_sum,
        wo, x_in, wd, cot, ins, atts, w2, packed, d_act, resid, normed, act, d_both, dmn, outp,
        gw2, gwd, da, gwo, *refs,
    ):
        a, b, s, r1, r2, t1, t2 = split(refs, (3, 3, 3, 5, 5, 6, 6))
        x, z, y, c = place()
        me = y * 2 + c
        partners = hail("xf")
        pairs = ((wo_in, wo), (cot_in, cot), (wd_in, wd), (rows_in, x_in))
        held = [fetch(src, dst, ins.at[n]) for n, (src, dst) in enumerate(pairs)]
        pl.semaphore_wait(pltpu.get_barrier_semaphore(), partners)
        gather = RowGather(att, atts, *a)
        ring = RingGather(w2own, w2, half_lead, *b)
        gather.start()
        ring.start()

        def place_rows(n, size):
            return pl.ds(pl.multiple_of(n * size, size), size)

        held[0].wait()
        whole = jnp.concatenate([wo[f, g] for g in range(8) for f in range(8)], axis=0)

        def pack(n):
            j = lax.broadcasted_iota(jnp.int32, (512, WIDE), 0) + n * 512
            k = lax.broadcasted_iota(jnp.int32, (512, WIDE), 1)
            hit = ((k // 16) * 15 + k % 16 == j) & (k % 16 < 15)
            packed[pl.ds(n * 512, 512), :] = dot(
                jnp.where(hit, 1.0, 0.0).astype(BF), whole
            ).astype(BF)

        pack(0)
        ring.relay_z()
        gather.relay()
        pack(1)
        ring.relay_x(0)
        held[1].wait()
        held[2].wait()

        @pl.loop(0, 2)
        def _(n):
            part = place_rows(n, 512)
            d_act[part, :] = dot_nt(cot[part, :], wd[...])

        ring.relay_x(1)
        held[3].wait()
        gather.land()
        gather.finish()

        @pl.loop(0, 2)
        def _(n):
            part = place_rows(n, 512)
            heads = jnp.concatenate([atts[f, part, :] for f in range(8)], axis=1)
            v = x_in[part, :].astype(F32) + dot(heads, packed[...])
            resid[part, :] = v
            normed[part, :] = (v * inverse_rms(v)).astype(BF)

        ring.land(0)
        ring.land(1)
        ring.finish()
        w2_all = w2.reshape(WIDE, 768)

        @pl.loop(0, 2)
        def _(n):
            part = place_rows(n, 512)
            both = dot(normed[part, :], w2_all[...])
            gate, up = both[:, 0:384], both[:, 384:768]
            sigma = 1.0 / (1.0 + jnp.exp(-gate))
            silu = gate * sigma
            act[part, :] = (silu * up).astype(BF)
            d = d_act[part, :]
            d_both[part, 0:384] = (d * up * sigma * (1.0 + gate * (1.0 - sigma))).astype(BF)
            d_both[part, 384:768] = (d * silu).astype(BF)

        sum_n, sum_o = RowSum(dmn, *r1), RowSum(outp, *r2)
        ring_2, ring_d = RingSum(gw2, False, *t1), RingSum(gwd, True, *t2)

        def back(core):
            to = [((y + n) % 4) * 2 + core for n in (2, 1, 3, 0)]
            v = jnp.concatenate([d_both[place_rows(n, 128), :] for n in to], axis=0)
            v = dot_nt(v, w2_all[...]).astype(BF)
            for n in range(4):
                dmn[to[n]] = v[128 * n : 128 * n + 128]

        order = [(2, 1), (2, 0), (1, 1), (3, 1), (1, 0), (3, 0), (0, 1), (0, 0)]
        where = [((x + p) % 4) * 2 + (1 - z if q else z) for p, q in order]

        def weights(which):
            v = jnp.concatenate([normed[:, place_rows(where[n], 128)] for n in which], axis=1)
            v = dot_tn(v, d_both[...]).astype(BF)
            for n, m in enumerate(which):
                gw2[where[m]] = v[128 * n : 128 * n + 128].reshape(8, 16, 768)

        weights((0, 1))
        ring_2.start(0)
        ring_2.start(1)
        back(1 - c)
        for d in (2, 1, 3, 0):
            sum_n.hand(d)
        gwd[...] = dot_tn(act[...], cot[...]).astype(BF).reshape(8, 48, WIDE)
        ring_d.start(0)
        ring_d.start(1)
        back(c)
        sum_n.relay()
        weights((2, 3, 4, 5, 6, 7))
        ring_2.relay(0)
        ring_d.relay(0)

        @pl.loop(0, 2)
        def _(n):
            v = dot(act[place_rows(n, 512), :], wd[...]).astype(BF)
            for k in range(4):
                outp[n * 4 + k] = v[128 * k : 128 * k + 128]

        sum_o.start()
        ring_2.relay(1)
        ring_d.relay(1)
        sum_o.relay()

        mine = place_rows(me, 128)
        v = resid[mine, :]
        inv = inverse_rms(v)
        e = sum_n.total()
        mean = jnp.sum(e * v, axis=1, keepdims=True) * (1.0 / WIDTH)
        d_v = cot[mine, :].astype(F32) + inv * e - v * (inv * inv * inv * mean)
        d_resid[...] = d_v
        mixed = d_v.astype(BF)
        d_att = dot_nt(mixed, packed[...]).astype(BF)
        for f in range(8):
            da[f] = d_att[:, f * 128 : (f + 1) * 128]
        swap = Swap(da, d_heads, *s)
        swap.start()
        spread = spread_value(WIDE)
        heads = jnp.concatenate([atts[f, mine, :] for f in range(8)], axis=1)
        gw = dot_tn(dot(heads, spread).astype(BF), mixed).astype(BF)
        for g in range(8):
            for f in range(8):
                n = (8 * g + f) * 16
                gwo[f, g * 16 : (g + 1) * 16, :] = gw[n : n + 16]
        written = fetch(gwo, gwo_out, ins.at[4])
        ring_2.total(0)
        ring_d.total(0)
        output[...] = dot_nt(spread[0:WIDTH], (v + sum_o.total()).astype(BF)).astype(BF)
        gw2_sum[...] = ring_2.total(1).astype(BF)
        gwd_sum[...] = ring_d.total(1)
        swap.finish()
        sum_n.finish()
        sum_o.finish()
        ring_2.finish()
        ring_d.finish()
        written.wait()

    return comm_call(
        "feed",
        3,
        kernel,
        (
            shaped((WIDTH, 128), BF),
            shaped((128, WIDE), F32),
            shaped((8, 128, 128), BF),
            shaped((8, 128, WIDE), BF),
            shaped((8, 16, 768), BF),
            shaped((48, WIDE), F32),
        ),
        [ANY] * 6,
        (VMEM, VMEM, ANY, ANY, VMEM, VMEM),
        [
            pltpu.VMEM((8, 8, 16, WIDE), BF),
            pltpu.VMEM((1024, WIDE), BF),
            pltpu.VMEM((384, WIDE), BF),
            pltpu.VMEM((1024, WIDE), BF),
            DMA((5,)),
            pltpu.VMEM((8, 1024, 128), BF),
            pltpu.VMEM((8, 8, 16, 768), BF),
            pltpu.VMEM((WIDE, WIDE), BF),
            pltpu.VMEM((1024, 384), F32),
            pltpu.VMEM((1024, WIDE), F32),
            pltpu.VMEM((1024, WIDE), BF),
            pltpu.VMEM((1024, 384), BF),
            pltpu.VMEM((1024, 768), BF),
            pltpu.VMEM((8, 128, WIDE), BF),
            pltpu.VMEM((8, 128, WIDE), BF),
            pltpu.VMEM((8, 8, 16, 768), BF),
            pltpu.VMEM((8, 48, WIDE), BF),
            pltpu.VMEM((8, 128, 128), BF),
            pltpu.VMEM((8, 128, WIDE), BF),
        ]
        + RowGather.sems
        + RingGather.sems
        + Swap.sems
        + RowSum.scratch((128, WIDE)) * 2
        + RingSum.scratch((8, 16, 768), False)
        + RingSum.scratch((48, WIDE), True),
        (att, w2own, wo, rows, wd, cot),
    )


def last(
    dkv, gwo, dq, cos_t, sin_t, w1, normed, rows, d_resid, gw2s, gwd, gain1, gain2, w_q, w_k, w_v,
    w_gate, w_up,
):
    def kernel(
        dkv, gwo_in, dq_in, cos_in, sin_in, w1_in, normed_in, rows_in, dr, gw2s, wd, gain1, gain2,
        w_q, w_k, w_v, w_gate, w_up,
        gh, g_attn, g_mlp, g_q, g_k, g_v, g_o, g_gate, g_up, g_down,
        own, gwo, dq, cos_t, sin_t, w1, normed, rows, ins,
        blk, from_core, gwos, gw1, dnq, d_kv, dn, one, two, gw1s, hs, hr, *refs,
    ):
        a, b, d, e, e2, s1, s2 = split(refs, (6, 5, 5, 6, 6, 3, 3))
        x, z, y, c = place()
        me = y * 2 + c
        partners = hail("xf")
        pairs = [
            (gwo_in, gwo),
            (dkv.at[c], own),
            (dq_in, dq),
            (cos_in, cos_t),
            (sin_in, sin_t),
            (w1_in, w1),
            (normed_in, normed),
            (rows_in.at[me], rows),
        ]
        held = [fetch(src, dst, ins.at[n]) for n, (src, dst) in enumerate(pairs)]
        pl.semaphore_wait(pltpu.get_barrier_semaphore(), partners)
        order = [(2, 1), (2, 0), (1, 1), (3, 1), (1, 0), (3, 0), (0, 1), (0, 0)]
        where = [((x + p) % 4) * 2 + (1 - z if q else z) for p, q in order]
        hand = [
            send(dkv.at[1 - c, g], from_core.at[n], hs.at[n], hr.at[n], at(x, z, y, 1 - c))
            for n, g in enumerate(where)
        ]
        held[0].wait()
        sum_w = RowSum(gwo, *b)
        sum_w.start()
        swap2 = Swap(gw2s, two, *s2)
        swap2.start()
        ring = RingSum(blk, False, *a)
        held[1].wait()

        def fold(n):
            g = where[n]
            hand[n].wait_recv()
            blk[g] = (own[g].astype(F32) + from_core[n].astype(F32)).astype(BF)

        fold(0)
        ring.start(0)
        fold(1)
        ring.start(1)
        for n in range(2, 6):
            fold(n)
        sum_w.relay()
        for n in range(2, 6):
            held[n].wait()
        spread = spread_value(WIDTH)
        gains = columns_of_gains(gain1, gain2)

        def place_rows(n, size):
            return pl.ds(pl.multiple_of(n * size, size), size)

        def queries(n):
            part = place_rows(n, 512)
            v = dq[part, :]
            v = (v * cos_t[part, :] - partner(v) * sin_t[part, :]).astype(BF)
            d_kv[part, 0:128] = v
            dnq[part, :] = dot_nt(v, w1[:, 0:128])

        queries(0)
        ring.relay(0)
        queries(1)
        ring.relay(1)
        fold(6)
        fold(7)
        held[6].wait()
        gw1[:, :, :, 0:128] = (
            dot_tn(normed[...], d_kv[:, 0:128]).astype(BF).reshape(8, 8, 16, 128)
        )
        gwos[...] = sum_w.total().astype(BF).reshape(8, 16, WIDE)
        ring_o = RingSum(gwos, True, *e2)
        ring_o.start(0)
        ring_o.start(1)
        ring.total(0)
        swap2.finish()
        total = jnp.zeros((15, 1), F32)
        for m, ref, w in ((0, g_gate, w_gate), (384, g_up, w_up)):
            for n in range(0, 8, 2):
                part = jnp.concatenate(
                    [
                        two[f, :, m + 48 * k : m + 48 * k + 40].astype(F32)[0:15]
                        for k in (n, n + 1)
                        for f in range(8)
                    ],
                    axis=1,
                )
                spot = pl.ds(n * 320, 640)
                ref[:, spot] = part * gains[:, 1:2]
                total += jnp.sum(part * w[:, spot].astype(F32), axis=1, keepdims=True)
        g_mlp[...] = jnp.broadcast_to(total, (15, 128))

        def squeeze(v):
            top = v.astype(BF)
            low = (v - top.astype(F32)).astype(BF)
            return dot_nt(top, spread) + dot_nt(low, spread)

        g_down[...] = squeeze(wd[...])[0:40]
        ring_o.relay(0)
        ring_o.relay(1)

        v = ring.total(1)
        turned = v * cos_t[...] - partner(v) * sin_t[...]
        d_kv[:, 128:256] = jnp.where(lanes_of((1024, 128)) < 64, turned, v).astype(BF)
        sum_n = RowSum(dn, *d)

        def back(core):
            to = [((y + n) % 4) * 2 + core for n in (2, 1, 3, 0)]
            parts = [place_rows(n, 128) for n in to]
            v = jnp.concatenate([d_kv[p, 128:256] for p in parts], axis=0)
            v = dot_nt(v, w1[:, 128:256])
            for n, p in enumerate(parts):
                dn[to[n]] = (dnq[p, :] + v[128 * n : 128 * n + 128]).astype(BF)

        back(1 - c)
        for n in (2, 1, 3, 0):
            sum_n.hand(n)
        ring_1 = RingSum(gw1, False, *e)

        def weights_k(which):
            parts = [place_rows(where[n], 128) for n in which]
            v = jnp.concatenate([normed[:, p] for p in parts], axis=1)
            v = dot_tn(v, d_kv[:, 128:256]).astype(BF)
            for n, m in enumerate(which):
                gw1[where[m], :, :, 128:256] = v[128 * n : 128 * n + 128].reshape(8, 16, 128)

        weights_k((0, 1))
        ring_1.start(0)
        ring_1.start(1)
        back(c)
        sum_n.relay()
        weights_k((2, 3, 4, 5, 6, 7))
        ring_1.relay(0)
        ring_1.relay(1)
        ring_o.total(0)
        ring_1.total(0)
        g_o[...] = squeeze(ring_o.total(1))[0:15]
        gw1s[...] = ring_1.total(1).astype(BF)
        swap1 = Swap(gw1s, one, *s1)
        swap1.start()

        held[7].wait()
        xs = rows[...].astype(F32)
        inv = inverse_rms(xs)
        t = sum_n.total()
        mean = jnp.sum(t * xs, axis=1, keepdims=True) * (1.0 / WIDTH)
        d_x = dr[...] + inv * t - xs * (inv * inv * inv * mean)
        gh[...] = dot_nt(spread, d_x.astype(BF)).astype(BF)
        swap1.finish()
        ones = [one[f].astype(F32)[0:15] for f in range(8)]
        r_q = jnp.concatenate([v[:, 0:128] for v in ones], axis=1)[:, 0:WIDTH]

        def heads(n):
            return jnp.concatenate(
                [
                    sum(ones[f][:, n : n + 64] for f in range(8) if OWNED_KV[f] == h)
                    for h in range(5)
                ],
                axis=1,
            )

        total = jnp.zeros((15, 1), F32)
        for part, w, ref in ((r_q, w_q, g_q), (heads(128), w_k, g_k), (heads(192), w_v, g_v)):
            ref[...] = part * gains[:, 0:1]
            total += jnp.sum(part * w[...].astype(F32), axis=1, keepdims=True)
        g_attn[...] = jnp.broadcast_to(total, (15, 128))
        for copy in hand:
            copy.wait_send()
        ring.finish()
        ring_1.finish()
        ring_o.finish()
        sum_w.finish()
        sum_n.finish()

    return comm_call(
        "last",
        6,
        kernel,
        (
            shaped((WIDTH, 128), BF),
            shaped((15, 128), F32),
            shaped((15, 128), F32),
            shaped((15, WIDTH), F32),
            shaped((15, 320), F32),
            shaped((15, 320), F32),
            shaped((15, WIDTH), F32),
            shaped((15, 2560), F32),
            shaped((15, 2560), F32),
            shaped((40, WIDTH), F32),
        ),
        [ANY] * 8 + [VMEM] * 10,
        (VMEM,) * 10,
        [
            pltpu.VMEM((8, 1024, 128), BF),
            pltpu.VMEM((8, 128, WIDE), BF),
            pltpu.VMEM((1024, 128), F32),
            pltpu.VMEM((1024, 128), F32),
            pltpu.VMEM((1024, 128), F32),
            pltpu.VMEM((WIDE, 256), BF),
            pltpu.VMEM((1024, WIDE), BF),
            pltpu.VMEM((128, WIDE), BF),
            DMA((8,)),
            pltpu.VMEM((8, 1024, 128), BF),
            pltpu.VMEM((8, 1024, 128), BF),
            pltpu.VMEM((8, 16, WIDE), BF),
            pltpu.VMEM((8, 8, 16, 256), BF),
            pltpu.VMEM((1024, WIDE), F32),
            pltpu.VMEM((1024, 256), BF),
            pltpu.VMEM((8, 128, WIDE), BF),
            pltpu.VMEM((8, 16, 256), BF),
            pltpu.VMEM((8, 16, 768), BF),
            pltpu.VMEM((8, 16, 256), BF),
            DMA((8,)),
            DMA((8,)),
        ]
        + RingSum.scratch((1024, 128), False)
        + RowSum.scratch((128, WIDE)) * 2
        + RingSum.scratch((8, 16, 256), False)
        + RingSum.scratch((16, WIDE), True)
        + Swap.sems * 2,
        (
            dkv, gwo, dq, cos_t, sin_t, w1, normed, rows, d_resid, gw2s, gwd, gain1, gain2, w_q,
            w_k, w_v, w_gate, w_up,
        ),
    )


def lanes_of(shape):
    return lax.broadcasted_iota(jnp.int32, shape, len(shape) - 1)


def partner(v):
    lane = lanes_of(v.shape)
    return jnp.where(lane % 64 < 32, pltpu.roll(v, 96, 1), pltpu.roll(v, 32, 1))


def doc_ends(lengths):
    return lengths[0], lengths[0] + lengths[1]


def doc_start(pos, ends):
    return jnp.where(pos < ends[0], 0, jnp.where(pos < ends[1], ends[0], ends[1]))

def layout(order, inverse):
    @pl.loop(0, 64)
    def _(n):
        inverse[order[n]] = n

    i = lax.axis_index("ctx")
    f = i % 8
    upper = (f == 3) | (f == 5)
    return i // 8, (
        jnp.where(upper, 1, 0),
        jnp.where(upper | (f == 1) | (f == 4), 1, 0),
    )


def key_range(span, ends):
    begin = doc_start(span * 128, ends) // 128
    count = span - begin + 1
    runs = (count + 3) // 8
    return begin, runs, jnp.where(count > runs * 8, 1, 0)


def attend(lengths, order, q, kv):
    def kernel(lengths, order, q_ref, kv_ref, o_ref, lse_ref, s_ref, inverse):
        group, sel = layout(order, inverse)
        ends = doc_ends(lengths)

        @pl.loop(0, 8)
        def _(b):
            span = order[group * 8 + b]
            begin, runs, rest = key_range(span, ends)
            pos = span * 128 + lanes_of((1, 256)) % 128
            low = doc_start(pos, ends)
            rows = pl.ds(pl.multiple_of(b * 128, 128), 128)
            none = jnp.zeros((128, 128), BF)
            pair = jnp.concatenate(
                [
                    jnp.concatenate([q_ref[0, rows, :], none], axis=1),
                    jnp.concatenate([none, q_ref[1, rows, :]], axis=1),
                ],
                axis=0,
            )

            def load(h, t, n):
                return jnp.concatenate(
                    [
                        kv_ref[sel[h], pl.ds(inverse[jnp.minimum(t + i, 63)] * 128, 128), :]
                        for i in range(n)
                    ],
                    axis=0,
                )

            def held(t, n):
                return pl.ds(pl.multiple_of((t - begin) * 128, 512), n * 128)

            def scores(n, t, high):
                kpos = t * 128 + lax.broadcasted_iota(jnp.int32, (n * 128, 1), 0)
                allowed = (kpos >= low) & (kpos <= pos)
                keys = jnp.concatenate([load(0, t, n), load(1, t, n)], axis=1)
                s = jnp.where(allowed, dot_nt(keys, pair), MASKED)
                s_ref[held(t, n), :] = s
                return jnp.maximum(high, jnp.max(s.reshape(n * 16, 8, 256), axis=0))

            def over(step, state):
                state = lax.fori_loop(0, runs, lambda j, v: step(8, begin + j * 8, v), state)
                return lax.fori_loop(0, rest, lambda j, v: step(4, begin + runs * 8, v), state)

            high = over(scores, jnp.full((8, 256), MASKED, F32))
            high = jnp.max(high, axis=0, keepdims=True)

            def weigh(n, t, state):
                total, acc = state
                p = jnp.exp(s_ref[held(t, n), :] - high)
                total = total + jnp.sum(p.reshape(n * 16, 8, 256), axis=0)
                values = jnp.where(lanes_of((n * 128, 128)) < 64, pltpu.roll(load(0, t, n), 64, 1), load(1, t, n))
                return total, acc + dot_tn(values, p.astype(BF))

            total, acc = over(weigh, (jnp.zeros((8, 256), F32), jnp.zeros((128, 256), F32)))
            total = jnp.sum(total, axis=0, keepdims=True)
            lse = high + jnp.log(total)
            lse_ref[b, 0:1, :] = lse[:, 0:128]
            lse_ref[b, 1:2, :] = lse[:, 128:256]
            acc = acc / total
            acc = jnp.concatenate([acc[0:64, 0:128], acc[64:128, 128:256]], axis=0)
            o_ref[rows, :] = acc.T.astype(BF)

    return pl.pallas_call(
        kernel,
        in_specs=[SMEM, SMEM, VMEM, VMEM],
        out_specs=(VMEM, VMEM),
        scratch_shapes=[pltpu.VMEM((40 * 128, 256), F32), pltpu.SMEM((64,), jnp.int32)],
        out_shape=(shaped((1024, 128), BF), shaped((8, 8, 128), F32)),
        compiler_params=pltpu.CompilerParams(vmem_limit_bytes=LIMIT),
        name="attend",
    )(lengths, order, q, kv)


def attend_back(lengths, order, q, kv, d_att, att, lse):
    def kernel(
        lengths, order, q_ref, kv_ref, d_ref, o_ref, lse_ref, dq_ref, dkv_ref, acc_ref, inverse
    ):
        lane = lanes_of((128, 128))
        group, sel = layout(order, inverse)
        ends = doc_ends(lengths)

        @pl.loop(0, 16)
        def _(n):
            for s in (0, 1):
                part = pl.ds(pl.multiple_of(n * 512, 512), 512)
                acc_ref[s, part, :] = jnp.zeros((512, 128), F32)

        @pl.loop(0, 8)
        def _(b):
            span = order[group * 8 + b]
            begin, runs, rest = key_range(span, ends)
            pos = span * 128 + lanes_of((1, 128))
            low = doc_start(pos, ends)
            rows = pl.ds(pl.multiple_of(b * 128, 128), 128)
            d_both = d_ref[rows, :].astype(F32)
            d_pad = (
                jnp.where(lane >= 64, pltpu.roll(d_both, 64, 1), 0.0).astype(BF),
                jnp.where(lane >= 64, d_both, 0.0).astype(BF),
            )
            pair = [jnp.concatenate([q_ref[h, rows, :], d_pad[h]], axis=0) for h in (0, 1)]
            mixed = (d_both * o_ref[rows, :].astype(F32)).T
            delta = [jnp.sum(mixed[64 * h : 64 * h + 64], axis=0, keepdims=True) for h in (0, 1)]
            lses = [lse_ref[b, h : h + 1, :] for h in (0, 1)]

            def step(n, t, state):
                where = [inverse[jnp.minimum(t + i, 63)] * 128 for i in range(n)]
                where = [pl.ds(pl.multiple_of(v, 128), 128) for v in where]
                kpos = t * 128 + lax.broadcasted_iota(jnp.int32, (n * 128, 1), 0)
                allowed = (kpos >= low) & (kpos <= pos)
                d_ss, kvs = [], []
                for h in (0, 1):
                    kv_t = jnp.concatenate([kv_ref[sel[h], w, :] for w in where], axis=0)
                    kvs.append(kv_t)
                    both = dot_nt(kv_t, pair[h])
                    p = jnp.where(allowed, jnp.exp(both[:, 0:128] - lses[h]), 0.0)
                    d_s = (p * (both[:, 128:256] - delta[h])).astype(BF)
                    d_ss.append(d_s)
                    d_kv = dot(jnp.concatenate([d_s, p.astype(BF)], axis=1), pair[h])
                    for i, w in enumerate(where):
                        acc_ref[sel[h], w, :] += d_kv[i * 128 : (i + 1) * 128]
                lanes = lanes_of((n * 128, 128))
                keys = jnp.where(lanes < 64, kvs[0], pltpu.roll(kvs[1], 64, 1))
                return state + dot_tn(keys, jnp.concatenate(d_ss, axis=1))

            state = jnp.zeros((128, 256), F32)
            state = lax.fori_loop(0, runs, lambda j, v: step(8, begin + j * 8, v), state)
            state = lax.fori_loop(0, rest, lambda j, v: step(4, begin + runs * 8, v), state)
            state = jnp.concatenate([state[0:64, 0:128], state[64:128, 128:256]], axis=0)
            dq_ref[rows, :] = state.T * 0.125

        @pl.loop(0, 16)
        def _(n):
            for s in (0, 1):
                part = pl.ds(pl.multiple_of(n * 512, 512), 512)
                dkv_ref[s, part, :] = acc_ref[s, part, :].astype(BF)

    return pl.pallas_call(
        kernel,
        in_specs=[SMEM, SMEM] + [VMEM] * 5,
        out_specs=(VMEM, VMEM),
        scratch_shapes=[pltpu.VMEM((2, 8192, 128), F32), pltpu.SMEM((64,), jnp.int32)],
        out_shape=(shaped((1024, 128), F32), shaped((2, 8192, 128), BF)),
        compiler_params=pltpu.CompilerParams(vmem_limit_bytes=LIMIT),
        name="attend_back",
    )(lengths, order, q, kv, d_att, att, lse)


def hand_out(parts):
    def kernel(*refs):
        n = len(refs) // 2
        for k, (src, dst) in enumerate(zip(refs[:n], refs[n:])):
            if dst.shape == (15,):
                wide = jnp.concatenate([src[...], jnp.zeros((113, 128), F32)], axis=0)
                dst[...] = wide.T[0:1, 0:15].reshape(15)
            else:
                dst[...] = src[...]

    shapes = [(15,) if v.shape == (15, 128) else v.shape for v in parts]
    return pl.pallas_call(
        kernel,
        out_shape=tuple(shaped(s, v.dtype) for s, v in zip(shapes, parts)),
        in_specs=[VMEM] * len(parts),
        out_specs=(VMEM,) * len(parts),
        compiler_params=pltpu.CompilerParams(vmem_limit_bytes=LIMIT),
        name="hand_out",
    )(*parts)


def local(
    hidden, attn_gain, w_q, w_k, w_v, w_o, mlp_gain, w_gate, w_up, w_down, cotangent,
    doc_lengths, span_order,
):
    frequency = ROPE_BASE ** (-2.0 * (np.arange(128) % 32) / HEAD)
    frequency = jnp.asarray(frequency, F32).reshape(1, 128)

    rows, w1, wds, wo, cot, w2own, normed, q, kv, cos_t, sin_t = first(
        hidden.T, cotangent.T, w_q, w_k, w_v, w_o, w_gate, w_up, w_down, attn_gain, mlp_gain,
        doc_lengths, span_order, frequency,
    )
    kv = kv.reshape(2, 8192, 128)
    att, lse = attend(doc_lengths, span_order, q, kv)
    output, d_resid, d_heads, gwo, gw2s, gwds = feed(
        att, w2own, wo, rows.reshape(1024, WIDE), wds.reshape(384, WIDE), cot.reshape(1024, WIDE)
    )
    d_att = d_heads.reshape(1024, 128)
    dq, dkv = attend_back(doc_lengths, span_order, q, kv, d_att, att, lse)
    grads = last(
        dkv.reshape(2, 8, 1024, 128), gwo, dq, cos_t, sin_t, w1.reshape(WIDE, 256), normed, rows,
        d_resid, gw2s, gwds, attn_gain, mlp_gain, w_q, w_k, w_v, w_gate, w_up,
    )
    output, grad_hidden, g_attn, g_mlp, g_q, g_k, g_v, g_o, g_gate, g_up, g_down = hand_out(
        (output,) + tuple(grads)
    )
    return (
        output.T, grad_hidden.T, g_attn, g_q, g_k, g_v, g_o, g_mlp, g_gate, g_up, g_down
    )


def solution(mesh):
    both = ("fsdp", "ctx")
    wide, thin, part = P(both, None), P(both), P("fsdp")
    return jax.shard_map(
        local,
        mesh=mesh,
        in_specs=(wide, thin, wide, wide, wide, wide, thin, wide, wide, wide, wide, part, part),
        out_specs=(wide, wide, thin, wide, wide, wide, wide, thin, wide, wide, wide),
        check_vma=False,
    )
```

```python
import jax
import jax.numpy as jnp
import numpy as np
from jax import lax
from jax.experimental import pallas as pl
from jax.experimental.pallas import tpu as pltpu
from jax.sharding import PartitionSpec as P

HEAD = 64
EPSILON = 1e-05
ROPE_BASE = 100000.0
MASKED = -1e30
WIDE = 1024
WIDTH = 960
BF = jnp.bfloat16
F32 = jnp.float32
MESH = pl.DeviceIdType.MESH
DMA = pltpu.SemaphoreType.DMA
ANY = pl.BlockSpec(memory_space=pl.ANY)
VMEM = pl.BlockSpec(memory_space=pltpu.VMEM)
SMEM = pl.BlockSpec(memory_space=pltpu.SMEM)
LIMIT = 56 * 2**20
OWNED_KV = (0, 1, 1, 2, 2, 3, 4, 4)


def dot(a, b):
    return lax.dot_general(a, b, (((1,), (0,)), ((), ())), preferred_element_type=F32)


def dot_nt(a, b):
    return lax.dot_general(a, b, (((1,), (1,)), ((), ())), preferred_element_type=F32)


def dot_tn(a, b):
    return lax.dot_general(a, b, (((0,), (0,)), ((), ())), preferred_element_type=F32)


def shaped(shape, dtype):
    return jax.ShapeDtypeStruct(shape, dtype)


def place():
    i = lax.axis_index("ctx")
    return i // 16, (i // 8) % 2, (i // 2) % 4, i % 2


def at(x, z, y, c):
    return {"ctx": (((x + 4) % 4) * 2 + z) * 8 + ((y + 4) % 4) * 2 + c}


def send(src, dst, ssem, rsem, device):
    copy = pltpu.make_async_remote_copy(
        src, dst, ssem, rsem, device_id=device, device_id_type=MESH
    )
    copy.start()
    return copy


def hail(kinds):
    x, z, y, c = place()
    who = []
    if "x" in kinds:
        who += [at(x + 1, z, y, c), at(x - 1, z, y, c), at(x, 1 - z, y, c)]
    if "f" in kinds:
        who += [at(x, z, y + d, (c + e) % 2) for d in range(4) for e in range(2) if d + e]
    elif "y" in kinds:
        who += [at(x, z, y + d, c) for d in (1, 2, 3)] + [at(x, z, y, 1 - c)]
    barrier = pltpu.get_barrier_semaphore()
    for device in who:
        pl.semaphore_signal(barrier, inc=1, device_id=device, device_id_type=MESH)
    return len(who)


def greet(kinds):
    pl.semaphore_wait(pltpu.get_barrier_semaphore(), hail(kinds))


def half_lead(ref, k):
    n = ref.shape[0] // 2
    return ref.at[pl.ds(k * n, n)]


def half_lanes(ref, k):
    n = ref.shape[-1] // 2
    return ref.at[:, pl.ds(k * n, n)]


class RingGather:
    sems = [DMA((9,)), DMA((9,)), DMA(())]

    def __init__(self, src, dst, half, ssem, rsem, lsem, arrived=None):
        self.src, self.dst, self.half = src, dst, half
        self.ssem, self.rsem, self.lsem = ssem, rsem, lsem
        self.arrived = arrived or (lambda block: None)
        self.copies = {}

    def push(self, n, src, dst, device):
        self.copies[n] = send(src, dst, self.ssem.at[n], self.rsem.at[n], device)

    def start(self):
        x, z, y, c = place()
        me = self.dst.at[x * 2 + z]
        self.push(0, self.src, me, at(x, 1 - z, y, c))
        self.push(1, self.src, me, at(x + 1, z, y, c))
        self.push(2, self.src, me, at(x - 1, z, y, c))
        self.local = pltpu.make_async_copy(self.src, me, self.lsem)
        self.local.start()

    def relay_z(self):
        x, z, y, c = place()
        block = self.dst.at[x * 2 + 1 - z]
        self.copies[0].wait_recv()
        self.push(3, block, block, at(x + 1, z, y, c))
        self.push(4, block, block, at(x - 1, z, y, c))
        self.arrived(x * 2 + 1 - z)

    def relay_x(self, k):
        x, z, y, c = place()
        zz = z if k == 0 else 1 - z
        left, right = ((x + 3) % 4) * 2 + zz, ((x + 1) % 4) * 2 + zz
        self.copies[1 + 2 * k].wait_recv()
        part = self.half(self.dst.at[left], 0)
        self.push(5 + 2 * k, part, part, at(x + 1, z, y, c))
        self.arrived(left)
        self.copies[2 + 2 * k].wait_recv()
        part = self.half(self.dst.at[right], 1)
        self.push(6 + 2 * k, part, part, at(x - 1, z, y, c))
        self.arrived(right)

    def land(self, k):
        x, z, y, c = place()
        zz = z if k == 0 else 1 - z
        self.copies[5 + 2 * k].wait_recv()
        self.copies[6 + 2 * k].wait_recv()
        self.arrived(((x + 2) % 4) * 2 + zz)

    def sent(self):
        for n in range(9):
            self.copies[n].wait_send()

    def finish(self):
        self.local.wait()
        self.sent()


class CrossGather:
    sems = [DMA((8,)), DMA((8,)), DMA(())]

    def __init__(self, src, dst, half, ssem, rsem, lsem, arrived=None):
        self.src, self.dst, self.half = src, dst, half
        self.ssem, self.rsem, self.lsem = ssem, rsem, lsem
        self.arrived = arrived or (lambda block: None)
        self.copies = {}

    def push(self, n, src, dst, device):
        self.copies[n] = send(src, dst, self.ssem.at[n], self.rsem.at[n], device)

    def start(self):
        x, z, y, c = place()
        me = self.dst.at[x * 2 + z]
        self.push(1, self.src, me, at(x + 1, z, y, c))
        self.push(2, self.src, me, at(x - 1, z, y, c))
        self.push(0, self.src, me, at(x, 1 - z, y, c))
        self.local = pltpu.make_async_copy(self.src, me, self.lsem)
        self.local.start()

    def relay(self):
        x, z, y, c = place()
        for n, step, side in ((1, 3, 0), (2, 1, 1)):
            block = ((x + step) % 4) * 2 + z
            whole = self.dst.at[block]
            self.copies[n].wait_recv()
            part = self.half(whole, side)
            self.push(2 + n, part, part, at(x + 4 - step, z, y, c))
            self.push(4 + n, whole, whole, at(x, 1 - z, y, c))
            self.arrived(block)

    def far(self):
        x, z, y, c = place()
        block = ((x + 2) % 4) * 2 + z
        whole = self.dst.at[block]
        self.copies[3].wait_recv()
        self.copies[4].wait_recv()
        self.push(7, whole, whole, at(x, 1 - z, y, c))
        self.arrived(block)

    def land(self):
        x, z, y, c = place()
        for n, step in ((0, 0), (5, 3), (6, 1), (7, 2)):
            self.copies[n].wait_recv()
            self.arrived(((x + step) % 4) * 2 + 1 - z)

    def finish(self):
        self.local.wait()
        for n in range(8):
            self.copies[n].wait_send()


class RowGather:
    sems = [DMA((8,)), DMA((8,)), DMA(())]

    def __init__(self, src, dst, ssem, rsem, lsem):
        self.src, self.dst = src, dst
        self.ssem, self.rsem, self.lsem = ssem, rsem, lsem
        self.copies = {}

    def push(self, n, src, dst, device):
        self.copies[n] = send(src, dst, self.ssem.at[n], self.rsem.at[n], device)

    def start(self):
        x, z, y, c = place()
        me = self.dst.at[y * 2 + c]
        self.push(1, self.src, me, at(x, z, y + 1, c))
        self.push(2, self.src, me, at(x, z, y - 1, c))
        self.push(0, self.src, me, at(x, z, y, 1 - c))
        self.local = pltpu.make_async_copy(self.src, me, self.lsem)
        self.local.start()

    def relay(self):
        x, z, y, c = place()
        for n, step, side in ((1, 3, 0), (2, 1, 1)):
            self.copies[n].wait_recv()
            block = self.dst.at[((y + step) % 4) * 2 + c]
            part = half_lead(block, side)
            self.push(2 + n, part, part, at(x, z, y + 4 - step, c))
            self.push(4 + n, block, block, at(x, z, y, 1 - c))

    def land(self):
        x, z, y, c = place()
        self.copies[3].wait_recv()
        self.copies[4].wait_recv()
        block = self.dst.at[((y + 2) % 4) * 2 + c]
        self.push(7, block, block, at(x, z, y, 1 - c))

    def finish(self):
        self.local.wait()
        for n in (0, 5, 6, 7):
            self.copies[n].wait_recv()
        for n in range(8):
            self.copies[n].wait_send()


class Swap:
    sems = [DMA((8,)), DMA((8,)), DMA(())]

    def __init__(self, src, dst, ssem, rsem, lsem):
        self.src, self.dst = src, dst
        self.ssem, self.rsem, self.lsem = ssem, rsem, lsem

    def start(self):
        x, z, y, c = place()
        me = y * 2 + c
        self.copies = []
        for d in (2, 1, 3, 0):
            for e in (0, 1):
                if d + e:
                    n = d * 2 + e
                    to = ((y + d) % 4) * 2 + (c + e) % 2
                    self.copies.append(
                        send(
                            self.src.at[to],
                            self.dst.at[me],
                            self.ssem.at[n],
                            self.rsem.at[n],
                            at(x, z, y + d, (c + e) % 2),
                        )
                    )
        self.local = pltpu.make_async_copy(self.src.at[me], self.dst.at[me], self.lsem)
        self.local.start()

    def finish(self):
        self.local.wait()
        for copy in self.copies:
            copy.wait()


class RowSum:
    @staticmethod
    def scratch(shape):
        return [
            pltpu.VMEM((4,) + shape, BF),
            pltpu.VMEM((4,) + shape, BF),
            pltpu.VMEM((2, shape[0] // 2) + shape[1:], BF),
            pltpu.VMEM((2,) + shape, BF),
            DMA((8,)),
            DMA((8,)),
        ]

    def __init__(self, blk, first, mixed, parts, heard, ssem, rsem):
        self.blk, self.first, self.mixed = blk, first, mixed
        self.parts, self.heard = parts, heard
        self.ssem, self.rsem = ssem, rsem
        self.copies = {}

    def push(self, n, src, dst, device):
        self.copies[n] = send(src, dst, self.ssem.at[n], self.rsem.at[n], device)

    def hand(self, d):
        x, z, y, c = place()
        to = ((y + d) % 4) * 2 + 1 - c
        self.push(d, self.blk.at[to], self.first.at[d], at(x, z, y, 1 - c))

    def start(self):
        for d in (2, 1, 3, 0):
            self.hand(d)

    def both(self, d):
        x, z, y, c = place()
        self.copies[d].wait_recv()
        return self.blk[((y + d) % 4) * 2 + c].astype(F32) + self.first[d].astype(F32)

    def far(self):
        x, z, y, c = place()
        self.mixed[2] = self.both(2).astype(BF)
        for side, step in ((0, 1), (1, 3)):
            part = half_lead(self.mixed.at[2], side)
            self.push(4 + side, part, self.parts.at[side], at(x, z, y + step, c))

    def near(self):
        x, z, y, c = place()
        for side, step in ((0, 1), (1, 3)):
            sums = self.both(step)
            n = sums.shape[0] // 2
            self.copies[4 + side].wait_recv()
            part = self.parts[side].astype(F32)
            self.mixed[step, pl.ds(side * n, n)] = (sums[side * n : side * n + n] + part).astype(BF)
            self.mixed[step, pl.ds(n - side * n, n)] = sums[n - side * n : 2 * n - side * n].astype(BF)
            self.push(6 + side, self.mixed.at[step], self.heard.at[side], at(x, z, y + step, c))

    def total(self):
        total = self.both(0)
        for side in (0, 1):
            self.copies[6 + side].wait_recv()
            total = total + self.heard[side].astype(F32)
        return total

    def finish(self):
        for n in range(8):
            self.copies[n].wait_send()


class CrossSum:
    @staticmethod
    def scratch(shape, lanes):
        if lanes:
            part = shape[:-1] + (shape[-1] // 2,)
        else:
            part = (shape[0] // 2,) + shape[1:]
        return [
            pltpu.VMEM((4,) + shape, BF),
            pltpu.VMEM((4,) + shape, BF),
            pltpu.VMEM((2,) + part, BF),
            pltpu.VMEM((2,) + shape, BF),
            DMA((8,)),
            DMA((8,)),
        ]

    def __init__(self, blk, lanes, first, mixed, parts, heard, ssem, rsem):
        self.blk, self.half = blk, half_lanes if lanes else half_lead
        self.first, self.mixed, self.parts, self.heard = first, mixed, parts, heard
        self.ssem, self.rsem = ssem, rsem
        self.copies = {}

    def push(self, n, src, dst, device):
        self.copies[n] = send(src, dst, self.ssem.at[n], self.rsem.at[n], device)

    def hand(self, d):
        x, z, y, c = place()
        to = ((x + d) % 4) * 2 + 1 - z
        self.push(d, self.blk.at[to], self.first.at[d], at(x, 1 - z, y, c))

    def both(self, d):
        x, z, y, c = place()
        self.copies[d].wait_recv()
        return self.blk[((x + d) % 4) * 2 + z].astype(F32) + self.first[d].astype(F32)

    def far(self):
        x, z, y, c = place()
        self.mixed[2] = self.both(2).astype(BF)
        for side, step in ((0, 1), (1, 3)):
            part = self.half(self.mixed.at[2], side)
            self.push(4 + side, part, self.parts.at[side], at(x + step, z, y, c))

    def near(self):
        x, z, y, c = place()
        for side, step in ((0, 1), (1, 3)):
            mixed = self.mixed.at[step]
            mixed[...] = self.both(step).astype(BF)
            self.copies[4 + side].wait_recv()
            mine = self.half(mixed, side)
            mine[...] = (mine[...].astype(F32) + self.parts[side].astype(F32)).astype(BF)
            self.push(6 + side, mixed, self.heard.at[side], at(x + step, z, y, c))

    def total(self):
        total = self.both(0)
        for side in (0, 1):
            self.copies[6 + side].wait_recv()
            total = total + self.heard[side].astype(F32)
        return total

    def finish(self):
        for n in range(8):
            self.copies[n].wait_send()


class RingSum:
    @staticmethod
    def scratch(shape, lanes):
        if lanes:
            part = shape[:-1] + (shape[-1] // 2,)
        else:
            part = (shape[0] // 2,) + shape[1:]
        return [
            pltpu.VMEM((4,) + part, BF),
            pltpu.VMEM((4,) + shape, BF),
            pltpu.VMEM((4,) + shape, BF),
            pltpu.VMEM((2,) + shape, BF),
            DMA((9,)),
            DMA((9,)),
        ]

    def __init__(self, blk, lanes, parts, mixed, heard, across, ssem, rsem):
        self.blk, self.half = blk, half_lanes if lanes else half_lead
        self.parts, self.mixed, self.heard, self.across = parts, mixed, heard, across
        self.ssem, self.rsem = ssem, rsem
        self.copies = {}

    def push(self, n, src, dst, device):
        self.copies[n] = send(src, dst, self.ssem.at[n], self.rsem.at[n], device)

    def start(self, k):
        x, z, y, c = place()
        zz = 1 - z if k == 0 else z
        far = self.blk.at[((x + 2) % 4) * 2 + zz]
        self.push(4 * k, self.half(far, 0), self.parts.at[2 * k], at(x + 1, z, y, c))
        self.push(4 * k + 1, self.half(far, 1), self.parts.at[2 * k + 1], at(x - 1, z, y, c))

    def relay(self, k):
        x, z, y, c = place()
        zz = 1 - z if k == 0 else z
        for side, step in ((0, 1), (1, 3)):
            n = 2 * k + side
            mixed = self.mixed.at[n]
            source = self.blk.at[((x + step) % 4) * 2 + zz]
            mine, other = self.half(source, side), self.half(source, 1 - side)
            self.half(mixed, 1 - side)[...] = other[...]
            self.copies[4 * k + side].wait_recv()
            self.half(mixed, side)[...] = (
                mine[...].astype(F32) + self.parts[n].astype(F32)
            ).astype(BF)
            self.push(4 * k + 2 + side, mixed, self.heard.at[n], at(x + step, z, y, c))

    def total(self, k):
        x, z, y, c = place()
        zz = 1 - z if k == 0 else z
        total = self.blk[x * 2 + zz].astype(F32)
        for side in (0, 1):
            self.copies[4 * k + 2 + side].wait_recv()
            total = total + self.heard[2 * k + side].astype(F32)
        if k == 0:
            self.across[0] = total.astype(BF)
            self.push(8, self.across.at[0], self.across.at[1], at(x, 1 - z, y, c))
            return None
        self.copies[8].wait_recv()
        return total + self.across[1].astype(F32)

    def finish(self):
        for n in range(9):
            self.copies[n].wait_send()


def fetch(src, dst, sem):
    copy = pltpu.make_async_copy(src, dst, sem)
    copy.start()
    return copy


def columns_of_gains(gain1, gain2):
    gap = jnp.zeros((1, 113), F32)
    return jnp.concatenate(
        [
            jnp.concatenate([ref[...].astype(F32).reshape(1, 15), gap], axis=1)
            for ref in (gain1, gain2)
        ]
        + [jnp.zeros((126, 128), F32)],
        axis=0,
    ).T[0:15]


def comm_call(name, number, kernel, out_shape, in_specs, out_specs, scratch, args):
    return pl.pallas_call(
        kernel,
        out_shape=out_shape,
        in_specs=in_specs,
        out_specs=out_specs,
        scratch_shapes=scratch,
        compiler_params=pltpu.CompilerParams(
            collective_id=number, has_side_effects=True, vmem_limit_bytes=LIMIT
        ),
        name=name,
    )(*args)


def split(refs, counts):
    parts, begin = [], 0
    for n in counts:
        parts.append(refs[begin : begin + n])
        begin += n
    return parts


def spread_value(rows):
    j = lax.broadcasted_iota(jnp.int32, (rows, WIDE), 0)
    k = lax.broadcasted_iota(jnp.int32, (rows, WIDE), 1)
    hit = ((k // 16) * 15 + k % 16 == j) & (k % 16 < 15)
    return jnp.where(hit, 1.0, 0.0).astype(BF)


def first(
    hidden_t, cot_t, w_q, w_k, w_v, w_o, w_gate, w_up, w_down, gain1, gain2, lengths, span_order, freq
):
    def kernel(
        hidden_t, cot_t, w_q, w_k, w_v, w_o, w_gate, w_up, w_down, gain1, gain2, lengths, order, freq,
        rows_out, w1_out, wds, wo, cot, w2own, normed_out, q_out, kv2, cos_out, sin_out,
        rows, w1, normed, q_rot, cos_t, sin_t, xp, cp, wp1, wp2, wop, wdp, wos, w1own, kv, outs,
        *sems,
    ):
        a, b, d, e, e2, ac, ao, b2, k0, k1, (hs, hr) = split(sems, (3,) * 10 + (2,))
        x, z, y, c = place()
        partners = hail("xf")

        gains = columns_of_gains(gain1, gain2)
        q = jnp.concatenate([w_q[...].astype(F32), jnp.zeros((15, 64), F32)], axis=1)
        q, k, v = (w * gains[:, 0:1] for w in (q, w_k[...].astype(F32), w_v[...].astype(F32)))
        wp1[...] = jnp.zeros(wp1.shape, BF)
        for f in range(8):
            n = OWNED_KV[f] * 64
            wp1[f, 0:15, 0:128] = q[:, 128 * f : 128 * f + 128].astype(BF)
            wp1[f, 0:15, 128:256] = jnp.concatenate(
                [k[:, n : n + 64], v[:, n : n + 64]], axis=1
            ).astype(BF)
        spread = spread_value(WIDTH)
        xp[...] = dot_tn(hidden_t[...], spread).astype(BF)

        wop[...] = jnp.zeros(wop.shape, BF)
        wop[0:15, :] = dot(w_o[...], spread).astype(BF)
        wdp[...] = jnp.zeros(wdp.shape, BF)
        wdp[0:40, :] = dot(w_down[...], spread).astype(BF)

        pl.semaphore_wait(pltpu.get_barrier_semaphore(), partners)
        swap = Swap(wp1, w1own, *b)
        swap.start()
        gather = RowGather(xp, rows, *a)
        gather.start()
        early = [RingGather(wdp, wds, half_lanes, *e2), RingGather(wop, wos, half_lanes, *e)]
        ring_d, ring_o = early
        for ring in early:
            ring.start()
        cp[...] = dot_tn(cot_t[...], spread).astype(BF)
        for ring in early:
            ring.relay_z()
        swap.finish()
        ring_1 = RingGather(w1own, w1, half_lead, *d)
        ring_1.start()
        for k in (0, 1):
            for ring in early:
                ring.relay_x(k)
        gather.relay()
        gather_c = RowGather(cp, cot, *ac)
        gather_c.start()
        ring_1.relay_z()

        wp2[...] = jnp.zeros(wp2.shape, BF)
        gap = jnp.zeros((15, 8), F32)
        for m, ref in ((0, w_gate), (384, w_up)):
            w = ref[...].astype(F32) * gains[:, 1:2]
            for f in range(8):
                parts = []
                for g in range(8):
                    n = (8 * g + f) * 40
                    parts += [w[:, n : n + 40], gap]
                wp2[f, 0:15, m : m + 384] = jnp.concatenate(parts, axis=1).astype(BF)
        ring_1.relay_x(0)
        ring_1.relay_x(1)

        lane = lanes_of((1, 128))
        sign = jnp.where(lane % 64 < 32, -1.0, 1.0)
        ends = doc_ends(lengths)

        @pl.loop(0, 8)
        def _(n):
            pos = order[(x * 2 + z) * 8 + n] * 128
            pos = pos + lax.broadcasted_iota(jnp.int32, (128, 1), 0)
            angle = (pos - doc_start(pos, ends)).astype(F32) * freq[...]
            part = pl.ds(pl.multiple_of(n * 128, 128), 128)
            cos_t[part, :] = jnp.cos(angle)
            sin_t[part, :] = sign * jnp.sin(angle)

        written = [fetch(cos_t, cos_out, outs.at[0]), fetch(sin_t, sin_out, outs.at[1])]
        gather.land()
        for k in (0, 1):
            for ring in early + [ring_1]:
                ring.land(k)
        gather.finish()
        ring_o.local.wait()
        gather_o = RowGather(wos, wo, *ao)
        gather_o.start()
        swap2 = Swap(wp2, w2own, *b2)
        swap2.start()
        ring_1.local.wait()
        written += [fetch(rows, rows_out, outs.at[2]), fetch(w1, w1_out, outs.at[3])]

        w = w1.reshape(WIDE, 256)
        lane = lanes_of((256, 128))

        def project(n):
            part = pl.ds(n * 256, 256)
            xs = jnp.concatenate([rows[2 * n], rows[2 * n + 1]], axis=0).astype(F32)
            v = (xs * inverse_rms(xs)).astype(BF)
            normed[part, :] = v
            out = dot(v, w[...])
            cos_v, sin_v = cos_t[part, :], sin_t[part, :]
            qs, ks = out[:, 0:128], out[:, 128:256]
            qs = (qs * cos_v + partner(qs) * sin_v).astype(BF).astype(F32) * 0.125
            kv[part, :] = jnp.where(lane < 64, ks * cos_v + partner(ks) * sin_v, ks).astype(BF)
            q_rot[0, part, :] = jnp.where(lane < 64, qs, 0.0).astype(BF)
            q_rot[1, part, :] = jnp.where(lane < 64, pltpu.roll(qs, 64, 1), 0.0).astype(BF)

        hand = []

        def pass_on(piece):
            n = len(hand)
            hand.append(send(piece, piece, hs.at[n], hr.at[n], at(x, z, y, 1 - c)))

        key_rings = []
        for h, (kind, own) in enumerate(((RingGather, k0), (CrossGather, k1))):
            mine = kv.at[pl.ds(512 * h, 512)]
            spot = pl.ds(512 * h, 512)
            ring = kind(
                mine,
                kv2.at[c, :, spot],
                half_lead,
                *own,
                arrived=lambda block, spot=spot: pass_on(kv2.at[c, block, spot]),
            )
            project(2 * h)
            project(2 * h + 1)
            ring.start()
            n = len(hand)
            hand.append(
                send(
                    mine, kv2.at[c, x * 2 + z, spot], hs.at[n], hr.at[n], at(x, z, y, 1 - c)
                )
            )
            key_rings.append(ring)
            if h == 0:
                gather_c.relay()

        written += [fetch(normed, normed_out, outs.at[4]), fetch(q_rot, q_out, outs.at[5])]
        ring_a, ring_b = key_rings
        ring_a.relay_z()
        gather_o.relay()
        ring_b.relay()
        ring_a.relay_x(0)
        gather_c.land()
        ring_a.relay_x(1)
        ring_b.far()
        gather_o.land()
        ring_a.land(0)
        ring_a.land(1)
        ring_b.land()
        for copy in hand:
            copy.wait()
        swap2.finish()
        gather_o.finish()
        gather_c.finish()
        for ring in [ring_d] + key_rings:
            ring.finish()
        for ring in (ring_1, ring_o):
            ring.sent()
        for copy in written:
            copy.wait()

    return comm_call(
        "first",
        1,
        kernel,
        (
            shaped((8, 128, WIDE), BF),
            shaped((8, 8, 16, 256), BF),
            shaped((8, 48, WIDE), BF),
            shaped((8, 8, 16, WIDE), BF),
            shaped((8, 128, WIDE), BF),
            shaped((8, 16, 768), BF),
            shaped((1024, WIDE), BF),
            shaped((2, 1024, 128), BF),
            shaped((2, 8, 1024, 128), BF),
            shaped((1024, 128), F32),
            shaped((1024, 128), F32),
        ),
        [VMEM] * 11 + [SMEM, SMEM, VMEM],
        (ANY,) * 11,
        [
            pltpu.VMEM((8, 128, WIDE), BF),
            pltpu.VMEM((8, 8, 16, 256), BF),
            pltpu.VMEM((1024, WIDE), BF),
            pltpu.VMEM((2, 1024, 128), BF),
            pltpu.VMEM((1024, 128), F32),
            pltpu.VMEM((1024, 128), F32),
            pltpu.VMEM((128, WIDE), BF),
            pltpu.VMEM((128, WIDE), BF),
            pltpu.VMEM((8, 16, 256), BF),
            pltpu.VMEM((8, 16, 768), BF),
            pltpu.VMEM((16, WIDE), BF),
            pltpu.VMEM((48, WIDE), BF),
            pltpu.VMEM((8, 16, WIDE), BF),
            pltpu.VMEM((8, 16, 256), BF),
            pltpu.VMEM((1024, 128), BF),
            DMA((6,)),
        ]
        + RowGather.sems
        + Swap.sems
        + RingGather.sems * 3
        + RowGather.sems * 2
        + Swap.sems
        + RingGather.sems
        + CrossGather.sems
        + [DMA((16,)), DMA((16,))],
        (
            hidden_t, cot_t, w_q, w_k, w_v, w_o, w_gate, w_up, w_down, gain1, gain2, lengths,
            span_order, freq,
        ),
    )


def inverse_rms(v):
    return lax.rsqrt(jnp.sum(v * v, axis=1, keepdims=True) * (1.0 / WIDTH) + EPSILON)


def feed(att, w2own, wo, rows, wd, cot):
    def kernel(
        att, w2own, wo_in, rows_in, wd_in, cot_in,
        outp_out, resid_out, d_resid, d_heads, gwo_out, gw2_sum, gwd_sum,
        wo, x_in, wd, cot, ins, atts, w2, packed, d_act, resid, normed, act, d_both, dmn, outp,
        gw2, gwd, da, gwo, *refs,
    ):
        a, b, s, r1, t1, t2 = split(refs, (3, 3, 3, 6, 6, 6))
        x, z, y, c = place()
        me = y * 2 + c
        partners = hail("xf")
        pairs = ((wo_in, wo), (cot_in, cot), (wd_in, wd), (rows_in, x_in))
        held = [fetch(src, dst, ins.at[n]) for n, (src, dst) in enumerate(pairs)]
        pl.semaphore_wait(pltpu.get_barrier_semaphore(), partners)
        gather = RowGather(att, atts, *a)
        ring = RingGather(w2own, w2, half_lead, *b)
        gather.start()
        ring.start()

        def place_rows(n, size):
            return pl.ds(pl.multiple_of(n * size, size), size)

        held[0].wait()
        whole = jnp.concatenate([wo[f, g] for g in range(8) for f in range(8)], axis=0)

        def pack(n):
            j = lax.broadcasted_iota(jnp.int32, (512, WIDE), 0) + n * 512
            k = lax.broadcasted_iota(jnp.int32, (512, WIDE), 1)
            hit = ((k // 16) * 15 + k % 16 == j) & (k % 16 < 15)
            packed[pl.ds(n * 512, 512), :] = dot(
                jnp.where(hit, 1.0, 0.0).astype(BF), whole
            ).astype(BF)

        pack(0)
        ring.relay_z()
        gather.relay()
        pack(1)
        ring.relay_x(0)
        held[1].wait()
        held[2].wait()

        @pl.loop(0, 2)
        def _(n):
            part = place_rows(n, 512)
            d_act[part, :] = dot_nt(cot[part, :], wd[...])

        ring.relay_x(1)
        held[3].wait()
        gather.land()
        gather.finish()

        @pl.loop(0, 2)
        def _(n):
            part = place_rows(n, 512)
            heads = jnp.concatenate([atts[f, part, :] for f in range(8)], axis=1)
            v = x_in[part, :].astype(F32) + dot(heads, packed[...])
            resid[part, :] = v
            normed[part, :] = (v * inverse_rms(v)).astype(BF)

        ring.land(0)
        ring.land(1)
        ring.finish()
        w2_all = w2.reshape(WIDE, 768)

        @pl.loop(0, 2)
        def _(n):
            part = place_rows(n, 512)
            both = dot(normed[part, :], w2_all[...])
            gate, up = both[:, 0:384], both[:, 384:768]
            sigma = 1.0 / (1.0 + jnp.exp(-gate))
            silu = gate * sigma
            act[part, :] = (silu * up).astype(BF)
            d = d_act[part, :]
            d_both[part, 0:384] = (d * up * sigma * (1.0 + gate * (1.0 - sigma))).astype(BF)
            d_both[part, 384:768] = (d * silu).astype(BF)

        sum_n = RowSum(dmn, *r1)
        ring_2, ring_d = RingSum(gw2, False, *t1), CrossSum(gwd, True, *t2)

        def back(core):
            to = [((y + n) % 4) * 2 + core for n in (2, 1, 3, 0)]
            v = jnp.concatenate([d_both[place_rows(n, 128), :] for n in to], axis=0)
            v = dot_nt(v, w2_all[...]).astype(BF)
            for n in range(4):
                dmn[to[n]] = v[128 * n : 128 * n + 128]

        order = [(2, 1), (2, 0), (1, 1), (3, 1), (1, 0), (3, 0), (0, 1), (0, 0)]
        where = [((x + p) % 4) * 2 + (1 - z if q else z) for p, q in order]

        def weights(which):
            v = jnp.concatenate([normed[:, place_rows(where[n], 128)] for n in which], axis=1)
            v = dot_tn(v, d_both[...]).astype(BF)
            for n, m in enumerate(which):
                gw2[where[m]] = v[128 * n : 128 * n + 128].reshape(8, 16, 768)

        weights((0, 1))
        ring_2.start(0)
        ring_2.start(1)
        back(1 - c)
        for d in (2, 1, 3, 0):
            sum_n.hand(d)
        gwd[...] = dot_tn(act[...], cot[...]).astype(BF).reshape(8, 48, WIDE)
        for d in (2, 1, 3, 0):
            ring_d.hand(d)
        back(c)
        sum_n.far()
        weights((2, 3, 4, 5, 6, 7))
        sum_n.near()
        ring_2.relay(0)
        ring_d.far()

        @pl.loop(0, 2)
        def _(n):
            v = dot(act[place_rows(n, 512), :], wd[...]).astype(BF)
            for k in range(4):
                outp[n * 4 + k] = v[128 * k : 128 * k + 128]

        written = [fetch(outp, outp_out, ins.at[5])]
        ring_2.relay(1)
        ring_d.near()

        mine = place_rows(me, 128)
        v = resid[mine, :]
        inv = inverse_rms(v)
        e = sum_n.total()
        mean = jnp.sum(e * v, axis=1, keepdims=True) * (1.0 / WIDTH)
        d_v = cot[mine, :].astype(F32) + inv * e - v * (inv * inv * inv * mean)
        d_resid[...] = d_v
        mixed = d_v.astype(BF)
        d_att = dot_nt(mixed, packed[...]).astype(BF)
        for f in range(8):
            da[f] = d_att[:, f * 128 : (f + 1) * 128]
        swap = Swap(da, d_heads, *s)
        swap.start()
        spread = spread_value(WIDE)
        heads = jnp.concatenate([atts[f, mine, :] for f in range(8)], axis=1)
        gw = dot_tn(dot(heads, spread).astype(BF), mixed).astype(BF)
        for g in range(8):
            for f in range(8):
                n = (8 * g + f) * 16
                gwo[f, g * 16 : (g + 1) * 16, :] = gw[n : n + 16]
        written += [fetch(gwo, gwo_out, ins.at[4])]
        ring_2.total(0)
        resid_out[...] = v
        gw2_sum[...] = ring_2.total(1).astype(BF)
        gwd_sum[...] = ring_d.total()
        swap.finish()
        sum_n.finish()
        ring_2.finish()
        ring_d.finish()
        for copy in written:
            copy.wait()

    return comm_call(
        "feed",
        3,
        kernel,
        (
            shaped((8, 128, WIDE), BF),
            shaped((128, WIDE), F32),
            shaped((128, WIDE), F32),
            shaped((8, 128, 128), BF),
            shaped((8, 128, WIDE), BF),
            shaped((8, 16, 768), BF),
            shaped((48, WIDE), F32),
        ),
        [ANY] * 6,
        (ANY, VMEM, VMEM, ANY, ANY, VMEM, VMEM),
        [
            pltpu.VMEM((8, 8, 16, WIDE), BF),
            pltpu.VMEM((1024, WIDE), BF),
            pltpu.VMEM((384, WIDE), BF),
            pltpu.VMEM((1024, WIDE), BF),
            DMA((6,)),
            pltpu.VMEM((8, 1024, 128), BF),
            pltpu.VMEM((8, 8, 16, 768), BF),
            pltpu.VMEM((WIDE, WIDE), BF),
            pltpu.VMEM((1024, 384), F32),
            pltpu.VMEM((1024, WIDE), F32),
            pltpu.VMEM((1024, WIDE), BF),
            pltpu.VMEM((1024, 384), BF),
            pltpu.VMEM((1024, 768), BF),
            pltpu.VMEM((8, 128, WIDE), BF),
            pltpu.VMEM((8, 128, WIDE), BF),
            pltpu.VMEM((8, 8, 16, 768), BF),
            pltpu.VMEM((8, 48, WIDE), BF),
            pltpu.VMEM((8, 128, 128), BF),
            pltpu.VMEM((8, 128, WIDE), BF),
        ]
        + RowGather.sems
        + RingGather.sems
        + Swap.sems
        + RowSum.scratch((128, WIDE))
        + RingSum.scratch((8, 16, 768), False)
        + CrossSum.scratch((48, WIDE), True),
        (att, w2own, wo, rows, wd, cot),
    )


def last(
    dkv, gwo, outp, dq, cos_t, sin_t, w1, normed, rows, resid, d_resid, gw2s, gwd, gain1, gain2,
    w_q, w_k, w_v, w_gate, w_up,
):
    def kernel(
        dkv, gwo_in, outp_in, dq_in, cos_in, sin_in, w1_in, normed_in, rows_in, resid, dr, gw2s, wd,
        gain1, gain2,
        w_q, w_k, w_v, w_gate, w_up,
        output, gh, g_attn, g_mlp, g_q, g_k, g_v, g_o, g_gate, g_up, g_down,
        own, gwo, outp, dq, cos_t, sin_t, w1, normed, rows, ins,
        blk_a, blk_b, from_core, gwos, gw1, dnq, d_kv, dn, one, two, gw1s, hs, hr, *refs,
    ):
        a, a2, b, b2, d, e, e2, s1, s2 = split(refs, (6, 6, 6, 6, 6, 6, 6, 3, 3))
        x, z, y, c = place()
        me = y * 2 + c
        partners = hail("xf")
        pairs = [
            (gwo_in, gwo),
            (dkv.at[c], own),
            (dq_in, dq),
            (cos_in, cos_t),
            (sin_in, sin_t),
            (w1_in, w1),
            (normed_in, normed),
            (rows_in.at[me], rows),
            (outp_in, outp),
        ]
        held = [fetch(src, dst, ins.at[n]) for n, (src, dst) in enumerate(pairs)]
        pl.semaphore_wait(pltpu.get_barrier_semaphore(), partners)
        order = [(2, 1), (2, 0), (1, 1), (3, 1), (0, 1), (1, 0), (3, 0), (0, 0)]
        where = [((x + p) % 4) * 2 + (1 - z if q else z) for p, q in order]
        hand = [
            send(dkv.at[1 - c, g], from_core.at[n], hs.at[n], hr.at[n], at(x, z, y, 1 - c))
            for n, g in enumerate(where)
        ]
        ring_a, ring_b = RingSum(blk_a, False, *a), CrossSum(blk_b, False, *a2)
        held[1].wait()

        def fold(n):
            g = where[n]
            hand[n].wait_recv()
            both = (own[g].astype(F32) + from_core[n].astype(F32)).astype(BF)
            blk_a[g] = both[0:512]
            blk_b[g] = both[512:1024]

        fold(0)
        ring_a.start(0)
        ring_b.hand(2)
        fold(1)
        ring_a.start(1)
        for n, step in ((2, 1), (3, 3), (4, 0)):
            fold(n)
            ring_b.hand(step)
        for n in (5, 6, 7):
            fold(n)
        held[0].wait()
        sum_w = RowSum(gwo, *b)
        sum_w.start()
        swap2 = Swap(gw2s, two, *s2)
        swap2.start()
        held[8].wait()
        sum_o = RowSum(outp, *b2)
        sum_o.start()
        for n in range(2, 6):
            held[n].wait()
        spread = spread_value(WIDTH)
        gains = columns_of_gains(gain1, gain2)

        def place_rows(n, size):
            return pl.ds(pl.multiple_of(n * size, size), size)

        def queries(n):
            part = place_rows(n, 512)
            v = dq[part, :]
            v = (v * cos_t[part, :] - partner(v) * sin_t[part, :]).astype(BF)
            d_kv[part, 0:128] = v
            dnq[part, :] = dot_nt(v, w1[:, 0:128])

        queries(0)
        ring_a.relay(0)
        sum_w.far()
        ring_b.far()
        queries(1)
        ring_a.relay(1)
        sum_o.far()
        sum_w.near()
        ring_b.near()
        held[6].wait()
        gw1[:, :, :, 0:128] = (
            dot_tn(normed[...], d_kv[:, 0:128]).astype(BF).reshape(8, 8, 16, 128)
        )
        ring_a.total(0)
        sum_o.near()
        gwos[...] = sum_w.total().astype(BF).reshape(8, 16, WIDE)
        swap2.finish()
        total = jnp.zeros((15, 1), F32)
        for m, ref, w in ((0, g_gate, w_gate), (384, g_up, w_up)):
            for n in range(0, 8, 2):
                part = jnp.concatenate(
                    [
                        two[f, :, m + 48 * k : m + 48 * k + 40].astype(F32)[0:15]
                        for k in (n, n + 1)
                        for f in range(8)
                    ],
                    axis=1,
                )
                spot = pl.ds(n * 320, 640)
                ref[:, spot] = part * gains[:, 1:2]
                total += jnp.sum(part * w[:, spot].astype(F32), axis=1, keepdims=True)
        g_mlp[...] = jnp.broadcast_to(total, (15, 128))

        def squeeze(v):
            top = v.astype(BF)
            low = (v - top.astype(F32)).astype(BF)
            return dot_nt(top, spread) + dot_nt(low, spread)

        g_down[...] = squeeze(wd[...])[0:40]
        output[...] = dot_nt(spread, (resid[...] + sum_o.total()).astype(BF)).astype(BF)

        v = jnp.concatenate([ring_a.total(1), ring_b.total()], axis=0)
        turned = v * cos_t[...] - partner(v) * sin_t[...]
        d_kv[:, 128:256] = jnp.where(lanes_of((1024, 128)) < 64, turned, v).astype(BF)
        sum_n = RowSum(dn, *d)

        def back(core):
            to = [((y + n) % 4) * 2 + core for n in (2, 1, 3, 0)]
            parts = [place_rows(n, 128) for n in to]
            v = jnp.concatenate([d_kv[p, 128:256] for p in parts], axis=0)
            v = dot_nt(v, w1[:, 128:256])
            for n, p in enumerate(parts):
                dn[to[n]] = (dnq[p, :] + v[128 * n : 128 * n + 128]).astype(BF)

        back(1 - c)
        for n in (2, 1, 3, 0):
            sum_n.hand(n)
        ring_1 = RingSum(gw1, False, *e)

        def weights_k(which):
            parts = [place_rows(where[n], 128) for n in which]
            v = jnp.concatenate([normed[:, p] for p in parts], axis=1)
            v = dot_tn(v, d_kv[:, 128:256]).astype(BF)
            for n, m in enumerate(which):
                gw1[where[m], :, :, 128:256] = v[128 * n : 128 * n + 128].reshape(8, 16, 128)

        weights_k((0, 1))
        ring_1.start(0)
        ring_1.start(1)
        ring_o = RingSum(gwos, True, *e2)
        ring_o.start(0)
        ring_o.start(1)
        back(c)
        sum_n.far()
        weights_k((2, 3, 4, 5, 6, 7))
        sum_n.near()
        for k in (0, 1):
            ring_1.relay(k)
            ring_o.relay(k)
        ring_1.total(0)
        ring_o.total(0)
        gw1s[...] = ring_1.total(1).astype(BF)
        swap1 = Swap(gw1s, one, *s1)
        swap1.start()
        g_o[...] = squeeze(ring_o.total(1))[0:15]

        held[7].wait()
        xs = rows[...].astype(F32)
        inv = inverse_rms(xs)
        t = sum_n.total()
        mean = jnp.sum(t * xs, axis=1, keepdims=True) * (1.0 / WIDTH)
        d_x = dr[...] + inv * t - xs * (inv * inv * inv * mean)
        gh[...] = dot_nt(spread, d_x.astype(BF)).astype(BF)
        swap1.finish()
        ones = [one[f].astype(F32)[0:15] for f in range(8)]
        r_q = jnp.concatenate([v[:, 0:128] for v in ones], axis=1)[:, 0:WIDTH]

        def heads(n):
            return jnp.concatenate(
                [
                    sum(ones[f][:, n : n + 64] for f in range(8) if OWNED_KV[f] == h)
                    for h in range(5)
                ],
                axis=1,
            )

        total = jnp.zeros((15, 1), F32)
        for part, w, ref in ((r_q, w_q, g_q), (heads(128), w_k, g_k), (heads(192), w_v, g_v)):
            ref[...] = part * gains[:, 0:1]
            total += jnp.sum(part * w[...].astype(F32), axis=1, keepdims=True)
        g_attn[...] = jnp.broadcast_to(total, (15, 128))
        for copy in hand:
            copy.wait_send()
        ring_a.finish()
        ring_b.finish()
        ring_1.finish()
        ring_o.finish()
        sum_w.finish()
        sum_o.finish()
        sum_n.finish()

    return comm_call(
        "last",
        6,
        kernel,
        (
            shaped((WIDTH, 128), BF),
            shaped((WIDTH, 128), BF),
            shaped((15, 128), F32),
            shaped((15, 128), F32),
            shaped((15, WIDTH), F32),
            shaped((15, 320), F32),
            shaped((15, 320), F32),
            shaped((15, WIDTH), F32),
            shaped((15, 2560), F32),
            shaped((15, 2560), F32),
            shaped((40, WIDTH), F32),
        ),
        [ANY] * 9 + [VMEM] * 11,
        (VMEM,) * 11,
        [
            pltpu.VMEM((8, 1024, 128), BF),
            pltpu.VMEM((8, 128, WIDE), BF),
            pltpu.VMEM((8, 128, WIDE), BF),
            pltpu.VMEM((1024, 128), F32),
            pltpu.VMEM((1024, 128), F32),
            pltpu.VMEM((1024, 128), F32),
            pltpu.VMEM((WIDE, 256), BF),
            pltpu.VMEM((1024, WIDE), BF),
            pltpu.VMEM((128, WIDE), BF),
            DMA((9,)),
            pltpu.VMEM((8, 512, 128), BF),
            pltpu.VMEM((8, 512, 128), BF),
            pltpu.VMEM((8, 1024, 128), BF),
            pltpu.VMEM((8, 16, WIDE), BF),
            pltpu.VMEM((8, 8, 16, 256), BF),
            pltpu.VMEM((1024, WIDE), F32),
            pltpu.VMEM((1024, 256), BF),
            pltpu.VMEM((8, 128, WIDE), BF),
            pltpu.VMEM((8, 16, 256), BF),
            pltpu.VMEM((8, 16, 768), BF),
            pltpu.VMEM((8, 16, 256), BF),
            DMA((8,)),
            DMA((8,)),
        ]
        + RingSum.scratch((512, 128), False)
        + CrossSum.scratch((512, 128), False)
        + RowSum.scratch((128, WIDE)) * 3
        + RingSum.scratch((8, 16, 256), False)
        + RingSum.scratch((16, WIDE), True)
        + Swap.sems * 2,
        (
            dkv, gwo, outp, dq, cos_t, sin_t, w1, normed, rows, resid, d_resid, gw2s, gwd, gain1,
            gain2, w_q, w_k, w_v, w_gate, w_up,
        ),
    )


def lanes_of(shape):
    return lax.broadcasted_iota(jnp.int32, shape, len(shape) - 1)


def partner(v):
    lane = lanes_of(v.shape)
    return jnp.where(lane % 64 < 32, pltpu.roll(v, 96, 1), pltpu.roll(v, 32, 1))


def doc_ends(lengths):
    return lengths[0], lengths[0] + lengths[1]


def doc_start(pos, ends):
    return jnp.where(pos < ends[0], 0, jnp.where(pos < ends[1], ends[0], ends[1]))

def layout(order, inverse):
    @pl.loop(0, 64)
    def _(n):
        inverse[order[n]] = n

    i = lax.axis_index("ctx")
    f = i % 8
    upper = (f == 3) | (f == 5)
    return i // 8, (
        jnp.where(upper, 1, 0),
        jnp.where(upper | (f == 1) | (f == 4), 1, 0),
    )


def key_range(span, ends):
    begin = doc_start(span * 128, ends) // 128
    count = span - begin + 1
    runs = (count + 3) // 8
    return begin, runs, jnp.where(count > runs * 8, 1, 0)


def attend(lengths, order, q, kv):
    def kernel(lengths, order, q_ref, kv_ref, o_ref, lse_ref, s_ref, inverse):
        group, sel = layout(order, inverse)
        ends = doc_ends(lengths)

        @pl.loop(0, 8)
        def _(b):
            span = order[group * 8 + b]
            begin, runs, rest = key_range(span, ends)
            pos = span * 128 + lanes_of((1, 256)) % 128
            low = doc_start(pos, ends)
            rows = pl.ds(pl.multiple_of(b * 128, 128), 128)
            none = jnp.zeros((128, 128), BF)
            pair = jnp.concatenate(
                [
                    jnp.concatenate([q_ref[0, rows, :], none], axis=1),
                    jnp.concatenate([none, q_ref[1, rows, :]], axis=1),
                ],
                axis=0,
            )

            def load(h, t, n):
                return jnp.concatenate(
                    [
                        kv_ref[sel[h], pl.ds(inverse[jnp.minimum(t + i, 63)] * 128, 128), :]
                        for i in range(n)
                    ],
                    axis=0,
                )

            def held(t, n):
                return pl.ds(pl.multiple_of((t - begin) * 128, 512), n * 128)

            def scores(n, t, high):
                kpos = t * 128 + lax.broadcasted_iota(jnp.int32, (n * 128, 1), 0)
                allowed = (kpos >= low) & (kpos <= pos)
                keys = jnp.concatenate([load(0, t, n), load(1, t, n)], axis=1)
                s = jnp.where(allowed, dot_nt(keys, pair), MASKED)
                s_ref[held(t, n), :] = s
                return jnp.maximum(high, jnp.max(s.reshape(n * 16, 8, 256), axis=0))

            def over(step, state):
                state = lax.fori_loop(0, runs, lambda j, v: step(8, begin + j * 8, v), state)
                return lax.fori_loop(0, rest, lambda j, v: step(4, begin + runs * 8, v), state)

            high = over(scores, jnp.full((8, 256), MASKED, F32))
            high = jnp.max(high, axis=0, keepdims=True)

            def weigh(n, t, state):
                total, acc = state
                p = jnp.exp(s_ref[held(t, n), :] - high)
                total = total + jnp.sum(p.reshape(n * 16, 8, 256), axis=0)
                values = jnp.where(lanes_of((n * 128, 128)) < 64, pltpu.roll(load(0, t, n), 64, 1), load(1, t, n))
                return total, acc + dot_tn(values, p.astype(BF))

            total, acc = over(weigh, (jnp.zeros((8, 256), F32), jnp.zeros((128, 256), F32)))
            total = jnp.sum(total, axis=0, keepdims=True)
            lse = high + jnp.log(total)
            lse_ref[b, 0:1, :] = lse[:, 0:128]
            lse_ref[b, 1:2, :] = lse[:, 128:256]
            acc = acc / total
            acc = jnp.concatenate([acc[0:64, 0:128], acc[64:128, 128:256]], axis=0)
            o_ref[rows, :] = acc.T.astype(BF)

    return pl.pallas_call(
        kernel,
        in_specs=[SMEM, SMEM, VMEM, VMEM],
        out_specs=(VMEM, VMEM),
        scratch_shapes=[pltpu.VMEM((40 * 128, 256), F32), pltpu.SMEM((64,), jnp.int32)],
        out_shape=(shaped((1024, 128), BF), shaped((8, 8, 128), F32)),
        compiler_params=pltpu.CompilerParams(vmem_limit_bytes=LIMIT),
        name="attend",
    )(lengths, order, q, kv)


def attend_back(lengths, order, q, kv, d_att, att, lse):
    def kernel(
        lengths, order, q_ref, kv_ref, d_ref, o_ref, lse_ref, dq_ref, dkv_ref, acc_ref, inverse
    ):
        lane = lanes_of((128, 128))
        group, sel = layout(order, inverse)
        ends = doc_ends(lengths)

        @pl.loop(0, 16)
        def _(n):
            for s in (0, 1):
                part = pl.ds(pl.multiple_of(n * 512, 512), 512)
                acc_ref[s, part, :] = jnp.zeros((512, 128), F32)

        @pl.loop(0, 8)
        def _(b):
            span = order[group * 8 + b]
            begin, runs, rest = key_range(span, ends)
            pos = span * 128 + lanes_of((1, 128))
            low = doc_start(pos, ends)
            rows = pl.ds(pl.multiple_of(b * 128, 128), 128)
            d_both = d_ref[rows, :].astype(F32)
            d_pad = (
                jnp.where(lane >= 64, pltpu.roll(d_both, 64, 1), 0.0).astype(BF),
                jnp.where(lane >= 64, d_both, 0.0).astype(BF),
            )
            pair = [jnp.concatenate([q_ref[h, rows, :], d_pad[h]], axis=0) for h in (0, 1)]
            mixed = (d_both * o_ref[rows, :].astype(F32)).T
            delta = [jnp.sum(mixed[64 * h : 64 * h + 64], axis=0, keepdims=True) for h in (0, 1)]
            lses = [lse_ref[b, h : h + 1, :] for h in (0, 1)]

            def step(n, t, state):
                where = [inverse[jnp.minimum(t + i, 63)] * 128 for i in range(n)]
                where = [pl.ds(pl.multiple_of(v, 128), 128) for v in where]
                kpos = t * 128 + lax.broadcasted_iota(jnp.int32, (n * 128, 1), 0)
                allowed = (kpos >= low) & (kpos <= pos)
                d_ss, kvs = [], []
                for h in (0, 1):
                    kv_t = jnp.concatenate([kv_ref[sel[h], w, :] for w in where], axis=0)
                    kvs.append(kv_t)
                    both = dot_nt(kv_t, pair[h])
                    p = jnp.where(allowed, jnp.exp(both[:, 0:128] - lses[h]), 0.0)
                    d_s = (p * (both[:, 128:256] - delta[h])).astype(BF)
                    d_ss.append(d_s)
                    d_kv = dot(jnp.concatenate([d_s, p.astype(BF)], axis=1), pair[h])
                    for i, w in enumerate(where):
                        acc_ref[sel[h], w, :] += d_kv[i * 128 : (i + 1) * 128]
                lanes = lanes_of((n * 128, 128))
                keys = jnp.where(lanes < 64, kvs[0], pltpu.roll(kvs[1], 64, 1))
                return state + dot_tn(keys, jnp.concatenate(d_ss, axis=1))

            state = jnp.zeros((128, 256), F32)
            state = lax.fori_loop(0, runs, lambda j, v: step(8, begin + j * 8, v), state)
            state = lax.fori_loop(0, rest, lambda j, v: step(4, begin + runs * 8, v), state)
            state = jnp.concatenate([state[0:64, 0:128], state[64:128, 128:256]], axis=0)
            dq_ref[rows, :] = state.T * 0.125

        @pl.loop(0, 16)
        def _(n):
            for s in (0, 1):
                part = pl.ds(pl.multiple_of(n * 512, 512), 512)
                dkv_ref[s, part, :] = acc_ref[s, part, :].astype(BF)

    return pl.pallas_call(
        kernel,
        in_specs=[SMEM, SMEM] + [VMEM] * 5,
        out_specs=(VMEM, VMEM),
        scratch_shapes=[pltpu.VMEM((2, 8192, 128), F32), pltpu.SMEM((64,), jnp.int32)],
        out_shape=(shaped((1024, 128), F32), shaped((2, 8192, 128), BF)),
        compiler_params=pltpu.CompilerParams(vmem_limit_bytes=LIMIT),
        name="attend_back",
    )(lengths, order, q, kv, d_att, att, lse)


def hand_out(parts):
    def kernel(*refs):
        n = len(refs) // 2
        for k, (src, dst) in enumerate(zip(refs[:n], refs[n:])):
            if dst.shape == (15,):
                wide = jnp.concatenate([src[...], jnp.zeros((113, 128), F32)], axis=0)
                dst[...] = wide.T[0:1, 0:15].reshape(15)
            else:
                dst[...] = src[...]

    shapes = [(15,) if v.shape == (15, 128) else v.shape for v in parts]
    return pl.pallas_call(
        kernel,
        out_shape=tuple(shaped(s, v.dtype) for s, v in zip(shapes, parts)),
        in_specs=[VMEM] * len(parts),
        out_specs=(VMEM,) * len(parts),
        compiler_params=pltpu.CompilerParams(vmem_limit_bytes=LIMIT),
        name="hand_out",
    )(*parts)


def local(
    hidden, attn_gain, w_q, w_k, w_v, w_o, mlp_gain, w_gate, w_up, w_down, cotangent,
    doc_lengths, span_order,
):
    frequency = ROPE_BASE ** (-2.0 * (np.arange(128) % 32) / HEAD)
    frequency = jnp.asarray(frequency, F32).reshape(1, 128)

    rows, w1, wds, wo, cot, w2own, normed, q, kv, cos_t, sin_t = first(
        hidden.T, cotangent.T, w_q, w_k, w_v, w_o, w_gate, w_up, w_down, attn_gain, mlp_gain,
        doc_lengths, span_order, frequency,
    )
    kv = kv.reshape(2, 8192, 128)
    att, lse = attend(doc_lengths, span_order, q, kv)
    outp, resid, d_resid, d_heads, gwo, gw2s, gwds = feed(
        att, w2own, wo, rows.reshape(1024, WIDE), wds.reshape(384, WIDE), cot.reshape(1024, WIDE)
    )
    d_att = d_heads.reshape(1024, 128)
    dq, dkv = attend_back(doc_lengths, span_order, q, kv, d_att, att, lse)
    grads = last(
        dkv.reshape(2, 8, 1024, 128), gwo, outp, dq, cos_t, sin_t, w1.reshape(WIDE, 256), normed,
        rows, resid, d_resid, gw2s, gwds, attn_gain, mlp_gain, w_q, w_k, w_v, w_gate, w_up,
    )
    output, grad_hidden, g_attn, g_mlp, g_q, g_k, g_v, g_o, g_gate, g_up, g_down = hand_out(grads)
    return (
        output.T, grad_hidden.T, g_attn, g_q, g_k, g_v, g_o, g_mlp, g_gate, g_up, g_down
    )


def solution(mesh):
    both = ("fsdp", "ctx")
    wide, thin, part = P(both, None), P(both), P("fsdp")
    return jax.shard_map(
        local,
        mesh=mesh,
        in_specs=(wide, thin, wide, wide, wide, wide, thin, wide, wide, wide, wide, part, part),
        out_specs=(wide, wide, thin, wide, wide, wide, wide, thin, wide, wide, wide),
        check_vma=False,
    )
```

```python
import jax
import jax.numpy as jnp
import numpy as np
from jax import lax
from jax.experimental import pallas as pl
from jax.experimental.pallas import tpu as pltpu
from jax.sharding import PartitionSpec as P

HEAD = 64
EPSILON = 1e-05
ROPE_BASE = 100000.0
MASKED = -1e30
WIDE = 1024
WIDTH = 960
BF = jnp.bfloat16
F32 = jnp.float32
MESH = pl.DeviceIdType.MESH
DMA = pltpu.SemaphoreType.DMA
ANY = pl.BlockSpec(memory_space=pl.ANY)
VMEM = pl.BlockSpec(memory_space=pltpu.VMEM)
SMEM = pl.BlockSpec(memory_space=pltpu.SMEM)
LIMIT = 56 * 2**20
OWNED_KV = (0, 1, 1, 2, 2, 3, 4, 4)


def dot(a, b):
    return lax.dot_general(a, b, (((1,), (0,)), ((), ())), preferred_element_type=F32)


def dot_nt(a, b):
    return lax.dot_general(a, b, (((1,), (1,)), ((), ())), preferred_element_type=F32)


def dot_tn(a, b):
    return lax.dot_general(a, b, (((0,), (0,)), ((), ())), preferred_element_type=F32)


def shaped(shape, dtype):
    return jax.ShapeDtypeStruct(shape, dtype)


def place():
    i = lax.axis_index("ctx")
    return i // 16, (i // 8) % 2, (i // 2) % 4, i % 2


def at(x, z, y, c):
    return {"ctx": (((x + 4) % 4) * 2 + z) * 8 + ((y + 4) % 4) * 2 + c}


def send(src, dst, ssem, rsem, device):
    copy = pltpu.make_async_remote_copy(
        src, dst, ssem, rsem, device_id=device, device_id_type=MESH
    )
    copy.start()
    return copy


def hail(kinds):
    x, z, y, c = place()
    who = []
    if "x" in kinds:
        who += [at(x + 1, z, y, c), at(x - 1, z, y, c), at(x, 1 - z, y, c)]
    if "f" in kinds:
        who += [at(x, z, y + d, (c + e) % 2) for d in range(4) for e in range(2) if d + e]
    elif "y" in kinds:
        who += [at(x, z, y + d, c) for d in (1, 2, 3)] + [at(x, z, y, 1 - c)]
    barrier = pltpu.get_barrier_semaphore()
    for device in who:
        pl.semaphore_signal(barrier, inc=1, device_id=device, device_id_type=MESH)
    return len(who)


def greet(kinds):
    pl.semaphore_wait(pltpu.get_barrier_semaphore(), hail(kinds))


def half_lead(ref, k):
    n = ref.shape[0] // 2
    return ref.at[pl.ds(k * n, n)]


def half_lanes(ref, k):
    n = ref.shape[-1] // 2
    return ref.at[:, pl.ds(k * n, n)]


class RingGather:
    sems = [DMA((9,)), DMA((9,)), DMA(())]

    def __init__(self, src, dst, half, ssem, rsem, lsem, arrived=None):
        self.src, self.dst, self.half = src, dst, half
        self.ssem, self.rsem, self.lsem = ssem, rsem, lsem
        self.arrived = arrived or (lambda block: None)
        self.copies = {}

    def push(self, n, src, dst, device):
        self.copies[n] = send(src, dst, self.ssem.at[n], self.rsem.at[n], device)

    def start(self):
        x, z, y, c = place()
        me = self.dst.at[x * 2 + z]
        self.push(0, self.src, me, at(x, 1 - z, y, c))
        self.push(1, self.src, me, at(x + 1, z, y, c))
        self.push(2, self.src, me, at(x - 1, z, y, c))
        self.local = pltpu.make_async_copy(self.src, me, self.lsem)
        self.local.start()

    def relay_z(self):
        x, z, y, c = place()
        block = self.dst.at[x * 2 + 1 - z]
        self.copies[0].wait_recv()
        self.push(3, block, block, at(x + 1, z, y, c))
        self.push(4, block, block, at(x - 1, z, y, c))
        self.arrived(x * 2 + 1 - z)

    def relay_x(self, k):
        x, z, y, c = place()
        zz = z if k == 0 else 1 - z
        left, right = ((x + 3) % 4) * 2 + zz, ((x + 1) % 4) * 2 + zz
        self.copies[1 + 2 * k].wait_recv()
        part = self.half(self.dst.at[left], 0)
        self.push(5 + 2 * k, part, part, at(x + 1, z, y, c))
        self.arrived(left)
        self.copies[2 + 2 * k].wait_recv()
        part = self.half(self.dst.at[right], 1)
        self.push(6 + 2 * k, part, part, at(x - 1, z, y, c))
        self.arrived(right)

    def land(self, k):
        x, z, y, c = place()
        zz = z if k == 0 else 1 - z
        self.copies[5 + 2 * k].wait_recv()
        self.copies[6 + 2 * k].wait_recv()
        self.arrived(((x + 2) % 4) * 2 + zz)

    def sent(self):
        for n in range(9):
            self.copies[n].wait_send()

    def finish(self):
        self.local.wait()
        self.sent()


class CrossGather:
    sems = [DMA((8,)), DMA((8,)), DMA(())]

    def __init__(self, src, dst, half, ssem, rsem, lsem, arrived=None):
        self.src, self.dst, self.half = src, dst, half
        self.ssem, self.rsem, self.lsem = ssem, rsem, lsem
        self.arrived = arrived or (lambda block: None)
        self.copies = {}

    def push(self, n, src, dst, device):
        self.copies[n] = send(src, dst, self.ssem.at[n], self.rsem.at[n], device)

    def start(self):
        x, z, y, c = place()
        me = self.dst.at[x * 2 + z]
        self.push(1, self.src, me, at(x + 1, z, y, c))
        self.push(2, self.src, me, at(x - 1, z, y, c))
        self.push(0, self.src, me, at(x, 1 - z, y, c))
        self.local = pltpu.make_async_copy(self.src, me, self.lsem)
        self.local.start()

    def relay(self):
        x, z, y, c = place()
        for n, step, side in ((1, 3, 0), (2, 1, 1)):
            block = ((x + step) % 4) * 2 + z
            whole = self.dst.at[block]
            self.copies[n].wait_recv()
            part = self.half(whole, side)
            self.push(2 + n, part, part, at(x + 4 - step, z, y, c))
            self.push(4 + n, whole, whole, at(x, 1 - z, y, c))
            self.arrived(block)

    def far(self):
        x, z, y, c = place()
        block = ((x + 2) % 4) * 2 + z
        whole = self.dst.at[block]
        self.copies[3].wait_recv()
        self.copies[4].wait_recv()
        self.push(7, whole, whole, at(x, 1 - z, y, c))
        self.arrived(block)

    def land(self):
        x, z, y, c = place()
        for n, step in ((0, 0), (5, 3), (6, 1), (7, 2)):
            self.copies[n].wait_recv()
            self.arrived(((x + step) % 4) * 2 + 1 - z)

    def finish(self):
        self.local.wait()
        for n in range(8):
            self.copies[n].wait_send()


class RowGather:
    sems = [DMA((8,)), DMA((8,)), DMA(())]

    def __init__(self, src, dst, ssem, rsem, lsem):
        self.src, self.dst = src, dst
        self.ssem, self.rsem, self.lsem = ssem, rsem, lsem
        self.copies = {}

    def push(self, n, src, dst, device):
        self.copies[n] = send(src, dst, self.ssem.at[n], self.rsem.at[n], device)

    def start(self):
        x, z, y, c = place()
        me = self.dst.at[y * 2 + c]
        self.push(1, self.src, me, at(x, z, y + 1, c))
        self.push(2, self.src, me, at(x, z, y - 1, c))
        self.push(0, self.src, me, at(x, z, y, 1 - c))
        self.local = pltpu.make_async_copy(self.src, me, self.lsem)
        self.local.start()

    def relay(self):
        x, z, y, c = place()
        for n, step, side in ((1, 3, 0), (2, 1, 1)):
            self.copies[n].wait_recv()
            block = self.dst.at[((y + step) % 4) * 2 + c]
            part = half_lead(block, side)
            self.push(2 + n, part, part, at(x, z, y + 4 - step, c))
            self.push(4 + n, block, block, at(x, z, y, 1 - c))

    def land(self):
        x, z, y, c = place()
        self.copies[3].wait_recv()
        self.copies[4].wait_recv()
        block = self.dst.at[((y + 2) % 4) * 2 + c]
        self.push(7, block, block, at(x, z, y, 1 - c))

    def finish(self):
        self.local.wait()
        for n in (0, 5, 6, 7):
            self.copies[n].wait_recv()
        for n in range(8):
            self.copies[n].wait_send()


class Swap:
    sems = [DMA((8,)), DMA((8,)), DMA(())]

    def __init__(self, src, dst, ssem, rsem, lsem):
        self.src, self.dst = src, dst
        self.ssem, self.rsem, self.lsem = ssem, rsem, lsem

    def start(self):
        x, z, y, c = place()
        me = y * 2 + c
        self.copies = []
        for d in (2, 1, 3, 0):
            for e in (0, 1):
                if d + e:
                    n = d * 2 + e
                    to = ((y + d) % 4) * 2 + (c + e) % 2
                    self.copies.append(
                        send(
                            self.src.at[to],
                            self.dst.at[me],
                            self.ssem.at[n],
                            self.rsem.at[n],
                            at(x, z, y + d, (c + e) % 2),
                        )
                    )
        self.local = pltpu.make_async_copy(self.src.at[me], self.dst.at[me], self.lsem)
        self.local.start()

    def finish(self):
        self.local.wait()
        for copy in self.copies:
            copy.wait()


class RowSum:
    @staticmethod
    def scratch(shape):
        return [
            pltpu.VMEM((4,) + shape, BF),
            pltpu.VMEM((4,) + shape, BF),
            pltpu.VMEM((2, shape[0] // 2) + shape[1:], BF),
            pltpu.VMEM((2,) + shape, BF),
            DMA((8,)),
            DMA((8,)),
        ]

    def __init__(self, blk, first, mixed, parts, heard, ssem, rsem, source=None):
        self.blk, self.first, self.mixed = blk, first, mixed
        self.source = blk if source is None else source
        self.parts, self.heard = parts, heard
        self.ssem, self.rsem = ssem, rsem
        self.copies = {}

    def push(self, n, src, dst, device):
        self.copies[n] = send(src, dst, self.ssem.at[n], self.rsem.at[n], device)

    def hand(self, d):
        x, z, y, c = place()
        to = ((y + d) % 4) * 2 + 1 - c
        self.push(d, self.source.at[to], self.first.at[d], at(x, z, y, 1 - c))

    def start(self):
        for d in (2, 1, 3, 0):
            self.hand(d)

    def both(self, d):
        x, z, y, c = place()
        self.copies[d].wait_recv()
        return self.blk.at[((y + d) % 4) * 2 + c][...].astype(F32) + self.first[d].astype(F32)

    def far(self):
        x, z, y, c = place()
        self.mixed[2] = self.both(2).astype(BF)
        for side, step in ((0, 1), (1, 3)):
            part = half_lead(self.mixed.at[2], side)
            self.push(4 + side, part, self.parts.at[side], at(x, z, y + step, c))

    def near(self):
        x, z, y, c = place()
        for side, step in ((0, 1), (1, 3)):
            sums = self.both(step)
            n = sums.shape[0] // 2
            self.copies[4 + side].wait_recv()
            part = self.parts[side].astype(F32)
            self.mixed[step, pl.ds(side * n, n)] = (sums[side * n : side * n + n] + part).astype(BF)
            self.mixed[step, pl.ds(n - side * n, n)] = sums[n - side * n : 2 * n - side * n].astype(BF)
            self.push(6 + side, self.mixed.at[step], self.heard.at[side], at(x, z, y + step, c))

    def total(self):
        total = self.both(0)
        for side in (0, 1):
            self.copies[6 + side].wait_recv()
            total = total + self.heard[side].astype(F32)
        return total

    def finish(self):
        for n in range(8):
            self.copies[n].wait_send()


class CrossSum:
    @staticmethod
    def scratch(shape, lanes):
        if lanes:
            part = shape[:-1] + (shape[-1] // 2,)
        else:
            part = (shape[0] // 2,) + shape[1:]
        return [
            pltpu.VMEM((4,) + shape, BF),
            pltpu.VMEM((4,) + shape, BF),
            pltpu.VMEM((2,) + part, BF),
            pltpu.VMEM((2,) + shape, BF),
            DMA((8,)),
            DMA((8,)),
        ]

    def __init__(self, blk, lanes, first, mixed, parts, heard, ssem, rsem):
        self.blk, self.half = blk, half_lanes if lanes else half_lead
        self.first, self.mixed, self.parts, self.heard = first, mixed, parts, heard
        self.ssem, self.rsem = ssem, rsem
        self.copies = {}

    def push(self, n, src, dst, device):
        self.copies[n] = send(src, dst, self.ssem.at[n], self.rsem.at[n], device)

    def hand(self, d):
        x, z, y, c = place()
        to = ((x + d) % 4) * 2 + 1 - z
        self.push(d, self.blk.at[to], self.first.at[d], at(x, 1 - z, y, c))

    def both(self, d):
        x, z, y, c = place()
        self.copies[d].wait_recv()
        return self.blk[((x + d) % 4) * 2 + z].astype(F32) + self.first[d].astype(F32)

    def far(self):
        x, z, y, c = place()
        self.mixed[2] = self.both(2).astype(BF)
        for side, step in ((0, 1), (1, 3)):
            part = self.half(self.mixed.at[2], side)
            self.push(4 + side, part, self.parts.at[side], at(x + step, z, y, c))

    def near(self):
        x, z, y, c = place()
        for side, step in ((0, 1), (1, 3)):
            mixed = self.mixed.at[step]
            mixed[...] = self.both(step).astype(BF)
            self.copies[4 + side].wait_recv()
            mine = self.half(mixed, side)
            mine[...] = (mine[...].astype(F32) + self.parts[side].astype(F32)).astype(BF)
            self.push(6 + side, mixed, self.heard.at[side], at(x + step, z, y, c))

    def total(self):
        total = self.both(0)
        for side in (0, 1):
            self.copies[6 + side].wait_recv()
            total = total + self.heard[side].astype(F32)
        return total

    def finish(self):
        for n in range(8):
            self.copies[n].wait_send()


class RingSum:
    @staticmethod
    def scratch(shape, lanes):
        if lanes:
            part = shape[:-1] + (shape[-1] // 2,)
        else:
            part = (shape[0] // 2,) + shape[1:]
        return [
            pltpu.VMEM((4,) + part, BF),
            pltpu.VMEM((4,) + shape, BF),
            pltpu.VMEM((4,) + shape, BF),
            pltpu.VMEM((2,) + shape, BF),
            DMA((9,)),
            DMA((9,)),
        ]

    def __init__(self, blk, lanes, parts, mixed, heard, across, ssem, rsem):
        self.blk, self.half = blk, half_lanes if lanes else half_lead
        self.parts, self.mixed, self.heard, self.across = parts, mixed, heard, across
        self.ssem, self.rsem = ssem, rsem
        self.copies = {}

    def push(self, n, src, dst, device):
        self.copies[n] = send(src, dst, self.ssem.at[n], self.rsem.at[n], device)

    def start(self, k):
        x, z, y, c = place()
        zz = 1 - z if k == 0 else z
        far = self.blk.at[((x + 2) % 4) * 2 + zz]
        self.push(4 * k, self.half(far, 0), self.parts.at[2 * k], at(x + 1, z, y, c))
        self.push(4 * k + 1, self.half(far, 1), self.parts.at[2 * k + 1], at(x - 1, z, y, c))

    def relay(self, k):
        x, z, y, c = place()
        zz = 1 - z if k == 0 else z
        for side, step in ((0, 1), (1, 3)):
            n = 2 * k + side
            mixed = self.mixed.at[n]
            source = self.blk.at[((x + step) % 4) * 2 + zz]
            mine, other = self.half(source, side), self.half(source, 1 - side)
            self.half(mixed, 1 - side)[...] = other[...]
            self.copies[4 * k + side].wait_recv()
            self.half(mixed, side)[...] = (
                mine[...].astype(F32) + self.parts[n].astype(F32)
            ).astype(BF)
            self.push(4 * k + 2 + side, mixed, self.heard.at[n], at(x + step, z, y, c))

    def total(self, k):
        x, z, y, c = place()
        zz = 1 - z if k == 0 else z
        total = self.blk[x * 2 + zz].astype(F32)
        for side in (0, 1):
            self.copies[4 * k + 2 + side].wait_recv()
            total = total + self.heard[2 * k + side].astype(F32)
        if k == 0:
            self.across[0] = total.astype(BF)
            self.push(8, self.across.at[0], self.across.at[1], at(x, 1 - z, y, c))
            return None
        self.copies[8].wait_recv()
        return total + self.across[1].astype(F32)

    def finish(self):
        for n in range(9):
            self.copies[n].wait_send()


def fetch(src, dst, sem):
    copy = pltpu.make_async_copy(src, dst, sem)
    copy.start()
    return copy


def columns_of_gains(gain1, gain2):
    gap = jnp.zeros((1, 113), F32)
    return jnp.concatenate(
        [
            jnp.concatenate([ref[...].astype(F32).reshape(1, 15), gap], axis=1)
            for ref in (gain1, gain2)
        ]
        + [jnp.zeros((126, 128), F32)],
        axis=0,
    ).T[0:15]


def row_of(column):
    wide = jnp.concatenate([column, jnp.zeros((113, 1), F32)], axis=0)
    return jnp.broadcast_to(wide, (128, 128)).T[0:1, 0:15].reshape(15)


def comm_call(name, number, kernel, out_shape, in_specs, out_specs, scratch, args):
    return pl.pallas_call(
        kernel,
        out_shape=out_shape,
        in_specs=in_specs,
        out_specs=out_specs,
        scratch_shapes=scratch,
        compiler_params=pltpu.CompilerParams(
            collective_id=number, has_side_effects=True, vmem_limit_bytes=LIMIT
        ),
        name=name,
    )(*args)


def split(refs, counts):
    parts, begin = [], 0
    for n in counts:
        parts.append(refs[begin : begin + n])
        begin += n
    return parts


def spread_value(rows):
    j = lax.broadcasted_iota(jnp.int32, (rows, WIDE), 0)
    k = lax.broadcasted_iota(jnp.int32, (rows, WIDE), 1)
    hit = ((k // 16) * 15 + k % 16 == j) & (k % 16 < 15)
    return jnp.where(hit, 1.0, 0.0).astype(BF)


def first(
    hidden_t, cot_t, w_q, w_k, w_v, w_o, w_gate, w_up, w_down, gain1, gain2, lengths, span_order, freq
):
    def kernel(
        hidden_t, cot_t, w_q, w_k, w_v, w_o, w_gate, w_up, w_down, gain1, gain2, lengths, order, freq,
        rows_out, w1_out, wds, wo, cot, w2own, normed_out, q_out, kv2, cos_out, sin_out,
        rows, w1, normed, q_rot, cos_t, sin_t, xp, cp, wp1, wp2, wop, wdp, wos, w1own, kv, outs,
        *sems,
    ):
        a, a2, b, d, e, e2, ac, ao, b2, k0, k1, (hs, hr) = split(sems, (3,) * 11 + (2,))
        x, z, y, c = place()
        partners = hail("xf")

        gains = columns_of_gains(gain1, gain2)
        q = jnp.concatenate([w_q[...].astype(F32), jnp.zeros((15, 64), F32)], axis=1)
        q, k, v = (w * gains[:, 0:1] for w in (q, w_k[...].astype(F32), w_v[...].astype(F32)))
        wp1[...] = jnp.zeros(wp1.shape, BF)
        for f in range(8):
            n = OWNED_KV[f] * 64
            wp1[f, 0:15, 0:128] = q[:, 128 * f : 128 * f + 128].astype(BF)
            wp1[f, 0:15, 128:256] = jnp.concatenate(
                [k[:, n : n + 64], v[:, n : n + 64]], axis=1
            ).astype(BF)
        spread = spread_value(WIDTH)
        xp[...] = dot_tn(hidden_t[...], spread).astype(BF)

        wop[...] = jnp.zeros(wop.shape, BF)
        wop[0:15, :] = dot(w_o[...], spread).astype(BF)
        wdp[...] = jnp.zeros(wdp.shape, BF)
        wdp[0:40, :] = dot(w_down[...], spread).astype(BF)

        pl.semaphore_wait(pltpu.get_barrier_semaphore(), partners)
        swap = Swap(wp1, w1own, *b)
        swap.start()
        gathers = []
        for k, own in ((0, a), (64, a2)):
            spot = pl.ds(k, 64)
            gathers.append(RowGather(xp.at[spot], rows.at[:, spot], *own))
        for gather in gathers:
            gather.start()
        early = [RingGather(wdp, wds, half_lanes, *e2), RingGather(wop, wos, half_lanes, *e)]
        ring_d, ring_o = early
        for ring in early:
            ring.start()
        cp[...] = dot_tn(cot_t[...], spread).astype(BF)

        lane = lanes_of((1, 128))
        sign = jnp.where(lane % 64 < 32, -1.0, 1.0)
        ends = doc_ends(lengths)

        @pl.loop(0, 8)
        def _(n):
            pos = order[(x * 2 + z) * 8 + n] * 128
            pos = pos + lax.broadcasted_iota(jnp.int32, (128, 1), 0)
            angle = (pos - doc_start(pos, ends)).astype(F32) * freq[...]
            part = pl.ds(pl.multiple_of(n * 128, 128), 128)
            cos_t[part, :] = jnp.cos(angle)
            sin_t[part, :] = sign * jnp.sin(angle)

        written = [fetch(cos_t, cos_out, outs.at[0]), fetch(sin_t, sin_out, outs.at[1])]
        wp2[...] = jnp.zeros(wp2.shape, BF)
        gap = jnp.zeros((15, 8), F32)
        for m, ref in ((0, w_gate), (384, w_up)):
            w = ref[...].astype(F32) * gains[:, 1:2]
            for f in range(8):
                parts = []
                for g in range(8):
                    n = (8 * g + f) * 40
                    parts += [w[:, n : n + 40], gap]
                wp2[f, 0:15, m : m + 384] = jnp.concatenate(parts, axis=1).astype(BF)

        for ring in early:
            ring.relay_z()
        swap.finish()
        ring_1 = RingGather(w1own, w1, half_lead, *d)
        ring_1.start()
        for k in (0, 1):
            for ring in early:
                ring.relay_x(k)
        for gather in gathers:
            gather.relay()
        gather_c = RowGather(cp, cot, *ac)
        gather_c.start()
        ring_1.relay_z()

        ring_1.relay_x(0)
        ring_1.relay_x(1)

        for gather in gathers:
            gather.land()
        for k in (0, 1):
            for ring in early + [ring_1]:
                ring.land(k)
        for gather in gathers:
            gather.finish()
        ring_o.local.wait()
        gather_o = RowGather(wos, wo, *ao)
        gather_o.start()
        swap2 = Swap(wp2, w2own, *b2)
        swap2.start()
        ring_1.local.wait()
        written += [fetch(rows, rows_out, outs.at[2]), fetch(w1, w1_out, outs.at[3])]

        w = w1.reshape(WIDE, 256)
        lane = lanes_of((256, 128))

        def project(n):
            part = pl.ds(n * 256, 256)
            xs = jnp.concatenate([rows[2 * n], rows[2 * n + 1]], axis=0).astype(F32)
            v = (xs * inverse_rms(xs)).astype(BF)
            normed[part, :] = v
            out = dot(v, w[...])
            cos_v, sin_v = cos_t[part, :], sin_t[part, :]
            qs, ks = out[:, 0:128], out[:, 128:256]
            qs = (qs * cos_v + partner(qs) * sin_v).astype(BF).astype(F32) * 0.125
            kv[part, :] = jnp.where(lane < 64, ks * cos_v + partner(ks) * sin_v, ks).astype(BF)
            q_rot[0, part, :] = jnp.where(lane < 64, qs, 0.0).astype(BF)
            q_rot[1, part, :] = jnp.where(lane < 64, pltpu.roll(qs, 64, 1), 0.0).astype(BF)

        hand = []

        def pass_on(piece):
            n = len(hand)
            hand.append(send(piece, piece, hs.at[n], hr.at[n], at(x, z, y, 1 - c)))

        key_rings = []
        for h, (kind, own) in enumerate(((RingGather, k0), (CrossGather, k1))):
            mine = kv.at[pl.ds(512 * h, 512)]
            spot = pl.ds(512 * h, 512)
            ring = kind(
                mine,
                kv2.at[c, :, spot],
                half_lead,
                *own,
                arrived=lambda block, spot=spot: pass_on(kv2.at[c, block, spot]),
            )
            project(2 * h)
            project(2 * h + 1)
            ring.start()
            n = len(hand)
            hand.append(
                send(
                    mine, kv2.at[c, x * 2 + z, spot], hs.at[n], hr.at[n], at(x, z, y, 1 - c)
                )
            )
            key_rings.append(ring)
            if h == 0:
                gather_c.relay()

        written += [fetch(normed, normed_out, outs.at[4]), fetch(q_rot, q_out, outs.at[5])]
        ring_a, ring_b = key_rings
        ring_a.relay_z()
        gather_o.relay()
        ring_b.relay()
        ring_a.relay_x(0)
        gather_c.land()
        ring_a.relay_x(1)
        ring_b.far()
        gather_o.land()
        ring_a.land(0)
        ring_a.land(1)
        ring_b.land()
        for copy in hand:
            copy.wait()
        swap2.finish()
        gather_o.finish()
        gather_c.finish()
        for ring in [ring_d] + key_rings:
            ring.finish()
        for ring in (ring_1, ring_o):
            ring.sent()
        for copy in written:
            copy.wait()

    return comm_call(
        "first",
        1,
        kernel,
        (
            shaped((8, 128, WIDE), BF),
            shaped((8, 8, 16, 256), BF),
            shaped((8, 48, WIDE), BF),
            shaped((8, 8, 16, WIDE), BF),
            shaped((8, 128, WIDE), BF),
            shaped((8, 16, 768), BF),
            shaped((1024, WIDE), BF),
            shaped((2, 1024, 128), BF),
            shaped((2, 8, 1024, 128), BF),
            shaped((1024, 128), F32),
            shaped((1024, 128), F32),
        ),
        [VMEM] * 11 + [SMEM, SMEM, VMEM],
        (ANY,) * 11,
        [
            pltpu.VMEM((8, 128, WIDE), BF),
            pltpu.VMEM((8, 8, 16, 256), BF),
            pltpu.VMEM((1024, WIDE), BF),
            pltpu.VMEM((2, 1024, 128), BF),
            pltpu.VMEM((1024, 128), F32),
            pltpu.VMEM((1024, 128), F32),
            pltpu.VMEM((128, WIDE), BF),
            pltpu.VMEM((128, WIDE), BF),
            pltpu.VMEM((8, 16, 256), BF),
            pltpu.VMEM((8, 16, 768), BF),
            pltpu.VMEM((16, WIDE), BF),
            pltpu.VMEM((48, WIDE), BF),
            pltpu.VMEM((8, 16, WIDE), BF),
            pltpu.VMEM((8, 16, 256), BF),
            pltpu.VMEM((1024, 128), BF),
            DMA((6,)),
        ]
        + RowGather.sems * 2
        + Swap.sems
        + RingGather.sems * 3
        + RowGather.sems * 2
        + Swap.sems
        + RingGather.sems
        + CrossGather.sems
        + [DMA((16,)), DMA((16,))],
        (
            hidden_t, cot_t, w_q, w_k, w_v, w_o, w_gate, w_up, w_down, gain1, gain2, lengths,
            span_order, freq,
        ),
    )


def inverse_rms(v):
    return lax.rsqrt(jnp.sum(v * v, axis=1, keepdims=True) * (1.0 / WIDTH) + EPSILON)


def feed(att, w2own, wo, rows, wd, cot):
    def kernel(
        att, w2own, wo_in, rows_in, wd_in, cot_in,
        outp_out, resid_out, d_resid, d_heads, gwo_out, gw2_sum, gwd_sum,
        wo, x_in, wd, cot, ins, atts, w2, packed, d_act, resid, normed, act, d_both, dmn, outp,
        gw2, gwd, da, gwo, *refs,
    ):
        a, a2, b, b2, s, r1, r2, t1, t2 = split(refs, (3, 3, 3, 3, 3, 6, 6, 6, 6))
        x, z, y, c = place()
        me = y * 2 + c
        partners = hail("xf")
        pairs = ((wo_in, wo), (cot_in, cot), (wd_in, wd), (rows_in, x_in))
        held = [fetch(src, dst, ins.at[n]) for n, (src, dst) in enumerate(pairs)]
        pl.semaphore_wait(pltpu.get_barrier_semaphore(), partners)
        gathers = []
        for k, own in ((0, a), (512, a2)):
            spot = pl.ds(k, 512)
            gathers.append(RowGather(att.at[spot], atts.at[:, spot], *own))
        low, high = pl.ds(0, 4), pl.ds(4, 4)
        ring_a = RingGather(w2own.at[low], w2.at[:, low], half_lead, *b)
        ring_b = CrossGather(w2own.at[high], w2.at[:, high], half_lead, *b2)
        for part in gathers + [ring_a, ring_b]:
            part.start()

        def place_rows(n, size):
            return pl.ds(pl.multiple_of(n * size, size), size)

        held[0].wait()
        whole = jnp.concatenate([wo[f, g] for g in range(8) for f in range(8)], axis=0)

        def pack(n):
            j = lax.broadcasted_iota(jnp.int32, (512, WIDE), 0) + n * 512
            k = lax.broadcasted_iota(jnp.int32, (512, WIDE), 1)
            hit = ((k // 16) * 15 + k % 16 == j) & (k % 16 < 15)
            packed[pl.ds(n * 512, 512), :] = dot(
                jnp.where(hit, 1.0, 0.0).astype(BF), whole
            ).astype(BF)

        pack(0)
        ring_a.relay_z()
        gathers[0].relay()
        ring_b.relay()
        ring_a.relay_x(0)
        gathers[1].relay()
        pack(1)
        held[1].wait()
        held[2].wait()

        @pl.loop(0, 2)
        def _(n):
            part = place_rows(n, 512)
            d_act[part, :] = dot_nt(cot[part, :], wd[...])

        ring_a.relay_x(1)
        ring_b.far()
        held[3].wait()
        for n, gather in enumerate(gathers):
            gather.land()
            gather.finish()
            part = pl.ds(512 * n, 512)
            heads = jnp.concatenate([atts[f, part, :] for f in range(8)], axis=1)
            v = x_in[part, :].astype(F32) + dot(heads, packed[...])
            resid[part, :] = v
            normed[part, :] = (v * inverse_rms(v)).astype(BF)

        ring_a.land(0)
        ring_a.land(1)
        ring_b.land()
        ring_a.finish()
        ring_b.finish()
        w2_all = w2.reshape(WIDE, 768)

        @pl.loop(0, 2)
        def _(n):
            part = place_rows(n, 512)
            both = dot(normed[part, :], w2_all[...])
            gate, up = both[:, 0:384], both[:, 384:768]
            sigma = 1.0 / (1.0 + jnp.exp(-gate))
            silu = gate * sigma
            act[part, :] = (silu * up).astype(BF)
            d = d_act[part, :]
            d_both[part, 0:384] = (d * up * sigma * (1.0 + gate * (1.0 - sigma))).astype(BF)
            d_both[part, 384:768] = (d * silu).astype(BF)

        sums = [RowSum(dmn.at[:, pl.ds(k, 64)], *own) for k, own in ((0, r1), (64, r2))]
        ring_2, ring_d = RingSum(gw2, False, *t1), CrossSum(gwd, True, *t2)

        def back(core):
            to = [((y + n) % 4) * 2 + core for n in (2, 1, 3, 0)]
            v = jnp.concatenate([d_both[place_rows(n, 128), :] for n in to], axis=0)
            v = dot_nt(v, w2_all[...]).astype(BF)
            for n in range(4):
                dmn[to[n]] = v[128 * n : 128 * n + 128]

        order = [(2, 1), (2, 0), (1, 1), (3, 1), (1, 0), (3, 0), (0, 1), (0, 0)]
        where = [((x + p) % 4) * 2 + (1 - z if q else z) for p, q in order]

        def weights(which):
            v = jnp.concatenate([normed[:, place_rows(where[n], 128)] for n in which], axis=1)
            v = dot_tn(v, d_both[...]).astype(BF)
            for n, m in enumerate(which):
                gw2[where[m]] = v[128 * n : 128 * n + 128].reshape(8, 16, 768)

        weights((0, 1))
        ring_2.start(0)
        ring_2.start(1)
        back(1 - c)
        for d in (2, 1, 3, 0):
            for part in sums:
                part.hand(d)
        gwd[...] = dot_tn(act[...], cot[...]).astype(BF).reshape(8, 48, WIDE)
        for d in (2, 1, 3, 0):
            ring_d.hand(d)
        back(c)
        for part in sums:
            part.far()
        weights((2, 3, 4, 5, 6, 7))
        ring_2.relay(0)
        for part in sums:
            part.near()
        ring_2.relay(1)
        ring_d.far()

        @pl.loop(0, 2)
        def _(n):
            v = dot(act[place_rows(n, 512), :], wd[...]).astype(BF)
            for k in range(4):
                outp[n * 4 + k] = v[128 * k : 128 * k + 128]

        written = [fetch(outp, outp_out, ins.at[5])]
        ring_d.near()

        mine = place_rows(me, 128)
        v = resid[mine, :]
        inv = inverse_rms(v)
        e = jnp.concatenate([part.total() for part in sums], axis=0)
        mean = jnp.sum(e * v, axis=1, keepdims=True) * (1.0 / WIDTH)
        d_v = cot[mine, :].astype(F32) + inv * e - v * (inv * inv * inv * mean)
        d_resid[...] = d_v
        mixed = d_v.astype(BF)
        d_att = dot_nt(mixed, packed[...]).astype(BF)
        for f in range(8):
            da[f] = d_att[:, f * 128 : (f + 1) * 128]
        swap = Swap(da, d_heads, *s)
        swap.start()
        spread = spread_value(WIDE)
        heads = jnp.concatenate([atts[f, mine, :] for f in range(8)], axis=1)
        gw = dot_tn(dot(heads, spread).astype(BF), mixed).astype(BF)
        for g in range(8):
            for f in range(8):
                n = (8 * g + f) * 16
                gwo[f, g * 16 : (g + 1) * 16, :] = gw[n : n + 16]
        written += [fetch(gwo, gwo_out, ins.at[4])]
        ring_2.total(0)
        resid_out[...] = v
        gw2_sum[...] = ring_2.total(1).astype(BF)
        gwd_sum[...] = ring_d.total()
        swap.finish()
        for part in sums:
            part.finish()
        ring_2.finish()
        ring_d.finish()
        for copy in written:
            copy.wait()

    return comm_call(
        "feed",
        3,
        kernel,
        (
            shaped((8, 128, WIDE), BF),
            shaped((128, WIDE), F32),
            shaped((128, WIDE), F32),
            shaped((8, 128, 128), BF),
            shaped((8, 128, WIDE), BF),
            shaped((8, 16, 768), BF),
            shaped((48, WIDE), F32),
        ),
        [ANY] * 6,
        (ANY, VMEM, VMEM, ANY, ANY, VMEM, VMEM),
        [
            pltpu.VMEM((8, 8, 16, WIDE), BF),
            pltpu.VMEM((1024, WIDE), BF),
            pltpu.VMEM((384, WIDE), BF),
            pltpu.VMEM((1024, WIDE), BF),
            DMA((6,)),
            pltpu.VMEM((8, 1024, 128), BF),
            pltpu.VMEM((8, 8, 16, 768), BF),
            pltpu.VMEM((WIDE, WIDE), BF),
            pltpu.VMEM((1024, 384), F32),
            pltpu.VMEM((1024, WIDE), F32),
            pltpu.VMEM((1024, WIDE), BF),
            pltpu.VMEM((1024, 384), BF),
            pltpu.VMEM((1024, 768), BF),
            pltpu.VMEM((8, 128, WIDE), BF),
            pltpu.VMEM((8, 128, WIDE), BF),
            pltpu.VMEM((8, 8, 16, 768), BF),
            pltpu.VMEM((8, 48, WIDE), BF),
            pltpu.VMEM((8, 128, 128), BF),
            pltpu.VMEM((8, 128, WIDE), BF),
        ]
        + RowGather.sems * 2
        + RingGather.sems
        + CrossGather.sems
        + Swap.sems
        + RowSum.scratch((64, WIDE)) * 2
        + RingSum.scratch((8, 16, 768), False)
        + CrossSum.scratch((48, WIDE), True),
        (att, w2own, wo, rows, wd, cot),
    )


def last(
    dkv, gwo, outp, dq, cos_t, sin_t, w1, normed, rows, resid, d_resid, gw2s, gwd, gain1, gain2,
    w_q, w_k, w_v, w_gate, w_up,
):
    def kernel(
        dkv, gwo_in, outp_in, dq_in, cos_in, sin_in, w1_in, normed_in, rows_in, resid, dr, gw2s, wd,
        gain1, gain2,
        w_q, w_k, w_v, w_gate, w_up,
        output, gh, g_attn, g_mlp, g_q, g_k, g_v, g_o, g_gate, g_up, g_down,
        own, gwo, outp, dq, cos_t, sin_t, w1, normed, rows, ins,
        blk_a, blk_b, from_core, gwos, gw1, dnq, d_kv, dn, one, two, gw1s, hs, hr, *refs,
    ):
        a, a2, b, b2, d, d2, e, e2, s1, s2 = split(refs, (6, 6, 6, 6, 6, 6, 6, 6, 3, 3))
        x, z, y, c = place()
        me = y * 2 + c
        partners = hail("xf")
        pairs = [
            (gwo_in, gwo),
            (dkv.at[c], own),
            (dq_in, dq),
            (cos_in, cos_t),
            (sin_in, sin_t),
            (w1_in, w1),
            (normed_in, normed),
            (rows_in.at[me], rows),
            (outp_in, outp),
        ]
        held = {n: fetch(*pairs[n], ins.at[n]) for n in (0, 8, 1)}
        pl.semaphore_wait(pltpu.get_barrier_semaphore(), partners)
        order = [(2, 1), (2, 0), (1, 1), (3, 1), (0, 1), (1, 0), (3, 0), (0, 0)]
        where = [((x + p) % 4) * 2 + (1 - z if q else z) for p, q in order]
        sum_w = RowSum(gwo, *b, source=gwo_in)
        sum_o = RowSum(outp, *b2, source=outp_in)
        ring_a, ring_b = RingSum(blk_a, False, *a), CrossSum(blk_b, False, *a2)
        hand = {}

        def pass_on(n):
            hand[n] = send(
                dkv.at[1 - c, where[n]], from_core.at[n], hs.at[n], hr.at[n], at(x, z, y, 1 - c)
            )

        swap2 = Swap(gw2s, two, *s2)
        swap2.start()
        sum_w.hand(2)
        sum_o.hand(2)
        pass_on(0)
        pass_on(1)
        for step in (1, 3):
            sum_w.hand(step)
            sum_o.hand(step)
        for n in (2, 3, 4):
            pass_on(n)
        sum_w.hand(0)
        sum_o.hand(0)
        for n in (5, 6, 7):
            pass_on(n)
        for n in range(2, 8):
            held[n] = fetch(*pairs[n], ins.at[n])

        def fold(n):
            g = where[n]
            hand[n].wait_recv()
            both = (own[g].astype(F32) + from_core[n].astype(F32)).astype(BF)
            blk_a[g] = both[0:512]
            blk_b[g] = both[512:1024]

        held[0].wait()
        sum_w.far()
        held[8].wait()
        sum_o.far()
        held[1].wait()
        fold(0)
        ring_a.start(0)
        ring_b.hand(2)
        fold(1)
        ring_a.start(1)
        for n, step in ((2, 1), (3, 3), (4, 0)):
            fold(n)
            ring_b.hand(step)
        ring_a.relay(0)
        ring_b.far()
        fold(5)
        fold(6)
        ring_a.relay(1)
        sum_w.near()
        fold(7)
        ring_b.near()
        ring_a.total(0)
        sum_o.near()
        for n in range(2, 6):
            held[n].wait()
        spread = spread_value(WIDTH)
        gains = columns_of_gains(gain1, gain2)

        def place_rows(n, size):
            return pl.ds(pl.multiple_of(n * size, size), size)

        def queries(n):
            part = place_rows(n, 512)
            v = dq[part, :]
            v = (v * cos_t[part, :] - partner(v) * sin_t[part, :]).astype(BF)
            d_kv[part, 0:128] = v
            dnq[part, :] = dot_nt(v, w1[:, 0:128])

        queries(0)
        queries(1)
        held[6].wait()
        gw1[:, :, :, 0:128] = (
            dot_tn(normed[...], d_kv[:, 0:128]).astype(BF).reshape(8, 8, 16, 128)
        )
        gwos[...] = sum_w.total().astype(BF).reshape(8, 16, WIDE)
        swap2.finish()
        total = jnp.zeros((15, 1), F32)
        for m, ref, w in ((0, g_gate, w_gate), (384, g_up, w_up)):
            for n in range(0, 8, 2):
                part = jnp.concatenate(
                    [
                        two[f, :, m + 48 * k : m + 48 * k + 40].astype(F32)[0:15]
                        for k in (n, n + 1)
                        for f in range(8)
                    ],
                    axis=1,
                )
                spot = pl.ds(n * 320, 640)
                ref[:, spot] = part * gains[:, 1:2]
                total += jnp.sum(part * w[:, spot].astype(F32), axis=1, keepdims=True)
        g_mlp[...] = row_of(total)

        def squeeze(v):
            top = v.astype(BF)
            low = (v - top.astype(F32)).astype(BF)
            return dot_nt(top, spread) + dot_nt(low, spread)

        g_down[...] = squeeze(wd[...])[0:40]
        output[...] = dot_nt(spread, (resid[...] + sum_o.total()).astype(BF)).astype(BF)

        v = jnp.concatenate([ring_a.total(1), ring_b.total()], axis=0)
        turned = v * cos_t[...] - partner(v) * sin_t[...]
        d_kv[:, 128:256] = jnp.where(lanes_of((1024, 128)) < 64, turned, v).astype(BF)
        sums = [RowSum(dn.at[:, pl.ds(k, 64)], *own) for k, own in ((0, d), (64, d2))]

        def back(core):
            to = [((y + n) % 4) * 2 + core for n in (2, 1, 3, 0)]
            parts = [place_rows(n, 128) for n in to]
            v = jnp.concatenate([d_kv[p, 128:256] for p in parts], axis=0)
            v = dot_nt(v, w1[:, 128:256])
            for n, p in enumerate(parts):
                dn[to[n]] = (dnq[p, :] + v[128 * n : 128 * n + 128]).astype(BF)

        back(1 - c)
        for n in (2, 1, 3, 0):
            for part in sums:
                part.hand(n)
        ring_1 = RingSum(gw1, False, *e)

        def weights_k(which):
            parts = [place_rows(where[n], 128) for n in which]
            v = jnp.concatenate([normed[:, p] for p in parts], axis=1)
            v = dot_tn(v, d_kv[:, 128:256]).astype(BF)
            for n, m in enumerate(which):
                gw1[where[m], :, :, 128:256] = v[128 * n : 128 * n + 128].reshape(8, 16, 128)

        weights_k((0, 1))
        ring_1.start(0)
        ring_1.start(1)
        ring_o = RingSum(gwos, True, *e2)
        ring_o.start(0)
        ring_o.start(1)
        back(c)
        for part in sums:
            part.far()
        weights_k((2, 3, 4, 5, 6, 7))
        for part in sums:
            part.near()
        for k in (0, 1):
            ring_1.relay(k)
            ring_o.relay(k)
        ring_1.total(0)
        ring_o.total(0)
        gw1s[...] = ring_1.total(1).astype(BF)
        swap1 = Swap(gw1s, one, *s1)
        swap1.start()
        g_o[...] = squeeze(ring_o.total(1))[0:15]

        held[7].wait()
        xs = rows[...].astype(F32)
        inv = inverse_rms(xs)
        t = jnp.concatenate([part.total() for part in sums], axis=0)
        mean = jnp.sum(t * xs, axis=1, keepdims=True) * (1.0 / WIDTH)
        d_x = dr[...] + inv * t - xs * (inv * inv * inv * mean)
        gh[...] = dot_nt(spread, d_x.astype(BF)).astype(BF)
        swap1.finish()
        ones = [one[f].astype(F32)[0:15] for f in range(8)]
        r_q = jnp.concatenate([v[:, 0:128] for v in ones], axis=1)[:, 0:WIDTH]

        def heads(n):
            return jnp.concatenate(
                [
                    sum(ones[f][:, n : n + 64] for f in range(8) if OWNED_KV[f] == h)
                    for h in range(5)
                ],
                axis=1,
            )

        total = jnp.zeros((15, 1), F32)
        for part, w, ref in ((r_q, w_q, g_q), (heads(128), w_k, g_k), (heads(192), w_v, g_v)):
            ref[...] = part * gains[:, 0:1]
            total += jnp.sum(part * w[...].astype(F32), axis=1, keepdims=True)
        g_attn[...] = row_of(total)
        for copy in hand.values():
            copy.wait_send()
        ring_a.finish()
        ring_b.finish()
        ring_1.finish()
        ring_o.finish()
        sum_w.finish()
        sum_o.finish()
        for part in sums:
            part.finish()

    return comm_call(
        "last",
        6,
        kernel,
        (
            shaped((WIDTH, 128), BF),
            shaped((WIDTH, 128), BF),
            shaped((15,), F32),
            shaped((15,), F32),
            shaped((15, WIDTH), F32),
            shaped((15, 320), F32),
            shaped((15, 320), F32),
            shaped((15, WIDTH), F32),
            shaped((15, 2560), F32),
            shaped((15, 2560), F32),
            shaped((40, WIDTH), F32),
        ),
        [ANY] * 9 + [VMEM] * 11,
        (VMEM,) * 11,
        [
            pltpu.VMEM((8, 1024, 128), BF),
            pltpu.VMEM((8, 128, WIDE), BF),
            pltpu.VMEM((8, 128, WIDE), BF),
            pltpu.VMEM((1024, 128), F32),
            pltpu.VMEM((1024, 128), F32),
            pltpu.VMEM((1024, 128), F32),
            pltpu.VMEM((WIDE, 256), BF),
            pltpu.VMEM((1024, WIDE), BF),
            pltpu.VMEM((128, WIDE), BF),
            DMA((9,)),
            pltpu.VMEM((8, 512, 128), BF),
            pltpu.VMEM((8, 512, 128), BF),
            pltpu.VMEM((8, 1024, 128), BF),
            pltpu.VMEM((8, 16, WIDE), BF),
            pltpu.VMEM((8, 8, 16, 256), BF),
            pltpu.VMEM((1024, WIDE), F32),
            pltpu.VMEM((1024, 256), BF),
            pltpu.VMEM((8, 128, WIDE), BF),
            pltpu.VMEM((8, 16, 256), BF),
            pltpu.VMEM((8, 16, 768), BF),
            pltpu.VMEM((8, 16, 256), BF),
            DMA((8,)),
            DMA((8,)),
        ]
        + RingSum.scratch((512, 128), False)
        + CrossSum.scratch((512, 128), False)
        + RowSum.scratch((128, WIDE)) * 2
        + RowSum.scratch((64, WIDE)) * 2
        + RingSum.scratch((8, 16, 256), False)
        + RingSum.scratch((16, WIDE), True)
        + Swap.sems * 2,
        (
            dkv, gwo, outp, dq, cos_t, sin_t, w1, normed, rows, resid, d_resid, gw2s, gwd, gain1,
            gain2, w_q, w_k, w_v, w_gate, w_up,
        ),
    )


def lanes_of(shape):
    return lax.broadcasted_iota(jnp.int32, shape, len(shape) - 1)


def partner(v):
    lane = lanes_of(v.shape)
    return jnp.where(lane % 64 < 32, pltpu.roll(v, 96, 1), pltpu.roll(v, 32, 1))


def doc_ends(lengths):
    return lengths[0], lengths[0] + lengths[1]


def doc_start(pos, ends):
    return jnp.where(pos < ends[0], 0, jnp.where(pos < ends[1], ends[0], ends[1]))

def layout(order, inverse):
    @pl.loop(0, 64)
    def _(n):
        inverse[order[n]] = n

    i = lax.axis_index("ctx")
    f = i % 8
    upper = (f == 3) | (f == 5)
    return i // 8, (
        jnp.where(upper, 1, 0),
        jnp.where(upper | (f == 1) | (f == 4), 1, 0),
    )


def key_range(span, ends):
    begin = doc_start(span * 128, ends) // 128
    count = span - begin + 1
    runs = (count + 3) // 8
    return begin, runs, jnp.where(count > runs * 8, 1, 0)


def attend(lengths, order, q, kv):
    def kernel(lengths, order, q_ref, kv_ref, o_ref, lse_ref, s_ref, inverse):
        group, sel = layout(order, inverse)
        ends = doc_ends(lengths)

        @pl.loop(0, 8)
        def _(b):
            span = order[group * 8 + b]
            begin, runs, rest = key_range(span, ends)
            pos = span * 128 + lanes_of((1, 256)) % 128
            low = doc_start(pos, ends)
            rows = pl.ds(pl.multiple_of(b * 128, 128), 128)
            none = jnp.zeros((128, 128), BF)
            pair = jnp.concatenate(
                [
                    jnp.concatenate([q_ref[0, rows, :], none], axis=1),
                    jnp.concatenate([none, q_ref[1, rows, :]], axis=1),
                ],
                axis=0,
            )

            def load(h, t, n):
                return jnp.concatenate(
                    [
                        kv_ref[sel[h], pl.ds(inverse[jnp.minimum(t + i, 63)] * 128, 128), :]
                        for i in range(n)
                    ],
                    axis=0,
                )

            def held(t, n):
                return pl.ds(pl.multiple_of((t - begin) * 128, 512), n * 128)

            def scores(n, t, high):
                kpos = t * 128 + lax.broadcasted_iota(jnp.int32, (n * 128, 1), 0)
                allowed = (kpos >= low) & (kpos <= pos)
                keys = jnp.concatenate([load(0, t, n), load(1, t, n)], axis=1)
                s = jnp.where(allowed, dot_nt(keys, pair), MASKED)
                s_ref[held(t, n), :] = s
                return jnp.maximum(high, jnp.max(s.reshape(n * 16, 8, 256), axis=0))

            def over(step, state):
                state = lax.fori_loop(0, runs, lambda j, v: step(8, begin + j * 8, v), state)
                return lax.fori_loop(0, rest, lambda j, v: step(4, begin + runs * 8, v), state)

            high = over(scores, jnp.full((8, 256), MASKED, F32))
            high = jnp.max(high, axis=0, keepdims=True)

            def weigh(n, t, state):
                total, acc = state
                p = jnp.exp(s_ref[held(t, n), :] - high)
                total = total + jnp.sum(p.reshape(n * 16, 8, 256), axis=0)
                values = jnp.where(lanes_of((n * 128, 128)) < 64, pltpu.roll(load(0, t, n), 64, 1), load(1, t, n))
                return total, acc + dot_tn(values, p.astype(BF))

            total, acc = over(weigh, (jnp.zeros((8, 256), F32), jnp.zeros((128, 256), F32)))
            total = jnp.sum(total, axis=0, keepdims=True)
            lse = high + jnp.log(total)
            lse_ref[b, 0:1, :] = lse[:, 0:128]
            lse_ref[b, 1:2, :] = lse[:, 128:256]
            acc = acc / total
            acc = jnp.concatenate([acc[0:64, 0:128], acc[64:128, 128:256]], axis=0)
            o_ref[rows, :] = acc.T.astype(BF)

    return pl.pallas_call(
        kernel,
        in_specs=[SMEM, SMEM, VMEM, VMEM],
        out_specs=(VMEM, VMEM),
        scratch_shapes=[pltpu.VMEM((40 * 128, 256), F32), pltpu.SMEM((64,), jnp.int32)],
        out_shape=(shaped((1024, 128), BF), shaped((8, 8, 128), F32)),
        compiler_params=pltpu.CompilerParams(vmem_limit_bytes=LIMIT),
        name="attend",
    )(lengths, order, q, kv)


def attend_back(lengths, order, q, kv, d_att, att, lse):
    def kernel(
        lengths, order, q_ref, kv_in, d_ref, o_ref, lse_ref, dq_ref, dkv_out, acc_ref, inverse,
        kv_ref, dkv_ref, sems,
    ):
        held = fetch(kv_in, kv_ref, sems.at[16])
        lane = lanes_of((128, 128))
        group, sel = layout(order, inverse)
        ends = doc_ends(lengths)

        @pl.loop(0, 16)
        def _(n):
            for s in (0, 1):
                part = pl.ds(pl.multiple_of(n * 512, 512), 512)
                acc_ref[s, part, :] = jnp.zeros((512, 128), F32)

        held.wait()

        @pl.loop(0, 8)
        def _(b):
            span = order[group * 8 + b]
            begin, runs, rest = key_range(span, ends)
            pos = span * 128 + lanes_of((1, 128))
            low = doc_start(pos, ends)
            rows = pl.ds(pl.multiple_of(b * 128, 128), 128)
            d_both = d_ref[rows, :].astype(F32)
            d_pad = (
                jnp.where(lane >= 64, pltpu.roll(d_both, 64, 1), 0.0).astype(BF),
                jnp.where(lane >= 64, d_both, 0.0).astype(BF),
            )
            pair = [jnp.concatenate([q_ref[h, rows, :], d_pad[h]], axis=0) for h in (0, 1)]
            mixed = (d_both * o_ref[rows, :].astype(F32)).T
            delta = [jnp.sum(mixed[64 * h : 64 * h + 64], axis=0, keepdims=True) for h in (0, 1)]
            lses = [lse_ref[b, h : h + 1, :] for h in (0, 1)]

            def step(n, t, state):
                where = [inverse[jnp.minimum(t + i, 63)] * 128 for i in range(n)]
                where = [pl.ds(pl.multiple_of(v, 128), 128) for v in where]
                kpos = t * 128 + lax.broadcasted_iota(jnp.int32, (n * 128, 1), 0)
                allowed = (kpos >= low) & (kpos <= pos)
                d_ss, kvs = [], []
                for h in (0, 1):
                    kv_t = jnp.concatenate([kv_ref[sel[h], w, :] for w in where], axis=0)
                    kvs.append(kv_t)
                    both = dot_nt(kv_t, pair[h])
                    p = jnp.where(allowed, jnp.exp(both[:, 0:128] - lses[h]), 0.0)
                    d_s = (p * (both[:, 128:256] - delta[h])).astype(BF)
                    d_ss.append(d_s)
                    d_kv = dot(jnp.concatenate([d_s, p.astype(BF)], axis=1), pair[h])
                    for i, w in enumerate(where):
                        acc_ref[sel[h], w, :] += d_kv[i * 128 : (i + 1) * 128]
                lanes = lanes_of((n * 128, 128))
                keys = jnp.where(lanes < 64, kvs[0], pltpu.roll(kvs[1], 64, 1))
                return state + dot_tn(keys, jnp.concatenate(d_ss, axis=1))

            state = jnp.zeros((128, 256), F32)
            state = lax.fori_loop(0, runs, lambda j, v: step(8, begin + j * 8, v), state)
            state = lax.fori_loop(0, rest, lambda j, v: step(4, begin + runs * 8, v), state)
            state = jnp.concatenate([state[0:64, 0:128], state[64:128, 128:256]], axis=0)
            dq_ref[rows, :] = state.T * 0.125

        written = []
        for n in range(8):
            for s in (0, 1):
                part = pl.ds(n * 1024, 1024)
                dkv_ref[s, part, :] = acc_ref[s, part, :].astype(BF)
                written.append(
                    fetch(dkv_ref.at[s, part], dkv_out.at[s, part], sems.at[2 * n + s])
                )
        for copy in written:
            copy.wait()

    return pl.pallas_call(
        kernel,
        in_specs=[SMEM, SMEM, VMEM, ANY] + [VMEM] * 3,
        out_specs=(VMEM, ANY),
        scratch_shapes=[
            pltpu.VMEM((2, 8192, 128), F32),
            pltpu.SMEM((64,), jnp.int32),
            pltpu.VMEM((2, 8192, 128), BF),
            pltpu.VMEM((2, 8192, 128), BF),
            DMA((17,)),
        ],
        out_shape=(shaped((1024, 128), F32), shaped((2, 8192, 128), BF)),
        compiler_params=pltpu.CompilerParams(vmem_limit_bytes=LIMIT),
        name="attend_back",
    )(lengths, order, q, kv, d_att, att, lse)


def hand_out(parts):
    def kernel(*refs):
        for src, dst in zip(refs[: len(parts)], refs[len(parts) :]):
            dst[...] = src[...]

    return pl.pallas_call(
        kernel,
        out_shape=tuple(shaped(v.shape, v.dtype) for v in parts),
        in_specs=[VMEM] * len(parts),
        out_specs=(VMEM,) * len(parts),
        compiler_params=pltpu.CompilerParams(vmem_limit_bytes=LIMIT),
        name="hand_out",
    )(*parts)


def local(
    hidden, attn_gain, w_q, w_k, w_v, w_o, mlp_gain, w_gate, w_up, w_down, cotangent,
    doc_lengths, span_order,
):
    frequency = ROPE_BASE ** (-2.0 * (np.arange(128) % 32) / HEAD)
    frequency = jnp.asarray(frequency, F32).reshape(1, 128)

    rows, w1, wds, wo, cot, w2own, normed, q, kv, cos_t, sin_t = first(
        hidden.T, cotangent.T, w_q, w_k, w_v, w_o, w_gate, w_up, w_down, attn_gain, mlp_gain,
        doc_lengths, span_order, frequency,
    )
    kv = kv.reshape(2, 8192, 128)
    att, lse = attend(doc_lengths, span_order, q, kv)
    outp, resid, d_resid, d_heads, gwo, gw2s, gwds = feed(
        att, w2own, wo, rows.reshape(1024, WIDE), wds.reshape(384, WIDE), cot.reshape(1024, WIDE)
    )
    d_att = d_heads.reshape(1024, 128)
    dq, dkv = attend_back(doc_lengths, span_order, q, kv, d_att, att, lse)
    grads = last(
        dkv.reshape(2, 8, 1024, 128), gwo, outp, dq, cos_t, sin_t, w1.reshape(WIDE, 256), normed,
        rows, resid, d_resid, gw2s, gwds, attn_gain, mlp_gain, w_q, w_k, w_v, w_gate, w_up,
    )
    output, grad_hidden, g_attn, g_mlp, g_q, g_k, g_v, g_o, g_gate, g_up, g_down = hand_out(grads)
    return (
        output.T, grad_hidden.T, g_attn, g_q, g_k, g_v, g_o, g_mlp, g_gate, g_up, g_down
    )


def solution(mesh):
    both = ("fsdp", "ctx")
    wide, thin, part = P(both, None), P(both), P("fsdp")
    return jax.shard_map(
        local,
        mesh=mesh,
        in_specs=(wide, thin, wide, wide, wide, wide, thin, wide, wide, wide, wide, part, part),
        out_specs=(wide, wide, thin, wide, wide, wide, wide, thin, wide, wide, wide),
        check_vma=False,
    )
```

```python
import jax
import jax.numpy as jnp
import numpy as np
from jax import lax
from jax.experimental import pallas as pl
from jax.experimental.pallas import tpu as pltpu
from jax.sharding import PartitionSpec as P

HEAD = 64
EPSILON = 1e-05
ROPE_BASE = 100000.0
MASKED = -1e30
WIDE = 1024
WIDTH = 960
BF = jnp.bfloat16
F32 = jnp.float32
MESH = pl.DeviceIdType.MESH
DMA = pltpu.SemaphoreType.DMA
ANY = pl.BlockSpec(memory_space=pl.ANY)
VMEM = pl.BlockSpec(memory_space=pltpu.VMEM)
SMEM = pl.BlockSpec(memory_space=pltpu.SMEM)
LIMIT = 56 * 2**20
OWNED_KV = (0, 1, 1, 2, 2, 3, 4, 4)


def dot(a, b):
    return lax.dot_general(a, b, (((1,), (0,)), ((), ())), preferred_element_type=F32)


def dot_nt(a, b):
    return lax.dot_general(a, b, (((1,), (1,)), ((), ())), preferred_element_type=F32)


def dot_tn(a, b):
    return lax.dot_general(a, b, (((0,), (0,)), ((), ())), preferred_element_type=F32)


def shaped(shape, dtype):
    return jax.ShapeDtypeStruct(shape, dtype)


def place():
    i = lax.axis_index("ctx")
    return i // 16, (i // 8) % 2, (i // 2) % 4, i % 2


def at(x, z, y, c):
    return {"ctx": (((x + 4) % 4) * 2 + z) * 8 + ((y + 4) % 4) * 2 + c}


def send(src, dst, ssem, rsem, device):
    copy = pltpu.make_async_remote_copy(
        src, dst, ssem, rsem, device_id=device, device_id_type=MESH
    )
    copy.start()
    return copy


def hail(kinds):
    x, z, y, c = place()
    who = []
    if "x" in kinds:
        who += [at(x + 1, z, y, c), at(x - 1, z, y, c), at(x, 1 - z, y, c)]
    if "f" in kinds:
        who += [at(x, z, y + d, (c + e) % 2) for d in range(4) for e in range(2) if d + e]
    elif "y" in kinds:
        who += [at(x, z, y + d, c) for d in (1, 2, 3)] + [at(x, z, y, 1 - c)]
    barrier = pltpu.get_barrier_semaphore()
    for device in who:
        pl.semaphore_signal(barrier, inc=1, device_id=device, device_id_type=MESH)
    return len(who)


def greet(kinds):
    pl.semaphore_wait(pltpu.get_barrier_semaphore(), hail(kinds))


def half_lead(ref, k):
    n = ref.shape[0] // 2
    return ref.at[pl.ds(k * n, n)]


def half_lanes(ref, k):
    n = ref.shape[-1] // 2
    return ref.at[:, pl.ds(k * n, n)]


class RingGather:
    sems = [DMA((9,)), DMA((9,)), DMA(())]

    def __init__(self, src, dst, half, ssem, rsem, lsem, arrived=None):
        self.src, self.dst, self.half = src, dst, half
        self.ssem, self.rsem, self.lsem = ssem, rsem, lsem
        self.arrived = arrived or (lambda block: None)
        self.copies = {}

    def push(self, n, src, dst, device):
        self.copies[n] = send(src, dst, self.ssem.at[n], self.rsem.at[n], device)

    def start(self):
        x, z, y, c = place()
        me = self.dst.at[x * 2 + z]
        self.push(0, self.src, me, at(x, 1 - z, y, c))
        self.push(1, self.src, me, at(x + 1, z, y, c))
        self.push(2, self.src, me, at(x - 1, z, y, c))
        self.local = pltpu.make_async_copy(self.src, me, self.lsem)
        self.local.start()

    def relay_z(self):
        x, z, y, c = place()
        block = self.dst.at[x * 2 + 1 - z]
        self.copies[0].wait_recv()
        self.push(3, block, block, at(x + 1, z, y, c))
        self.push(4, block, block, at(x - 1, z, y, c))
        self.arrived(x * 2 + 1 - z)

    def relay_x(self, k):
        x, z, y, c = place()
        zz = z if k == 0 else 1 - z
        left, right = ((x + 3) % 4) * 2 + zz, ((x + 1) % 4) * 2 + zz
        self.copies[1 + 2 * k].wait_recv()
        part = self.half(self.dst.at[left], 0)
        self.push(5 + 2 * k, part, part, at(x + 1, z, y, c))
        self.arrived(left)
        self.copies[2 + 2 * k].wait_recv()
        part = self.half(self.dst.at[right], 1)
        self.push(6 + 2 * k, part, part, at(x - 1, z, y, c))
        self.arrived(right)

    def land(self, k):
        x, z, y, c = place()
        zz = z if k == 0 else 1 - z
        self.copies[5 + 2 * k].wait_recv()
        self.copies[6 + 2 * k].wait_recv()
        self.arrived(((x + 2) % 4) * 2 + zz)

    def sent(self):
        for n in range(9):
            self.copies[n].wait_send()

    def finish(self):
        self.local.wait()
        self.sent()


class CrossGather:
    sems = [DMA((8,)), DMA((8,)), DMA(())]

    def __init__(self, src, dst, half, ssem, rsem, lsem, arrived=None):
        self.src, self.dst, self.half = src, dst, half
        self.ssem, self.rsem, self.lsem = ssem, rsem, lsem
        self.arrived = arrived or (lambda block: None)
        self.copies = {}

    def push(self, n, src, dst, device):
        self.copies[n] = send(src, dst, self.ssem.at[n], self.rsem.at[n], device)

    def start(self):
        x, z, y, c = place()
        me = self.dst.at[x * 2 + z]
        self.push(1, self.src, me, at(x + 1, z, y, c))
        self.push(2, self.src, me, at(x - 1, z, y, c))
        self.push(0, self.src, me, at(x, 1 - z, y, c))
        self.local = pltpu.make_async_copy(self.src, me, self.lsem)
        self.local.start()

    def relay(self):
        x, z, y, c = place()
        for n, step, side in ((1, 3, 0), (2, 1, 1)):
            block = ((x + step) % 4) * 2 + z
            whole = self.dst.at[block]
            self.copies[n].wait_recv()
            part = self.half(whole, side)
            self.push(2 + n, part, part, at(x + 4 - step, z, y, c))
            self.push(4 + n, whole, whole, at(x, 1 - z, y, c))
            self.arrived(block)

    def far(self):
        x, z, y, c = place()
        block = ((x + 2) % 4) * 2 + z
        whole = self.dst.at[block]
        self.copies[3].wait_recv()
        self.copies[4].wait_recv()
        self.push(7, whole, whole, at(x, 1 - z, y, c))
        self.arrived(block)

    def land(self):
        x, z, y, c = place()
        for n, step in ((0, 0), (5, 3), (6, 1), (7, 2)):
            self.copies[n].wait_recv()
            self.arrived(((x + step) % 4) * 2 + 1 - z)

    def finish(self):
        self.local.wait()
        for n in range(8):
            self.copies[n].wait_send()


class RowGather:
    sems = [DMA((8,)), DMA((8,)), DMA(())]

    def __init__(self, src, dst, ssem, rsem, lsem):
        self.src, self.dst = src, dst
        self.ssem, self.rsem, self.lsem = ssem, rsem, lsem
        self.copies = {}

    def push(self, n, src, dst, device):
        self.copies[n] = send(src, dst, self.ssem.at[n], self.rsem.at[n], device)

    def start(self):
        x, z, y, c = place()
        me = self.dst.at[y * 2 + c]
        self.push(1, self.src, me, at(x, z, y + 1, c))
        self.push(2, self.src, me, at(x, z, y - 1, c))
        self.push(0, self.src, me, at(x, z, y, 1 - c))
        self.local = pltpu.make_async_copy(self.src, me, self.lsem)
        self.local.start()

    def relay(self):
        x, z, y, c = place()
        for n, step, side in ((1, 3, 0), (2, 1, 1)):
            self.copies[n].wait_recv()
            block = self.dst.at[((y + step) % 4) * 2 + c]
            part = half_lead(block, side)
            self.push(2 + n, part, part, at(x, z, y + 4 - step, c))
            self.push(4 + n, block, block, at(x, z, y, 1 - c))

    def land(self):
        x, z, y, c = place()
        self.copies[3].wait_recv()
        self.copies[4].wait_recv()
        block = self.dst.at[((y + 2) % 4) * 2 + c]
        self.push(7, block, block, at(x, z, y, 1 - c))

    def finish(self):
        self.local.wait()
        for n in (0, 5, 6, 7):
            self.copies[n].wait_recv()
        for n in range(8):
            self.copies[n].wait_send()


class Swap:
    sems = [DMA((8,)), DMA((8,)), DMA(())]

    def __init__(self, src, dst, ssem, rsem, lsem):
        self.src, self.dst = src, dst
        self.ssem, self.rsem, self.lsem = ssem, rsem, lsem

    def start(self):
        x, z, y, c = place()
        me = y * 2 + c
        self.copies = []
        for d in (2, 1, 3, 0):
            for e in (0, 1):
                if d + e:
                    n = d * 2 + e
                    to = ((y + d) % 4) * 2 + (c + e) % 2
                    self.copies.append(
                        send(
                            self.src.at[to],
                            self.dst.at[me],
                            self.ssem.at[n],
                            self.rsem.at[n],
                            at(x, z, y + d, (c + e) % 2),
                        )
                    )
        self.local = pltpu.make_async_copy(self.src.at[me], self.dst.at[me], self.lsem)
        self.local.start()

    def finish(self):
        self.local.wait()
        for copy in self.copies:
            copy.wait()


class RowSum:
    @staticmethod
    def scratch(shape):
        return [
            pltpu.VMEM((4,) + shape, BF),
            pltpu.VMEM((4,) + shape, BF),
            pltpu.VMEM((2, shape[0] // 2) + shape[1:], BF),
            pltpu.VMEM((2,) + shape, BF),
            DMA((8,)),
            DMA((8,)),
        ]

    def __init__(self, blk, first, mixed, parts, heard, ssem, rsem, source=None):
        self.blk, self.first, self.mixed = blk, first, mixed
        self.source = blk if source is None else source
        self.parts, self.heard = parts, heard
        self.ssem, self.rsem = ssem, rsem
        self.copies = {}

    def push(self, n, src, dst, device):
        self.copies[n] = send(src, dst, self.ssem.at[n], self.rsem.at[n], device)

    def hand(self, d):
        x, z, y, c = place()
        to = ((y + d) % 4) * 2 + 1 - c
        self.push(d, self.source.at[to], self.first.at[d], at(x, z, y, 1 - c))

    def start(self):
        for d in (2, 1, 3, 0):
            self.hand(d)

    def both(self, d):
        x, z, y, c = place()
        self.copies[d].wait_recv()
        return self.blk.at[((y + d) % 4) * 2 + c][...].astype(F32) + self.first[d].astype(F32)

    def far(self):
        x, z, y, c = place()
        self.mixed[2] = self.both(2).astype(BF)
        for side, step in ((0, 1), (1, 3)):
            part = half_lead(self.mixed.at[2], side)
            self.push(4 + side, part, self.parts.at[side], at(x, z, y + step, c))

    def near(self):
        x, z, y, c = place()
        for side, step in ((0, 1), (1, 3)):
            sums = self.both(step)
            n = sums.shape[0] // 2
            self.copies[4 + side].wait_recv()
            part = self.parts[side].astype(F32)
            self.mixed[step, pl.ds(side * n, n)] = (sums[side * n : side * n + n] + part).astype(BF)
            self.mixed[step, pl.ds(n - side * n, n)] = sums[n - side * n : 2 * n - side * n].astype(BF)
            self.push(6 + side, self.mixed.at[step], self.heard.at[side], at(x, z, y + step, c))

    def total(self):
        total = self.both(0)
        for side in (0, 1):
            self.copies[6 + side].wait_recv()
            total = total + self.heard[side].astype(F32)
        return total

    def finish(self):
        for n in range(8):
            self.copies[n].wait_send()


class CrossSum:
    @staticmethod
    def scratch(shape, lanes):
        if lanes:
            part = shape[:-1] + (shape[-1] // 2,)
        else:
            part = (shape[0] // 2,) + shape[1:]
        return [
            pltpu.VMEM((4,) + shape, BF),
            pltpu.VMEM((4,) + shape, BF),
            pltpu.VMEM((2,) + part, BF),
            pltpu.VMEM((2,) + shape, BF),
            DMA((8,)),
            DMA((8,)),
        ]

    def __init__(self, blk, lanes, first, mixed, parts, heard, ssem, rsem):
        self.blk, self.half = blk, half_lanes if lanes else half_lead
        self.first, self.mixed, self.parts, self.heard = first, mixed, parts, heard
        self.ssem, self.rsem = ssem, rsem
        self.copies = {}

    def push(self, n, src, dst, device):
        self.copies[n] = send(src, dst, self.ssem.at[n], self.rsem.at[n], device)

    def hand(self, d):
        x, z, y, c = place()
        to = ((x + d) % 4) * 2 + 1 - z
        self.push(d, self.blk.at[to], self.first.at[d], at(x, 1 - z, y, c))

    def both(self, d):
        x, z, y, c = place()
        self.copies[d].wait_recv()
        return self.blk[((x + d) % 4) * 2 + z].astype(F32) + self.first[d].astype(F32)

    def far(self):
        x, z, y, c = place()
        self.mixed[2] = self.both(2).astype(BF)
        for side, step in ((0, 1), (1, 3)):
            part = self.half(self.mixed.at[2], side)
            self.push(4 + side, part, self.parts.at[side], at(x + step, z, y, c))

    def near(self):
        x, z, y, c = place()
        for side, step in ((0, 1), (1, 3)):
            mixed = self.mixed.at[step]
            mixed[...] = self.both(step).astype(BF)
            self.copies[4 + side].wait_recv()
            mine = self.half(mixed, side)
            mine[...] = (mine[...].astype(F32) + self.parts[side].astype(F32)).astype(BF)
            self.push(6 + side, mixed, self.heard.at[side], at(x + step, z, y, c))

    def total(self):
        total = self.both(0)
        for side in (0, 1):
            self.copies[6 + side].wait_recv()
            total = total + self.heard[side].astype(F32)
        return total

    def finish(self):
        for n in range(8):
            self.copies[n].wait_send()


class RingSum:
    @staticmethod
    def scratch(shape, lanes):
        if lanes:
            part = shape[:-1] + (shape[-1] // 2,)
        else:
            part = (shape[0] // 2,) + shape[1:]
        return [
            pltpu.VMEM((4,) + part, BF),
            pltpu.VMEM((4,) + shape, BF),
            pltpu.VMEM((4,) + shape, BF),
            pltpu.VMEM((2,) + shape, BF),
            DMA((9,)),
            DMA((9,)),
        ]

    def __init__(self, blk, lanes, parts, mixed, heard, across, ssem, rsem):
        self.blk, self.half = blk, half_lanes if lanes else half_lead
        self.parts, self.mixed, self.heard, self.across = parts, mixed, heard, across
        self.ssem, self.rsem = ssem, rsem
        self.copies = {}

    def push(self, n, src, dst, device):
        self.copies[n] = send(src, dst, self.ssem.at[n], self.rsem.at[n], device)

    def start(self, k):
        x, z, y, c = place()
        zz = 1 - z if k == 0 else z
        far = self.blk.at[((x + 2) % 4) * 2 + zz]
        self.push(4 * k, self.half(far, 0), self.parts.at[2 * k], at(x + 1, z, y, c))
        self.push(4 * k + 1, self.half(far, 1), self.parts.at[2 * k + 1], at(x - 1, z, y, c))

    def relay(self, k):
        x, z, y, c = place()
        zz = 1 - z if k == 0 else z
        for side, step in ((0, 1), (1, 3)):
            n = 2 * k + side
            mixed = self.mixed.at[n]
            source = self.blk.at[((x + step) % 4) * 2 + zz]
            mine, other = self.half(source, side), self.half(source, 1 - side)
            self.half(mixed, 1 - side)[...] = other[...]
            self.copies[4 * k + side].wait_recv()
            self.half(mixed, side)[...] = (
                mine[...].astype(F32) + self.parts[n].astype(F32)
            ).astype(BF)
            self.push(4 * k + 2 + side, mixed, self.heard.at[n], at(x + step, z, y, c))

    def total(self, k):
        x, z, y, c = place()
        zz = 1 - z if k == 0 else z
        total = self.blk[x * 2 + zz].astype(F32)
        for side in (0, 1):
            self.copies[4 * k + 2 + side].wait_recv()
            total = total + self.heard[2 * k + side].astype(F32)
        if k == 0:
            self.across[0] = total.astype(BF)
            self.push(8, self.across.at[0], self.across.at[1], at(x, 1 - z, y, c))
            return None
        self.copies[8].wait_recv()
        return total + self.across[1].astype(F32)

    def finish(self):
        for n in range(9):
            self.copies[n].wait_send()


def fetch(src, dst, sem):
    copy = pltpu.make_async_copy(src, dst, sem)
    copy.start()
    return copy


def columns_of_gains(gain1, gain2):
    gap = jnp.zeros((1, 113), F32)
    return jnp.concatenate(
        [
            jnp.concatenate([ref[...].astype(F32).reshape(1, 15), gap], axis=1)
            for ref in (gain1, gain2)
        ]
        + [jnp.zeros((126, 128), F32)],
        axis=0,
    ).T[0:15]


def row_of(column):
    wide = jnp.concatenate([column, jnp.zeros((113, 1), F32)], axis=0)
    return jnp.broadcast_to(wide, (128, 128)).T[0:1, 0:15].reshape(15)


def comm_call(name, number, kernel, out_shape, in_specs, out_specs, scratch, args):
    return pl.pallas_call(
        kernel,
        out_shape=out_shape,
        in_specs=in_specs,
        out_specs=out_specs,
        scratch_shapes=scratch,
        compiler_params=pltpu.CompilerParams(
            collective_id=number, has_side_effects=True, vmem_limit_bytes=LIMIT
        ),
        name=name,
    )(*args)


def split(refs, counts):
    parts, begin = [], 0
    for n in counts:
        parts.append(refs[begin : begin + n])
        begin += n
    return parts


def spread_value(rows):
    j = lax.broadcasted_iota(jnp.int32, (rows, WIDE), 0)
    k = lax.broadcasted_iota(jnp.int32, (rows, WIDE), 1)
    hit = ((k // 16) * 15 + k % 16 == j) & (k % 16 < 15)
    return jnp.where(hit, 1.0, 0.0).astype(BF)


def first(
    hidden_t, cot_t, w_q, w_k, w_v, w_o, w_gate, w_up, w_down, gain1, gain2, lengths, span_order, freq
):
    def kernel(
        hidden_t, cot_t, w_q, w_k, w_v, w_o, w_gate, w_up, w_down, gain1, gain2, lengths, order, freq,
        rows_out, w1_out, wds, wo, cot, w2own, normed_out, q_out, kv2, cos_out, sin_out,
        rows, w1, normed, q_rot, cos_t, sin_t, xp, cp, wp1, wp2, wop, wdp, wos, w1own, kv, outs,
        *sems,
    ):
        a, a2, b, d, e, e2, ac, ao, b2, k0, k1, (hs, hr) = split(sems, (3,) * 11 + (2,))
        x, z, y, c = place()
        partners = hail("xf")

        gains = columns_of_gains(gain1, gain2)
        q = jnp.concatenate([w_q[...].astype(F32), jnp.zeros((15, 64), F32)], axis=1)
        q, k, v = (w * gains[:, 0:1] for w in (q, w_k[...].astype(F32), w_v[...].astype(F32)))
        wp1[...] = jnp.zeros(wp1.shape, BF)
        for f in range(8):
            n = OWNED_KV[f] * 64
            wp1[f, 0:15, 0:128] = q[:, 128 * f : 128 * f + 128].astype(BF)
            wp1[f, 0:15, 128:256] = jnp.concatenate(
                [k[:, n : n + 64], v[:, n : n + 64]], axis=1
            ).astype(BF)
        spread = spread_value(WIDTH)
        xp[...] = dot_tn(hidden_t[...], spread).astype(BF)

        wop[...] = jnp.zeros(wop.shape, BF)
        wop[0:15, :] = dot(w_o[...], spread).astype(BF)
        wdp[...] = jnp.zeros(wdp.shape, BF)
        wdp[0:40, :] = dot(w_down[...], spread).astype(BF)

        pl.semaphore_wait(pltpu.get_barrier_semaphore(), partners)
        swap = Swap(wp1, w1own, *b)
        swap.start()
        gathers = []
        for k, own in ((0, a), (64, a2)):
            spot = pl.ds(k, 64)
            gathers.append(RowGather(xp.at[spot], rows.at[:, spot], *own))
        for gather in gathers:
            gather.start()
        early = [CrossGather(wdp, wds, half_lanes, *e2), RingGather(wop, wos, half_lanes, *e)]
        ring_d, ring_o = early
        ring_o.start()
        cp[...] = dot_tn(cot_t[...], spread).astype(BF)

        lane = lanes_of((1, 128))
        sign = jnp.where(lane % 64 < 32, -1.0, 1.0)
        ends = doc_ends(lengths)

        @pl.loop(0, 8)
        def _(n):
            pos = order[(x * 2 + z) * 8 + n] * 128
            pos = pos + lax.broadcasted_iota(jnp.int32, (128, 1), 0)
            angle = (pos - doc_start(pos, ends)).astype(F32) * freq[...]
            part = pl.ds(pl.multiple_of(n * 128, 128), 128)
            cos_t[part, :] = jnp.cos(angle)
            sin_t[part, :] = sign * jnp.sin(angle)

        written = [fetch(cos_t, cos_out, outs.at[0]), fetch(sin_t, sin_out, outs.at[1])]
        wp2[...] = jnp.zeros(wp2.shape, BF)
        gap = jnp.zeros((15, 8), F32)
        for m, ref in ((0, w_gate), (384, w_up)):
            w = ref[...].astype(F32) * gains[:, 1:2]
            for f in range(8):
                parts = []
                for g in range(8):
                    n = (8 * g + f) * 40
                    parts += [w[:, n : n + 40], gap]
                wp2[f, 0:15, m : m + 384] = jnp.concatenate(parts, axis=1).astype(BF)

        ring_o.relay_z()
        swap.finish()
        ring_1 = RingGather(w1own, w1, half_lead, *d)
        ring_1.start()
        ring_d.start()
        ring_o.relay_x(0)
        ring_o.relay_x(1)
        for gather in gathers:
            gather.relay()
        gather_c = RowGather(cp, cot, *ac)
        gather_c.start()
        ring_1.relay_z()
        ring_d.relay()

        for k in (0, 1):
            ring_1.relay_x(k)

        for gather in gathers:
            gather.land()
        for k in (0, 1):
            for ring in (ring_1, ring_o):
                ring.land(k)
        for gather in gathers:
            gather.finish()
        ring_o.local.wait()
        gather_o = RowGather(wos, wo, *ao)
        gather_o.start()
        swap2 = Swap(wp2, w2own, *b2)
        swap2.start()
        ring_1.local.wait()
        written += [fetch(rows, rows_out, outs.at[2]), fetch(w1, w1_out, outs.at[3])]

        w = w1.reshape(WIDE, 256)
        lane = lanes_of((256, 128))

        def project(n):
            part = pl.ds(n * 256, 256)
            xs = jnp.concatenate([rows[2 * n], rows[2 * n + 1]], axis=0).astype(F32)
            v = (xs * inverse_rms(xs)).astype(BF)
            normed[part, :] = v
            out = dot(v, w[...])
            cos_v, sin_v = cos_t[part, :], sin_t[part, :]
            qs, ks = out[:, 0:128], out[:, 128:256]
            qs = (qs * cos_v + partner(qs) * sin_v).astype(BF).astype(F32) * 0.125
            kv[part, :] = jnp.where(lane < 64, ks * cos_v + partner(ks) * sin_v, ks).astype(BF)
            q_rot[0, part, :] = jnp.where(lane < 64, qs, 0.0).astype(BF)
            q_rot[1, part, :] = jnp.where(lane < 64, pltpu.roll(qs, 64, 1), 0.0).astype(BF)

        hand = []

        def pass_on(piece):
            n = len(hand)
            hand.append(send(piece, piece, hs.at[n], hr.at[n], at(x, z, y, 1 - c)))

        key_rings = []
        for h, (kind, own) in enumerate(((RingGather, k0), (CrossGather, k1))):
            mine = kv.at[pl.ds(512 * h, 512)]
            spot = pl.ds(512 * h, 512)
            ring = kind(
                mine,
                kv2.at[c, :, spot],
                half_lead,
                *own,
                arrived=lambda block, spot=spot: pass_on(kv2.at[c, block, spot]),
            )
            project(2 * h)
            project(2 * h + 1)
            ring.start()
            n = len(hand)
            hand.append(
                send(
                    mine, kv2.at[c, x * 2 + z, spot], hs.at[n], hr.at[n], at(x, z, y, 1 - c)
                )
            )
            key_rings.append(ring)
            if h == 0:
                gather_c.relay()

        written += [fetch(normed, normed_out, outs.at[4]), fetch(q_rot, q_out, outs.at[5])]
        ring_a, ring_b = key_rings
        ring_a.relay_z()
        ring_d.far()
        gather_o.relay()
        ring_b.relay()
        ring_a.relay_x(0)
        gather_c.land()
        ring_a.relay_x(1)
        ring_b.far()
        gather_o.land()
        ring_a.land(0)
        ring_a.land(1)
        ring_b.land()
        for copy in hand:
            copy.wait()
        ring_d.land()
        swap2.finish()
        gather_o.finish()
        gather_c.finish()
        for ring in [ring_d] + key_rings:
            ring.finish()
        for ring in (ring_1, ring_o):
            ring.sent()
        for copy in written:
            copy.wait()

    return comm_call(
        "first",
        1,
        kernel,
        (
            shaped((8, 128, WIDE), BF),
            shaped((8, 8, 16, 256), BF),
            shaped((8, 48, WIDE), BF),
            shaped((8, 8, 16, WIDE), BF),
            shaped((8, 128, WIDE), BF),
            shaped((8, 16, 768), BF),
            shaped((1024, WIDE), BF),
            shaped((2, 1024, 128), BF),
            shaped((2, 8, 1024, 128), BF),
            shaped((1024, 128), F32),
            shaped((1024, 128), F32),
        ),
        [VMEM] * 11 + [SMEM, SMEM, VMEM],
        (ANY,) * 11,
        [
            pltpu.VMEM((8, 128, WIDE), BF),
            pltpu.VMEM((8, 8, 16, 256), BF),
            pltpu.VMEM((1024, WIDE), BF),
            pltpu.VMEM((2, 1024, 128), BF),
            pltpu.VMEM((1024, 128), F32),
            pltpu.VMEM((1024, 128), F32),
            pltpu.VMEM((128, WIDE), BF),
            pltpu.VMEM((128, WIDE), BF),
            pltpu.VMEM((8, 16, 256), BF),
            pltpu.VMEM((8, 16, 768), BF),
            pltpu.VMEM((16, WIDE), BF),
            pltpu.VMEM((48, WIDE), BF),
            pltpu.VMEM((8, 16, WIDE), BF),
            pltpu.VMEM((8, 16, 256), BF),
            pltpu.VMEM((1024, 128), BF),
            DMA((6,)),
        ]
        + RowGather.sems * 2
        + Swap.sems
        + RingGather.sems * 2
        + CrossGather.sems
        + RowGather.sems * 2
        + Swap.sems
        + RingGather.sems
        + CrossGather.sems
        + [DMA((16,)), DMA((16,))],
        (
            hidden_t, cot_t, w_q, w_k, w_v, w_o, w_gate, w_up, w_down, gain1, gain2, lengths,
            span_order, freq,
        ),
    )


def inverse_rms(v):
    return lax.rsqrt(jnp.sum(v * v, axis=1, keepdims=True) * (1.0 / WIDTH) + EPSILON)


def feed(att, w2own, wo, rows, wd, cot):
    def kernel(
        att, w2own, wo_in, rows_in, wd_in, cot_in,
        outp_out, resid_out, d_resid, d_heads, gwo_out, gw2_sum, gwd_sum,
        wo, x_in, wd, cot, ins, atts, w2, packed, d_act, resid, normed, act, d_both, dmn, outp,
        gw2, gwd, da, gwo, *refs,
    ):
        a, a2, b, b2, s, r1, r2, t1, t2 = split(refs, (3, 3, 3, 3, 3, 6, 6, 6, 6))
        x, z, y, c = place()
        me = y * 2 + c
        partners = hail("xf")
        pairs = ((wo_in, wo), (cot_in, cot), (wd_in, wd), (rows_in, x_in))
        held = [fetch(src, dst, ins.at[n]) for n, (src, dst) in enumerate(pairs)]
        pl.semaphore_wait(pltpu.get_barrier_semaphore(), partners)
        gathers = []
        for k, own in ((0, a), (512, a2)):
            spot = pl.ds(k, 512)
            gathers.append(RowGather(att.at[spot], atts.at[:, spot], *own))
        low, high = pl.ds(0, 4), pl.ds(4, 4)
        ring_a = RingGather(w2own.at[low], w2.at[:, low], half_lead, *b)
        ring_b = CrossGather(w2own.at[high], w2.at[:, high], half_lead, *b2)
        for part in gathers + [ring_a, ring_b]:
            part.start()

        def place_rows(n, size):
            return pl.ds(pl.multiple_of(n * size, size), size)

        held[0].wait()
        whole = jnp.concatenate([wo[f, g] for g in range(8) for f in range(8)], axis=0)

        def pack(n):
            j = lax.broadcasted_iota(jnp.int32, (512, WIDE), 0) + n * 512
            k = lax.broadcasted_iota(jnp.int32, (512, WIDE), 1)
            hit = ((k // 16) * 15 + k % 16 == j) & (k % 16 < 15)
            packed[pl.ds(n * 512, 512), :] = dot(
                jnp.where(hit, 1.0, 0.0).astype(BF), whole
            ).astype(BF)

        pack(0)
        ring_a.relay_z()
        gathers[0].relay()
        ring_b.relay()
        ring_a.relay_x(0)
        gathers[1].relay()
        pack(1)
        held[1].wait()
        held[2].wait()

        @pl.loop(0, 2)
        def _(n):
            part = place_rows(n, 512)
            d_act[part, :] = dot_nt(cot[part, :], wd[...])

        ring_a.relay_x(1)
        ring_b.far()
        held[3].wait()
        for n, gather in enumerate(gathers):
            gather.land()
            gather.finish()
            part = pl.ds(512 * n, 512)
            heads = jnp.concatenate([atts[f, part, :] for f in range(8)], axis=1)
            v = x_in[part, :].astype(F32) + dot(heads, packed[...])
            resid[part, :] = v
            normed[part, :] = (v * inverse_rms(v)).astype(BF)

        ring_a.land(0)
        ring_a.land(1)
        ring_b.land()
        ring_a.finish()
        ring_b.finish()
        w2_all = w2.reshape(WIDE, 768)

        @pl.loop(0, 2)
        def _(n):
            part = place_rows(n, 512)
            both = dot(normed[part, :], w2_all[...])
            gate, up = both[:, 0:384], both[:, 384:768]
            sigma = 1.0 / (1.0 + jnp.exp(-gate))
            silu = gate * sigma
            act[part, :] = (silu * up).astype(BF)
            d = d_act[part, :]
            d_both[part, 0:384] = (d * up * sigma * (1.0 + gate * (1.0 - sigma))).astype(BF)
            d_both[part, 384:768] = (d * silu).astype(BF)

        sums = [RowSum(dmn.at[:, pl.ds(k, 64)], *own) for k, own in ((0, r1), (64, r2))]
        ring_2, ring_d = RingSum(gw2, False, *t1), CrossSum(gwd, True, *t2)

        def back(core):
            to = [((y + n) % 4) * 2 + core for n in (2, 1, 3, 0)]
            v = jnp.concatenate([d_both[place_rows(n, 128), :] for n in to], axis=0)
            v = dot_nt(v, w2_all[...]).astype(BF)
            for n in range(4):
                dmn[to[n]] = v[128 * n : 128 * n + 128]

        order = [(2, 1), (2, 0), (1, 1), (3, 1), (1, 0), (3, 0), (0, 1), (0, 0)]
        where = [((x + p) % 4) * 2 + (1 - z if q else z) for p, q in order]

        def weights(which):
            v = jnp.concatenate([normed[:, place_rows(where[n], 128)] for n in which], axis=1)
            v = dot_tn(v, d_both[...]).astype(BF)
            for n, m in enumerate(which):
                gw2[where[m]] = v[128 * n : 128 * n + 128].reshape(8, 16, 768)

        weights((0, 1))
        ring_2.start(0)
        ring_2.start(1)
        back(1 - c)
        for d in (2, 1, 3, 0):
            for part in sums:
                part.hand(d)
        gwd[...] = dot_tn(act[...], cot[...]).astype(BF).reshape(8, 48, WIDE)
        for d in (2, 1, 3, 0):
            ring_d.hand(d)
        back(c)
        for part in sums:
            part.far()
        weights((2, 3, 4, 5, 6, 7))
        for part in sums:
            part.near()
        ring_2.relay(0)
        ring_d.far()

        @pl.loop(0, 2)
        def _(n):
            v = dot(act[place_rows(n, 512), :], wd[...]).astype(BF)
            for k in range(4):
                outp[n * 4 + k] = v[128 * k : 128 * k + 128]

        written = [fetch(outp, outp_out, ins.at[5])]
        ring_2.relay(1)
        ring_d.near()

        mine = place_rows(me, 128)
        v = resid[mine, :]
        inv = inverse_rms(v)
        e = jnp.concatenate([part.total() for part in sums], axis=0)
        mean = jnp.sum(e * v, axis=1, keepdims=True) * (1.0 / WIDTH)
        d_v = cot[mine, :].astype(F32) + inv * e - v * (inv * inv * inv * mean)
        d_resid[...] = d_v
        mixed = d_v.astype(BF)
        d_att = dot_nt(mixed, packed[...]).astype(BF)
        for f in range(8):
            da[f] = d_att[:, f * 128 : (f + 1) * 128]
        swap = Swap(da, d_heads, *s)
        swap.start()
        spread = spread_value(WIDE)
        heads = jnp.concatenate([atts[f, mine, :] for f in range(8)], axis=1)
        gw = dot_tn(dot(heads, spread).astype(BF), mixed).astype(BF)
        for g in range(8):
            for f in range(8):
                n = (8 * g + f) * 16
                gwo[f, g * 16 : (g + 1) * 16, :] = gw[n : n + 16]
        written += [fetch(gwo, gwo_out, ins.at[4])]
        ring_2.total(0)
        resid_out[...] = v
        gw2_sum[...] = ring_2.total(1).astype(BF)
        gwd_sum[...] = ring_d.total()
        swap.finish()
        for part in sums:
            part.finish()
        ring_2.finish()
        ring_d.finish()
        for copy in written:
            copy.wait()

    return comm_call(
        "feed",
        3,
        kernel,
        (
            shaped((8, 128, WIDE), BF),
            shaped((128, WIDE), F32),
            shaped((128, WIDE), F32),
            shaped((8, 128, 128), BF),
            shaped((8, 128, WIDE), BF),
            shaped((8, 16, 768), BF),
            shaped((48, WIDE), F32),
        ),
        [ANY] * 6,
        (ANY, VMEM, VMEM, ANY, ANY, VMEM, VMEM),
        [
            pltpu.VMEM((8, 8, 16, WIDE), BF),
            pltpu.VMEM((1024, WIDE), BF),
            pltpu.VMEM((384, WIDE), BF),
            pltpu.VMEM((1024, WIDE), BF),
            DMA((6,)),
            pltpu.VMEM((8, 1024, 128), BF),
            pltpu.VMEM((8, 8, 16, 768), BF),
            pltpu.VMEM((WIDE, WIDE), BF),
            pltpu.VMEM((1024, 384), F32),
            pltpu.VMEM((1024, WIDE), F32),
            pltpu.VMEM((1024, WIDE), BF),
            pltpu.VMEM((1024, 384), BF),
            pltpu.VMEM((1024, 768), BF),
            pltpu.VMEM((8, 128, WIDE), BF),
            pltpu.VMEM((8, 128, WIDE), BF),
            pltpu.VMEM((8, 8, 16, 768), BF),
            pltpu.VMEM((8, 48, WIDE), BF),
            pltpu.VMEM((8, 128, 128), BF),
            pltpu.VMEM((8, 128, WIDE), BF),
        ]
        + RowGather.sems * 2
        + RingGather.sems
        + CrossGather.sems
        + Swap.sems
        + RowSum.scratch((64, WIDE)) * 2
        + RingSum.scratch((8, 16, 768), False)
        + CrossSum.scratch((48, WIDE), True),
        (att, w2own, wo, rows, wd, cot),
    )


def last(
    dkv, gwo, outp, dq, cos_t, sin_t, w1, normed, rows, resid, d_resid, gw2s, gwd, gain1, gain2,
    w_q, w_k, w_v, w_gate, w_up,
):
    def kernel(
        dkv, gwo_in, outp_in, dq_in, cos_in, sin_in, w1_in, normed_in, rows_in, resid, dr, gw2s, wd,
        gain1, gain2,
        w_q, w_k, w_v, w_gate, w_up,
        output, gh, g_attn, g_mlp, g_q, g_k, g_v, g_o, g_gate, g_up, g_down,
        own, gwo, outp, dq, cos_t, sin_t, w1, normed, rows, ins,
        blk_a, blk_b, from_core, gwos, gw1, dnq, d_kv, dn, one, two, gw1s, hs, hr, *refs,
    ):
        a, a2, b, b2, d, d2, e, e2, s1, s2 = split(refs, (6, 6, 6, 6, 6, 6, 6, 6, 3, 3))
        x, z, y, c = place()
        me = y * 2 + c
        partners = hail("xf")
        pairs = [
            (gwo_in, gwo),
            (dkv.at[c], own),
            (dq_in, dq),
            (cos_in, cos_t),
            (sin_in, sin_t),
            (w1_in, w1),
            (normed_in, normed),
            (rows_in.at[me], rows),
            (outp_in, outp),
        ]
        held = {n: fetch(*pairs[n], ins.at[n]) for n in (0, 8, 1)}
        pl.semaphore_wait(pltpu.get_barrier_semaphore(), partners)
        order = [(2, 1), (2, 0), (1, 1), (3, 1), (0, 1), (1, 0), (3, 0), (0, 0)]
        where = [((x + p) % 4) * 2 + (1 - z if q else z) for p, q in order]
        sum_w = RowSum(gwo, *b, source=gwo_in)
        sum_o = RowSum(outp, *b2, source=outp_in)
        ring_a, ring_b = RingSum(blk_a, False, *a), CrossSum(blk_b, False, *a2)
        hand = {}

        def pass_on(n):
            hand[n] = send(
                dkv.at[1 - c, where[n]], from_core.at[n], hs.at[n], hr.at[n], at(x, z, y, 1 - c)
            )

        swap2 = Swap(gw2s, two, *s2)
        swap2.start()
        sum_w.hand(2)
        sum_o.hand(2)
        pass_on(0)
        pass_on(1)
        for step in (1, 3):
            sum_w.hand(step)
            sum_o.hand(step)
        for n in (2, 3, 4):
            pass_on(n)
        sum_w.hand(0)
        sum_o.hand(0)
        for n in (5, 6, 7):
            pass_on(n)
        for n in range(2, 8):
            held[n] = fetch(*pairs[n], ins.at[n])

        def fold(n):
            g = where[n]
            hand[n].wait_recv()
            both = (own[g].astype(F32) + from_core[n].astype(F32)).astype(BF)
            blk_a[g] = both[0:512]
            blk_b[g] = both[512:1024]

        held[0].wait()
        sum_w.far()
        held[8].wait()
        sum_o.far()
        held[1].wait()
        fold(0)
        ring_a.start(0)
        ring_b.hand(2)
        fold(1)
        ring_a.start(1)
        for n, step in ((2, 1), (3, 3), (4, 0)):
            fold(n)
            ring_b.hand(step)
        ring_a.relay(0)
        ring_b.far()
        fold(5)
        fold(6)
        ring_a.relay(1)
        sum_w.near()
        fold(7)
        ring_b.near()
        ring_a.total(0)
        sum_o.near()
        for n in range(2, 6):
            held[n].wait()
        spread = spread_value(WIDTH)
        gains = columns_of_gains(gain1, gain2)

        def place_rows(n, size):
            return pl.ds(pl.multiple_of(n * size, size), size)

        def queries(n):
            part = place_rows(n, 512)
            v = dq[part, :]
            v = (v * cos_t[part, :] - partner(v) * sin_t[part, :]).astype(BF)
            d_kv[part, 0:128] = v
            dnq[part, :] = dot_nt(v, w1[:, 0:128])

        queries(0)
        queries(1)
        held[6].wait()
        gw1[:, :, :, 0:128] = (
            dot_tn(normed[...], d_kv[:, 0:128]).astype(BF).reshape(8, 8, 16, 128)
        )
        swap2.finish()
        total = jnp.zeros((15, 1), F32)
        for m, ref, w in ((0, g_gate, w_gate), (384, g_up, w_up)):
            for n in range(0, 8, 2):
                part = jnp.concatenate(
                    [
                        two[f, :, m + 48 * k : m + 48 * k + 40].astype(F32)[0:15]
                        for k in (n, n + 1)
                        for f in range(8)
                    ],
                    axis=1,
                )
                spot = pl.ds(n * 320, 640)
                ref[:, spot] = part * gains[:, 1:2]
                total += jnp.sum(part * w[:, spot].astype(F32), axis=1, keepdims=True)
        g_mlp[...] = row_of(total)

        def squeeze(v):
            top = v.astype(BF)
            low = (v - top.astype(F32)).astype(BF)
            return dot_nt(top, spread) + dot_nt(low, spread)

        g_down[...] = squeeze(wd[...])[0:40]
        v = jnp.concatenate([ring_a.total(1), ring_b.total()], axis=0)
        turned = v * cos_t[...] - partner(v) * sin_t[...]
        d_kv[:, 128:256] = jnp.where(lanes_of((1024, 128)) < 64, turned, v).astype(BF)
        sums = [RowSum(dn.at[:, pl.ds(k, 64)], *own) for k, own in ((0, d), (64, d2))]

        def back(core):
            to = [((y + n) % 4) * 2 + core for n in (2, 1, 3, 0)]
            parts = [place_rows(n, 128) for n in to]
            v = jnp.concatenate([d_kv[p, 128:256] for p in parts], axis=0)
            v = dot_nt(v, w1[:, 128:256])
            for n, p in enumerate(parts):
                dn[to[n]] = (dnq[p, :] + v[128 * n : 128 * n + 128]).astype(BF)

        back(1 - c)
        for n in (2, 1, 3, 0):
            for part in sums:
                part.hand(n)
        ring_1 = RingSum(gw1, False, *e)

        def weights_k(which):
            parts = [place_rows(where[n], 128) for n in which]
            v = jnp.concatenate([normed[:, p] for p in parts], axis=1)
            v = dot_tn(v, d_kv[:, 128:256]).astype(BF)
            for n, m in enumerate(which):
                gw1[where[m], :, :, 128:256] = v[128 * n : 128 * n + 128].reshape(8, 16, 128)

        weights_k((0, 1))
        ring_1.start(0)
        ring_1.start(1)
        gwos[...] = sum_w.total().astype(BF).reshape(8, 16, WIDE)
        ring_o = RingSum(gwos, True, *e2)
        ring_o.start(0)
        ring_o.start(1)
        back(c)
        for part in sums:
            part.far()
        weights_k((2, 3, 4, 5, 6, 7))
        for part in sums:
            part.near()
        for k in (0, 1):
            ring_1.relay(k)
            ring_o.relay(k)
        ring_1.total(0)
        ring_o.total(0)
        gw1s[...] = ring_1.total(1).astype(BF)
        swap1 = Swap(gw1s, one, *s1)
        swap1.start()
        output[...] = dot_nt(spread, (resid[...] + sum_o.total()).astype(BF)).astype(BF)
        g_o[...] = squeeze(ring_o.total(1))[0:15]

        held[7].wait()
        xs = rows[...].astype(F32)
        inv = inverse_rms(xs)
        t = jnp.concatenate([part.total() for part in sums], axis=0)
        mean = jnp.sum(t * xs, axis=1, keepdims=True) * (1.0 / WIDTH)
        d_x = dr[...] + inv * t - xs * (inv * inv * inv * mean)
        gh[...] = dot_nt(spread, d_x.astype(BF)).astype(BF)
        swap1.finish()
        ones = [one[f].astype(F32)[0:15] for f in range(8)]
        r_q = jnp.concatenate([v[:, 0:128] for v in ones], axis=1)[:, 0:WIDTH]

        def heads(n):
            return jnp.concatenate(
                [
                    sum(ones[f][:, n : n + 64] for f in range(8) if OWNED_KV[f] == h)
                    for h in range(5)
                ],
                axis=1,
            )

        total = jnp.zeros((15, 1), F32)
        for part, w, ref in ((r_q, w_q, g_q), (heads(128), w_k, g_k), (heads(192), w_v, g_v)):
            ref[...] = part * gains[:, 0:1]
            total += jnp.sum(part * w[...].astype(F32), axis=1, keepdims=True)
        g_attn[...] = row_of(total)
        for copy in hand.values():
            copy.wait_send()
        ring_a.finish()
        ring_b.finish()
        ring_1.finish()
        ring_o.finish()
        sum_w.finish()
        sum_o.finish()
        for part in sums:
            part.finish()

    return comm_call(
        "last",
        6,
        kernel,
        (
            shaped((WIDTH, 128), BF),
            shaped((WIDTH, 128), BF),
            shaped((15,), F32),
            shaped((15,), F32),
            shaped((15, WIDTH), F32),
            shaped((15, 320), F32),
            shaped((15, 320), F32),
            shaped((15, WIDTH), F32),
            shaped((15, 2560), F32),
            shaped((15, 2560), F32),
            shaped((40, WIDTH), F32),
        ),
        [ANY] * 9 + [VMEM] * 11,
        (VMEM,) * 11,
        [
            pltpu.VMEM((8, 1024, 128), BF),
            pltpu.VMEM((8, 128, WIDE), BF),
            pltpu.VMEM((8, 128, WIDE), BF),
            pltpu.VMEM((1024, 128), F32),
            pltpu.VMEM((1024, 128), F32),
            pltpu.VMEM((1024, 128), F32),
            pltpu.VMEM((WIDE, 256), BF),
            pltpu.VMEM((1024, WIDE), BF),
            pltpu.VMEM((128, WIDE), BF),
            DMA((9,)),
            pltpu.VMEM((8, 512, 128), BF),
            pltpu.VMEM((8, 512, 128), BF),
            pltpu.VMEM((8, 1024, 128), BF),
            pltpu.VMEM((8, 16, WIDE), BF),
            pltpu.VMEM((8, 8, 16, 256), BF),
            pltpu.VMEM((1024, WIDE), F32),
            pltpu.VMEM((1024, 256), BF),
            pltpu.VMEM((8, 128, WIDE), BF),
            pltpu.VMEM((8, 16, 256), BF),
            pltpu.VMEM((8, 16, 768), BF),
            pltpu.VMEM((8, 16, 256), BF),
            DMA((8,)),
            DMA((8,)),
        ]
        + RingSum.scratch((512, 128), False)
        + CrossSum.scratch((512, 128), False)
        + RowSum.scratch((128, WIDE)) * 2
        + RowSum.scratch((64, WIDE)) * 2
        + RingSum.scratch((8, 16, 256), False)
        + RingSum.scratch((16, WIDE), True)
        + Swap.sems * 2,
        (
            dkv, gwo, outp, dq, cos_t, sin_t, w1, normed, rows, resid, d_resid, gw2s, gwd, gain1,
            gain2, w_q, w_k, w_v, w_gate, w_up,
        ),
    )


def lanes_of(shape):
    return lax.broadcasted_iota(jnp.int32, shape, len(shape) - 1)


def partner(v):
    lane = lanes_of(v.shape)
    return jnp.where(lane % 64 < 32, pltpu.roll(v, 96, 1), pltpu.roll(v, 32, 1))


def doc_ends(lengths):
    return lengths[0], lengths[0] + lengths[1]


def doc_start(pos, ends):
    return jnp.where(pos < ends[0], 0, jnp.where(pos < ends[1], ends[0], ends[1]))

def layout(order, inverse):
    @pl.loop(0, 64)
    def _(n):
        inverse[order[n]] = n

    i = lax.axis_index("ctx")
    f = i % 8
    upper = (f == 3) | (f == 5)
    return i // 8, (
        jnp.where(upper, 1, 0),
        jnp.where(upper | (f == 1) | (f == 4), 1, 0),
    )


def key_range(span, ends):
    begin = doc_start(span * 128, ends) // 128
    count = span - begin + 1
    runs = (count + 3) // 8
    return begin, runs, jnp.where(count > runs * 8, 1, 0)


def attend(lengths, order, q, kv):
    def kernel(lengths, order, q_ref, kv_ref, o_ref, lse_ref, s_ref, inverse):
        group, sel = layout(order, inverse)
        ends = doc_ends(lengths)

        @pl.loop(0, 8)
        def _(b):
            span = order[group * 8 + b]
            begin, runs, rest = key_range(span, ends)
            pos = span * 128 + lanes_of((1, 256)) % 128
            low = doc_start(pos, ends)
            rows = pl.ds(pl.multiple_of(b * 128, 128), 128)
            none = jnp.zeros((128, 128), BF)
            pair = jnp.concatenate(
                [
                    jnp.concatenate([q_ref[0, rows, :], none], axis=1),
                    jnp.concatenate([none, q_ref[1, rows, :]], axis=1),
                ],
                axis=0,
            )

            def load(h, t, n):
                return jnp.concatenate(
                    [
                        kv_ref[sel[h], pl.ds(inverse[jnp.minimum(t + i, 63)] * 128, 128), :]
                        for i in range(n)
                    ],
                    axis=0,
                )

            def held(t, n):
                return pl.ds(pl.multiple_of((t - begin) * 128, 512), n * 128)

            def scores(n, t, high):
                kpos = t * 128 + lax.broadcasted_iota(jnp.int32, (n * 128, 1), 0)
                allowed = (kpos >= low) & (kpos <= pos)
                keys = jnp.concatenate([load(0, t, n), load(1, t, n)], axis=1)
                s = jnp.where(allowed, dot_nt(keys, pair), MASKED)
                s_ref[held(t, n), :] = s
                return jnp.maximum(high, jnp.max(s.reshape(n * 16, 8, 256), axis=0))

            def over(step, state):
                state = lax.fori_loop(0, runs, lambda j, v: step(8, begin + j * 8, v), state)
                return lax.fori_loop(0, rest, lambda j, v: step(4, begin + runs * 8, v), state)

            high = over(scores, jnp.full((8, 256), MASKED, F32))
            high = jnp.max(high, axis=0, keepdims=True)

            def weigh(n, t, state):
                total, acc = state
                p = jnp.exp(s_ref[held(t, n), :] - high)
                total = total + jnp.sum(p.reshape(n * 16, 8, 256), axis=0)
                values = jnp.where(lanes_of((n * 128, 128)) < 64, pltpu.roll(load(0, t, n), 64, 1), load(1, t, n))
                return total, acc + dot_tn(values, p.astype(BF))

            total, acc = over(weigh, (jnp.zeros((8, 256), F32), jnp.zeros((128, 256), F32)))
            total = jnp.sum(total, axis=0, keepdims=True)
            lse = high + jnp.log(total)
            lse_ref[b, 0:1, :] = lse[:, 0:128]
            lse_ref[b, 1:2, :] = lse[:, 128:256]
            acc = acc / total
            acc = jnp.concatenate([acc[0:64, 0:128], acc[64:128, 128:256]], axis=0)
            o_ref[rows, :] = acc.T.astype(BF)

    return pl.pallas_call(
        kernel,
        in_specs=[SMEM, SMEM, VMEM, VMEM],
        out_specs=(VMEM, VMEM),
        scratch_shapes=[pltpu.VMEM((40 * 128, 256), F32), pltpu.SMEM((64,), jnp.int32)],
        out_shape=(shaped((1024, 128), BF), shaped((8, 8, 128), F32)),
        compiler_params=pltpu.CompilerParams(vmem_limit_bytes=LIMIT),
        name="attend",
    )(lengths, order, q, kv)


def attend_back(lengths, order, q, kv, d_att, att, lse):
    def kernel(
        lengths, order, q_ref, kv_in, d_ref, o_ref, lse_ref, dq_ref, dkv_out, acc_ref, inverse,
        kv_ref, dkv_ref, sems,
    ):
        held = fetch(kv_in, kv_ref, sems.at[16])
        lane = lanes_of((128, 128))
        group, sel = layout(order, inverse)
        ends = doc_ends(lengths)

        @pl.loop(0, 16)
        def _(n):
            for s in (0, 1):
                part = pl.ds(pl.multiple_of(n * 512, 512), 512)
                acc_ref[s, part, :] = jnp.zeros((512, 128), F32)

        held.wait()

        @pl.loop(0, 8)
        def _(b):
            span = order[group * 8 + b]
            begin, runs, rest = key_range(span, ends)
            pos = span * 128 + lanes_of((1, 128))
            low = doc_start(pos, ends)
            rows = pl.ds(pl.multiple_of(b * 128, 128), 128)
            d_both = d_ref[rows, :].astype(F32)
            d_pad = (
                jnp.where(lane >= 64, pltpu.roll(d_both, 64, 1), 0.0).astype(BF),
                jnp.where(lane >= 64, d_both, 0.0).astype(BF),
            )
            pair = [jnp.concatenate([q_ref[h, rows, :], d_pad[h]], axis=0) for h in (0, 1)]
            mixed = (d_both * o_ref[rows, :].astype(F32)).T
            delta = [jnp.sum(mixed[64 * h : 64 * h + 64], axis=0, keepdims=True) for h in (0, 1)]
            lses = [lse_ref[b, h : h + 1, :] for h in (0, 1)]

            def step(n, t, state):
                where = [inverse[jnp.minimum(t + i, 63)] * 128 for i in range(n)]
                where = [pl.ds(pl.multiple_of(v, 128), 128) for v in where]
                kpos = t * 128 + lax.broadcasted_iota(jnp.int32, (n * 128, 1), 0)
                allowed = (kpos >= low) & (kpos <= pos)
                d_ss, kvs = [], []
                for h in (0, 1):
                    kv_t = jnp.concatenate([kv_ref[sel[h], w, :] for w in where], axis=0)
                    kvs.append(kv_t)
                    both = dot_nt(kv_t, pair[h])
                    p = jnp.where(allowed, jnp.exp(both[:, 0:128] - lses[h]), 0.0)
                    d_s = (p * (both[:, 128:256] - delta[h])).astype(BF)
                    d_ss.append(d_s)
                    d_kv = dot(jnp.concatenate([d_s, p.astype(BF)], axis=1), pair[h])
                    for i, w in enumerate(where):
                        acc_ref[sel[h], w, :] += d_kv[i * 128 : (i + 1) * 128]
                lanes = lanes_of((n * 128, 128))
                keys = jnp.where(lanes < 64, kvs[0], pltpu.roll(kvs[1], 64, 1))
                return state + dot_tn(keys, jnp.concatenate(d_ss, axis=1))

            state = jnp.zeros((128, 256), F32)
            state = lax.fori_loop(0, runs, lambda j, v: step(8, begin + j * 8, v), state)
            state = lax.fori_loop(0, rest, lambda j, v: step(4, begin + runs * 8, v), state)
            state = jnp.concatenate([state[0:64, 0:128], state[64:128, 128:256]], axis=0)
            dq_ref[rows, :] = state.T * 0.125

        written = []
        for n in range(8):
            for s in (0, 1):
                part = pl.ds(n * 1024, 1024)
                dkv_ref[s, part, :] = acc_ref[s, part, :].astype(BF)
                written.append(
                    fetch(dkv_ref.at[s, part], dkv_out.at[s, part], sems.at[2 * n + s])
                )
        for copy in written:
            copy.wait()

    return pl.pallas_call(
        kernel,
        in_specs=[SMEM, SMEM, VMEM, ANY] + [VMEM] * 3,
        out_specs=(VMEM, ANY),
        scratch_shapes=[
            pltpu.VMEM((2, 8192, 128), F32),
            pltpu.SMEM((64,), jnp.int32),
            pltpu.VMEM((2, 8192, 128), BF),
            pltpu.VMEM((2, 8192, 128), BF),
            DMA((17,)),
        ],
        out_shape=(shaped((1024, 128), F32), shaped((2, 8192, 128), BF)),
        compiler_params=pltpu.CompilerParams(vmem_limit_bytes=LIMIT),
        name="attend_back",
    )(lengths, order, q, kv, d_att, att, lse)


def hand_out(parts):
    def kernel(*refs):
        for src, dst in zip(refs[: len(parts)], refs[len(parts) :]):
            dst[...] = src[...]

    return pl.pallas_call(
        kernel,
        out_shape=tuple(shaped(v.shape, v.dtype) for v in parts),
        in_specs=[VMEM] * len(parts),
        out_specs=(VMEM,) * len(parts),
        compiler_params=pltpu.CompilerParams(vmem_limit_bytes=LIMIT),
        name="hand_out",
    )(*parts)


def local(
    hidden, attn_gain, w_q, w_k, w_v, w_o, mlp_gain, w_gate, w_up, w_down, cotangent,
    doc_lengths, span_order,
):
    frequency = ROPE_BASE ** (-2.0 * (np.arange(128) % 32) / HEAD)
    frequency = jnp.asarray(frequency, F32).reshape(1, 128)

    rows, w1, wds, wo, cot, w2own, normed, q, kv, cos_t, sin_t = first(
        hidden.T, cotangent.T, w_q, w_k, w_v, w_o, w_gate, w_up, w_down, attn_gain, mlp_gain,
        doc_lengths, span_order, frequency,
    )
    kv = kv.reshape(2, 8192, 128)
    att, lse = attend(doc_lengths, span_order, q, kv)
    outp, resid, d_resid, d_heads, gwo, gw2s, gwds = feed(
        att, w2own, wo, rows.reshape(1024, WIDE), wds.reshape(384, WIDE), cot.reshape(1024, WIDE)
    )
    d_att = d_heads.reshape(1024, 128)
    dq, dkv = attend_back(doc_lengths, span_order, q, kv, d_att, att, lse)
    grads = last(
        dkv.reshape(2, 8, 1024, 128), gwo, outp, dq, cos_t, sin_t, w1.reshape(WIDE, 256), normed,
        rows, resid, d_resid, gw2s, gwds, attn_gain, mlp_gain, w_q, w_k, w_v, w_gate, w_up,
    )
    output, grad_hidden, g_attn, g_mlp, g_q, g_k, g_v, g_o, g_gate, g_up, g_down = hand_out(grads)
    return (
        output.T, grad_hidden.T, g_attn, g_q, g_k, g_v, g_o, g_mlp, g_gate, g_up, g_down
    )


def solution(mesh):
    both = ("fsdp", "ctx")
    wide, thin, part = P(both, None), P(both), P("fsdp")
    return jax.shard_map(
        local,
        mesh=mesh,
        in_specs=(wide, thin, wide, wide, wide, wide, thin, wide, wide, wide, wide, part, part),
        out_specs=(wide, wide, thin, wide, wide, wide, wide, thin, wide, wide, wide),
        check_vma=False,
    )
```

```python
import jax
import jax.numpy as jnp
import numpy as np
from jax import lax
from jax.experimental import pallas as pl
from jax.experimental.pallas import tpu as pltpu
from jax.sharding import PartitionSpec as P

HEAD = 64
EPSILON = 1e-05
ROPE_BASE = 100000.0
MASKED = -1e30
WIDE = 1024
WIDTH = 960
BF = jnp.bfloat16
F32 = jnp.float32
MESH = pl.DeviceIdType.MESH
DMA = pltpu.SemaphoreType.DMA
ANY = pl.BlockSpec(memory_space=pl.ANY)
VMEM = pl.BlockSpec(memory_space=pltpu.VMEM)
SMEM = pl.BlockSpec(memory_space=pltpu.SMEM)
LIMIT = 56 * 2**20
OWNED_KV = (0, 1, 1, 2, 2, 3, 4, 4)


def dot(a, b):
    return lax.dot_general(a, b, (((1,), (0,)), ((), ())), preferred_element_type=F32)


def dot_nt(a, b):
    return lax.dot_general(a, b, (((1,), (1,)), ((), ())), preferred_element_type=F32)


def dot_tn(a, b):
    return lax.dot_general(a, b, (((0,), (0,)), ((), ())), preferred_element_type=F32)


def shaped(shape, dtype):
    return jax.ShapeDtypeStruct(shape, dtype)


def place():
    i = lax.axis_index("ctx")
    return i // 16, (i // 8) % 2, (i // 2) % 4, i % 2


def at(x, z, y, c):
    return {"ctx": (((x + 4) % 4) * 2 + z) * 8 + ((y + 4) % 4) * 2 + c}


def send(src, dst, ssem, rsem, device):
    copy = pltpu.make_async_remote_copy(
        src, dst, ssem, rsem, device_id=device, device_id_type=MESH
    )
    copy.start()
    return copy


def hail(kinds):
    x, z, y, c = place()
    who = []
    if "x" in kinds:
        who += [at(x + 1, z, y, c), at(x - 1, z, y, c), at(x, 1 - z, y, c)]
    if "f" in kinds:
        who += [at(x, z, y + d, (c + e) % 2) for d in range(4) for e in range(2) if d + e]
    elif "y" in kinds:
        who += [at(x, z, y + d, c) for d in (1, 2, 3)] + [at(x, z, y, 1 - c)]
    barrier = pltpu.get_barrier_semaphore()
    for device in who:
        pl.semaphore_signal(barrier, inc=1, device_id=device, device_id_type=MESH)
    return len(who)


def greet(kinds):
    pl.semaphore_wait(pltpu.get_barrier_semaphore(), hail(kinds))


def half_lead(ref, k):
    n = ref.shape[0] // 2
    return ref.at[pl.ds(k * n, n)]


def half_lanes(ref, k):
    n = ref.shape[-1] // 2
    return ref.at[:, pl.ds(k * n, n)]


class RingGather:
    sems = [DMA((9,)), DMA((9,)), DMA(())]

    def __init__(self, src, dst, half, ssem, rsem, lsem, arrived=None):
        self.src, self.dst, self.half = src, dst, half
        self.ssem, self.rsem, self.lsem = ssem, rsem, lsem
        self.arrived = arrived or (lambda block: None)
        self.copies = {}

    def push(self, n, src, dst, device):
        self.copies[n] = send(src, dst, self.ssem.at[n], self.rsem.at[n], device)

    def start(self):
        x, z, y, c = place()
        me = self.dst.at[x * 2 + z]
        self.push(0, self.src, me, at(x, 1 - z, y, c))
        self.push(1, self.src, me, at(x + 1, z, y, c))
        self.push(2, self.src, me, at(x - 1, z, y, c))
        self.local = pltpu.make_async_copy(self.src, me, self.lsem)
        self.local.start()

    def relay_z(self):
        x, z, y, c = place()
        block = self.dst.at[x * 2 + 1 - z]
        self.copies[0].wait_recv()
        self.push(3, block, block, at(x + 1, z, y, c))
        self.push(4, block, block, at(x - 1, z, y, c))
        self.arrived(x * 2 + 1 - z)

    def relay_x(self, k):
        x, z, y, c = place()
        zz = z if k == 0 else 1 - z
        left, right = ((x + 3) % 4) * 2 + zz, ((x + 1) % 4) * 2 + zz
        self.copies[1 + 2 * k].wait_recv()
        part = self.half(self.dst.at[left], 0)
        self.push(5 + 2 * k, part, part, at(x + 1, z, y, c))
        self.arrived(left)
        self.copies[2 + 2 * k].wait_recv()
        part = self.half(self.dst.at[right], 1)
        self.push(6 + 2 * k, part, part, at(x - 1, z, y, c))
        self.arrived(right)

    def land(self, k):
        x, z, y, c = place()
        zz = z if k == 0 else 1 - z
        self.copies[5 + 2 * k].wait_recv()
        self.copies[6 + 2 * k].wait_recv()
        self.arrived(((x + 2) % 4) * 2 + zz)

    def sent(self):
        for n in range(9):
            self.copies[n].wait_send()

    def finish(self):
        self.local.wait()
        self.sent()


class CrossGather:
    sems = [DMA((8,)), DMA((8,)), DMA(())]

    def __init__(self, src, dst, half, ssem, rsem, lsem, arrived=None):
        self.src, self.dst, self.half = src, dst, half
        self.ssem, self.rsem, self.lsem = ssem, rsem, lsem
        self.arrived = arrived or (lambda block: None)
        self.copies = {}

    def push(self, n, src, dst, device):
        self.copies[n] = send(src, dst, self.ssem.at[n], self.rsem.at[n], device)

    def start(self):
        x, z, y, c = place()
        me = self.dst.at[x * 2 + z]
        self.push(1, self.src, me, at(x + 1, z, y, c))
        self.push(2, self.src, me, at(x - 1, z, y, c))
        self.push(0, self.src, me, at(x, 1 - z, y, c))
        self.local = pltpu.make_async_copy(self.src, me, self.lsem)
        self.local.start()

    def relay(self):
        x, z, y, c = place()
        for n, step, side in ((1, 3, 0), (2, 1, 1)):
            block = ((x + step) % 4) * 2 + z
            whole = self.dst.at[block]
            self.copies[n].wait_recv()
            part = self.half(whole, side)
            self.push(2 + n, part, part, at(x + 4 - step, z, y, c))
            self.push(4 + n, whole, whole, at(x, 1 - z, y, c))
            self.arrived(block)

    def far(self):
        x, z, y, c = place()
        block = ((x + 2) % 4) * 2 + z
        whole = self.dst.at[block]
        self.copies[3].wait_recv()
        self.copies[4].wait_recv()
        self.push(7, whole, whole, at(x, 1 - z, y, c))
        self.arrived(block)

    def land(self):
        x, z, y, c = place()
        for n, step in ((0, 0), (5, 3), (6, 1), (7, 2)):
            self.copies[n].wait_recv()
            self.arrived(((x + step) % 4) * 2 + 1 - z)

    def finish(self):
        self.local.wait()
        for n in range(8):
            self.copies[n].wait_send()


class RowGather:
    sems = [DMA((8,)), DMA((8,)), DMA(())]

    def __init__(self, src, dst, ssem, rsem, lsem):
        self.src, self.dst = src, dst
        self.ssem, self.rsem, self.lsem = ssem, rsem, lsem
        self.copies = {}

    def push(self, n, src, dst, device):
        self.copies[n] = send(src, dst, self.ssem.at[n], self.rsem.at[n], device)

    def start(self):
        x, z, y, c = place()
        me = self.dst.at[y * 2 + c]
        self.push(1, self.src, me, at(x, z, y + 1, c))
        self.push(2, self.src, me, at(x, z, y - 1, c))
        self.push(0, self.src, me, at(x, z, y, 1 - c))
        self.local = pltpu.make_async_copy(self.src, me, self.lsem)
        self.local.start()

    def relay(self):
        x, z, y, c = place()
        for n, step, side in ((1, 3, 0), (2, 1, 1)):
            self.copies[n].wait_recv()
            block = self.dst.at[((y + step) % 4) * 2 + c]
            part = half_lead(block, side)
            self.push(2 + n, part, part, at(x, z, y + 4 - step, c))
            self.push(4 + n, block, block, at(x, z, y, 1 - c))

    def land(self):
        x, z, y, c = place()
        self.copies[3].wait_recv()
        self.copies[4].wait_recv()
        block = self.dst.at[((y + 2) % 4) * 2 + c]
        self.push(7, block, block, at(x, z, y, 1 - c))

    def finish(self):
        self.local.wait()
        for n in (0, 5, 6, 7):
            self.copies[n].wait_recv()
        for n in range(8):
            self.copies[n].wait_send()


class Swap:
    sems = [DMA((8,)), DMA((8,)), DMA(())]

    def __init__(self, src, dst, ssem, rsem, lsem):
        self.src, self.dst = src, dst
        self.ssem, self.rsem, self.lsem = ssem, rsem, lsem

    def start(self):
        x, z, y, c = place()
        me = y * 2 + c
        self.copies = []
        for d in (2, 1, 3, 0):
            for e in (0, 1):
                if d + e:
                    n = d * 2 + e
                    to = ((y + d) % 4) * 2 + (c + e) % 2
                    self.copies.append(
                        send(
                            self.src.at[to],
                            self.dst.at[me],
                            self.ssem.at[n],
                            self.rsem.at[n],
                            at(x, z, y + d, (c + e) % 2),
                        )
                    )
        self.local = pltpu.make_async_copy(self.src.at[me], self.dst.at[me], self.lsem)
        self.local.start()

    def finish(self):
        self.local.wait()
        for copy in self.copies:
            copy.wait()


class RowSum:
    @staticmethod
    def scratch(shape):
        return [
            pltpu.VMEM((4,) + shape, BF),
            pltpu.VMEM((4,) + shape, BF),
            pltpu.VMEM((2, shape[0] // 2) + shape[1:], BF),
            pltpu.VMEM((2,) + shape, BF),
            DMA((8,)),
            DMA((8,)),
        ]

    def __init__(self, blk, first, mixed, parts, heard, ssem, rsem, source=None):
        self.blk, self.first, self.mixed = blk, first, mixed
        self.source = blk if source is None else source
        self.parts, self.heard = parts, heard
        self.ssem, self.rsem = ssem, rsem
        self.copies = {}

    def push(self, n, src, dst, device):
        self.copies[n] = send(src, dst, self.ssem.at[n], self.rsem.at[n], device)

    def hand(self, d):
        x, z, y, c = place()
        to = ((y + d) % 4) * 2 + 1 - c
        self.push(d, self.source.at[to], self.first.at[d], at(x, z, y, 1 - c))

    def start(self):
        for d in (2, 1, 3, 0):
            self.hand(d)

    def both(self, d):
        x, z, y, c = place()
        self.copies[d].wait_recv()
        return self.blk.at[((y + d) % 4) * 2 + c][...].astype(F32) + self.first[d].astype(F32)

    def far(self):
        x, z, y, c = place()
        self.mixed[2] = self.both(2).astype(BF)
        for side, step in ((0, 1), (1, 3)):
            part = half_lead(self.mixed.at[2], side)
            self.push(4 + side, part, self.parts.at[side], at(x, z, y + step, c))

    def near(self):
        x, z, y, c = place()
        for side, step in ((0, 1), (1, 3)):
            sums = self.both(step)
            n = sums.shape[0] // 2
            self.copies[4 + side].wait_recv()
            part = self.parts[side].astype(F32)
            self.mixed[step, pl.ds(side * n, n)] = (sums[side * n : side * n + n] + part).astype(BF)
            self.mixed[step, pl.ds(n - side * n, n)] = sums[n - side * n : 2 * n - side * n].astype(BF)
            self.push(6 + side, self.mixed.at[step], self.heard.at[side], at(x, z, y + step, c))

    def total(self):
        total = self.both(0)
        for side in (0, 1):
            self.copies[6 + side].wait_recv()
            total = total + self.heard[side].astype(F32)
        return total

    def finish(self):
        for n in range(8):
            self.copies[n].wait_send()


class CrossSum:
    @staticmethod
    def scratch(shape, lanes):
        if lanes:
            part = shape[:-1] + (shape[-1] // 2,)
        else:
            part = (shape[0] // 2,) + shape[1:]
        return [
            pltpu.VMEM((4,) + shape, BF),
            pltpu.VMEM((4,) + shape, BF),
            pltpu.VMEM((2,) + part, BF),
            pltpu.VMEM((2,) + shape, BF),
            DMA((8,)),
            DMA((8,)),
        ]

    def __init__(self, blk, lanes, first, mixed, parts, heard, ssem, rsem):
        self.blk, self.half = blk, half_lanes if lanes else half_lead
        self.first, self.mixed, self.parts, self.heard = first, mixed, parts, heard
        self.ssem, self.rsem = ssem, rsem
        self.copies = {}

    def push(self, n, src, dst, device):
        self.copies[n] = send(src, dst, self.ssem.at[n], self.rsem.at[n], device)

    def hand(self, d):
        x, z, y, c = place()
        to = ((x + d) % 4) * 2 + 1 - z
        self.push(d, self.blk.at[to], self.first.at[d], at(x, 1 - z, y, c))

    def both(self, d):
        x, z, y, c = place()
        self.copies[d].wait_recv()
        return self.blk[((x + d) % 4) * 2 + z].astype(F32) + self.first[d].astype(F32)

    def far(self):
        x, z, y, c = place()
        self.mixed[2] = self.both(2).astype(BF)
        for side, step in ((0, 1), (1, 3)):
            part = self.half(self.mixed.at[2], side)
            self.push(4 + side, part, self.parts.at[side], at(x + step, z, y, c))

    def near(self):
        x, z, y, c = place()
        for side, step in ((0, 1), (1, 3)):
            mixed = self.mixed.at[step]
            mixed[...] = self.both(step).astype(BF)
            self.copies[4 + side].wait_recv()
            mine = self.half(mixed, side)
            mine[...] = (mine[...].astype(F32) + self.parts[side].astype(F32)).astype(BF)
            self.push(6 + side, mixed, self.heard.at[side], at(x + step, z, y, c))

    def total(self):
        total = self.both(0)
        for side in (0, 1):
            self.copies[6 + side].wait_recv()
            total = total + self.heard[side].astype(F32)
        return total

    def finish(self):
        for n in range(8):
            self.copies[n].wait_send()


class RingSum:
    @staticmethod
    def scratch(shape, lanes):
        if lanes:
            part = shape[:-1] + (shape[-1] // 2,)
        else:
            part = (shape[0] // 2,) + shape[1:]
        return [
            pltpu.VMEM((4,) + part, BF),
            pltpu.VMEM((4,) + shape, BF),
            pltpu.VMEM((4,) + shape, BF),
            pltpu.VMEM((2,) + shape, BF),
            DMA((9,)),
            DMA((9,)),
        ]

    def __init__(self, blk, lanes, parts, mixed, heard, across, ssem, rsem):
        self.blk, self.half = blk, half_lanes if lanes else half_lead
        self.parts, self.mixed, self.heard, self.across = parts, mixed, heard, across
        self.ssem, self.rsem = ssem, rsem
        self.copies = {}

    def push(self, n, src, dst, device):
        self.copies[n] = send(src, dst, self.ssem.at[n], self.rsem.at[n], device)

    def start(self, k):
        x, z, y, c = place()
        zz = 1 - z if k == 0 else z
        far = self.blk.at[((x + 2) % 4) * 2 + zz]
        self.push(4 * k, self.half(far, 0), self.parts.at[2 * k], at(x + 1, z, y, c))
        self.push(4 * k + 1, self.half(far, 1), self.parts.at[2 * k + 1], at(x - 1, z, y, c))

    def relay(self, k):
        x, z, y, c = place()
        zz = 1 - z if k == 0 else z
        for side, step in ((0, 1), (1, 3)):
            n = 2 * k + side
            mixed = self.mixed.at[n]
            source = self.blk.at[((x + step) % 4) * 2 + zz]
            mine, other = self.half(source, side), self.half(source, 1 - side)
            self.half(mixed, 1 - side)[...] = other[...]
            self.copies[4 * k + side].wait_recv()
            self.half(mixed, side)[...] = (
                mine[...].astype(F32) + self.parts[n].astype(F32)
            ).astype(BF)
            self.push(4 * k + 2 + side, mixed, self.heard.at[n], at(x + step, z, y, c))

    def total(self, k):
        x, z, y, c = place()
        zz = 1 - z if k == 0 else z
        total = self.blk[x * 2 + zz].astype(F32)
        for side in (0, 1):
            self.copies[4 * k + 2 + side].wait_recv()
            total = total + self.heard[2 * k + side].astype(F32)
        if k == 0:
            self.across[0] = total.astype(BF)
            self.push(8, self.across.at[0], self.across.at[1], at(x, 1 - z, y, c))
            return None
        self.copies[8].wait_recv()
        return total + self.across[1].astype(F32)

    def finish(self):
        for n in range(9):
            self.copies[n].wait_send()


def fetch(src, dst, sem):
    copy = pltpu.make_async_copy(src, dst, sem)
    copy.start()
    return copy


def columns_of_gains(gain1, gain2):
    gap = jnp.zeros((1, 113), F32)
    return jnp.concatenate(
        [
            jnp.concatenate([ref[...].astype(F32).reshape(1, 15), gap], axis=1)
            for ref in (gain1, gain2)
        ]
        + [jnp.zeros((126, 128), F32)],
        axis=0,
    ).T[0:15]


def row_of(column):
    wide = jnp.concatenate([column, jnp.zeros((113, 1), F32)], axis=0)
    return jnp.broadcast_to(wide, (128, 128)).T[0:1, 0:15].reshape(15)


def comm_call(name, number, kernel, out_shape, in_specs, out_specs, scratch, args):
    return pl.pallas_call(
        kernel,
        out_shape=out_shape,
        in_specs=in_specs,
        out_specs=out_specs,
        scratch_shapes=scratch,
        compiler_params=pltpu.CompilerParams(
            collective_id=number, has_side_effects=True, vmem_limit_bytes=LIMIT
        ),
        name=name,
    )(*args)


def split(refs, counts):
    parts, begin = [], 0
    for n in counts:
        parts.append(refs[begin : begin + n])
        begin += n
    return parts


def spread_value(rows):
    j = lax.broadcasted_iota(jnp.int32, (rows, WIDE), 0)
    k = lax.broadcasted_iota(jnp.int32, (rows, WIDE), 1)
    hit = ((k // 16) * 15 + k % 16 == j) & (k % 16 < 15)
    return jnp.where(hit, 1.0, 0.0).astype(BF)


def first(
    hidden_t, cot_t, w_q, w_k, w_v, w_o, w_gate, w_up, w_down, gain1, gain2, lengths, span_order, freq
):
    def kernel(
        hidden_t, cot_t, w_q, w_k, w_v, w_o, w_gate, w_up, w_down, gain1, gain2, lengths, order, freq,
        rows_out, w1_out, wds, wo, cot, w2own, normed_out, q_out, kv2, cos_out, sin_out,
        rows, w1, normed, q_rot, cos_t, sin_t, xp, cp, wp1, wp2, wop, wdp, wos, w1own, kv, outs,
        *sems,
    ):
        a, a2, b, d, e, e2, ac, ao, b2, k0, k1, (hs, hr) = split(sems, (3,) * 11 + (2,))
        x, z, y, c = place()
        partners = hail("xf")

        gains = columns_of_gains(gain1, gain2)
        q = jnp.concatenate([w_q[...].astype(F32), jnp.zeros((15, 64), F32)], axis=1)
        q, k, v = (w * gains[:, 0:1] for w in (q, w_k[...].astype(F32), w_v[...].astype(F32)))
        wp1[...] = jnp.zeros(wp1.shape, BF)
        for f in range(8):
            n = OWNED_KV[f] * 64
            wp1[f, 0:15, 0:128] = q[:, 128 * f : 128 * f + 128].astype(BF)
            wp1[f, 0:15, 128:256] = jnp.concatenate(
                [k[:, n : n + 64], v[:, n : n + 64]], axis=1
            ).astype(BF)
        spread = spread_value(WIDTH)
        xp[...] = dot_tn(hidden_t[...], spread).astype(BF)

        wop[...] = jnp.zeros(wop.shape, BF)
        wop[0:15, :] = dot(w_o[...], spread).astype(BF)
        wdp[...] = jnp.zeros(wdp.shape, BF)
        wdp[0:40, :] = dot(w_down[...], spread).astype(BF)

        pl.semaphore_wait(pltpu.get_barrier_semaphore(), partners)
        swap = Swap(wp1, w1own, *b)
        swap.start()
        gathers = []
        for k, own in ((0, a), (64, a2)):
            spot = pl.ds(k, 64)
            gathers.append(RowGather(xp.at[spot], rows.at[:, spot], *own))
        for gather in gathers:
            gather.start()
        early = [CrossGather(wdp, wds, half_lanes, *e2), RingGather(wop, wos, half_lanes, *e)]
        ring_d, ring_o = early
        ring_o.start()
        cp[...] = dot_tn(cot_t[...], spread).astype(BF)

        lane = lanes_of((1, 128))
        sign = jnp.where(lane % 64 < 32, -1.0, 1.0)
        ends = doc_ends(lengths)

        @pl.loop(0, 8)
        def _(n):
            pos = order[(x * 2 + z) * 8 + n] * 128
            pos = pos + lax.broadcasted_iota(jnp.int32, (128, 1), 0)
            angle = (pos - doc_start(pos, ends)).astype(F32) * freq[...]
            part = pl.ds(pl.multiple_of(n * 128, 128), 128)
            cos_t[part, :] = jnp.cos(angle)
            sin_t[part, :] = sign * jnp.sin(angle)

        written = [fetch(cos_t, cos_out, outs.at[0]), fetch(sin_t, sin_out, outs.at[1])]
        wp2[...] = jnp.zeros(wp2.shape, BF)
        gap = jnp.zeros((15, 8), F32)
        for m, ref in ((0, w_gate), (384, w_up)):
            w = ref[...].astype(F32) * gains[:, 1:2]
            for f in range(8):
                parts = []
                for g in range(8):
                    n = (8 * g + f) * 40
                    parts += [w[:, n : n + 40], gap]
                wp2[f, 0:15, m : m + 384] = jnp.concatenate(parts, axis=1).astype(BF)

        ring_o.relay_z()
        swap.finish()
        ring_1 = RingGather(w1own, w1, half_lead, *d)
        ring_1.start()
        ring_d.start()
        ring_o.relay_x(0)
        ring_o.relay_x(1)
        for gather in gathers:
            gather.relay()
        gather_c = RowGather(cp, cot, *ac)
        gather_c.start()
        ring_1.relay_z()
        ring_d.relay()

        for k in (0, 1):
            ring_1.relay_x(k)

        for gather in gathers:
            gather.land()
        for k in (0, 1):
            for ring in (ring_1, ring_o):
                ring.land(k)
        for gather in gathers:
            gather.finish()
        ring_o.local.wait()
        gather_o = RowGather(wos, wo, *ao)
        gather_o.start()
        swap2 = Swap(wp2, w2own, *b2)
        swap2.start()
        ring_1.local.wait()
        written += [fetch(rows, rows_out, outs.at[2]), fetch(w1, w1_out, outs.at[3])]

        w = w1.reshape(WIDE, 256)
        lane = lanes_of((256, 128))

        def project(n):
            part = pl.ds(n * 256, 256)
            xs = jnp.concatenate([rows[2 * n], rows[2 * n + 1]], axis=0).astype(F32)
            v = (xs * inverse_rms(xs)).astype(BF)
            normed[part, :] = v
            out = dot(v, w[...])
            cos_v, sin_v = cos_t[part, :], sin_t[part, :]
            qs, ks = out[:, 0:128], out[:, 128:256]
            qs = (qs * cos_v + partner(qs) * sin_v).astype(BF).astype(F32) * 0.125
            kv[part, :] = jnp.where(lane < 64, ks * cos_v + partner(ks) * sin_v, ks).astype(BF)
            q_rot[0, part, :] = jnp.where(lane < 64, qs, 0.0).astype(BF)
            q_rot[1, part, :] = jnp.where(lane < 64, pltpu.roll(qs, 64, 1), 0.0).astype(BF)

        hand = []

        def pass_on(piece):
            n = len(hand)
            hand.append(send(piece, piece, hs.at[n], hr.at[n], at(x, z, y, 1 - c)))

        key_rings = []
        for h, (kind, own) in enumerate(((RingGather, k0), (CrossGather, k1))):
            mine = kv.at[pl.ds(512 * h, 512)]
            spot = pl.ds(512 * h, 512)
            ring = kind(
                mine,
                kv2.at[c, :, spot],
                half_lead,
                *own,
                arrived=lambda block, spot=spot: pass_on(kv2.at[c, block, spot]),
            )
            project(2 * h)
            project(2 * h + 1)
            ring.start()
            n = len(hand)
            hand.append(
                send(
                    mine, kv2.at[c, x * 2 + z, spot], hs.at[n], hr.at[n], at(x, z, y, 1 - c)
                )
            )
            key_rings.append(ring)
            if h == 0:
                gather_c.relay()

        written += [fetch(normed, normed_out, outs.at[4]), fetch(q_rot, q_out, outs.at[5])]
        ring_a, ring_b = key_rings
        ring_a.relay_z()
        ring_d.far()
        gather_o.relay()
        ring_b.relay()
        ring_a.relay_x(0)
        gather_c.land()
        ring_a.relay_x(1)
        ring_b.far()
        gather_o.land()
        ring_a.land(0)
        ring_a.land(1)
        ring_b.land()
        for copy in hand:
            copy.wait()
        ring_d.land()
        swap2.finish()
        gather_o.finish()
        gather_c.finish()
        for ring in [ring_d] + key_rings:
            ring.finish()
        for ring in (ring_1, ring_o):
            ring.sent()
        for copy in written:
            copy.wait()

    return comm_call(
        "first",
        1,
        kernel,
        (
            shaped((8, 128, WIDE), BF),
            shaped((8, 8, 16, 256), BF),
            shaped((8, 48, WIDE), BF),
            shaped((8, 8, 16, WIDE), BF),
            shaped((8, 128, WIDE), BF),
            shaped((8, 16, 768), BF),
            shaped((1024, WIDE), BF),
            shaped((2, 1024, 128), BF),
            shaped((2, 8, 1024, 128), BF),
            shaped((1024, 128), F32),
            shaped((1024, 128), F32),
        ),
        [VMEM] * 11 + [SMEM, SMEM, VMEM],
        (ANY,) * 11,
        [
            pltpu.VMEM((8, 128, WIDE), BF),
            pltpu.VMEM((8, 8, 16, 256), BF),
            pltpu.VMEM((1024, WIDE), BF),
            pltpu.VMEM((2, 1024, 128), BF),
            pltpu.VMEM((1024, 128), F32),
            pltpu.VMEM((1024, 128), F32),
            pltpu.VMEM((128, WIDE), BF),
            pltpu.VMEM((128, WIDE), BF),
            pltpu.VMEM((8, 16, 256), BF),
            pltpu.VMEM((8, 16, 768), BF),
            pltpu.VMEM((16, WIDE), BF),
            pltpu.VMEM((48, WIDE), BF),
            pltpu.VMEM((8, 16, WIDE), BF),
            pltpu.VMEM((8, 16, 256), BF),
            pltpu.VMEM((1024, 128), BF),
            DMA((6,)),
        ]
        + RowGather.sems * 2
        + Swap.sems
        + RingGather.sems * 2
        + CrossGather.sems
        + RowGather.sems * 2
        + Swap.sems
        + RingGather.sems
        + CrossGather.sems
        + [DMA((16,)), DMA((16,))],
        (
            hidden_t, cot_t, w_q, w_k, w_v, w_o, w_gate, w_up, w_down, gain1, gain2, lengths,
            span_order, freq,
        ),
    )


def inverse_rms(v):
    return lax.rsqrt(jnp.sum(v * v, axis=1, keepdims=True) * (1.0 / WIDTH) + EPSILON)


def feed(att, w2own, wo, rows, wd, cot):
    def kernel(
        att, w2own, wo_in, rows_in, wd_in, cot_in,
        outp_out, resid_out, d_resid, d_heads, gwo_out, gw2_sum, gwd_sum,
        wo, x_in, wd, cot, ins, atts, w2, packed, d_act, resid, normed, act, d_both, dmn, outp,
        gw2, gwd, da, gwo, *refs,
    ):
        a, a2, b, b2, s, r1, r2, t1, t2 = split(refs, (3, 3, 3, 3, 3, 6, 6, 6, 6))
        x, z, y, c = place()
        me = y * 2 + c
        partners = hail("xf")
        pairs = ((wo_in, wo), (cot_in, cot), (wd_in, wd), (rows_in, x_in))
        held = [fetch(src, dst, ins.at[n]) for n, (src, dst) in enumerate(pairs)]
        pl.semaphore_wait(pltpu.get_barrier_semaphore(), partners)
        gathers = []
        for k, own in ((0, a), (512, a2)):
            spot = pl.ds(k, 512)
            gathers.append(RowGather(att.at[spot], atts.at[:, spot], *own))
        low, high = pl.ds(0, 4), pl.ds(4, 4)
        ring_a = RingGather(w2own.at[low], w2.at[:, low], half_lead, *b)
        ring_b = CrossGather(w2own.at[high], w2.at[:, high], half_lead, *b2)
        for part in gathers + [ring_a, ring_b]:
            part.start()

        def place_rows(n, size):
            return pl.ds(pl.multiple_of(n * size, size), size)

        held[0].wait()
        whole = jnp.concatenate([wo[f, g] for g in range(8) for f in range(8)], axis=0)

        def pack(n):
            j = lax.broadcasted_iota(jnp.int32, (512, WIDE), 0) + n * 512
            k = lax.broadcasted_iota(jnp.int32, (512, WIDE), 1)
            hit = ((k // 16) * 15 + k % 16 == j) & (k % 16 < 15)
            packed[pl.ds(n * 512, 512), :] = dot(
                jnp.where(hit, 1.0, 0.0).astype(BF), whole
            ).astype(BF)

        pack(0)
        ring_a.relay_z()
        gathers[0].relay()
        ring_b.relay()
        ring_a.relay_x(0)
        gathers[1].relay()
        pack(1)
        held[1].wait()
        held[2].wait()

        @pl.loop(0, 2)
        def _(n):
            part = place_rows(n, 512)
            d_act[part, :] = dot_nt(cot[part, :], wd[...])

        ring_a.relay_x(1)
        ring_b.far()
        held[3].wait()
        for n, gather in enumerate(gathers):
            gather.land()
            gather.finish()
            part = pl.ds(512 * n, 512)
            heads = jnp.concatenate([atts[f, part, :] for f in range(8)], axis=1)
            v = x_in[part, :].astype(F32) + dot(heads, packed[...])
            resid[part, :] = v
            normed[part, :] = (v * inverse_rms(v)).astype(BF)

        ring_a.land(0)
        ring_a.land(1)
        ring_b.land()
        ring_a.finish()
        ring_b.finish()
        w2_all = w2.reshape(WIDE, 768)

        @pl.loop(0, 2)
        def _(n):
            part = place_rows(n, 512)
            both = dot(normed[part, :], w2_all[...])
            gate, up = both[:, 0:384], both[:, 384:768]
            sigma = 1.0 / (1.0 + jnp.exp(-gate))
            silu = gate * sigma
            act[part, :] = (silu * up).astype(BF)
            d = d_act[part, :]
            d_both[part, 0:384] = (d * up * sigma * (1.0 + gate * (1.0 - sigma))).astype(BF)
            d_both[part, 384:768] = (d * silu).astype(BF)

        sums = [RowSum(dmn.at[:, pl.ds(k, 64)], *own) for k, own in ((0, r1), (64, r2))]
        ring_2, ring_d = RingSum(gw2, False, *t1), CrossSum(gwd, True, *t2)

        def back(core):
            to = [((y + n) % 4) * 2 + core for n in (2, 1, 3, 0)]
            v = jnp.concatenate([d_both[place_rows(n, 128), :] for n in to], axis=0)
            v = dot_nt(v, w2_all[...]).astype(BF)
            for n in range(4):
                dmn[to[n]] = v[128 * n : 128 * n + 128]

        order = [(2, 1), (2, 0), (1, 1), (3, 1), (1, 0), (3, 0), (0, 1), (0, 0)]
        where = [((x + p) % 4) * 2 + (1 - z if q else z) for p, q in order]

        def weights(which):
            v = jnp.concatenate([normed[:, place_rows(where[n], 128)] for n in which], axis=1)
            v = dot_tn(v, d_both[...]).astype(BF)
            for n, m in enumerate(which):
                gw2[where[m]] = v[128 * n : 128 * n + 128].reshape(8, 16, 768)

        weights((0, 1))
        ring_2.start(0)
        ring_2.start(1)
        back(1 - c)
        for d in (2, 1, 3, 0):
            for part in sums:
                part.hand(d)
        gwd[...] = dot_tn(act[...], cot[...]).astype(BF).reshape(8, 48, WIDE)
        for d in (2, 1, 3, 0):
            ring_d.hand(d)
        back(c)
        for part in sums:
            part.far()
        weights((2, 3, 4, 5, 6, 7))
        for part in sums:
            part.near()
        ring_2.relay(0)
        ring_d.far()

        @pl.loop(0, 2)
        def _(n):
            v = dot(act[place_rows(n, 512), :], wd[...]).astype(BF)
            for k in range(4):
                outp[n * 4 + k] = v[128 * k : 128 * k + 128]

        written = [fetch(outp, outp_out, ins.at[5])]
        ring_2.relay(1)

        mine = place_rows(me, 128)
        v = resid[mine, :]
        inv = inverse_rms(v)
        e = jnp.concatenate([part.total() for part in sums], axis=0)
        mean = jnp.sum(e * v, axis=1, keepdims=True) * (1.0 / WIDTH)
        d_v = cot[mine, :].astype(F32) + inv * e - v * (inv * inv * inv * mean)
        d_resid[...] = d_v
        mixed = d_v.astype(BF)
        d_att = dot_nt(mixed, packed[...]).astype(BF)
        for f in range(8):
            da[f] = d_att[:, f * 128 : (f + 1) * 128]
        swap = Swap(da, d_heads, *s)
        swap.start()
        ring_d.near()
        ring_2.total(0)
        spread = spread_value(WIDE)
        heads = jnp.concatenate([atts[f, mine, :] for f in range(8)], axis=1)
        gw = dot_tn(dot(heads, spread).astype(BF), mixed).astype(BF)
        for g in range(8):
            for f in range(8):
                n = (8 * g + f) * 16
                gwo[f, g * 16 : (g + 1) * 16, :] = gw[n : n + 16]
        written += [fetch(gwo, gwo_out, ins.at[4])]
        resid_out[...] = v
        gw2_sum[...] = ring_2.total(1).astype(BF)
        gwd_sum[...] = ring_d.total()
        swap.finish()
        for part in sums:
            part.finish()
        ring_2.finish()
        ring_d.finish()
        for copy in written:
            copy.wait()

    return comm_call(
        "feed",
        3,
        kernel,
        (
            shaped((8, 128, WIDE), BF),
            shaped((128, WIDE), F32),
            shaped((128, WIDE), F32),
            shaped((8, 128, 128), BF),
            shaped((8, 128, WIDE), BF),
            shaped((8, 16, 768), BF),
            shaped((48, WIDE), F32),
        ),
        [ANY] * 6,
        (ANY, VMEM, VMEM, ANY, ANY, VMEM, VMEM),
        [
            pltpu.VMEM((8, 8, 16, WIDE), BF),
            pltpu.VMEM((1024, WIDE), BF),
            pltpu.VMEM((384, WIDE), BF),
            pltpu.VMEM((1024, WIDE), BF),
            DMA((6,)),
            pltpu.VMEM((8, 1024, 128), BF),
            pltpu.VMEM((8, 8, 16, 768), BF),
            pltpu.VMEM((WIDE, WIDE), BF),
            pltpu.VMEM((1024, 384), F32),
            pltpu.VMEM((1024, WIDE), F32),
            pltpu.VMEM((1024, WIDE), BF),
            pltpu.VMEM((1024, 384), BF),
            pltpu.VMEM((1024, 768), BF),
            pltpu.VMEM((8, 128, WIDE), BF),
            pltpu.VMEM((8, 128, WIDE), BF),
            pltpu.VMEM((8, 8, 16, 768), BF),
            pltpu.VMEM((8, 48, WIDE), BF),
            pltpu.VMEM((8, 128, 128), BF),
            pltpu.VMEM((8, 128, WIDE), BF),
        ]
        + RowGather.sems * 2
        + RingGather.sems
        + CrossGather.sems
        + Swap.sems
        + RowSum.scratch((64, WIDE)) * 2
        + RingSum.scratch((8, 16, 768), False)
        + CrossSum.scratch((48, WIDE), True),
        (att, w2own, wo, rows, wd, cot),
    )


def last(
    dkv, gwo, outp, dq, cos_t, sin_t, w1, normed, rows, resid, d_resid, gw2s, gwd, gain1, gain2,
    w_q, w_k, w_v, w_gate, w_up,
):
    def kernel(
        dkv, gwo_in, outp_in, dq_in, cos_in, sin_in, w1_in, normed_in, rows_in, resid, dr, gw2s, wd,
        gain1, gain2,
        w_q, w_k, w_v, w_gate, w_up,
        output, gh, g_attn, g_mlp, g_q, g_k, g_v, g_o, g_gate, g_up, g_down,
        own, gwo, outp, dq, cos_t, sin_t, w1, normed, rows, ins,
        blk_a, blk_b, from_core, gwos, gw1, dnq, d_kv, dn, one, two, gw1s, hs, hr, *refs,
    ):
        a, a2, b, b2, d, d2, e, e2, s1, s2 = split(refs, (6, 6, 6, 6, 6, 6, 6, 6, 3, 3))
        x, z, y, c = place()
        me = y * 2 + c
        partners = hail("xf")
        pairs = [
            (gwo_in, gwo),
            (dkv.at[c], own),
            (dq_in, dq),
            (cos_in, cos_t),
            (sin_in, sin_t),
            (w1_in, w1),
            (normed_in, normed),
            (rows_in.at[me], rows),
            (outp_in, outp),
        ]
        held = {n: fetch(*pairs[n], ins.at[n]) for n in (0, 8, 1)}
        pl.semaphore_wait(pltpu.get_barrier_semaphore(), partners)
        order = [(2, 1), (2, 0), (1, 1), (3, 1), (0, 1), (1, 0), (3, 0), (0, 0)]
        where = [((x + p) % 4) * 2 + (1 - z if q else z) for p, q in order]
        sum_w = RowSum(gwo, *b, source=gwo_in)
        sum_o = RowSum(outp, *b2, source=outp_in)
        ring_a, ring_b = RingSum(blk_a, False, *a), CrossSum(blk_b, False, *a2)
        hand = {}

        def pass_on(n):
            hand[n] = send(
                dkv.at[1 - c, where[n]], from_core.at[n], hs.at[n], hr.at[n], at(x, z, y, 1 - c)
            )

        swap2 = Swap(gw2s, two, *s2)
        swap2.start()
        sum_w.hand(2)
        sum_o.hand(2)
        pass_on(0)
        pass_on(1)
        for step in (1, 3):
            sum_w.hand(step)
            sum_o.hand(step)
        for n in (2, 3, 4):
            pass_on(n)
        sum_w.hand(0)
        sum_o.hand(0)
        for n in (5, 6, 7):
            pass_on(n)
        for n in range(2, 8):
            held[n] = fetch(*pairs[n], ins.at[n])

        def fold(n):
            g = where[n]
            hand[n].wait_recv()
            both = (own[g].astype(F32) + from_core[n].astype(F32)).astype(BF)
            blk_a[g] = both[0:512]
            blk_b[g] = both[512:1024]

        held[0].wait()
        sum_w.far()
        held[8].wait()
        sum_o.far()
        held[1].wait()
        fold(0)
        ring_a.start(0)
        ring_b.hand(2)
        fold(1)
        ring_a.start(1)
        for n, step in ((2, 1), (3, 3), (4, 0)):
            fold(n)
            ring_b.hand(step)
        ring_a.relay(0)
        ring_b.far()
        fold(5)
        fold(6)
        ring_a.relay(1)
        sum_w.near()
        fold(7)
        ring_b.near()
        ring_a.total(0)
        sum_o.near()
        for n in range(2, 6):
            held[n].wait()
        spread = spread_value(WIDTH)
        gains = columns_of_gains(gain1, gain2)

        def place_rows(n, size):
            return pl.ds(pl.multiple_of(n * size, size), size)

        def queries(n):
            part = place_rows(n, 512)
            v = dq[part, :]
            v = (v * cos_t[part, :] - partner(v) * sin_t[part, :]).astype(BF)
            d_kv[part, 0:128] = v
            dnq[part, :] = dot_nt(v, w1[:, 0:128])

        queries(0)
        queries(1)
        held[6].wait()
        gw1[:, :, :, 0:128] = (
            dot_tn(normed[...], d_kv[:, 0:128]).astype(BF).reshape(8, 8, 16, 128)
        )
        swap2.finish()
        total = jnp.zeros((15, 1), F32)
        for m, ref, w in ((0, g_gate, w_gate), (384, g_up, w_up)):
            for n in range(0, 8, 2):
                part = jnp.concatenate(
                    [
                        two[f, :, m + 48 * k : m + 48 * k + 40].astype(F32)[0:15]
                        for k in (n, n + 1)
                        for f in range(8)
                    ],
                    axis=1,
                )
                spot = pl.ds(n * 320, 640)
                ref[:, spot] = part * gains[:, 1:2]
                total += jnp.sum(part * w[:, spot].astype(F32), axis=1, keepdims=True)
        g_mlp[...] = row_of(total)

        def squeeze(v):
            top = v.astype(BF)
            low = (v - top.astype(F32)).astype(BF)
            return dot_nt(top, spread) + dot_nt(low, spread)

        g_down[...] = squeeze(wd[...])[0:40]
        v = jnp.concatenate([ring_a.total(1), ring_b.total()], axis=0)
        turned = v * cos_t[...] - partner(v) * sin_t[...]
        d_kv[:, 128:256] = jnp.where(lanes_of((1024, 128)) < 64, turned, v).astype(BF)
        sums = [RowSum(dn.at[:, pl.ds(k, 64)], *own) for k, own in ((0, d), (64, d2))]

        def back(core):
            to = [((y + n) % 4) * 2 + core for n in (2, 1, 3, 0)]
            parts = [place_rows(n, 128) for n in to]
            v = jnp.concatenate([d_kv[p, 128:256] for p in parts], axis=0)
            v = dot_nt(v, w1[:, 128:256])
            for n, p in enumerate(parts):
                dn[to[n]] = (dnq[p, :] + v[128 * n : 128 * n + 128]).astype(BF)

        back(1 - c)
        for n in (2, 1, 3, 0):
            for part in sums:
                part.hand(n)
        ring_1 = RingSum(gw1, False, *e)

        def weights_k(which):
            parts = [place_rows(where[n], 128) for n in which]
            v = jnp.concatenate([normed[:, p] for p in parts], axis=1)
            v = dot_tn(v, d_kv[:, 128:256]).astype(BF)
            for n, m in enumerate(which):
                gw1[where[m], :, :, 128:256] = v[128 * n : 128 * n + 128].reshape(8, 16, 128)

        weights_k((0, 1))
        ring_1.start(0)
        ring_1.start(1)
        gwos[...] = sum_w.total().astype(BF).reshape(8, 16, WIDE)
        ring_o = RingSum(gwos, True, *e2)
        ring_o.start(0)
        ring_o.start(1)
        back(c)
        for part in sums:
            part.far()
        weights_k((2, 3, 4, 5, 6, 7))
        for part in sums:
            part.near()
        for k in (0, 1):
            ring_1.relay(k)
            ring_o.relay(k)
        ring_1.total(0)
        ring_o.total(0)
        gw1s[...] = ring_1.total(1).astype(BF)
        swap1 = Swap(gw1s, one, *s1)
        swap1.start()
        output[...] = dot_nt(spread, (resid[...] + sum_o.total()).astype(BF)).astype(BF)
        g_o[...] = squeeze(ring_o.total(1))[0:15]

        held[7].wait()
        xs = rows[...].astype(F32)
        inv = inverse_rms(xs)
        t = jnp.concatenate([part.total() for part in sums], axis=0)
        mean = jnp.sum(t * xs, axis=1, keepdims=True) * (1.0 / WIDTH)
        d_x = dr[...] + inv * t - xs * (inv * inv * inv * mean)
        gh[...] = dot_nt(spread, d_x.astype(BF)).astype(BF)
        swap1.finish()
        ones = [one[f].astype(F32)[0:15] for f in range(8)]
        r_q = jnp.concatenate([v[:, 0:128] for v in ones], axis=1)[:, 0:WIDTH]

        def heads(n):
            return jnp.concatenate(
                [
                    sum(ones[f][:, n : n + 64] for f in range(8) if OWNED_KV[f] == h)
                    for h in range(5)
                ],
                axis=1,
            )

        total = jnp.zeros((15, 1), F32)
        for part, w, ref in ((r_q, w_q, g_q), (heads(128), w_k, g_k), (heads(192), w_v, g_v)):
            ref[...] = part * gains[:, 0:1]
            total += jnp.sum(part * w[...].astype(F32), axis=1, keepdims=True)
        g_attn[...] = row_of(total)
        for copy in hand.values():
            copy.wait_send()
        ring_a.finish()
        ring_b.finish()
        ring_1.finish()
        ring_o.finish()
        sum_w.finish()
        sum_o.finish()
        for part in sums:
            part.finish()

    return comm_call(
        "last",
        6,
        kernel,
        (
            shaped((WIDTH, 128), BF),
            shaped((WIDTH, 128), BF),
            shaped((15,), F32),
            shaped((15,), F32),
            shaped((15, WIDTH), F32),
            shaped((15, 320), F32),
            shaped((15, 320), F32),
            shaped((15, WIDTH), F32),
            shaped((15, 2560), F32),
            shaped((15, 2560), F32),
            shaped((40, WIDTH), F32),
        ),
        [ANY] * 9 + [VMEM] * 11,
        (VMEM,) * 11,
        [
            pltpu.VMEM((8, 1024, 128), BF),
            pltpu.VMEM((8, 128, WIDE), BF),
            pltpu.VMEM((8, 128, WIDE), BF),
            pltpu.VMEM((1024, 128), F32),
            pltpu.VMEM((1024, 128), F32),
            pltpu.VMEM((1024, 128), F32),
            pltpu.VMEM((WIDE, 256), BF),
            pltpu.VMEM((1024, WIDE), BF),
            pltpu.VMEM((128, WIDE), BF),
            DMA((9,)),
            pltpu.VMEM((8, 512, 128), BF),
            pltpu.VMEM((8, 512, 128), BF),
            pltpu.VMEM((8, 1024, 128), BF),
            pltpu.VMEM((8, 16, WIDE), BF),
            pltpu.VMEM((8, 8, 16, 256), BF),
            pltpu.VMEM((1024, WIDE), F32),
            pltpu.VMEM((1024, 256), BF),
            pltpu.VMEM((8, 128, WIDE), BF),
            pltpu.VMEM((8, 16, 256), BF),
            pltpu.VMEM((8, 16, 768), BF),
            pltpu.VMEM((8, 16, 256), BF),
            DMA((8,)),
            DMA((8,)),
        ]
        + RingSum.scratch((512, 128), False)
        + CrossSum.scratch((512, 128), False)
        + RowSum.scratch((128, WIDE)) * 2
        + RowSum.scratch((64, WIDE)) * 2
        + RingSum.scratch((8, 16, 256), False)
        + RingSum.scratch((16, WIDE), True)
        + Swap.sems * 2,
        (
            dkv, gwo, outp, dq, cos_t, sin_t, w1, normed, rows, resid, d_resid, gw2s, gwd, gain1,
            gain2, w_q, w_k, w_v, w_gate, w_up,
        ),
    )


def lanes_of(shape):
    return lax.broadcasted_iota(jnp.int32, shape, len(shape) - 1)


def partner(v):
    lane = lanes_of(v.shape)
    return jnp.where(lane % 64 < 32, pltpu.roll(v, 96, 1), pltpu.roll(v, 32, 1))


def doc_ends(lengths):
    return lengths[0], lengths[0] + lengths[1]


def doc_start(pos, ends):
    return jnp.where(pos < ends[0], 0, jnp.where(pos < ends[1], ends[0], ends[1]))

def layout(order, inverse):
    @pl.loop(0, 64)
    def _(n):
        inverse[order[n]] = n

    i = lax.axis_index("ctx")
    f = i % 8
    upper = (f == 3) | (f == 5)
    return i // 8, (
        jnp.where(upper, 1, 0),
        jnp.where(upper | (f == 1) | (f == 4), 1, 0),
    )


def key_range(span, ends):
    begin = doc_start(span * 128, ends) // 128
    count = span - begin + 1
    runs = (count + 3) // 8
    return begin, runs, jnp.where(count > runs * 8, 1, 0)


def attend(lengths, order, q, kv):
    def kernel(lengths, order, q_ref, kv_ref, o_ref, lse_ref, s_ref, inverse):
        group, sel = layout(order, inverse)
        ends = doc_ends(lengths)

        @pl.loop(0, 8)
        def _(b):
            span = order[group * 8 + b]
            begin, runs, rest = key_range(span, ends)
            pos = span * 128 + lanes_of((1, 256)) % 128
            low = doc_start(pos, ends)
            rows = pl.ds(pl.multiple_of(b * 128, 128), 128)
            none = jnp.zeros((128, 128), BF)
            pair = jnp.concatenate(
                [
                    jnp.concatenate([q_ref[0, rows, :], none], axis=1),
                    jnp.concatenate([none, q_ref[1, rows, :]], axis=1),
                ],
                axis=0,
            )

            def load(h, t, n):
                return jnp.concatenate(
                    [
                        kv_ref[sel[h], pl.ds(inverse[jnp.minimum(t + i, 63)] * 128, 128), :]
                        for i in range(n)
                    ],
                    axis=0,
                )

            def held(t, n):
                return pl.ds(pl.multiple_of((t - begin) * 128, 512), n * 128)

            def scores(n, t, high):
                kpos = t * 128 + lax.broadcasted_iota(jnp.int32, (n * 128, 1), 0)
                allowed = (kpos >= low) & (kpos <= pos)
                keys = jnp.concatenate([load(0, t, n), load(1, t, n)], axis=1)
                s = jnp.where(allowed, dot_nt(keys, pair), MASKED)
                s_ref[held(t, n), :] = s
                return jnp.maximum(high, jnp.max(s.reshape(n * 16, 8, 256), axis=0))

            def over(step, state):
                state = lax.fori_loop(0, runs, lambda j, v: step(8, begin + j * 8, v), state)
                return lax.fori_loop(0, rest, lambda j, v: step(4, begin + runs * 8, v), state)

            high = over(scores, jnp.full((8, 256), MASKED, F32))
            high = jnp.max(high, axis=0, keepdims=True)

            def weigh(n, t, state):
                total, acc = state
                p = jnp.exp(s_ref[held(t, n), :] - high)
                total = total + jnp.sum(p.reshape(n * 16, 8, 256), axis=0)
                values = jnp.where(lanes_of((n * 128, 128)) < 64, pltpu.roll(load(0, t, n), 64, 1), load(1, t, n))
                return total, acc + dot_tn(values, p.astype(BF))

            total, acc = over(weigh, (jnp.zeros((8, 256), F32), jnp.zeros((128, 256), F32)))
            total = jnp.sum(total, axis=0, keepdims=True)
            lse = high + jnp.log(total)
            lse_ref[b, 0:1, :] = lse[:, 0:128]
            lse_ref[b, 1:2, :] = lse[:, 128:256]
            acc = acc / total
            acc = jnp.concatenate([acc[0:64, 0:128], acc[64:128, 128:256]], axis=0)
            o_ref[rows, :] = acc.T.astype(BF)

    return pl.pallas_call(
        kernel,
        in_specs=[SMEM, SMEM, VMEM, VMEM],
        out_specs=(VMEM, VMEM),
        scratch_shapes=[pltpu.VMEM((40 * 128, 256), F32), pltpu.SMEM((64,), jnp.int32)],
        out_shape=(shaped((1024, 128), BF), shaped((8, 8, 128), F32)),
        compiler_params=pltpu.CompilerParams(vmem_limit_bytes=LIMIT),
        name="attend",
    )(lengths, order, q, kv)


def attend_back(lengths, order, q, kv, d_att, att, lse):
    def kernel(
        lengths, order, q_ref, kv_in, d_ref, o_ref, lse_ref, dq_ref, dkv_out, acc_ref, inverse,
        kv_ref, dkv_ref, sems,
    ):
        held = fetch(kv_in, kv_ref, sems.at[16])
        lane = lanes_of((128, 128))
        group, sel = layout(order, inverse)
        ends = doc_ends(lengths)

        @pl.loop(0, 16)
        def _(n):
            for s in (0, 1):
                part = pl.ds(pl.multiple_of(n * 512, 512), 512)
                acc_ref[s, part, :] = jnp.zeros((512, 128), F32)

        held.wait()

        @pl.loop(0, 8)
        def _(b):
            span = order[group * 8 + b]
            begin, runs, rest = key_range(span, ends)
            pos = span * 128 + lanes_of((1, 128))
            low = doc_start(pos, ends)
            rows = pl.ds(pl.multiple_of(b * 128, 128), 128)
            d_both = d_ref[rows, :].astype(F32)
            d_pad = (
                jnp.where(lane >= 64, pltpu.roll(d_both, 64, 1), 0.0).astype(BF),
                jnp.where(lane >= 64, d_both, 0.0).astype(BF),
            )
            pair = [jnp.concatenate([q_ref[h, rows, :], d_pad[h]], axis=0) for h in (0, 1)]
            mixed = (d_both * o_ref[rows, :].astype(F32)).T
            delta = [jnp.sum(mixed[64 * h : 64 * h + 64], axis=0, keepdims=True) for h in (0, 1)]
            lses = [lse_ref[b, h : h + 1, :] for h in (0, 1)]

            def step(n, t, state):
                where = [inverse[jnp.minimum(t + i, 63)] * 128 for i in range(n)]
                where = [pl.ds(pl.multiple_of(v, 128), 128) for v in where]
                kpos = t * 128 + lax.broadcasted_iota(jnp.int32, (n * 128, 1), 0)
                allowed = (kpos >= low) & (kpos <= pos)
                d_ss, kvs = [], []
                for h in (0, 1):
                    kv_t = jnp.concatenate([kv_ref[sel[h], w, :] for w in where], axis=0)
                    kvs.append(kv_t)
                    both = dot_nt(kv_t, pair[h])
                    p = jnp.where(allowed, jnp.exp(both[:, 0:128] - lses[h]), 0.0)
                    d_s = (p * (both[:, 128:256] - delta[h])).astype(BF)
                    d_ss.append(d_s)
                    d_kv = dot(jnp.concatenate([d_s, p.astype(BF)], axis=1), pair[h])
                    for i, w in enumerate(where):
                        acc_ref[sel[h], w, :] += d_kv[i * 128 : (i + 1) * 128]
                lanes = lanes_of((n * 128, 128))
                keys = jnp.where(lanes < 64, kvs[0], pltpu.roll(kvs[1], 64, 1))
                return state + dot_tn(keys, jnp.concatenate(d_ss, axis=1))

            state = jnp.zeros((128, 256), F32)
            state = lax.fori_loop(0, runs, lambda j, v: step(8, begin + j * 8, v), state)
            state = lax.fori_loop(0, rest, lambda j, v: step(4, begin + runs * 8, v), state)
            state = jnp.concatenate([state[0:64, 0:128], state[64:128, 128:256]], axis=0)
            dq_ref[rows, :] = state.T * 0.125

        written = []
        for n in range(8):
            for s in (0, 1):
                part = pl.ds(n * 1024, 1024)
                dkv_ref[s, part, :] = acc_ref[s, part, :].astype(BF)
                written.append(
                    fetch(dkv_ref.at[s, part], dkv_out.at[s, part], sems.at[2 * n + s])
                )
        for copy in written:
            copy.wait()

    return pl.pallas_call(
        kernel,
        in_specs=[SMEM, SMEM, VMEM, ANY] + [VMEM] * 3,
        out_specs=(VMEM, ANY),
        scratch_shapes=[
            pltpu.VMEM((2, 8192, 128), F32),
            pltpu.SMEM((64,), jnp.int32),
            pltpu.VMEM((2, 8192, 128), BF),
            pltpu.VMEM((2, 8192, 128), BF),
            DMA((17,)),
        ],
        out_shape=(shaped((1024, 128), F32), shaped((2, 8192, 128), BF)),
        compiler_params=pltpu.CompilerParams(vmem_limit_bytes=LIMIT),
        name="attend_back",
    )(lengths, order, q, kv, d_att, att, lse)


def hand_out(parts):
    def kernel(*refs):
        for src, dst in zip(refs[: len(parts)], refs[len(parts) :]):
            dst[...] = src[...]

    return pl.pallas_call(
        kernel,
        out_shape=tuple(shaped(v.shape, v.dtype) for v in parts),
        in_specs=[VMEM] * len(parts),
        out_specs=(VMEM,) * len(parts),
        compiler_params=pltpu.CompilerParams(vmem_limit_bytes=LIMIT),
        name="hand_out",
    )(*parts)


def local(
    hidden, attn_gain, w_q, w_k, w_v, w_o, mlp_gain, w_gate, w_up, w_down, cotangent,
    doc_lengths, span_order,
):
    frequency = ROPE_BASE ** (-2.0 * (np.arange(128) % 32) / HEAD)
    frequency = jnp.asarray(frequency, F32).reshape(1, 128)

    rows, w1, wds, wo, cot, w2own, normed, q, kv, cos_t, sin_t = first(
        hidden.T, cotangent.T, w_q, w_k, w_v, w_o, w_gate, w_up, w_down, attn_gain, mlp_gain,
        doc_lengths, span_order, frequency,
    )
    kv = kv.reshape(2, 8192, 128)
    att, lse = attend(doc_lengths, span_order, q, kv)
    outp, resid, d_resid, d_heads, gwo, gw2s, gwds = feed(
        att, w2own, wo, rows.reshape(1024, WIDE), wds.reshape(384, WIDE), cot.reshape(1024, WIDE)
    )
    d_att = d_heads.reshape(1024, 128)
    dq, dkv = attend_back(doc_lengths, span_order, q, kv, d_att, att, lse)
    grads = last(
        dkv.reshape(2, 8, 1024, 128), gwo, outp, dq, cos_t, sin_t, w1.reshape(WIDE, 256), normed,
        rows, resid, d_resid, gw2s, gwds, attn_gain, mlp_gain, w_q, w_k, w_v, w_gate, w_up,
    )
    output, grad_hidden, g_attn, g_mlp, g_q, g_k, g_v, g_o, g_gate, g_up, g_down = hand_out(grads)
    return (
        output.T, grad_hidden.T, g_attn, g_q, g_k, g_v, g_o, g_mlp, g_gate, g_up, g_down
    )


def solution(mesh):
    both = ("fsdp", "ctx")
    wide, thin, part = P(both, None), P(both), P("fsdp")
    return jax.shard_map(
        local,
        mesh=mesh,
        in_specs=(wide, thin, wide, wide, wide, wide, thin, wide, wide, wide, wide, part, part),
        out_specs=(wide, wide, thin, wide, wide, wide, wide, thin, wide, wide, wide),
        check_vma=False,
    )
```
